32 devices in a mesh: row: 4 (over z), col: 8 (over y, x, core).
Axes of the slice: x: 2, y: 2, z: 4, core: 2. Of those that a mesh axis runs over, the one named last changes fastest.
Arguments:
- config: float32 [6, 4096], P(None, ('row', 'col')), as said below
- start: float32 [6, 4096], P(None, ('row', 'col')), may hold values from -6 to 6
- tile_list: int32 [4, 8, 8, 5], P('row', 'col'), may hold values from -1 to 7, as said below
- tile_count: int32 [4, 8], P('row', 'col'), may hold values from 1 to 8, as said below
Outputs:
- coefficients: float32 [4], replicated
- mode: float32 [6, 4096], P(None, ('row', 'col'))
The draws below stay inside these ranges and needn't reach their ends.
Inputs may be any that keep to these rules, and one draw needn't show every extreme that they name: `tile_list`: entry k of device (r, c) is used when k < tile_count[r, c]; its first value is a row tile 0 to 7, its second a column tile 0 to 3, the last three are offsets in -1, 0, 1, not all zero. Unused entries hold values of the same law. `tile_count`: some device uses all 8 entries. `config`: rows 3 to 5 are unit vectors. No two ellipsoids intersect, within a tile or across tiles placed by a list entry's offsets.
All inputs are finite; a program needn't handle non-finite values.
Results may differ from the reference program's by a relative error of at most 0.0003.
Values sent between devices are 32-bit elements; how exact they have to be, the bound alone decides.
No kernel may reach another device: no remote copies, remote signals or barrier semaphores. Data moves between devices by JAX's collectives and lax.ppermute only.
A program may use at most 64 MiB of HBM per device.

```python
import math
import jax
import jax.numpy as jnp
from jax import lax

TILE = 128
MAXT = 8
PARTICLES = 4096
N_ROW = 4
N_COL = 8


def draw_config(key, part):
    keys = jax.random.split(jax.random.fold_in(key, 5), 5)
    ordinal = jnp.arange(PARTICLES, dtype=jnp.int32) % TILE
    lattice_x = (ordinal % 4).astype(jnp.float32) * 1.25
    lattice_y = (ordinal // 4 % 4).astype(jnp.float32) * 1.25
    lattice_z = (ordinal // 16).astype(jnp.float32) * 3.5
    shake_xy = jax.random.uniform(keys[0], (2, PARTICLES), jnp.float32, -0.06, 0.06)
    tilt = jax.random.uniform(keys[3], (PARTICLES,), jnp.float32, 0.0, 0.25)
    shake_z = jax.random.uniform(keys[2], (PARTICLES,), jnp.float32, -0.1, 0.1)
    turn = jax.random.uniform(keys[4], (PARTICLES,), jnp.float32, 0.0, 2.0 * math.pi)
    rows = [lattice_x + shake_xy[0], lattice_y + shake_xy[1], lattice_z + shake_z, jnp.sin(tilt) * jnp.cos(turn), jnp.sin(tilt) * jnp.sin(turn), jnp.cos(tilt)]
    return jnp.stack(rows).astype(jnp.float32)


def list_tables(key):
    keys = jax.random.split(jax.random.fold_in(key, 71), 8)
    row_ids = jnp.arange(N_ROW, dtype=jnp.int32)[:, None]
    col_ids = jnp.arange(N_COL, dtype=jnp.int32)[None, :]
    first = jax.random.randint(keys[0], (N_ROW, N_COL, MAXT), 0, N_COL, dtype=jnp.int32)
    second = jax.random.randint(keys[1], (N_ROW, N_COL, MAXT), 0, N_ROW, dtype=jnp.int32)
    rotate_a = jax.random.randint(keys[2], (), 0, N_COL, dtype=jnp.int32)
    rotate_b = jax.random.randint(keys[3], (), 0, N_ROW, dtype=jnp.int32)
    first = first.at[:, :, 0].set((col_ids + row_ids + rotate_a) % N_COL)
    second = second.at[:, :, 0].set((row_ids + col_ids + rotate_b) % N_ROW)
    chosen = jax.random.randint(keys[4], (N_ROW, N_COL, MAXT), 0, 26, dtype=jnp.int32)
    code = chosen + (chosen >= 13).astype(jnp.int32)
    offset_x = code // 9 - 1
    offset_y = code // 3 % 3 - 1
    offset_z = code % 3 - 1
    table = jnp.stack([first, second, offset_x, offset_y, offset_z], axis=-1).astype(jnp.int32)
    factor_a = jax.random.randint(keys[5], (N_ROW * N_COL,), 0, MAXT, dtype=jnp.int32)
    factor_b = jax.random.randint(keys[6], (N_ROW * N_COL,), 0, MAXT, dtype=jnp.int32)
    counts = 1 + factor_a * factor_b // MAXT
    busiest = jax.random.randint(keys[7], (), 0, N_ROW * N_COL, dtype=jnp.int32)
    counts = counts.at[busiest].set(MAXT)
    return (table, counts.reshape(N_ROW, N_COL).astype(jnp.int32))


def draw_tile_list(key, part):
    return list_tables(key)[0]


def draw_tile_count(key, part):
    return list_tables(key)[1]


def level_of(rng, shape, cuts, smallest, largest):
    def one(axis_at, shards_of):
        heights = jax.random.uniform(jax.random.fold_in(jax.random.fold_in(rng, 6), axis_at), (shards_of,), jnp.float32, smallest / len(cuts), largest / len(cuts))
        return jnp.repeat(jnp.exp(heights), shape[axis_at] // shards_of).reshape((-1,) + (1,) * (len(shape) - axis_at - 1))

    loudness = one(*cuts[0])
    for cut in cuts[1:]:
        loudness = loudness * one(*cut)
    return loudness


def bell_draw(key, extent, width, limit, shards=(), kind=jnp.bfloat16):
    drawn = jax.random.normal(key, extent, jnp.float32) * width
    if len(shards) > 0:
        drawn = level_of(key, extent, shards, -0.22, 0.18) * drawn
    return jnp.clip(drawn, min=-limit, max=limit).astype(kind)


def setup_inputs(seed: int = 0) -> dict:
    key_list = jax.random.split(jax.random.key(seed), 5)
    config = draw_config(jax.random.fold_in(key_list[4], 71), 0)
    start = bell_draw(key_list[1], (6, PARTICLES), 1.0, 6.0, ((1, 32),), jnp.float32)
    tile_list = draw_tile_list(jax.random.fold_in(key_list[4], 71), 0)
    tile_count = draw_tile_count(jax.random.fold_in(key_list[4], 71), 0)
    return dict(config=config, start=start, tile_list=tile_list, tile_count=tile_count)


chi_shape = 0.8
chi_energy = (math.sqrt(5.0) - 1.0) / (math.sqrt(5.0) + 1.0)
well_depth = 0.005
cutoff_sq = 20.25
norm_eps = 1e-06

def rotate(heading, turn):
    moved = heading + jnp.cross(turn, heading, axis=0)
    return moved / jnp.sqrt(lax.optimization_barrier(jnp.sum(moved * moved, axis=0, keepdims=True)))

def place(frame, dof):
    return (frame[:3] + dof[:3], rotate(frame[3:], dof[3:]))

def pair_energy(separation, left_axis, right_axis):
    distance_sq = lax.optimization_barrier(jnp.sum(separation * separation, axis=0))
    distance = jnp.sqrt(distance_sq)
    direction = separation / distance
    along_left = lax.optimization_barrier(jnp.sum(direction * left_axis, axis=0))
    along_right = lax.optimization_barrier(jnp.sum(direction * right_axis, axis=0))
    cosine = lax.optimization_barrier(jnp.sum(left_axis * right_axis, axis=0))
    summed_sq = (along_left + along_right) ** 2
    differ_sq = (along_left - along_right) ** 2
    shape_term = 1.0 - 0.5 * chi_shape * (summed_sq / (1.0 + chi_shape * cosine) + differ_sq / (1.0 - chi_shape * cosine))
    contact = 1.0 / jnp.sqrt(shape_term)
    strength_one = 1.0 / jnp.sqrt(1.0 - chi_shape * chi_shape * cosine * cosine)
    strength_two = 1.0 - 0.5 * chi_energy * (summed_sq / (1.0 + chi_energy * cosine) + differ_sq / (1.0 - chi_energy * cosine))
    reduced = 1.0 / (distance - contact + 1.0)
    sixth = reduced ** 6
    switch = jnp.maximum(1.0 - distance_sq / cutoff_sq, 0.0) ** 3
    return 4.0 * well_depth * strength_one * strength_two * strength_two * (sixth * sixth - sixth) * switch

def cross_energy(dof_left, dof_right, left_frame, right_frame, brick_shift):
    left_centre, left_axis = place(left_frame, dof_left)
    right_centre, right_axis = place(right_frame, dof_right)
    separation = right_centre[:, None, :] + brick_shift[:, None, None] - left_centre[:, :, None]
    return jnp.sum(pair_energy(separation, left_axis[:, :, None], right_axis[:, None, :]))

def own_energy(dof, frame):
    centre, heading = place(frame, dof)
    ordinal = lax.iota(jnp.int32, frame.shape[1])
    upper_mask = (ordinal[:, None] < ordinal[None, :]).astype(frame.dtype)
    diagonal = (ordinal[:, None] == ordinal[None, :]).astype(frame.dtype)
    separation = centre[:, None, :] - centre[:, :, None]
    lifted = separation + jnp.stack([0.0 * diagonal, 0.0 * diagonal, 8.0 * diagonal])
    return jnp.sum(upper_mask * pair_energy(lifted, heading[:, :, None], heading[:, None, :]))

def cross_product(left_frame, right_frame, left_tangent, right_tangent, brick_shift):

    def gradient(dof_left, dof_right):
        return jax.grad(cross_energy, argnums=(0, 1))(dof_left, dof_right, left_frame, right_frame, brick_shift)
    anchor = (jnp.zeros_like(left_tangent), jnp.zeros_like(right_tangent))
    _, tangent = jax.jvp(gradient, anchor, (left_tangent, right_tangent))
    return tangent

def own_product(frame, vector):

    def gradient(dof):
        return jax.grad(own_energy)(dof, frame)
    _, tangent = jax.jvp(gradient, (jnp.zeros_like(vector),), (vector,))
    return tangent

def apply_hessian(config, vector, tile_list, tile_count):
    tiles = N_ROW * N_COL
    period = jnp.array([5.0, 5.0, 3.5 * (TILE // 16)], dtype=config.dtype)
    frames = config.reshape(6, tiles, TILE).transpose(1, 0, 2)
    pieces = vector.reshape(6, tiles, TILE).transpose(1, 0, 2)
    own_terms = lax.map(lambda both: own_product(both[0], both[1]), (frames, pieces))
    result = own_terms.transpose(1, 0, 2).reshape(6, tiles * TILE)
    entries = tile_list.reshape(tiles * MAXT, 5)
    ordinal = jnp.arange(tiles * MAXT, dtype=jnp.int32)
    row_of = ordinal // (N_COL * MAXT)
    col_of = ordinal // MAXT % N_COL
    active = ordinal % MAXT < tile_count.reshape(tiles)[ordinal // MAXT]

    def visit(total, item):
        entry, row_id, col_id, flag = item
        left = ((row_id * N_COL + entry[0]) * TILE).astype(jnp.int32)
        right = ((entry[1] * N_COL + col_id) * TILE).astype(jnp.int32)
        brick_shift = entry[2:5].astype(config.dtype) * period

        def compute(marker):
            return cross_product(lax.dynamic_slice_in_dim(config, left, TILE, 1), lax.dynamic_slice_in_dim(config, right, TILE, 1), lax.dynamic_slice_in_dim(vector, left, TILE, 1), lax.dynamic_slice_in_dim(vector, right, TILE, 1), brick_shift)

        def skip(marker):
            return (jnp.zeros((6, TILE), total.dtype), jnp.zeros((6, TILE), total.dtype))
        left_out, right_out = lax.cond(flag, compute, skip, flag)
        total = lax.dynamic_update_slice_in_dim(total, lax.dynamic_slice_in_dim(total, left, TILE, 1) + left_out, left, 1)
        total = lax.dynamic_update_slice_in_dim(total, lax.dynamic_slice_in_dim(total, right, TILE, 1) + right_out, right, 1)
        return (total, None)
    result, _ = lax.scan(visit, result, (entries, row_of, col_of, active))
    return result

def reference(config, start, tile_list, tile_count):
    total_entries = 6 * PARTICLES

    def mean_of(values):
        return jnp.sum(values) / total_entries
    first = start / jnp.sqrt(mean_of(start * start) + norm_eps)
    image = apply_hessian(config, first, tile_list, tile_count)
    alpha_one = mean_of(first * image)
    image = image - alpha_one * first
    beta_one = jnp.sqrt(mean_of(image * image) + norm_eps)
    second = image / beta_one
    image = apply_hessian(config, second, tile_list, tile_count) - beta_one * first
    alpha_two = mean_of(second * image)
    image = image - alpha_two * second
    beta_two = jnp.sqrt(mean_of(image * image) + norm_eps)
    mode = image / beta_two
    return (jnp.stack([alpha_one, beta_one, alpha_two, beta_two]), mode)
```

```python
import math

import jax
import jax.numpy as jnp
from jax import lax
from jax.sharding import PartitionSpec as P

chi_shape = 0.8
chi_energy = (math.sqrt(5.0) - 1.0) / (math.sqrt(5.0) + 1.0)
well_depth = 0.005
cutoff_sq = 20.25
norm_eps = 1e-06


def rotate(heading, turn):
    moved = heading + jnp.cross(turn, heading, axis=0)
    return moved / jnp.sqrt(jnp.sum(moved * moved, axis=0, keepdims=True))


def place(frame, dof):
    return (frame[:3] + dof[:3], rotate(frame[3:], dof[3:]))


def pair_energy(separation, left_axis, right_axis):
    distance_sq = jnp.sum(separation * separation, axis=0)
    distance = jnp.sqrt(distance_sq)
    direction = separation / distance
    along_left = jnp.sum(direction * left_axis, axis=0)
    along_right = jnp.sum(direction * right_axis, axis=0)
    cosine = jnp.sum(left_axis * right_axis, axis=0)
    summed_sq = (along_left + along_right) ** 2
    differ_sq = (along_left - along_right) ** 2
    shape_term = 1.0 - 0.5 * chi_shape * (
        summed_sq / (1.0 + chi_shape * cosine) + differ_sq / (1.0 - chi_shape * cosine)
    )
    contact = 1.0 / jnp.sqrt(shape_term)
    strength_one = 1.0 / jnp.sqrt(1.0 - chi_shape * chi_shape * cosine * cosine)
    strength_two = 1.0 - 0.5 * chi_energy * (
        summed_sq / (1.0 + chi_energy * cosine) + differ_sq / (1.0 - chi_energy * cosine)
    )
    reduced = 1.0 / (distance - contact + 1.0)
    sixth = reduced**6
    switch = jnp.maximum(1.0 - distance_sq / cutoff_sq, 0.0) ** 3
    return (
        4.0
        * well_depth
        * strength_one
        * strength_two
        * strength_two
        * (sixth * sixth - sixth)
        * switch
    )


def cross_energy(dof_left, dof_right, left_frame, right_frame, brick_shift):
    left_centre, left_axis = place(left_frame, dof_left)
    right_centre, right_axis = place(right_frame, dof_right)
    separation = right_centre[:, None, :] + brick_shift[:, None, None] - left_centre[:, :, None]
    return jnp.sum(pair_energy(separation, left_axis[:, :, None], right_axis[:, None, :]))


def own_energy(dof, frame):
    centre, heading = place(frame, dof)
    ordinal = lax.iota(jnp.int32, frame.shape[1])
    upper_mask = (ordinal[:, None] < ordinal[None, :]).astype(frame.dtype)
    diagonal = (ordinal[:, None] == ordinal[None, :]).astype(frame.dtype)
    separation = centre[:, None, :] - centre[:, :, None]
    lifted = separation + jnp.stack([0.0 * diagonal, 0.0 * diagonal, 8.0 * diagonal])
    return jnp.sum(upper_mask * pair_energy(lifted, heading[:, :, None], heading[:, None, :]))


def cross_product(left_frame, right_frame, left_tangent, right_tangent, brick_shift):

    def cross_gradient(dof_left, dof_right):
        return jax.grad(cross_energy, argnums=(0, 1))(
            dof_left, dof_right, left_frame, right_frame, brick_shift
        )

    anchor = (jnp.zeros_like(left_tangent), jnp.zeros_like(right_tangent))
    _, tangent = jax.jvp(cross_gradient, anchor, (left_tangent, right_tangent))
    return tangent


def own_product(frame, vector):

    def own_gradient(dof):
        return jax.grad(own_energy)(dof, frame)

    _, tangent = jax.jvp(own_gradient, (jnp.zeros_like(vector),), (vector,))
    return tangent


def local(config, start, tile_list, tile_count):
    dof, member = config.shape
    row_devices = lax.axis_size("row")
    col_devices = lax.axis_size("col")
    row_id = lax.axis_index("row")
    col_id = lax.axis_index("col")
    total_entries = dof * member * row_devices * col_devices
    period = jnp.array([5.0, 5.0, 3.5 * (member // 16)], dtype=jnp.float32)
    entries = tile_list[0, 0]
    used = tile_count[0, 0]

    def everywhere(values):
        gathered = lax.all_gather(values, ("row", "col"), axis=0, tiled=False)
        return gathered.reshape((row_devices, col_devices) + values.shape)

    def mean_of(values):
        return jnp.sum(values) / total_entries

    together = everywhere(jnp.concatenate([config, start], axis=0))
    all_start = together[:, :, dof:]
    row_frames = lax.dynamic_index_in_dim(together, row_id, 0, keepdims=False)[:, :dof]
    col_frames = lax.dynamic_index_in_dim(together, col_id, 1, keepdims=False)[:, :dof]

    def apply_hessian(vectors):
        row_vectors = lax.dynamic_index_in_dim(vectors, row_id, 0, keepdims=False)
        col_vectors = lax.dynamic_index_in_dim(vectors, col_id, 1, keepdims=False)
        vector = lax.dynamic_index_in_dim(row_vectors, col_id, 0, keepdims=False)
        own_term = own_product(config, vector)

        def visit(slot, totals):
            row_total, col_total = totals
            entry = entries[slot]
            left = entry[0]
            right = entry[1]
            brick_shift = entry[2:5].astype(jnp.float32) * period
            left_out, right_out = cross_product(
                row_frames[left],
                col_frames[right],
                row_vectors[left],
                col_vectors[right],
                brick_shift,
            )
            return (row_total.at[left].add(left_out), col_total.at[right].add(right_out))

        row_total, col_total = lax.fori_loop(
            0, used, visit, (jnp.zeros_like(row_vectors), jnp.zeros_like(col_vectors))
        )
        row_sum = lax.psum_scatter(row_total, "col", scatter_dimension=0, tiled=False)
        col_sum = lax.psum_scatter(col_total, "row", scatter_dimension=0, tiled=False)
        return own_term + row_sum + col_sum

    def next_vector(image, basis):
        alpha = mean_of(basis * image)
        residual = image - alpha * basis
        beta = jnp.sqrt(mean_of(residual * residual) + norm_eps)
        return (alpha, beta, residual / beta)

    def mine(values):
        return values[row_id, col_id]

    first = all_start / jnp.sqrt(mean_of(all_start * all_start) + norm_eps)
    alpha_one, beta_one, second = next_vector(everywhere(apply_hessian(first)), first)
    image = apply_hessian(second) - beta_one * mine(first)
    alpha_two, beta_two, mode = next_vector(everywhere(image), second)
    return (jnp.stack([alpha_one, beta_one, alpha_two, beta_two]), mine(mode))


def solution(mesh):
    placed = (
        P(None, ("row", "col")),
        P(None, ("row", "col")),
        P("row", "col", None, None),
        P("row", "col"),
    )
    return jax.shard_map(
        local, mesh=mesh, in_specs=placed, out_specs=(P(), P(None, ("row", "col"))), check_vma=False
    )
```

```python
import math

import jax
import jax.numpy as jnp
from jax import lax
from jax.sharding import PartitionSpec as P

chi_shape = 0.8
chi_energy = (math.sqrt(5.0) - 1.0) / (math.sqrt(5.0) + 1.0)
well_depth = 0.005
cutoff_sq = 20.25
norm_eps = 1e-06


def rotate(heading, turn):
    moved = heading + jnp.cross(turn, heading, axis=0)
    return moved / jnp.sqrt(jnp.sum(moved * moved, axis=0, keepdims=True))


def place(frame, dof):
    return (frame[:3] + dof[:3], rotate(frame[3:], dof[3:]))


def pair_energy(separation, left_axis, right_axis):
    distance_sq = jnp.sum(separation * separation, axis=0)
    distance = jnp.sqrt(distance_sq)
    direction = separation / distance
    along_left = jnp.sum(direction * left_axis, axis=0)
    along_right = jnp.sum(direction * right_axis, axis=0)
    cosine = jnp.sum(left_axis * right_axis, axis=0)
    summed_sq = (along_left + along_right) ** 2
    differ_sq = (along_left - along_right) ** 2
    shape_term = 1.0 - 0.5 * chi_shape * (
        summed_sq / (1.0 + chi_shape * cosine) + differ_sq / (1.0 - chi_shape * cosine)
    )
    contact = 1.0 / jnp.sqrt(shape_term)
    strength_one = 1.0 / jnp.sqrt(1.0 - chi_shape * chi_shape * cosine * cosine)
    strength_two = 1.0 - 0.5 * chi_energy * (
        summed_sq / (1.0 + chi_energy * cosine) + differ_sq / (1.0 - chi_energy * cosine)
    )
    reduced = 1.0 / (distance - contact + 1.0)
    sixth = reduced**6
    switch = jnp.maximum(1.0 - distance_sq / cutoff_sq, 0.0) ** 3
    return (
        4.0
        * well_depth
        * strength_one
        * strength_two
        * strength_two
        * (sixth * sixth - sixth)
        * switch
    )


def cross_energy(dof_left, dof_right, left_frame, right_frame, brick_shift):
    left_centre, left_axis = place(left_frame, dof_left)
    right_centre, right_axis = place(right_frame, dof_right)
    separation = right_centre[:, None, :] + brick_shift[:, None, None] - left_centre[:, :, None]
    return jnp.sum(pair_energy(separation, left_axis[:, :, None], right_axis[:, None, :]))


def own_energy(dof, frame):
    centre, heading = place(frame, dof)
    ordinal = lax.iota(jnp.int32, frame.shape[1])
    upper_mask = (ordinal[:, None] < ordinal[None, :]).astype(frame.dtype)
    diagonal = (ordinal[:, None] == ordinal[None, :]).astype(frame.dtype)
    separation = centre[:, None, :] - centre[:, :, None]
    lifted = separation + jnp.stack([0.0 * diagonal, 0.0 * diagonal, 8.0 * diagonal])
    return jnp.sum(upper_mask * pair_energy(lifted, heading[:, :, None], heading[:, None, :]))


def cross_product(left_frame, right_frame, left_tangent, right_tangent, brick_shift):

    def cross_gradient(dof_left, dof_right):
        return jax.grad(cross_energy, argnums=(0, 1))(
            dof_left, dof_right, left_frame, right_frame, brick_shift
        )

    anchor = (jnp.zeros_like(left_tangent), jnp.zeros_like(right_tangent))
    _, tangent = jax.jvp(cross_gradient, anchor, (left_tangent, right_tangent))
    return tangent


def own_product(frame, vector):

    def own_gradient(dof):
        return jax.grad(own_energy)(dof, frame)

    _, tangent = jax.jvp(own_gradient, (jnp.zeros_like(vector),), (vector,))
    return tangent


def local(config, start, tile_list, tile_count):
    dof, member = config.shape
    row_devices = lax.axis_size("row")
    col_devices = lax.axis_size("col")
    row_id = lax.axis_index("row")
    col_id = lax.axis_index("col")
    total_entries = dof * member * row_devices * col_devices
    period = jnp.array([5.0, 5.0, 3.5 * (member // 16)], dtype=jnp.float32)
    entries = tile_list[0, 0]
    used = tile_count[0, 0]

    def along(values, name, size):
        arrived = [values]
        for step in range(1, size):
            pairs = [(at, (at - step) % size) for at in range(size)]
            arrived.append(lax.ppermute(values, name, pairs))
        return jnp.roll(jnp.stack(arrived), lax.axis_index(name), axis=0)

    def everywhere(values):
        return along(along(values, "col", col_devices), "row", row_devices)

    def mean_of(values):
        return jnp.sum(values) / total_entries

    together = everywhere(jnp.concatenate([config, start], axis=0))
    all_start = together[:, :, dof:]
    row_frames = lax.dynamic_index_in_dim(together, row_id, 0, keepdims=False)[:, :dof]
    col_frames = lax.dynamic_index_in_dim(together, col_id, 1, keepdims=False)[:, :dof]

    def apply_hessian(vectors):
        row_vectors = lax.dynamic_index_in_dim(vectors, row_id, 0, keepdims=False)
        col_vectors = lax.dynamic_index_in_dim(vectors, col_id, 1, keepdims=False)
        vector = lax.dynamic_index_in_dim(row_vectors, col_id, 0, keepdims=False)
        own_term = own_product(config, vector)

        def visit(slot, totals):
            row_total, col_total = totals
            entry = entries[slot]
            left = entry[0]
            right = entry[1]
            brick_shift = entry[2:5].astype(jnp.float32) * period
            left_out, right_out = cross_product(
                row_frames[left],
                col_frames[right],
                row_vectors[left],
                col_vectors[right],
                brick_shift,
            )
            return (row_total.at[left].add(left_out), col_total.at[right].add(right_out))

        row_total, col_total = lax.fori_loop(
            0, used, visit, (jnp.zeros_like(row_vectors), jnp.zeros_like(col_vectors))
        )
        row_sum = lax.psum_scatter(row_total, "col", scatter_dimension=0, tiled=False)
        col_sum = lax.psum_scatter(col_total, "row", scatter_dimension=0, tiled=False)
        return own_term + row_sum + col_sum

    def next_vector(image, basis):
        alpha = mean_of(basis * image)
        residual = image - alpha * basis
        beta = jnp.sqrt(mean_of(residual * residual) + norm_eps)
        return (alpha, beta, residual / beta)

    def mine(values):
        return values[row_id, col_id]

    first = all_start / jnp.sqrt(mean_of(all_start * all_start) + norm_eps)
    alpha_one, beta_one, second = next_vector(everywhere(apply_hessian(first)), first)
    image = apply_hessian(second) - beta_one * mine(first)
    alpha_two, beta_two, mode = next_vector(everywhere(image), second)
    return (jnp.stack([alpha_one, beta_one, alpha_two, beta_two]), mine(mode))


def solution(mesh):
    placed = (
        P(None, ("row", "col")),
        P(None, ("row", "col")),
        P("row", "col", None, None),
        P("row", "col"),
    )
    return jax.shard_map(
        local, mesh=mesh, in_specs=placed, out_specs=(P(), P(None, ("row", "col"))), check_vma=False
    )
```

```python
import math

import jax
import jax.numpy as jnp
from jax import lax
from jax.sharding import PartitionSpec as P

chi_shape = 0.8
chi_energy = (math.sqrt(5.0) - 1.0) / (math.sqrt(5.0) + 1.0)
well_depth = 0.005
cutoff_sq = 20.25
norm_eps = 1e-06


def rotate(heading, turn):
    moved = heading + jnp.cross(turn, heading, axis=0)
    return moved / jnp.sqrt(jnp.sum(moved * moved, axis=0, keepdims=True))


def place(frame, dof):
    return (frame[:3] + dof[:3], rotate(frame[3:], dof[3:]))


def pair_energy(separation, left_axis, right_axis):
    distance_sq = jnp.sum(separation * separation, axis=0)
    distance = jnp.sqrt(distance_sq)
    direction = separation / distance
    along_left = jnp.sum(direction * left_axis, axis=0)
    along_right = jnp.sum(direction * right_axis, axis=0)
    cosine = jnp.sum(left_axis * right_axis, axis=0)
    summed_sq = (along_left + along_right) ** 2
    differ_sq = (along_left - along_right) ** 2
    shape_term = 1.0 - 0.5 * chi_shape * (
        summed_sq / (1.0 + chi_shape * cosine) + differ_sq / (1.0 - chi_shape * cosine)
    )
    contact = 1.0 / jnp.sqrt(shape_term)
    strength_one = 1.0 / jnp.sqrt(1.0 - chi_shape * chi_shape * cosine * cosine)
    strength_two = 1.0 - 0.5 * chi_energy * (
        summed_sq / (1.0 + chi_energy * cosine) + differ_sq / (1.0 - chi_energy * cosine)
    )
    reduced = 1.0 / (distance - contact + 1.0)
    sixth = reduced**6
    switch = jnp.maximum(1.0 - distance_sq / cutoff_sq, 0.0) ** 3
    return (
        4.0
        * well_depth
        * strength_one
        * strength_two
        * strength_two
        * (sixth * sixth - sixth)
        * switch
    )


def cross_energy(dof_left, dof_right, left_frame, right_frame, brick_shift):
    left_centre, left_axis = place(left_frame, dof_left)
    right_centre, right_axis = place(right_frame, dof_right)
    separation = right_centre[:, None, :] + brick_shift[:, None, None] - left_centre[:, :, None]
    return jnp.sum(pair_energy(separation, left_axis[:, :, None], right_axis[:, None, :]))


def own_energy(dof, frame):
    centre, heading = place(frame, dof)
    ordinal = lax.iota(jnp.int32, frame.shape[1])
    upper_mask = (ordinal[:, None] < ordinal[None, :]).astype(frame.dtype)
    diagonal = (ordinal[:, None] == ordinal[None, :]).astype(frame.dtype)
    separation = centre[:, None, :] - centre[:, :, None]
    lifted = separation + jnp.stack([0.0 * diagonal, 0.0 * diagonal, 8.0 * diagonal])
    return jnp.sum(upper_mask * pair_energy(lifted, heading[:, :, None], heading[:, None, :]))


def cross_product(left_frame, right_frame, left_tangent, right_tangent, brick_shift):

    def cross_gradient(dof_left, dof_right):
        return jax.grad(cross_energy, argnums=(0, 1))(
            dof_left, dof_right, left_frame, right_frame, brick_shift
        )

    anchor = (jnp.zeros_like(left_tangent), jnp.zeros_like(right_tangent))
    _, tangent = jax.jvp(cross_gradient, anchor, (left_tangent, right_tangent))
    return tangent


def own_product(frame, vector):

    def own_gradient(dof):
        return jax.grad(own_energy)(dof, frame)

    _, tangent = jax.jvp(own_gradient, (jnp.zeros_like(vector),), (vector,))
    return tangent


def local(config, start, tile_list, tile_count):
    dof, member = config.shape
    row_devices = lax.axis_size("row")
    col_devices = lax.axis_size("col")
    row_id = lax.axis_index("row")
    col_id = lax.axis_index("col")
    total_entries = dof * member * row_devices * col_devices
    period = jnp.array([5.0, 5.0, 3.5 * (member // 16)], dtype=jnp.float32)
    entries = tile_list[0, 0]
    used = tile_count[0, 0]

    def everywhere(values):
        copies = jnp.broadcast_to(values, (row_devices * col_devices,) + values.shape)
        arrived = lax.all_to_all(copies, ("row", "col"), 0, 0, tiled=True)
        return arrived.reshape((row_devices, col_devices) + values.shape)

    def mean_of(values):
        return jnp.sum(values) / total_entries

    together = everywhere(jnp.concatenate([config, start], axis=0))
    all_start = together[:, :, dof:]
    row_frames = lax.dynamic_index_in_dim(together, row_id, 0, keepdims=False)[:, :dof]
    col_frames = lax.dynamic_index_in_dim(together, col_id, 1, keepdims=False)[:, :dof]

    def apply_hessian(vectors):
        row_vectors = lax.dynamic_index_in_dim(vectors, row_id, 0, keepdims=False)
        col_vectors = lax.dynamic_index_in_dim(vectors, col_id, 1, keepdims=False)
        vector = lax.dynamic_index_in_dim(row_vectors, col_id, 0, keepdims=False)
        own_term = own_product(config, vector)

        def visit(slot, totals):
            row_total, col_total = totals
            entry = entries[slot]
            left = entry[0]
            right = entry[1]
            brick_shift = entry[2:5].astype(jnp.float32) * period
            left_out, right_out = cross_product(
                row_frames[left],
                col_frames[right],
                row_vectors[left],
                col_vectors[right],
                brick_shift,
            )
            return (row_total.at[left].add(left_out), col_total.at[right].add(right_out))

        row_total, col_total = lax.fori_loop(
            0, used, visit, (jnp.zeros_like(row_vectors), jnp.zeros_like(col_vectors))
        )
        row_sum = lax.psum_scatter(row_total, "col", scatter_dimension=0, tiled=False)
        col_sum = lax.psum_scatter(col_total, "row", scatter_dimension=0, tiled=False)
        return own_term + row_sum + col_sum

    def next_vector(image, basis):
        alpha = mean_of(basis * image)
        residual = image - alpha * basis
        beta = jnp.sqrt(mean_of(residual * residual) + norm_eps)
        return (alpha, beta, residual / beta)

    def mine(values):
        return values[row_id, col_id]

    first = all_start / jnp.sqrt(mean_of(all_start * all_start) + norm_eps)
    alpha_one, beta_one, second = next_vector(everywhere(apply_hessian(first)), first)
    image = apply_hessian(second) - beta_one * mine(first)
    alpha_two, beta_two, mode = next_vector(everywhere(image), second)
    return (jnp.stack([alpha_one, beta_one, alpha_two, beta_two]), mine(mode))


def solution(mesh):
    placed = (
        P(None, ("row", "col")),
        P(None, ("row", "col")),
        P("row", "col", None, None),
        P("row", "col"),
    )
    return jax.shard_map(
        local, mesh=mesh, in_specs=placed, out_specs=(P(), P(None, ("row", "col"))), check_vma=False
    )
```

```python
import functools
import math

import jax
import jax.numpy as jnp
from jax import lax
from jax.experimental import pallas as pl
from jax.experimental.pallas import tpu as pltpu
from jax.sharding import PartitionSpec as P

chi_shape = 0.8
chi_energy = (math.sqrt(5.0) - 1.0) / (math.sqrt(5.0) + 1.0)
well_depth = 0.005
cutoff_sq = 20.25
norm_eps = 1e-06

SUB = 8
FRAME = 8
LIST_ROW = 14
ROWS = 16
VMEM_LIMIT = 48 * 1024 * 1024


def dot3(a, b):
    return a[0] * b[0] + a[1] * b[1] + a[2] * b[2]


def cross3(a, b):
    return (
        a[1] * b[2] - a[2] * b[1],
        a[2] * b[0] - a[0] * b[2],
        a[0] * b[1] - a[1] * b[0],
    )


def bracket(chi, scaled, factor, p, a, b, eps, da, db, dc):
    f = factor * (a - scaled * b)
    g = factor * (b - scaled * a)
    y = p * (a * f + b * g)
    bent = chi * dc
    da_bent = da - bent * g
    db_bent = db - bent * f
    df = factor * (da_bent - scaled * db_bent)
    dg = factor * (db_bent - scaled * da_bent)
    half_dy = p * (f * da_bent + g * db - eps * y)
    return f, g, y, df, dg, half_dy


def pair_tangent(d, ui, uj, dd, dui, duj, lift):
    r_sq = dot3(d, d) + lift
    a = dot3(d, ui)
    b = dot3(d, uj)
    c = dot3(ui, uj)
    eps = dot3(d, dd)
    da = dot3(dd, ui) + dot3(d, dui)
    db = dot3(dd, uj) + dot3(d, duj)
    dc = dot3(dui, uj) + dot3(ui, duj)
    r_inv = lax.rsqrt(r_sq)
    p = r_inv * r_inv
    r = r_sq * r_inv
    x = jnp.maximum(1.0 - r_sq * (1.0 / cutoff_sq), 0.0)
    c_shape = chi_shape * c
    c_energy = chi_energy * c
    e1 = lax.rsqrt(1.0 - c_shape * c_shape)
    q = e1 * e1
    q2 = 1.0 / (1.0 - c_energy * c_energy)
    f, g, y, df, dg, hdy = bracket(chi_shape, c_shape, q, p, a, b, eps, da, db, dc)
    f2, g2, y2, df2, dg2, hdy2 = bracket(chi_energy, c_energy, q2, p, a, b, eps, da, db, dc)
    sigma = lax.rsqrt(1.0 - chi_shape * y)
    sigma_sq = sigma * sigma
    sigma_cu = sigma_sq * sigma
    psi = 1.0 - chi_energy * y2
    s = 1.0 / (r - sigma + 1.0)
    s_sq = s * s
    s6 = s_sq * s_sq * s_sq
    t0 = s6 * (s6 - 1.0)
    t1 = s6 * s * (6.0 - 12.0 * s6)
    t2 = s6 * s_sq * (156.0 * s6 - 42.0)
    ke = (4.0 * well_depth) * e1
    kx = ke * x
    vrr = kx * (6.0 / cutoff_sq**2)
    kxx = kx * x
    vr = kxx * (-3.0 / cutoff_sq)
    v = kxx * x
    psi_sq = psi * psi
    psi_sq_t0 = psi_sq * t0
    v_psi = v * psi
    v_psi_t0 = v_psi * t0
    v_psi_t1 = v_psi * t1
    v_psi_sq = v_psi * psi
    slope = v_psi * psi * t1
    pull = (-chi_shape) * p * sigma_cu
    h1 = pull * slope
    push = (-4.0 * chi_energy) * p
    h2 = push * v_psi_t0
    u_a = h1 * f + h2 * f2
    u_b = h1 * g + h2 * g2
    kc = chi_shape * c_shape * q
    u = v * psi_sq_t0
    fg = chi_shape * f * g
    fg2 = chi_energy * f2 * g2
    u_c = u * kc - (h1 * fg + h2 * fg2)
    u_r = r_inv * slope + 2.0 * vr * psi_sq_t0 - (h1 * y + h2 * y2)

    dy = 2.0 * hdy
    dy2 = 2.0 * hdy2
    d_sigma = chi_shape * sigma_cu * hdy
    d_rho = r_inv * eps - d_sigma
    d_psi = (-chi_energy) * dy2
    eps2 = 2.0 * eps
    kc_dc = kc * dc
    dv = v * kc_dc + vr * eps2
    dvr = vr * kc_dc + vrr * eps2
    d_psi2 = 2.0 * d_psi
    d_slope = dv * psi_sq * t1 + v_psi_t1 * d_psi2 + v_psi_sq * t2 * d_rho
    fall = p * eps2
    dh1 = h1 * ((3.0 * chi_shape) * sigma_sq * hdy - fall) + pull * d_slope
    dh2 = push * (dv * psi * t0 + v * d_psi * t0 + v_psi_t1 * d_rho) - h2 * fall
    du_a = dh1 * f + h1 * df + dh2 * f2 + h2 * df2
    du_b = dh1 * g + h1 * dg + dh2 * g2 + h2 * dg2
    d_kc = (chi_shape * chi_shape) * q * (2.0 * q - 1.0) * dc
    d_well = psi * d_psi2 * t0 + psi_sq * t1 * d_rho
    du = dv * psi_sq_t0 + v * d_well
    du_c = (
        du * kc
        + u * d_kc
        - (dh1 * fg + chi_shape * h1 * (df * g + f * dg))
        - (dh2 * fg2 + chi_energy * h2 * (df2 * g2 + f2 * dg2))
    )
    du_r = (
        r_inv * (d_slope - p * eps * slope)
        + 2.0 * (dvr * psi_sq_t0 + vr * d_well)
        - (dh1 * y + h1 * dy + dh2 * y2 + h2 * dy2)
    )
    return a, c, u_r, u_a, u_b, u_c, du_r, du_a, du_b, du_c


def tile_product(count, own, frame, moved, entry_tile, entry_shift, skew_ref):
    member = frame(own, 0).shape[1]

    def wide(row):
        return jnp.broadcast_to(row, (SUB, member))

    xi = [wide(frame(own, k)) for k in range(3)]
    ui = [wide(frame(own, k)) for k in range(3, 6)]
    dxi = [wide(moved(own, k)) for k in range(3)]
    dui = [wide(moved(own, k)) for k in range(3, 6)]
    first_row = (lax.broadcasted_iota(jnp.int32, (SUB, member), 0) == 0).astype(jnp.float32)

    sublane = lax.broadcasted_iota(jnp.int32, (SUB, member), 0)

    def skewed(row):
        block = wide(row)
        for bit in (1, 2, 4):
            block = jnp.where((sublane & bit) > 0, pltpu.roll(block, bit, 1), block)
        return block

    def visit_entry(entry, totals):
        partner = entry_tile(entry)
        shift = entry_shift(entry)
        for k in range(3):
            skew_ref[k] = skewed(frame(partner, k)) + shift[k]
        for k in range(3, 6):
            skew_ref[k] = skewed(frame(partner, k))
        for k in range(6):
            skew_ref[6 + k] = skewed(moved(partner, k))
        return lax.fori_loop(0, member // SUB, functools.partial(visit, entry), totals)

    def visit(entry, block, totals):
        other = [pltpu.roll(skew_ref[k], block * SUB, 1) for k in range(12)]
        d = [other[k] - xi[k] for k in range(3)]
        uj = other[3:6]
        dd = [other[6 + k] - dxi[k] for k in range(3)]
        duj = other[9:12]
        item = entry * (member // SUB) + block
        lift = first_row * jnp.where(item == 0, 2.0 * cutoff_sq, 0.0)
        a, c, u_r, u_a, u_b, u_c, du_r, du_a, du_b, du_c = pair_tangent(d, ui, uj, dd, dui, duj, lift)
        force = [du_r * d[k] + u_r * dd[k] + du_b * uj[k] + u_b * duj[k] for k in range(3)]
        turn = [du_a * d[k] + u_a * dd[k] + du_c * uj[k] + u_c * duj[k] for k in range(3)]
        news = force + turn + [du_a, u_a, u_a * a + u_c * c]
        return tuple(total + new for total, new in zip(totals, news))

    zero = jnp.zeros((SUB, member), jnp.float32)
    totals = lax.fori_loop(0, count, visit_entry, (zero,) * 9)
    sums = [jnp.sum(total, axis=0, keepdims=True) for total in totals]
    u = [row[:1] for row in ui]
    t = [row[:1] for row in dui]
    force = [-(sums[k] + u[k] * sums[6] + t[k] * sums[7]) for k in range(3)]
    turn = cross3(u, [sums[3 + k] - t[k] * sums[8] for k in range(3)])
    return force + list(cross3(turn, u))


def spread(rows, out_ref):
    member = rows[0].shape[1]
    fill = [jnp.zeros((1, member), jnp.float32)] * (SUB - len(rows))
    block = jnp.concatenate(rows + fill, axis=0)
    out_ref[...] = jnp.broadcast_to(block[None], out_ref.shape)


def pack_kernel(config_ref, start_ref, list_ref, out_ref):
    u = [config_ref[k : k + 1, :] for k in range(3, 6)]
    w = [start_ref[k : k + 1, :] for k in range(3, 6)]
    t = cross3(w, u)
    zero = jnp.zeros_like(u[0])
    block = jnp.concatenate(
        [start_ref[0:3, :], t[0], t[1], t[2], dot3(w, u), zero, config_ref[...], list_ref[...], zero], axis=0
    )
    out_ref[...] = jnp.broadcast_to(block[None], out_ref.shape)


def first_kernel(rows, cols, period, all_ref, out_ref, tile_ref, shift_ref, count_ref, skew_ref, code_ref, code_smem, sem):
    member = all_ref.shape[2]
    row_id = lax.axis_index("row")
    col_id = lax.axis_index("col")
    own = row_id * cols + col_id
    slots = SUB

    def field(line, at):
        return line if at == 0 else pltpu.roll(line, member - at * slots, 1)

    def encode(line, partner, side):
        offset = (field(line, 2) * 9.0 + field(line, 3) * 3.0 + field(line, 4)) * side + 13.0
        return partner * 27.0 + offset

    row_f = row_id.astype(jnp.float32)
    col_f = col_id.astype(jnp.float32)
    for col in range(cols):
        line = all_ref[row_id * cols + col, LIST_ROW : LIST_ROW + 1, :]
        code = encode(line, field(line, 1) * float(cols) + float(col), 1.0)
        code_ref[col : col + 1, :] = jnp.where(line == col_f, code, -1.0).astype(jnp.int32)
    for row in range(rows):
        line = all_ref[row * cols + col_id, LIST_ROW : LIST_ROW + 1, :]
        code = encode(line, float(row * cols) + line, -1.0)
        hit = (field(line, 1) == row_f) & (line >= 0.0)
        code_ref[cols + row : cols + row + 1, :] = jnp.where(hit, code, -1.0).astype(jnp.int32)
    copy = pltpu.make_async_copy(code_ref, code_smem, sem)
    copy.start()
    copy.wait()

    tile_ref[0] = own
    for k in range(3):
        shift_ref[k] = 0.0

    def gather(at, count):
        code = code_smem[at // slots, at % slots]

        @pl.when(code >= 0)
        def _():
            offset = code % 27
            tile_ref[count] = code // 27
            shift_ref[count * 3] = (offset // 9 - 1).astype(jnp.float32) * period[0]
            shift_ref[count * 3 + 1] = (offset // 3 % 3 - 1).astype(jnp.float32) * period[1]
            shift_ref[count * 3 + 2] = (offset % 3 - 1).astype(jnp.float32) * period[2]

        return count + (code >= 0).astype(jnp.int32)

    count = lax.fori_loop(0, (rows + cols) * slots, gather, jnp.int32(1))
    count_ref[0] = count
    product = tile_product(
        count,
        own,
        lambda tile, k: all_ref[tile, FRAME + k : FRAME + k + 1, :],
        lambda tile, k: all_ref[tile, k : k + 1, :],
        lambda entry: tile_ref[entry],
        lambda entry: [shift_ref[entry * 3 + k] for k in range(3)],
        skew_ref,
    )
    spread(product, out_ref)


def whole_sum(left_ref, right_ref):
    total = jnp.sum(left_ref[...] * right_ref[...], axis=0)
    return jnp.sum(jnp.sum(total, axis=0, keepdims=True), axis=1, keepdims=True)


def second_kernel(
    cols, total_entries, tile_ref, shift_ref, count_ref, all_ref, image_ref, out_ref, second_ref, scalar_ref, skew_ref, basis_ref
):
    own = lax.axis_index("row") * cols + lax.axis_index("col")
    member = all_ref.shape[2]
    basis_ref[...] = all_ref[:, 0:SUB, :]
    norm_sq = whole_sum(basis_ref, basis_ref) / total_entries + norm_eps
    alpha = whole_sum(basis_ref, image_ref) / total_entries / norm_sq
    second_ref[...] = image_ref[...] - alpha * basis_ref[...]
    beta = jnp.sqrt(whole_sum(second_ref, second_ref) / total_entries / norm_sq + norm_eps)
    scale = lax.rsqrt(norm_sq) / beta
    product = tile_product(
        count_ref[0],
        own,
        lambda tile, k: all_ref[tile, FRAME + k : FRAME + k + 1, :],
        lambda tile, k: second_ref[tile, k : k + 1, :],
        lambda entry: tile_ref[entry],
        lambda entry: [shift_ref[entry * 3 + k] for k in range(3)],
        skew_ref,
    )
    back = beta * lax.rsqrt(norm_sq)
    rows = product + [jnp.zeros((1, member), jnp.float32)]
    spread([row * scale - back * basis_ref[own, k : k + 1, :] for k, row in enumerate(rows)], out_ref)
    second_ref[...] = second_ref[...] * scale
    lane = lax.broadcasted_iota(jnp.int32, (1, member), 1)
    scalar_ref[...] = jnp.where(lane == 0, alpha, jnp.where(lane == 1, beta, 0.0))


def last_kernel(cols, total_entries, config_ref, second_ref, image_ref, scalar_ref, mode_ref, coefficient_ref):
    own = lax.axis_index("row") * cols + lax.axis_index("col")
    member = config_ref.shape[1]
    alpha = whole_sum(second_ref, image_ref) / total_entries
    rest = image_ref[...] - alpha * second_ref[...]
    total = jnp.sum(rest * rest, axis=0)
    total = jnp.sum(jnp.sum(total, axis=0, keepdims=True), axis=1, keepdims=True)
    beta = jnp.sqrt(total / total_entries + norm_eps)
    mine = (image_ref[own] - alpha * second_ref[own]) / beta
    u = [config_ref[k : k + 1, :] for k in range(3, 6)]
    turn = cross3(u, [mine[k : k + 1] for k in range(3, 6)])
    along = mine[6:7]
    mode_ref[...] = jnp.concatenate([mine[0:3]] + [turn[k] + along * u[k] for k in range(3)], axis=0)
    lane = lax.broadcasted_iota(jnp.int32, (1, member), 1)
    coefficient_ref[...] = jnp.where(lane == 2, alpha, jnp.where(lane == 3, beta, scalar_ref[...]))


def local(config, start, tile_list, tile_count):
    dof, member = config.shape
    row_devices = lax.axis_size("row")
    col_devices = lax.axis_size("col")
    devices = row_devices * col_devices
    total_entries = float(dof * member * devices)
    period = (5.0, 5.0, 3.5 * (member // 16))
    entries = tile_list[0, 0]
    slots, fields = entries.shape
    longest = (row_devices + col_devices) * slots + 1

    def shaped(*shape):
        return jax.ShapeDtypeStruct(shape, jnp.float32)

    def everywhere(copies):
        return lax.all_to_all(copies, ("row", "col"), 0, 0, tiled=True)

    params = pltpu.CompilerParams(vmem_limit_bytes=VMEM_LIMIT)
    vmem = pl.BlockSpec(memory_space=pltpu.VMEM)
    smem = pl.BlockSpec(memory_space=pltpu.SMEM)

    in_use = jnp.arange(slots, dtype=jnp.int32) < tile_count[0, 0]
    fields_f = jnp.where(in_use[:, None], entries, -9).astype(jnp.float32).T.reshape(1, fields * slots)
    list_row = jnp.pad(fields_f, ((0, 0), (0, member - fields * slots)), constant_values=-9.0)

    packed = pl.pallas_call(
        pack_kernel,
        out_shape=shaped(devices, ROWS, member),
        in_specs=[vmem] * 3,
        out_specs=vmem,
        compiler_params=params,
    )(config, start, list_row)
    together = everywhere(packed)

    image, tiles, shifts, count = pl.pallas_call(
        functools.partial(first_kernel, row_devices, col_devices, period),
        out_shape=(
            shaped(devices, SUB, member),
            jax.ShapeDtypeStruct((longest,), jnp.int32),
            shaped(longest * 3),
            jax.ShapeDtypeStruct((1,), jnp.int32),
        ),
        in_specs=[vmem],
        out_specs=(vmem, smem, smem, smem),
        scratch_shapes=[
            pltpu.VMEM((12, SUB, member), jnp.float32),
            pltpu.VMEM((row_devices + col_devices, member), jnp.int32),
            pltpu.SMEM((row_devices + col_devices, member), jnp.int32),
            pltpu.SemaphoreType.DMA,
        ],
        compiler_params=params,
    )(together)
    image = everywhere(image)

    residual, second, scalars = pl.pallas_call(
        functools.partial(second_kernel, col_devices, total_entries),
        out_shape=(shaped(devices, SUB, member), shaped(devices, SUB, member), shaped(1, member)),
        in_specs=[smem, smem, smem, vmem, vmem],
        out_specs=(vmem, vmem, vmem),
        scratch_shapes=[pltpu.VMEM((12, SUB, member), jnp.float32), pltpu.VMEM((devices, SUB, member), jnp.float32)],
        compiler_params=params,
    )(tiles, shifts, count, together, image)
    residual = everywhere(residual)

    mode, coefficients = pl.pallas_call(
        functools.partial(last_kernel, col_devices, total_entries),
        out_shape=(shaped(dof, member), shaped(1, member)),
        in_specs=[vmem] * 4,
        out_specs=(vmem, vmem),
        compiler_params=params,
    )(config, second, residual, scalars)
    return (coefficients[0, :4], mode)


def solution(mesh):
    placed = (
        P(None, ("row", "col")),
        P(None, ("row", "col")),
        P("row", "col", None, None),
        P("row", "col"),
    )
    return jax.shard_map(
        local, mesh=mesh, in_specs=placed, out_specs=(P(), P(None, ("row", "col"))), check_vma=False
    )
```

```python
import functools
import math

import jax
import jax.numpy as jnp
from jax import lax
from jax.experimental import pallas as pl
from jax.experimental.pallas import tpu as pltpu
from jax.sharding import PartitionSpec as P

chi_shape = 0.8
chi_energy = (math.sqrt(5.0) - 1.0) / (math.sqrt(5.0) + 1.0)
well_depth = 0.005
cutoff_sq = 20.25
norm_eps = 1e-06

SUB = 8
FRAME = 8
LIST_ROW = 14
ROWS = 16
CODE_BITS = 6
GROUP = 2
VMEM_LIMIT = 48 * 1024 * 1024


def dot3(a, b):
    return a[0] * b[0] + a[1] * b[1] + a[2] * b[2]


def cross3(a, b):
    return (
        a[1] * b[2] - a[2] * b[1],
        a[2] * b[0] - a[0] * b[2],
        a[0] * b[1] - a[1] * b[0],
    )


def bracket(chi, scaled, factor, p, a, b, eps, da, db, dc):
    f = factor * (a - scaled * b)
    g = factor * (b - scaled * a)
    y = p * (a * f + b * g)
    bent = chi * dc
    da_bent = da - bent * g
    db_bent = db - bent * f
    df = factor * (da_bent - scaled * db_bent)
    dg = factor * (db_bent - scaled * da_bent)
    half_dy = p * (f * da_bent + g * db - eps * y)
    return f, g, y, df, dg, half_dy


def pair_tangent(d, ui, uj, dd, dui, duj, lift):
    r_sq = dot3(d, d) + lift
    a = dot3(d, ui)
    b = dot3(d, uj)
    c = dot3(ui, uj)
    eps = dot3(d, dd)
    da = dot3(dd, ui) + dot3(d, dui)
    db = dot3(dd, uj) + dot3(d, duj)
    dc = dot3(dui, uj) + dot3(ui, duj)
    r_inv = lax.rsqrt(r_sq)
    p = r_inv * r_inv
    r = r_sq * r_inv
    x = jnp.maximum(1.0 - r_sq * (1.0 / cutoff_sq), 0.0)
    c_shape = chi_shape * c
    c_energy = chi_energy * c
    e1 = lax.rsqrt(1.0 - c_shape * c_shape)
    q = e1 * e1
    q2 = 1.0 / (1.0 - c_energy * c_energy)
    f, g, y, df, dg, hdy = bracket(chi_shape, c_shape, q, p, a, b, eps, da, db, dc)
    f2, g2, y2, df2, dg2, hdy2 = bracket(chi_energy, c_energy, q2, p, a, b, eps, da, db, dc)
    sigma = lax.rsqrt(1.0 - chi_shape * y)
    sigma_sq = sigma * sigma
    sigma_cu = sigma_sq * sigma
    psi = 1.0 - chi_energy * y2
    s = 1.0 / (r - sigma + 1.0)
    s_sq = s * s
    s6 = s_sq * s_sq * s_sq
    t0 = s6 * (s6 - 1.0)
    t1 = s6 * s * (6.0 - 12.0 * s6)
    t2 = s6 * s_sq * (156.0 * s6 - 42.0)
    ke = (4.0 * well_depth) * e1
    kx = ke * x
    vrr = kx * (6.0 / cutoff_sq**2)
    kxx = kx * x
    vr = kxx * (-3.0 / cutoff_sq)
    v = kxx * x
    psi_sq = psi * psi
    psi_sq_t0 = psi_sq * t0
    v_psi = v * psi
    v_psi_t0 = v_psi * t0
    v_psi_t1 = v_psi * t1
    v_psi_sq = v_psi * psi
    slope = v_psi * psi * t1
    pull = (-chi_shape) * p * sigma_cu
    h1 = pull * slope
    push = (-4.0 * chi_energy) * p
    h2 = push * v_psi_t0
    u_a = h1 * f + h2 * f2
    u_b = h1 * g + h2 * g2
    kc = chi_shape * c_shape * q
    u = v * psi_sq_t0
    fg = chi_shape * f * g
    fg2 = chi_energy * f2 * g2
    u_c = u * kc - (h1 * fg + h2 * fg2)
    u_r = r_inv * slope + 2.0 * vr * psi_sq_t0 - (h1 * y + h2 * y2)

    dy = 2.0 * hdy
    dy2 = 2.0 * hdy2
    d_sigma = chi_shape * sigma_cu * hdy
    d_rho = r_inv * eps - d_sigma
    d_psi = (-chi_energy) * dy2
    eps2 = 2.0 * eps
    kc_dc = kc * dc
    dv = v * kc_dc + vr * eps2
    dvr = vr * kc_dc + vrr * eps2
    d_psi2 = 2.0 * d_psi
    d_slope = dv * psi_sq * t1 + v_psi_t1 * d_psi2 + v_psi_sq * t2 * d_rho
    fall = p * eps2
    dh1 = h1 * ((3.0 * chi_shape) * sigma_sq * hdy - fall) + pull * d_slope
    dh2 = push * (dv * psi * t0 + v * d_psi * t0 + v_psi_t1 * d_rho) - h2 * fall
    du_a = dh1 * f + h1 * df + dh2 * f2 + h2 * df2
    du_b = dh1 * g + h1 * dg + dh2 * g2 + h2 * dg2
    d_kc = (chi_shape * chi_shape) * q * (2.0 * q - 1.0) * dc
    d_well = psi * d_psi2 * t0 + psi_sq * t1 * d_rho
    du = dv * psi_sq_t0 + v * d_well
    du_c = (
        du * kc
        + u * d_kc
        - (dh1 * fg + chi_shape * h1 * (df * g + f * dg))
        - (dh2 * fg2 + chi_energy * h2 * (df2 * g2 + f2 * dg2))
    )
    du_r = (
        r_inv * (d_slope - p * eps * slope)
        + 2.0 * (dvr * psi_sq_t0 + vr * d_well)
        - (dh1 * y + h1 * dy + dh2 * y2 + h2 * dy2)
    )
    return a, c, u_r, u_a, u_b, u_c, du_r, du_a, du_b, du_c


def offsets_of(code, period):
    return [((code >> bits & 3) - 1).astype(jnp.float32) * size for bits, size in zip((4, 2, 0), period)]


def skew_entry(entry, code, period, frame, moved, skew_ref):
    partner = code >> CODE_BITS
    shift = offsets_of(code, period)
    member = skew_ref.shape[3]
    sublane = lax.broadcasted_iota(jnp.int32, (SUB, member), 0)

    def skewed(row):
        block = jnp.broadcast_to(row, (SUB, member))
        for bit in (1, 2, 4):
            block = jnp.where((sublane & bit) > 0, pltpu.roll(block, bit, 1), block)
        return block

    for k in range(3):
        skew_ref[entry, k] = skewed(frame(partner, k)) + shift[k]
        skew_ref[entry, 3 + k] = skewed(frame(partner, 3 + k))
        skew_ref[entry, 6 + k] = skewed(moved(partner, k))
        skew_ref[entry, 9 + k] = skewed(moved(partner, 3 + k))


def near_blocks(code, period, own_frame, partner_frame):
    member = own_frame.shape[1]
    row = lax.broadcasted_iota(jnp.int32, (SUB, member), 0)
    shift = offsets_of(code, period)
    sign = jnp.where(row < 3, 1.0, jnp.where(row < 6, -1.0, 0.0))

    def doubled(block):
        centre = jnp.where(row < 3, block, 0.0)
        return centre + pltpu.roll(centre, 3, 0)

    moved = jnp.where(row % 3 == 0, shift[0], jnp.where(row % 3 == 1, shift[1], shift[2]))
    box = (doubled(partner_frame) + moved) * sign
    for bit in (1, 2, 4):
        box = jnp.maximum(box, pltpu.roll(box, bit, 1))
    here = doubled(own_frame) * sign
    blocks = member // SUB
    reach = []
    for k in range(blocks):
        gap = jnp.maximum(here - (pltpu.roll(box, k * SUB, 1) if k else box), 0.0)
        reach.append(jnp.sum(gap * gap, axis=0, keepdims=True))
    nearest = jnp.min(jnp.concatenate(reach, axis=0), axis=1, keepdims=True)
    weight = (1 << lax.broadcasted_iota(jnp.int32, (blocks, 1), 0)).astype(jnp.float32)
    return jnp.sum(jnp.where(nearest < cutoff_sq * 1.001, weight, 0.0)).astype(jnp.int32)


def tile_product(item_count, item_ref, own, frame, moved, skew_ref):
    member = skew_ref.shape[3]
    blocks = member // SUB

    def wide(row):
        return jnp.broadcast_to(row, (SUB, member))

    xi = [wide(frame(own, k)) for k in range(3)]
    ui = [wide(frame(own, k)) for k in range(3, 6)]
    dxi = [wide(moved(own, k)) for k in range(3)]
    dui = [wide(moved(own, k)) for k in range(3, 6)]
    first_row = (lax.broadcasted_iota(jnp.int32, (SUB, member), 0) == 0).astype(jnp.float32)

    def one(at):
        item = item_ref[at]
        entry = item // blocks
        turn_by = item % blocks * SUB
        other = [pltpu.roll(skew_ref[entry, k], turn_by, 1) for k in range(12)]
        d = [other[k] - xi[k] for k in range(3)]
        uj = other[3:6]
        dd = [other[6 + k] - dxi[k] for k in range(3)]
        duj = other[9:12]
        itself = jnp.where(item == 0, 2.0 * cutoff_sq, 0.0)
        unused = jnp.where(at < item_count, 0.0, 2.0 * cutoff_sq)
        lift = first_row * itself + unused
        a, c, u_r, u_a, u_b, u_c, du_r, du_a, du_b, du_c = pair_tangent(d, ui, uj, dd, dui, duj, lift)
        force = [du_r * d[k] + u_r * dd[k] + du_b * uj[k] + u_b * duj[k] for k in range(3)]
        turn = [du_a * d[k] + u_a * dd[k] + du_c * uj[k] + u_c * duj[k] for k in range(3)]
        return force + turn + [du_a, u_a, u_a * a + u_c * c]

    def visit(step, totals):
        news = [one(step * GROUP + part) for part in range(GROUP)]
        return tuple(sum(parts, total) for total, parts in zip(totals, zip(*news)))

    zero = jnp.zeros((SUB, member), jnp.float32)
    totals = lax.fori_loop(0, (item_count + GROUP - 1) // GROUP, visit, (zero,) * 9)
    sums = [jnp.sum(total, axis=0, keepdims=True) for total in totals]
    u = [row[:1] for row in ui]
    t = [row[:1] for row in dui]
    force = [-(sums[k] + u[k] * sums[6] + t[k] * sums[7]) for k in range(3)]
    turn = cross3(u, [sums[3 + k] - t[k] * sums[8] for k in range(3)])
    return force + list(cross3(turn, u))


def spread(rows, out_ref):
    member = rows[0].shape[1]
    fill = [jnp.zeros((1, member), jnp.float32)] * (SUB - len(rows))
    block = jnp.concatenate(rows + fill, axis=0)
    out_ref[...] = jnp.broadcast_to(block[None], out_ref.shape)


def pack_kernel(config_ref, start_ref, list_ref, out_ref):
    u = [config_ref[k : k + 1, :] for k in range(3, 6)]
    w = [start_ref[k : k + 1, :] for k in range(3, 6)]
    t = cross3(w, u)
    zero = jnp.zeros_like(u[0])
    block = jnp.concatenate(
        [start_ref[0:3, :], t[0], t[1], t[2], dot3(w, u), zero, config_ref[...], list_ref[...], zero], axis=0
    )
    out_ref[...] = jnp.broadcast_to(block[None], out_ref.shape)


def first_kernel(
    rows, cols, slots, period, all_ref, out_ref, entry_ref, item_ref, count_ref, skew_ref, code_ref, code_smem, sem
):
    member = all_ref.shape[2]
    row_id = lax.axis_index("row")
    col_id = lax.axis_index("col")
    own = row_id * cols + col_id
    blocks = member // SUB

    def field(line, at):
        return line if at == 0 else pltpu.roll(line, member - at * slots, 1)

    def encode(line, partner, side):
        offset = (field(line, 2) * 16.0 + field(line, 3) * 4.0 + field(line, 4)) * side + 21.0
        return partner * float(1 << CODE_BITS) + offset

    row_f = row_id.astype(jnp.float32)
    col_f = col_id.astype(jnp.float32)
    for col in range(cols):
        line = all_ref[row_id * cols + col, LIST_ROW : LIST_ROW + 1, :]
        code = encode(line, field(line, 1) * float(cols) + float(col), 1.0)
        code_ref[col : col + 1, :] = jnp.where(line == col_f, code, -1.0).astype(jnp.int32)
    for row in range(rows):
        line = all_ref[row * cols + col_id, LIST_ROW : LIST_ROW + 1, :]
        code = encode(line, float(row * cols) + line, -1.0)
        hit = (field(line, 1) == row_f) & (line >= 0.0)
        code_ref[cols + row : cols + row + 1, :] = jnp.where(hit, code, -1.0).astype(jnp.int32)
    copy = pltpu.make_async_copy(code_ref, code_smem, sem)
    copy.start()
    copy.wait()

    entry_ref[0] = own * (1 << CODE_BITS) + 21

    def gather(line, count):
        for slot in range(slots):
            code = code_smem[line, slot]
            entry_ref[count] = code
            count = count + (code >= 0).astype(jnp.int32)
        return count

    entries = lax.fori_loop(0, rows + cols, gather, jnp.int32(1))
    own_frame = all_ref[own, FRAME : FRAME + SUB, :]

    def frame(tile, k):
        return all_ref[tile, FRAME + k : FRAME + k + 1, :]

    def moved(tile, k):
        return all_ref[tile, k : k + 1, :]

    def prepare(entry, count):
        code = entry_ref[entry]
        skew_entry(entry, code, period, frame, moved, skew_ref)
        bits = near_blocks(code, period, own_frame, all_ref[code >> CODE_BITS, FRAME : FRAME + SUB, :])
        for block in range(blocks):
            item_ref[count] = entry * blocks + block
            count = count + (bits >> block & 1)
        return count

    items = lax.fori_loop(0, entries, prepare, jnp.int32(0))
    for part in range(GROUP):
        item_ref[items + part] = 0
    count_ref[0] = entries
    count_ref[1] = items
    spread(tile_product(items, item_ref, own, frame, moved, skew_ref), out_ref)


def whole_sum(left_ref, right_ref):
    total = jnp.sum(left_ref[...] * right_ref[...], axis=0)
    return jnp.sum(jnp.sum(total, axis=0, keepdims=True), axis=1, keepdims=True)


def second_kernel(
    cols,
    total_entries,
    period,
    entry_ref,
    item_ref,
    count_ref,
    all_ref,
    image_ref,
    out_ref,
    second_ref,
    scalar_ref,
    skew_ref,
    basis_ref,
):
    own = lax.axis_index("row") * cols + lax.axis_index("col")
    member = all_ref.shape[2]
    basis_ref[...] = all_ref[:, 0:SUB, :]
    norm_sq = whole_sum(basis_ref, basis_ref) / total_entries + norm_eps
    alpha = whole_sum(basis_ref, image_ref) / total_entries / norm_sq
    second_ref[...] = image_ref[...] - alpha * basis_ref[...]
    beta = jnp.sqrt(whole_sum(second_ref, second_ref) / total_entries / norm_sq + norm_eps)
    scale = lax.rsqrt(norm_sq) / beta

    def frame(tile, k):
        return all_ref[tile, FRAME + k : FRAME + k + 1, :]

    def moved(tile, k):
        return second_ref[tile, k : k + 1, :]

    def prepare(entry, carry):
        skew_entry(entry, entry_ref[entry], period, frame, moved, skew_ref)
        return carry

    lax.fori_loop(0, count_ref[0], prepare, 0)
    product = tile_product(count_ref[1], item_ref, own, frame, moved, skew_ref)
    back = beta * lax.rsqrt(norm_sq)
    rows = product + [jnp.zeros((1, member), jnp.float32)]
    spread([row * scale - back * basis_ref[own, k : k + 1, :] for k, row in enumerate(rows)], out_ref)
    second_ref[...] = second_ref[...] * scale
    lane = lax.broadcasted_iota(jnp.int32, (1, member), 1)
    scalar_ref[...] = jnp.where(lane == 0, alpha, jnp.where(lane == 1, beta, 0.0))


def last_kernel(cols, total_entries, config_ref, second_ref, image_ref, scalar_ref, mode_ref, coefficient_ref):
    own = lax.axis_index("row") * cols + lax.axis_index("col")
    member = config_ref.shape[1]
    alpha = whole_sum(second_ref, image_ref) / total_entries
    rest = image_ref[...] - alpha * second_ref[...]
    total = jnp.sum(rest * rest, axis=0)
    total = jnp.sum(jnp.sum(total, axis=0, keepdims=True), axis=1, keepdims=True)
    beta = jnp.sqrt(total / total_entries + norm_eps)
    mine = (image_ref[own] - alpha * second_ref[own]) / beta
    u = [config_ref[k : k + 1, :] for k in range(3, 6)]
    turn = cross3(u, [mine[k : k + 1] for k in range(3, 6)])
    along = mine[6:7]
    mode_ref[...] = jnp.concatenate([mine[0:3]] + [turn[k] + along * u[k] for k in range(3)], axis=0)
    lane = lax.broadcasted_iota(jnp.int32, (1, member), 1)
    coefficient_ref[...] = jnp.where(lane == 2, alpha, jnp.where(lane == 3, beta, scalar_ref[...]))


def local(config, start, tile_list, tile_count):
    dof, member = config.shape
    row_devices = lax.axis_size("row")
    col_devices = lax.axis_size("col")
    devices = row_devices * col_devices
    total_entries = float(dof * member * devices)
    period = (5.0, 5.0, 3.5 * (member // 16))
    entries = tile_list[0, 0]
    slots, fields = entries.shape
    longest = (row_devices + col_devices) * slots + 1

    def shaped(*shape):
        return jax.ShapeDtypeStruct(shape, jnp.float32)

    def everywhere(copies):
        return lax.all_to_all(copies, ("row", "col"), 0, 0, tiled=True)

    params = pltpu.CompilerParams(vmem_limit_bytes=VMEM_LIMIT)
    vmem = pl.BlockSpec(memory_space=pltpu.VMEM)
    smem = pl.BlockSpec(memory_space=pltpu.SMEM)

    in_use = jnp.arange(slots, dtype=jnp.int32) < tile_count[0, 0]
    fields_f = jnp.where(in_use[:, None], entries, -9).astype(jnp.float32).T.reshape(1, fields * slots)
    list_row = jnp.pad(fields_f, ((0, 0), (0, member - fields * slots)), constant_values=-9.0)

    packed = pl.pallas_call(
        pack_kernel,
        out_shape=shaped(devices, ROWS, member),
        in_specs=[vmem] * 3,
        out_specs=vmem,
        compiler_params=params,
    )(config, start, list_row)
    together = everywhere(packed)

    skew = pltpu.VMEM((longest, 12, SUB, member), jnp.float32)
    image, codes, items, counts = pl.pallas_call(
        functools.partial(first_kernel, row_devices, col_devices, slots, period),
        out_shape=(
            shaped(devices, SUB, member),
            jax.ShapeDtypeStruct((longest + 1,), jnp.int32),
            jax.ShapeDtypeStruct((longest * (member // SUB) + GROUP,), jnp.int32),
            jax.ShapeDtypeStruct((2,), jnp.int32),
        ),
        in_specs=[vmem],
        out_specs=(vmem, smem, smem, smem),
        scratch_shapes=[
            skew,
            pltpu.VMEM((row_devices + col_devices, member), jnp.int32),
            pltpu.SMEM((row_devices + col_devices, member), jnp.int32),
            pltpu.SemaphoreType.DMA,
        ],
        compiler_params=params,
    )(together)
    image = everywhere(image)

    residual, second, scalars = pl.pallas_call(
        functools.partial(second_kernel, col_devices, total_entries, period),
        out_shape=(shaped(devices, SUB, member), shaped(devices, SUB, member), shaped(1, member)),
        in_specs=[smem, smem, smem, vmem, vmem],
        out_specs=(vmem, vmem, vmem),
        scratch_shapes=[skew, pltpu.VMEM((devices, SUB, member), jnp.float32)],
        compiler_params=params,
    )(codes, items, counts, together, image)
    residual = everywhere(residual)

    mode, coefficients = pl.pallas_call(
        functools.partial(last_kernel, col_devices, total_entries),
        out_shape=(shaped(dof, member), shaped(1, member)),
        in_specs=[vmem] * 4,
        out_specs=(vmem, vmem),
        compiler_params=params,
    )(config, second, residual, scalars)
    return (coefficients[0, :4], mode)


def solution(mesh):
    placed = (
        P(None, ("row", "col")),
        P(None, ("row", "col")),
        P("row", "col", None, None),
        P("row", "col"),
    )
    return jax.shard_map(
        local, mesh=mesh, in_specs=placed, out_specs=(P(), P(None, ("row", "col"))), check_vma=False
    )
```

```python
import functools
import math

import jax
import jax.numpy as jnp
from jax import lax
from jax.experimental import pallas as pl
from jax.experimental.pallas import tpu as pltpu
from jax.sharding import PartitionSpec as P

chi_shape = 0.8
chi_energy = (math.sqrt(5.0) - 1.0) / (math.sqrt(5.0) + 1.0)
well_depth = 0.005
cutoff_sq = 20.25
norm_eps = 1e-06

SUB = 8
FRAME = 8
LIST_ROW = 14
ROWS = 16
CODE_BITS = 6
GROUP = 2
VMEM_LIMIT = 48 * 1024 * 1024


def dot3(a, b):
    return a[0] * b[0] + a[1] * b[1] + a[2] * b[2]


def cross3(a, b):
    return (
        a[1] * b[2] - a[2] * b[1],
        a[2] * b[0] - a[0] * b[2],
        a[0] * b[1] - a[1] * b[0],
    )


def bracket(chi, scaled, factor, p, a, b, eps, da, db, dc):
    f = factor * (a - scaled * b)
    g = factor * (b - scaled * a)
    y = p * (a * f + b * g)
    bent = chi * dc
    da_bent = da - bent * g
    db_bent = db - bent * f
    df = factor * (da_bent - scaled * db_bent)
    dg = factor * (db_bent - scaled * da_bent)
    half_dy = p * (f * da_bent + g * db - eps * y)
    return f, g, y, df, dg, half_dy


def pair_tangent(d, ui, uj, dd, dui, duj, lift):
    r_sq = dot3(d, d) + lift
    a = dot3(d, ui)
    b = dot3(d, uj)
    c = dot3(ui, uj)
    eps = dot3(d, dd)
    da = dot3(dd, ui) + dot3(d, dui)
    db = dot3(dd, uj) + dot3(d, duj)
    dc = dot3(dui, uj) + dot3(ui, duj)
    r_inv = lax.rsqrt(r_sq)
    p = r_inv * r_inv
    r = r_sq * r_inv
    x = jnp.maximum(1.0 - r_sq * (1.0 / cutoff_sq), 0.0)
    c_shape = chi_shape * c
    c_energy = chi_energy * c
    e1 = lax.rsqrt(1.0 - c_shape * c_shape)
    q = e1 * e1
    q2 = 1.0 / (1.0 - c_energy * c_energy)
    f, g, y, df, dg, hdy = bracket(chi_shape, c_shape, q, p, a, b, eps, da, db, dc)
    f2, g2, y2, df2, dg2, hdy2 = bracket(chi_energy, c_energy, q2, p, a, b, eps, da, db, dc)
    sigma = lax.rsqrt(1.0 - chi_shape * y)
    sigma_sq = sigma * sigma
    sigma_cu = sigma_sq * sigma
    psi = 1.0 - chi_energy * y2
    s = 1.0 / (r - sigma + 1.0)
    s_sq = s * s
    s6 = s_sq * s_sq * s_sq
    t0 = s6 * (s6 - 1.0)
    t1 = s6 * s * (6.0 - 12.0 * s6)
    t2 = s6 * s_sq * (156.0 * s6 - 42.0)
    ke = (4.0 * well_depth) * e1
    kx = ke * x
    vrr = kx * (6.0 / cutoff_sq**2)
    kxx = kx * x
    vr = kxx * (-3.0 / cutoff_sq)
    v = kxx * x
    psi_sq = psi * psi
    psi_sq_t0 = psi_sq * t0
    v_psi = v * psi
    v_psi_t0 = v_psi * t0
    v_psi_t1 = v_psi * t1
    v_psi_sq = v_psi * psi
    slope = v_psi * psi * t1
    pull = (-chi_shape) * p * sigma_cu
    h1 = pull * slope
    push = (-4.0 * chi_energy) * p
    h2 = push * v_psi_t0
    u_a = h1 * f + h2 * f2
    u_b = h1 * g + h2 * g2
    kc = chi_shape * c_shape * q
    u = v * psi_sq_t0
    fg = chi_shape * f * g
    fg2 = chi_energy * f2 * g2
    u_c = u * kc - (h1 * fg + h2 * fg2)
    u_r = r_inv * slope + 2.0 * vr * psi_sq_t0 - (h1 * y + h2 * y2)

    dy = 2.0 * hdy
    dy2 = 2.0 * hdy2
    d_sigma = chi_shape * sigma_cu * hdy
    d_rho = r_inv * eps - d_sigma
    d_psi = (-chi_energy) * dy2
    eps2 = 2.0 * eps
    kc_dc = kc * dc
    dv = v * kc_dc + vr * eps2
    dvr = vr * kc_dc + vrr * eps2
    d_psi2 = 2.0 * d_psi
    d_slope = dv * psi_sq * t1 + v_psi_t1 * d_psi2 + v_psi_sq * t2 * d_rho
    fall = p * eps2
    dh1 = h1 * ((3.0 * chi_shape) * sigma_sq * hdy - fall) + pull * d_slope
    dh2 = push * (dv * psi * t0 + v * d_psi * t0 + v_psi_t1 * d_rho) - h2 * fall
    du_a = dh1 * f + h1 * df + dh2 * f2 + h2 * df2
    du_b = dh1 * g + h1 * dg + dh2 * g2 + h2 * dg2
    d_kc = (chi_shape * chi_shape) * q * (2.0 * q - 1.0) * dc
    d_well = psi * d_psi2 * t0 + psi_sq * t1 * d_rho
    du = dv * psi_sq_t0 + v * d_well
    du_c = (
        du * kc
        + u * d_kc
        - (dh1 * fg + chi_shape * h1 * (df * g + f * dg))
        - (dh2 * fg2 + chi_energy * h2 * (df2 * g2 + f2 * dg2))
    )
    du_r = (
        r_inv * (d_slope - p * eps * slope)
        + 2.0 * (dvr * psi_sq_t0 + vr * d_well)
        - (dh1 * y + h1 * dy + dh2 * y2 + h2 * dy2)
    )
    return a, c, u_r, u_a, u_b, u_c, du_r, du_a, du_b, du_c


def offsets_of(code, period):
    return [((code >> bits & 3) - 1).astype(jnp.float32) * size for bits, size in zip((4, 2, 0), period)]


def offset_rows(code, period, member):
    row = lax.broadcasted_iota(jnp.int32, (SUB, member), 0)
    shift = offsets_of(code, period)
    third = jnp.where(row == 1, shift[1], shift[2])
    return jnp.where(row < 3, jnp.where(row == 0, shift[0], third), 0.0)


def skew_entry(entry, moved, frame, skew_ref):
    for s in range(SUB):
        at = pl.multiple_of(entry * (2 * SUB * SUB), SUB) + 2 * SUB * s
        skew_ref[pl.ds(at, SUB), :] = pltpu.roll(moved, s, 1) if s else moved
        skew_ref[pl.ds(at + SUB, SUB), :] = pltpu.roll(frame, s, 1) if s else frame


def near_blocks(own_frame, partner_frame):
    member = own_frame.shape[1]
    row = lax.broadcasted_iota(jnp.int32, (SUB, member), 0)
    sign = jnp.where(row < 3, 1.0, jnp.where(row < 6, -1.0, 0.0))

    def doubled(block):
        centre = jnp.where(row < 3, block, 0.0)
        return centre + pltpu.roll(centre, 3, 0)

    box = doubled(partner_frame) * sign
    for bit in (1, 2, 4):
        box = jnp.maximum(box, pltpu.roll(box, bit, 1))
    here = doubled(own_frame) * sign
    blocks = member // SUB
    reach = []
    for k in range(blocks):
        gap = jnp.maximum(here - (pltpu.roll(box, k * SUB, 1) if k else box), 0.0)
        reach.append(jnp.sum(gap * gap, axis=0, keepdims=True))
    nearest = jnp.min(jnp.concatenate(reach, axis=0), axis=1, keepdims=True)
    weight = (1 << lax.broadcasted_iota(jnp.int32, (blocks, 1), 0)).astype(jnp.float32)
    return jnp.sum(jnp.where(nearest < cutoff_sq * 1.001, weight, 0.0)).astype(jnp.int32)


def tile_product(item_count, item_ref, own_moved, own_frame, skew_ref):
    member = skew_ref.shape[1]
    blocks = member // SUB

    def wide(row):
        return jnp.broadcast_to(row, (SUB, member))

    xi = [wide(own_frame[k : k + 1]) for k in range(3)]
    ui = [wide(own_frame[k : k + 1]) for k in range(3, 6)]
    dxi = [wide(own_moved[k : k + 1]) for k in range(3)]
    dui = [wide(own_moved[k : k + 1]) for k in range(3, 6)]
    first_row = (lax.broadcasted_iota(jnp.int32, (SUB, member), 0) == 0).astype(jnp.float32)

    def one(at):
        item = item_ref[at]
        entry = item // blocks
        turn_by = item % blocks * SUB
        base = entry * (2 * SUB * SUB)

        def other(k):
            return pltpu.roll(skew_ref[pl.ds(base + k, SUB, stride=2 * SUB), :], turn_by, 1)

        d = [other(FRAME + k) - xi[k] for k in range(3)]
        uj = [other(FRAME + k) for k in range(3, 6)]
        dd = [other(k) - dxi[k] for k in range(3)]
        duj = [other(k) for k in range(3, 6)]
        itself = jnp.where(item == 0, 2.0 * cutoff_sq, 0.0)
        unused = jnp.where(at < item_count, 0.0, 2.0 * cutoff_sq)
        lift = first_row * itself + unused
        a, c, u_r, u_a, u_b, u_c, du_r, du_a, du_b, du_c = pair_tangent(d, ui, uj, dd, dui, duj, lift)
        force = [du_r * d[k] + u_r * dd[k] + du_b * uj[k] + u_b * duj[k] for k in range(3)]
        turn = [du_a * d[k] + u_a * dd[k] + du_c * uj[k] + u_c * duj[k] for k in range(3)]
        return force + turn + [du_a, u_a, u_a * a + u_c * c]

    def visit(step, totals):
        news = [one(step * GROUP + part) for part in range(GROUP)]
        return tuple(sum(parts, total) for total, parts in zip(totals, zip(*news)))

    zero = jnp.zeros((SUB, member), jnp.float32)
    totals = lax.fori_loop(0, (item_count + GROUP - 1) // GROUP, visit, (zero,) * 9)
    sums = [jnp.sum(total, axis=0, keepdims=True) for total in totals]
    u = [row[:1] for row in ui]
    t = [row[:1] for row in dui]
    force = [-(sums[k] + u[k] * sums[6] + t[k] * sums[7]) for k in range(3)]
    turn = cross3(u, [sums[3 + k] - t[k] * sums[8] for k in range(3)])
    return force + list(cross3(turn, u))


def spread(rows, out_ref):
    member = rows[0].shape[1]
    fill = [jnp.zeros((1, member), jnp.float32)] * (SUB - len(rows))
    block = jnp.concatenate(rows + fill, axis=0)
    out_ref[...] = jnp.broadcast_to(block[None], out_ref.shape)


def pack_kernel(config_ref, start_ref, list_ref, out_ref):
    u = [config_ref[k : k + 1, :] for k in range(3, 6)]
    w = [start_ref[k : k + 1, :] for k in range(3, 6)]
    t = cross3(w, u)
    zero = jnp.zeros_like(u[0])
    block = jnp.concatenate(
        [start_ref[0:3, :], t[0], t[1], t[2], dot3(w, u), zero, config_ref[...], list_ref[...], zero], axis=0
    )
    out_ref[...] = jnp.broadcast_to(block[None], out_ref.shape)


def first_kernel(
    rows, cols, slots, period, all_ref, out_ref, entry_ref, item_ref, count_ref, skew_ref, code_ref, code_smem, sem
):
    member = all_ref.shape[2]
    row_id = lax.axis_index("row")
    col_id = lax.axis_index("col")
    own = row_id * cols + col_id
    blocks = member // SUB

    def field(line, at):
        return line if at == 0 else pltpu.roll(line, member - at * slots, 1)

    def encode(line, partner, side):
        offset = (field(line, 2) * 16.0 + field(line, 3) * 4.0 + field(line, 4)) * side + 21.0
        return partner * float(1 << CODE_BITS) + offset

    row_f = row_id.astype(jnp.float32)
    col_f = col_id.astype(jnp.float32)
    for col in range(cols):
        line = all_ref[row_id * cols + col, LIST_ROW : LIST_ROW + 1, :]
        code = encode(line, field(line, 1) * float(cols) + float(col), 1.0)
        code_ref[col : col + 1, :] = jnp.where(line == col_f, code, -1.0).astype(jnp.int32)
    for row in range(rows):
        line = all_ref[row * cols + col_id, LIST_ROW : LIST_ROW + 1, :]
        code = encode(line, float(row * cols) + line, -1.0)
        hit = (field(line, 1) == row_f) & (line >= 0.0)
        code_ref[cols + row : cols + row + 1, :] = jnp.where(hit, code, -1.0).astype(jnp.int32)
    copy = pltpu.make_async_copy(code_ref, code_smem, sem)
    copy.start()
    copy.wait()

    entry_ref[0] = own * (1 << CODE_BITS) + 21

    def gather(line, count):
        for slot in range(slots):
            code = code_smem[line, slot]
            entry_ref[count] = code
            count = count + (code >= 0).astype(jnp.int32)
        return count

    entries = lax.fori_loop(0, rows + cols, gather, jnp.int32(1))
    own_frame = all_ref[own, FRAME : FRAME + SUB, :]

    def prepare(entry, count):
        code = entry_ref[entry]
        partner = code >> CODE_BITS
        frame = all_ref[partner, FRAME : FRAME + SUB, :] + offset_rows(code, period, member)
        skew_entry(entry, all_ref[partner, 0:SUB, :], frame, skew_ref)
        bits = near_blocks(own_frame, frame)
        for block in range(blocks):
            item_ref[count] = entry * blocks + block
            count = count + (bits >> block & 1)
        return count

    items = lax.fori_loop(0, entries, prepare, jnp.int32(0))
    for part in range(GROUP):
        item_ref[items + part] = 0
    count_ref[0] = entries
    count_ref[1] = items
    spread(tile_product(items, item_ref, all_ref[own, 0:SUB, :], own_frame, skew_ref), out_ref)


def whole_sum(left_ref, right_ref):
    total = jnp.sum(left_ref[...] * right_ref[...], axis=0)
    return jnp.sum(jnp.sum(total, axis=0, keepdims=True), axis=1, keepdims=True)


def second_kernel(
    cols,
    total_entries,
    period,
    entry_ref,
    item_ref,
    count_ref,
    all_ref,
    image_ref,
    out_ref,
    second_ref,
    scalar_ref,
    skew_ref,
    basis_ref,
):
    own = lax.axis_index("row") * cols + lax.axis_index("col")
    member = all_ref.shape[2]
    basis_ref[...] = all_ref[:, 0:SUB, :]
    norm_sq = whole_sum(basis_ref, basis_ref) / total_entries + norm_eps
    alpha = whole_sum(basis_ref, image_ref) / total_entries / norm_sq
    second_ref[...] = image_ref[...] - alpha * basis_ref[...]
    beta = jnp.sqrt(whole_sum(second_ref, second_ref) / total_entries / norm_sq + norm_eps)
    scale = lax.rsqrt(norm_sq) / beta

    def prepare(entry, carry):
        code = entry_ref[entry]
        partner = code >> CODE_BITS
        frame = all_ref[partner, FRAME : FRAME + SUB, :] + offset_rows(code, period, member)
        skew_entry(entry, second_ref[partner], frame, skew_ref)
        return carry

    lax.fori_loop(0, count_ref[0], prepare, 0)
    product = tile_product(count_ref[1], item_ref, second_ref[own], all_ref[own, FRAME : FRAME + SUB, :], skew_ref)
    back = beta * lax.rsqrt(norm_sq)
    rows = product + [jnp.zeros((1, member), jnp.float32)]
    spread([row * scale - back * basis_ref[own, k : k + 1, :] for k, row in enumerate(rows)], out_ref)
    second_ref[...] = second_ref[...] * scale
    lane = lax.broadcasted_iota(jnp.int32, (1, member), 1)
    scalar_ref[...] = jnp.where(lane == 0, alpha, jnp.where(lane == 1, beta, 0.0))


def last_kernel(cols, total_entries, config_ref, second_ref, image_ref, scalar_ref, mode_ref, coefficient_ref):
    own = lax.axis_index("row") * cols + lax.axis_index("col")
    member = config_ref.shape[1]
    alpha = whole_sum(second_ref, image_ref) / total_entries
    rest = image_ref[...] - alpha * second_ref[...]
    total = jnp.sum(rest * rest, axis=0)
    total = jnp.sum(jnp.sum(total, axis=0, keepdims=True), axis=1, keepdims=True)
    beta = jnp.sqrt(total / total_entries + norm_eps)
    mine = (image_ref[own] - alpha * second_ref[own]) / beta
    u = [config_ref[k : k + 1, :] for k in range(3, 6)]
    turn = cross3(u, [mine[k : k + 1] for k in range(3, 6)])
    along = mine[6:7]
    mode_ref[...] = jnp.concatenate([mine[0:3]] + [turn[k] + along * u[k] for k in range(3)], axis=0)
    lane = lax.broadcasted_iota(jnp.int32, (1, member), 1)
    coefficient_ref[...] = jnp.where(lane == 2, alpha, jnp.where(lane == 3, beta, scalar_ref[...]))


def local(config, start, tile_list, tile_count):
    dof, member = config.shape
    row_devices = lax.axis_size("row")
    col_devices = lax.axis_size("col")
    devices = row_devices * col_devices
    total_entries = float(dof * member * devices)
    period = (5.0, 5.0, 3.5 * (member // 16))
    entries = tile_list[0, 0]
    slots, fields = entries.shape
    longest = (row_devices + col_devices) * slots + 1

    def shaped(*shape):
        return jax.ShapeDtypeStruct(shape, jnp.float32)

    def everywhere(copies):
        return lax.all_to_all(copies, ("row", "col"), 0, 0, tiled=True)

    params = pltpu.CompilerParams(vmem_limit_bytes=VMEM_LIMIT)
    vmem = pl.BlockSpec(memory_space=pltpu.VMEM)
    smem = pl.BlockSpec(memory_space=pltpu.SMEM)

    in_use = jnp.arange(slots, dtype=jnp.int32) < tile_count[0, 0]
    fields_f = jnp.where(in_use[:, None], entries, -9).astype(jnp.float32).T.reshape(1, fields * slots)
    list_row = jnp.pad(fields_f, ((0, 0), (0, member - fields * slots)), constant_values=-9.0)

    packed = pl.pallas_call(
        pack_kernel,
        out_shape=shaped(devices, ROWS, member),
        in_specs=[vmem] * 3,
        out_specs=vmem,
        compiler_params=params,
    )(config, start, list_row)
    together = everywhere(packed)

    skew = pltpu.VMEM((longest * 2 * SUB * SUB, member), jnp.float32)
    image, codes, items, counts = pl.pallas_call(
        functools.partial(first_kernel, row_devices, col_devices, slots, period),
        out_shape=(
            shaped(devices, SUB, member),
            jax.ShapeDtypeStruct((longest + 1,), jnp.int32),
            jax.ShapeDtypeStruct((longest * (member // SUB) + GROUP,), jnp.int32),
            jax.ShapeDtypeStruct((2,), jnp.int32),
        ),
        in_specs=[vmem],
        out_specs=(vmem, smem, smem, smem),
        scratch_shapes=[
            skew,
            pltpu.VMEM((row_devices + col_devices, member), jnp.int32),
            pltpu.SMEM((row_devices + col_devices, member), jnp.int32),
            pltpu.SemaphoreType.DMA,
        ],
        compiler_params=params,
    )(together)
    image = everywhere(image)

    residual, second, scalars = pl.pallas_call(
        functools.partial(second_kernel, col_devices, total_entries, period),
        out_shape=(shaped(devices, SUB, member), shaped(devices, SUB, member), shaped(1, member)),
        in_specs=[smem, smem, smem, vmem, vmem],
        out_specs=(vmem, vmem, vmem),
        scratch_shapes=[skew, pltpu.VMEM((devices, SUB, member), jnp.float32)],
        compiler_params=params,
    )(codes, items, counts, together, image)
    residual = everywhere(residual)

    mode, coefficients = pl.pallas_call(
        functools.partial(last_kernel, col_devices, total_entries),
        out_shape=(shaped(dof, member), shaped(1, member)),
        in_specs=[vmem] * 4,
        out_specs=(vmem, vmem),
        compiler_params=params,
    )(config, second, residual, scalars)
    return (coefficients[0, :4], mode)


def solution(mesh):
    placed = (
        P(None, ("row", "col")),
        P(None, ("row", "col")),
        P("row", "col", None, None),
        P("row", "col"),
    )
    return jax.shard_map(
        local, mesh=mesh, in_specs=placed, out_specs=(P(), P(None, ("row", "col"))), check_vma=False
    )
```

```python
import functools
import math

import jax
import jax.numpy as jnp
from jax import lax
from jax.experimental import pallas as pl
from jax.experimental.pallas import tpu as pltpu
from jax.sharding import PartitionSpec as P

chi_shape = 0.8
chi_energy = (math.sqrt(5.0) - 1.0) / (math.sqrt(5.0) + 1.0)
well_depth = 0.005
cutoff_sq = 20.25
norm_eps = 1e-06

SUB = 8
FRAME = 8
LIST_ROW = 14
ROWS = 16
CODE_BITS = 6
GROUP = 2
VMEM_LIMIT = 48 * 1024 * 1024


def dot3(a, b):
    return a[0] * b[0] + a[1] * b[1] + a[2] * b[2]


def cross3(a, b):
    return (
        a[1] * b[2] - a[2] * b[1],
        a[2] * b[0] - a[0] * b[2],
        a[0] * b[1] - a[1] * b[0],
    )


def bracket(chi, scaled, factor, p, a, b, eps, da, db, dc):
    f = factor * (a - scaled * b)
    g = factor * (b - scaled * a)
    y = p * (a * f + b * g)
    bent = chi * dc
    da_bent = da - bent * g
    db_bent = db - bent * f
    df = factor * (da_bent - scaled * db_bent)
    dg = factor * (db_bent - scaled * da_bent)
    half_dy = p * (f * da_bent + g * db - eps * y)
    return f, g, y, df, dg, half_dy


def pair_tangent(d, ui, uj, dd, dui, duj, lift):
    r_sq = dot3(d, d) + lift
    a = dot3(d, ui)
    b = dot3(d, uj)
    c = dot3(ui, uj)
    eps = dot3(d, dd)
    da = dot3(dd, ui) + dot3(d, dui)
    db = dot3(dd, uj) + dot3(d, duj)
    dc = dot3(dui, uj) + dot3(ui, duj)
    r_inv = lax.rsqrt(r_sq)
    p = r_inv * r_inv
    r = r_sq * r_inv
    x = jnp.maximum(1.0 - r_sq * (1.0 / cutoff_sq), 0.0)
    c_shape = chi_shape * c
    c_energy = chi_energy * c
    e1 = lax.rsqrt(1.0 - c_shape * c_shape)
    q = e1 * e1
    q2 = 1.0 / (1.0 - c_energy * c_energy)
    f, g, y, df, dg, hdy = bracket(chi_shape, c_shape, q, p, a, b, eps, da, db, dc)
    f2, g2, y2, df2, dg2, hdy2 = bracket(chi_energy, c_energy, q2, p, a, b, eps, da, db, dc)
    sigma = lax.rsqrt(1.0 - chi_shape * y)
    sigma_sq = sigma * sigma
    sigma_cu = sigma_sq * sigma
    psi = 1.0 - chi_energy * y2
    s = 1.0 / (r - sigma + 1.0)
    s_sq = s * s
    s6 = s_sq * s_sq * s_sq
    t0 = s6 * (s6 - 1.0)
    t1 = s6 * s * (6.0 - 12.0 * s6)
    t2 = s6 * s_sq * (156.0 * s6 - 42.0)
    ke = (4.0 * well_depth) * e1
    kx = ke * x
    vrr = kx * (6.0 / cutoff_sq**2)
    kxx = kx * x
    vr = kxx * (-3.0 / cutoff_sq)
    v = kxx * x
    psi_sq = psi * psi
    psi_sq_t0 = psi_sq * t0
    v_psi = v * psi
    v_psi_t0 = v_psi * t0
    v_psi_t1 = v_psi * t1
    v_psi_sq = v_psi * psi
    slope = v_psi * psi * t1
    pull = (-chi_shape) * p * sigma_cu
    h1 = pull * slope
    push = (-4.0 * chi_energy) * p
    h2 = push * v_psi_t0
    u_a = h1 * f + h2 * f2
    u_b = h1 * g + h2 * g2
    kc = chi_shape * c_shape * q
    u = v * psi_sq_t0
    fg = chi_shape * f * g
    fg2 = chi_energy * f2 * g2
    u_c = u * kc - (h1 * fg + h2 * fg2)
    u_r = r_inv * slope + 2.0 * vr * psi_sq_t0 - (h1 * y + h2 * y2)

    dy = 2.0 * hdy
    dy2 = 2.0 * hdy2
    d_sigma = chi_shape * sigma_cu * hdy
    d_rho = r_inv * eps - d_sigma
    d_psi = (-chi_energy) * dy2
    eps2 = 2.0 * eps
    kc_dc = kc * dc
    dv = v * kc_dc + vr * eps2
    dvr = vr * kc_dc + vrr * eps2
    d_psi2 = 2.0 * d_psi
    d_slope = dv * psi_sq * t1 + v_psi_t1 * d_psi2 + v_psi_sq * t2 * d_rho
    fall = p * eps2
    dh1 = h1 * ((3.0 * chi_shape) * sigma_sq * hdy - fall) + pull * d_slope
    dh2 = push * (dv * psi * t0 + v * d_psi * t0 + v_psi_t1 * d_rho) - h2 * fall
    du_a = dh1 * f + h1 * df + dh2 * f2 + h2 * df2
    du_b = dh1 * g + h1 * dg + dh2 * g2 + h2 * dg2
    d_kc = (chi_shape * chi_shape) * q * (2.0 * q - 1.0) * dc
    d_well = psi * d_psi2 * t0 + psi_sq * t1 * d_rho
    du = dv * psi_sq_t0 + v * d_well
    du_c = (
        du * kc
        + u * d_kc
        - (dh1 * fg + chi_shape * h1 * (df * g + f * dg))
        - (dh2 * fg2 + chi_energy * h2 * (df2 * g2 + f2 * dg2))
    )
    du_r = (
        r_inv * (d_slope - p * eps * slope)
        + 2.0 * (dvr * psi_sq_t0 + vr * d_well)
        - (dh1 * y + h1 * dy + dh2 * y2 + h2 * dy2)
    )
    return a, c, u_r, u_a, u_b, u_c, du_r, du_a, du_b, du_c


def offsets_of(code, period):
    return [((code >> bits & 3) - 1).astype(jnp.float32) * size for bits, size in zip((4, 2, 0), period)]


def offset_rows(code, period, member):
    row = lax.broadcasted_iota(jnp.int32, (SUB, member), 0)
    shift = offsets_of(code, period)
    third = jnp.where(row == 1, shift[1], shift[2])
    return jnp.where(row < 3, jnp.where(row == 0, shift[0], third), 0.0)


def skew_entry(entry, moved, frame, skew_ref):
    for s in range(SUB):
        at = pl.multiple_of(entry * (2 * SUB * SUB), SUB) + 2 * SUB * s
        skew_ref[pl.ds(at, SUB), :] = pltpu.roll(moved, s, 1) if s else moved
        skew_ref[pl.ds(at + SUB, SUB), :] = pltpu.roll(frame, s, 1) if s else frame


def near_blocks(own_frame, partner_frame):
    member = own_frame.shape[1]
    row = lax.broadcasted_iota(jnp.int32, (SUB, member), 0)
    sign = jnp.where(row < 3, 1.0, jnp.where(row < 6, -1.0, 0.0))

    def doubled(block):
        centre = jnp.where(row < 3, block, 0.0)
        return centre + pltpu.roll(centre, 3, 0)

    box = doubled(partner_frame) * sign
    for bit in (1, 2, 4):
        box = jnp.maximum(box, pltpu.roll(box, bit, 1))
    here = doubled(own_frame) * sign
    blocks = member // SUB
    reach = []
    for k in range(blocks):
        gap = jnp.maximum(here - (pltpu.roll(box, k * SUB, 1) if k else box), 0.0)
        reach.append(jnp.sum(gap * gap, axis=0, keepdims=True))
    nearest = jnp.min(jnp.concatenate(reach, axis=0), axis=1, keepdims=True)
    weight = (1 << lax.broadcasted_iota(jnp.int32, (blocks, 1), 0)).astype(jnp.float32)
    return jnp.sum(jnp.where(nearest < cutoff_sq * 1.001, weight, 0.0)).astype(jnp.int32)


def tile_product(item_count, item_ref, own_moved, own_frame, skew_ref):
    member = skew_ref.shape[1]
    blocks = member // SUB

    def wide(row):
        return jnp.broadcast_to(row, (SUB, member))

    xi = [wide(own_frame[k : k + 1]) for k in range(3)]
    ui = [wide(own_frame[k : k + 1]) for k in range(3, 6)]
    dxi = [wide(own_moved[k : k + 1]) for k in range(3)]
    dui = [wide(own_moved[k : k + 1]) for k in range(3, 6)]
    first_row = (lax.broadcasted_iota(jnp.int32, (SUB, member), 0) == 0).astype(jnp.float32)

    def stacked(parts):
        return jnp.concatenate(parts, axis=0)

    def both(block):
        return stacked([block] * GROUP)

    x_own, u_own, dx_own, du_own = [[both(block) for block in blocks_of] for blocks_of in (xi, ui, dxi, dui)]

    def visit(step, totals):
        at = [step * GROUP + part for part in range(GROUP)]
        item = [item_ref[place] for place in at]
        base = [(one // blocks) * (2 * SUB * SUB) for one in item]
        turn_by = [one % blocks * SUB for one in item]
        unused = [jnp.where(place < item_count, 0.0, 2.0 * cutoff_sq) for place in at]
        itself = [jnp.where(one == 0, 2.0 * cutoff_sq, 0.0) for one in item]
        lift = stacked([first_row * one + two for one, two in zip(itself, unused)])

        def other(k):
            loaded = [skew_ref[pl.ds(start + k, SUB, stride=2 * SUB), :] for start in base]
            return stacked([pltpu.roll(block, by, 1) for block, by in zip(loaded, turn_by)])

        d = [other(FRAME + k) - x_own[k] for k in range(3)]
        uj = [other(FRAME + k) for k in range(3, 6)]
        dd = [other(k) - dx_own[k] for k in range(3)]
        duj = [other(k) for k in range(3, 6)]
        a, c, u_r, u_a, u_b, u_c, du_r, du_a, du_b, du_c = pair_tangent(d, u_own, uj, dd, du_own, duj, lift)
        force = [du_r * d[k] + u_r * dd[k] + du_b * uj[k] + u_b * duj[k] for k in range(3)]
        turn = [du_a * d[k] + u_a * dd[k] + du_c * uj[k] + u_c * duj[k] for k in range(3)]
        news = force + turn + [du_a, u_a, u_a * a + u_c * c]
        halves = [[new[part * SUB : (part + 1) * SUB] for part in range(GROUP)] for new in news]
        return tuple(sum(parts, total) for total, parts in zip(totals, halves))

    zero = jnp.zeros((SUB, member), jnp.float32)
    totals = lax.fori_loop(0, (item_count + GROUP - 1) // GROUP, visit, (zero,) * 9)
    sums = [jnp.sum(total, axis=0, keepdims=True) for total in totals]
    u = [row[:1] for row in ui]
    t = [row[:1] for row in dui]
    force = [-(sums[k] + u[k] * sums[6] + t[k] * sums[7]) for k in range(3)]
    turn = cross3(u, [sums[3 + k] - t[k] * sums[8] for k in range(3)])
    return force + list(cross3(turn, u))


def spread(rows, out_ref):
    member = rows[0].shape[1]
    fill = [jnp.zeros((1, member), jnp.float32)] * (SUB - len(rows))
    block = jnp.concatenate(rows + fill, axis=0)
    out_ref[...] = jnp.broadcast_to(block[None], out_ref.shape)


def pack_kernel(config_ref, start_ref, list_ref, out_ref):
    u = [config_ref[k : k + 1, :] for k in range(3, 6)]
    w = [start_ref[k : k + 1, :] for k in range(3, 6)]
    t = cross3(w, u)
    zero = jnp.zeros_like(u[0])
    block = jnp.concatenate(
        [start_ref[0:3, :], t[0], t[1], t[2], dot3(w, u), zero, config_ref[...], list_ref[...], zero], axis=0
    )
    out_ref[...] = jnp.broadcast_to(block[None], out_ref.shape)


def first_kernel(
    rows, cols, slots, period, all_ref, out_ref, entry_ref, item_ref, count_ref, skew_ref, code_ref, code_smem, sem
):
    member = all_ref.shape[2]
    row_id = lax.axis_index("row")
    col_id = lax.axis_index("col")
    own = col_id * rows + row_id
    blocks = member // SUB

    def field(line, at):
        return line if at == 0 else pltpu.roll(line, member - at * slots, 1)

    def encode(line, partner, side):
        offset = (field(line, 2) * 16.0 + field(line, 3) * 4.0 + field(line, 4)) * side + 21.0
        return partner * float(1 << CODE_BITS) + offset

    row_f = row_id.astype(jnp.float32)
    col_f = col_id.astype(jnp.float32)
    for col in range(cols):
        line = all_ref[col * rows + row_id, LIST_ROW : LIST_ROW + 1, :]
        code = encode(line, float(col * rows) + field(line, 1), 1.0)
        code_ref[col : col + 1, :] = jnp.where(line == col_f, code, -1.0).astype(jnp.int32)
    for row in range(rows):
        line = all_ref[col_id * rows + row, LIST_ROW : LIST_ROW + 1, :]
        code = encode(line, line * float(rows) + float(row), -1.0)
        hit = (field(line, 1) == row_f) & (line >= 0.0)
        code_ref[cols + row : cols + row + 1, :] = jnp.where(hit, code, -1.0).astype(jnp.int32)
    copy = pltpu.make_async_copy(code_ref, code_smem, sem)
    copy.start()
    copy.wait()

    entry_ref[0] = own * (1 << CODE_BITS) + 21

    def gather(line, count):
        for slot in range(slots):
            code = code_smem[line, slot]
            entry_ref[count] = code
            count = count + (code >= 0).astype(jnp.int32)
        return count

    entries = lax.fori_loop(0, rows + cols, gather, jnp.int32(1))
    own_frame = all_ref[own, FRAME : FRAME + SUB, :]

    def prepare(entry, count):
        code = entry_ref[entry]
        partner = code >> CODE_BITS
        frame = all_ref[partner, FRAME : FRAME + SUB, :] + offset_rows(code, period, member)
        skew_entry(entry, all_ref[partner, 0:SUB, :], frame, skew_ref)
        bits = near_blocks(own_frame, frame)
        for block in range(blocks):
            item_ref[count] = entry * blocks + block
            count = count + (bits >> block & 1)
        return count

    items = lax.fori_loop(0, entries, prepare, jnp.int32(0))
    for part in range(GROUP):
        item_ref[items + part] = 0
    count_ref[0] = entries
    count_ref[1] = items
    spread(tile_product(items, item_ref, all_ref[own, 0:SUB, :], own_frame, skew_ref), out_ref)


def whole_sum(left_ref, right_ref):
    total = jnp.sum(left_ref[...] * right_ref[...], axis=0)
    return jnp.sum(jnp.sum(total, axis=0, keepdims=True), axis=1, keepdims=True)


def second_kernel(
    rows,
    total_entries,
    period,
    entry_ref,
    item_ref,
    count_ref,
    all_ref,
    image_ref,
    out_ref,
    second_ref,
    scalar_ref,
    skew_ref,
    basis_ref,
):
    own = lax.axis_index("col") * rows + lax.axis_index("row")
    member = all_ref.shape[2]
    basis_ref[...] = all_ref[:, 0:SUB, :]
    norm_sq = whole_sum(basis_ref, basis_ref) / total_entries + norm_eps
    alpha = whole_sum(basis_ref, image_ref) / total_entries / norm_sq
    second_ref[...] = image_ref[...] - alpha * basis_ref[...]
    beta = jnp.sqrt(whole_sum(second_ref, second_ref) / total_entries / norm_sq + norm_eps)
    scale = lax.rsqrt(norm_sq) / beta

    def prepare(entry, carry):
        code = entry_ref[entry]
        partner = code >> CODE_BITS
        frame = all_ref[partner, FRAME : FRAME + SUB, :] + offset_rows(code, period, member)
        skew_entry(entry, second_ref[partner], frame, skew_ref)
        return carry

    lax.fori_loop(0, count_ref[0], prepare, 0)
    product = tile_product(count_ref[1], item_ref, second_ref[own], all_ref[own, FRAME : FRAME + SUB, :], skew_ref)
    back = beta * lax.rsqrt(norm_sq)
    lines = product + [jnp.zeros((1, member), jnp.float32)]
    spread([line * scale - back * basis_ref[own, k : k + 1, :] for k, line in enumerate(lines)], out_ref)
    second_ref[...] = second_ref[...] * scale
    lane = lax.broadcasted_iota(jnp.int32, (1, member), 1)
    scalar_ref[...] = jnp.where(lane == 0, alpha, jnp.where(lane == 1, beta, 0.0))


def last_kernel(rows, total_entries, config_ref, second_ref, image_ref, scalar_ref, mode_ref, coefficient_ref):
    own = lax.axis_index("col") * rows + lax.axis_index("row")
    member = config_ref.shape[1]
    alpha = whole_sum(second_ref, image_ref) / total_entries
    rest = image_ref[...] - alpha * second_ref[...]
    total = jnp.sum(rest * rest, axis=0)
    total = jnp.sum(jnp.sum(total, axis=0, keepdims=True), axis=1, keepdims=True)
    beta = jnp.sqrt(total / total_entries + norm_eps)
    mine = (image_ref[own] - alpha * second_ref[own]) / beta
    u = [config_ref[k : k + 1, :] for k in range(3, 6)]
    turn = cross3(u, [mine[k : k + 1] for k in range(3, 6)])
    along = mine[6:7]
    mode_ref[...] = jnp.concatenate([mine[0:3]] + [turn[k] + along * u[k] for k in range(3)], axis=0)
    lane = lax.broadcasted_iota(jnp.int32, (1, member), 1)
    coefficient_ref[...] = jnp.where(lane == 2, alpha, jnp.where(lane == 3, beta, scalar_ref[...]))


def local(config, start, tile_list, tile_count):
    dof, member = config.shape
    row_devices = lax.axis_size("row")
    col_devices = lax.axis_size("col")
    devices = row_devices * col_devices
    total_entries = float(dof * member * devices)
    period = (5.0, 5.0, 3.5 * (member // 16))
    entries = tile_list[0, 0]
    slots, fields = entries.shape
    longest = (row_devices + col_devices) * slots + 1

    def shaped(*shape):
        return jax.ShapeDtypeStruct(shape, jnp.float32)

    def everywhere(copies):
        column = lax.all_to_all(copies, "row", 0, 0, tiled=True)
        copies = jnp.broadcast_to(column, (col_devices,) + column.shape)
        arrived = lax.all_to_all(copies, "col", 0, 0, tiled=True)
        return arrived.reshape((devices,) + column.shape[1:])

    params = pltpu.CompilerParams(vmem_limit_bytes=VMEM_LIMIT)
    vmem = pl.BlockSpec(memory_space=pltpu.VMEM)
    smem = pl.BlockSpec(memory_space=pltpu.SMEM)

    in_use = jnp.arange(slots, dtype=jnp.int32) < tile_count[0, 0]
    fields_f = jnp.where(in_use[:, None], entries, -9).astype(jnp.float32).T.reshape(1, fields * slots)
    list_row = jnp.pad(fields_f, ((0, 0), (0, member - fields * slots)), constant_values=-9.0)

    packed = pl.pallas_call(
        pack_kernel,
        out_shape=shaped(row_devices, ROWS, member),
        in_specs=[vmem] * 3,
        out_specs=vmem,
        compiler_params=params,
    )(config, start, list_row)
    together = everywhere(packed)

    skew = pltpu.VMEM((longest * 2 * SUB * SUB, member), jnp.float32)
    image, codes, items, counts = pl.pallas_call(
        functools.partial(first_kernel, row_devices, col_devices, slots, period),
        out_shape=(
            shaped(row_devices, SUB, member),
            jax.ShapeDtypeStruct((longest + 1,), jnp.int32),
            jax.ShapeDtypeStruct((longest * (member // SUB) + GROUP,), jnp.int32),
            jax.ShapeDtypeStruct((2,), jnp.int32),
        ),
        in_specs=[vmem],
        out_specs=(vmem, smem, smem, smem),
        scratch_shapes=[
            skew,
            pltpu.VMEM((row_devices + col_devices, member), jnp.int32),
            pltpu.SMEM((row_devices + col_devices, member), jnp.int32),
            pltpu.SemaphoreType.DMA,
        ],
        compiler_params=params,
    )(together)
    image = everywhere(image)

    residual, second, scalars = pl.pallas_call(
        functools.partial(second_kernel, row_devices, total_entries, period),
        out_shape=(shaped(row_devices, SUB, member), shaped(devices, SUB, member), shaped(1, member)),
        in_specs=[smem, smem, smem, vmem, vmem],
        out_specs=(vmem, vmem, vmem),
        scratch_shapes=[skew, pltpu.VMEM((devices, SUB, member), jnp.float32)],
        compiler_params=params,
    )(codes, items, counts, together, image)
    residual = everywhere(residual)

    mode, coefficients = pl.pallas_call(
        functools.partial(last_kernel, row_devices, total_entries),
        out_shape=(shaped(dof, member), shaped(1, member)),
        in_specs=[vmem] * 4,
        out_specs=(vmem, vmem),
        compiler_params=params,
    )(config, second, residual, scalars)
    return (coefficients[0, :4], mode)


def solution(mesh):
    placed = (
        P(None, ("row", "col")),
        P(None, ("row", "col")),
        P("row", "col", None, None),
        P("row", "col"),
    )
    return jax.shard_map(
        local, mesh=mesh, in_specs=placed, out_specs=(P(), P(None, ("row", "col"))), check_vma=False
    )
```

```python
import functools
import math

import jax
import jax.numpy as jnp
from jax import lax
from jax.experimental import pallas as pl
from jax.experimental.pallas import tpu as pltpu
from jax.sharding import PartitionSpec as P

chi_shape = 0.8
chi_energy = (math.sqrt(5.0) - 1.0) / (math.sqrt(5.0) + 1.0)
well_depth = 0.005
cutoff_sq = 20.25
norm_eps = 1e-06

SUB = 8
LIST_ROW = 6
CODE_BITS = 6
GROUP = 2
TERMS = 20
HELD = 128
VMEM_LIMIT = 32 * 1024 * 1024


def dot3(a, b):
    return a[0] * b[0] + a[1] * b[1] + a[2] * b[2]


def cross3(a, b):
    return (
        a[1] * b[2] - a[2] * b[1],
        a[2] * b[0] - a[0] * b[2],
        a[0] * b[1] - a[1] * b[0],
    )


def bracket(chi, scaled, factor, p, a, b):
    f = factor * (a - scaled * b)
    g = factor * (b - scaled * a)
    y = p * (a * f + b * g)
    cross = factor * scaled
    f_c = chi * (cross * f - factor * g)
    g_c = chi * (cross * g - factor * f)
    return f, g, y, cross, f_c, g_c


def pair_coefficients(d, ui, uj, lift):
    r_sq = dot3(d, d) + lift
    a = dot3(d, ui)
    b = dot3(d, uj)
    c = dot3(ui, uj)
    r_inv = lax.rsqrt(r_sq)
    p = r_inv * r_inv
    p2 = 2.0 * p
    r = r_sq * r_inv
    x = jnp.maximum(1.0 - r_sq * (1.0 / cutoff_sq), 0.0)
    c_shape = chi_shape * c
    c_energy = chi_energy * c
    e1 = lax.rsqrt(1.0 - c_shape * c_shape)
    q = e1 * e1
    q2 = 1.0 / (1.0 - c_energy * c_energy)
    f, g, y, m, f_c, g_c = bracket(chi_shape, c_shape, q, p, a, b)
    f2, g2, y2, m2, f2_c, g2_c = bracket(chi_energy, c_energy, q2, p, a, b)
    sigma = lax.rsqrt(1.0 - chi_shape * y)
    sigma_sq = sigma * sigma
    psi = 1.0 - chi_energy * y2
    s = 1.0 / (r - sigma + 1.0)
    s_sq = s * s
    s6 = s_sq * s_sq * s_sq
    t0 = s6 * (s6 - 1.0)
    t1 = s6 * s * (6.0 - 12.0 * s6)
    t2 = s6 * s_sq * (156.0 * s6 - 42.0)
    ke = (4.0 * well_depth) * e1
    kx = ke * x
    v_ee = kx * (24.0 / cutoff_sq**2)
    kxx = kx * x
    v_e = kxx * (-6.0 / cutoff_sq)
    v = kxx * x
    psi_sq = psi * psi
    psi_sq_t0 = psi_sq * t0
    psi_sq_t1 = psi_sq * t1
    u = v * psi_sq_t0
    slope = v * psi_sq_t1
    slope2 = v * psi_sq * t2
    tau = (-0.5 * chi_shape) * sigma_sq * sigma
    push = (-2.0 * chi_energy) * psi
    v_t1 = v * t1
    d1 = slope * tau
    d2 = push * (v * t0)
    h1 = p2 * d1
    h2 = p2 * d2
    kc = chi_shape * c_shape * q
    fg = chi_shape * f * g
    fg2 = chi_energy * f2 * g2
    u_a = h1 * f + h2 * f2
    u_b = h1 * g + h2 * g2
    u_fg = h1 * fg + h2 * fg2
    u_c = u * kc - u_fg
    v_e_t0 = v_e * psi_sq_t0
    d_e = r_inv * slope + v_e_t0
    u_e = d_e - (h1 * y + h2 * y2)

    p2_sq = p2 * p2
    k11 = p2_sq * (tau * (slope2 * tau + (1.5 * chi_shape) * sigma_sq * slope))
    k12 = p2_sq * (push * v_t1 * tau)
    k22 = p2_sq * ((2.0 * chi_energy * chi_energy) * (v * t0))
    steep = v_e * psi_sq_t1 + slope2 * r_inv
    l1 = p2 * (steep * tau - h1)
    l2 = p2 * (push * (v_e * t0 + v_t1 * r_inv) - h2)
    j1 = (y, f, g, fg)
    j2 = (y2, f2, g2, fg2)
    w1 = [k11 * one + k12 * two for one, two in zip(j1, j2)]
    w2 = [k12 * one + k22 * two for one, two in zip(j1, j2)]

    def quadratic(m_at, n_at):
        return w1[m_at] * j1[n_at] + w2[m_at] * j2[n_at]

    d_ee = v_ee * psi_sq_t0 + r_inv * (2.0 * (v_e * psi_sq_t1)) + p * (slope2 - slope * r_inv)
    h_ee = quadratic(0, 0) - 2.0 * (l1 * y + l2 * y2) + d_ee
    h_ea = l1 * f + l2 * f2 - quadratic(0, 1)
    h_eb = l1 * g + l2 * g2 - quadratic(0, 2)
    h_ec = quadratic(0, 3) - (l1 * fg + l2 * fg2) + kc * u_e
    straight = h1 * q + h2 * q2
    h_aa = quadratic(1, 1) + straight
    h_ab = quadratic(1, 2) - (h1 * m + h2 * m2)
    h_ac = kc * u_a - quadratic(1, 3) + (h1 * f_c + h2 * f2_c)
    h_bb = quadratic(2, 2) + straight
    h_bc = kc * u_b - quadratic(2, 3) + (h1 * g_c + h2 * g2_c)
    bent = (chi_shape * h1) * (f_c * g + f * g_c) + (chi_energy * h2) * (f2_c * g2 + f2 * g2_c)
    twist = kc * kc + (chi_shape * chi_shape) * q * (2.0 * q - 1.0)
    h_cc = quadratic(3, 3) - bent - 2.0 * (kc * u_fg) + u * twist
    gradient = (u_e, u_a, u_b, u_c)
    return gradient, (h_ee, h_ea, h_eb, h_ec, h_aa, h_ab, h_ac, h_bb, h_bc, h_cc), u_a * a + u_c * c


def offsets_of(code, period):
    return [((code >> bits & 3) - 1).astype(jnp.float32) * size for bits, size in zip((4, 2, 0), period)]


def offset_rows(code, period, member):
    row = lax.broadcasted_iota(jnp.int32, (SUB, member), 0)
    shift = offsets_of(code, period)
    third = jnp.where(row == 1, shift[1], shift[2])
    return jnp.where(row < 3, jnp.where(row == 0, shift[0], third), 0.0)


def skew_entry(entry, block, skew_ref):
    for s in range(SUB):
        at = pl.multiple_of(entry * (SUB * SUB) + SUB * s, SUB)
        skew_ref[pl.ds(at, SUB), :] = pltpu.roll(block, s, 1) if s else block


def frame_of(code, period, frame_ref):
    member = frame_ref.shape[2]
    return frame_ref[code >> CODE_BITS] + offset_rows(code, period, member)


def near_blocks(own_frame, partner_frame):
    member = own_frame.shape[1]
    row = lax.broadcasted_iota(jnp.int32, (SUB, member), 0)
    sign = jnp.where(row < 3, 1.0, jnp.where(row < 6, -1.0, 0.0))

    def doubled(block):
        centre = jnp.where(row < 3, block, 0.0)
        return centre + pltpu.roll(centre, 3, 0)

    box = doubled(partner_frame) * sign
    for bit in (1, 2, 4):
        box = jnp.maximum(box, pltpu.roll(box, bit, 1))
    here = doubled(own_frame) * sign
    blocks = member // SUB
    reach = []
    for k in range(blocks):
        gap = jnp.maximum(here - (pltpu.roll(box, k * SUB, 1) if k else box), 0.0)
        reach.append(jnp.sum(gap * gap, axis=0, keepdims=True))
    nearest = jnp.min(jnp.concatenate(reach, axis=0), axis=1, keepdims=True)
    weight = (1 << lax.broadcasted_iota(jnp.int32, (blocks, 1), 0)).astype(jnp.float32)
    return jnp.sum(jnp.where(nearest < cutoff_sq * 1.001, weight, 0.0)).astype(jnp.int32)


def stacked(parts):
    return jnp.concatenate(parts, axis=0)


def wide(block, k):
    return jnp.broadcast_to(block[k : k + 1], (GROUP * SUB, block.shape[1]))


def turned(skew_ref, items, k):
    member = skew_ref.shape[1]
    blocks = member // SUB
    parts = []
    for item in items:
        start = item // blocks * (SUB * SUB) + k
        parts.append(pltpu.roll(skew_ref[pl.ds(start, SUB, stride=SUB), :], item % blocks * SUB, 1))
    return stacked(parts)


def folded(total):
    return jnp.sum(total, axis=0, keepdims=True)


def geometry(items, unused, own_frame, skew_ref):
    member = skew_ref.shape[1]
    first_row = (lax.broadcasted_iota(jnp.int32, (SUB, member), 0) == 0).astype(jnp.float32)
    itself = [jnp.where(item == 0, 2.0 * cutoff_sq, 0.0) for item in items]
    lift = stacked([first_row * one + jnp.where(two, 2.0 * cutoff_sq, 0.0) for one, two in zip(itself, unused)])
    d = [turned(skew_ref, items, k) - wide(own_frame, k) for k in range(3)]
    uj = [turned(skew_ref, items, 3 + k) for k in range(3)]
    ui = [wide(own_frame, 3 + k) for k in range(3)]
    gradient, hessian, spin = pair_coefficients(d, ui, uj, lift)
    return list(gradient) + list(hessian) + d + uj, (gradient[1], spin)


def group_items(step, item_ref, item_count):
    at = [step * GROUP + part for part in range(GROUP)]
    return [item_ref[place] for place in at], [place >= item_count for place in at]


def tile_product(entry_count, item_count, entry_ref, item_ref, coef_ref, kept_ref, own, frame_ref, moved_ref, period, scratch):
    skew_ref, frame_skew_ref = scratch
    member = skew_ref.shape[1]
    own_frame = frame_ref[own]
    own_moved = moved_ref[own]
    held = coef_ref.shape[0] // (TERMS * GROUP * SUB)
    steps = (item_count + GROUP - 1) // GROUP

    def prepare(entry, carry):
        skew_entry(entry, moved_ref[entry_ref[entry] >> CODE_BITS], skew_ref)
        return carry

    lax.fori_loop(0, entry_count, prepare, 0)

    def prepare_frame(entry, carry):
        skew_entry(entry, frame_of(entry_ref[entry], period, frame_ref), frame_skew_ref)
        return carry

    lax.fori_loop(0, jnp.where(steps > held, entry_count, 0), prepare_frame, 0)

    def apply(items, terms, totals):
        u_e, u_a, u_b, u_c, h_ee, h_ea, h_eb, h_ec, h_aa, h_ab, h_ac, h_bb, h_bc, h_cc = terms[:14]
        d = terms[14:17]
        uj = terms[17:20]
        ui = [wide(own_frame, 3 + k) for k in range(3)]
        dui = [wide(own_moved, 3 + k) for k in range(3)]
        dd = [turned(skew_ref, items, k) - wide(own_moved, k) for k in range(3)]
        duj = [turned(skew_ref, items, 3 + k) for k in range(3)]
        de = dot3(d, dd)
        da = dot3(dd, ui) + dot3(d, dui)
        db = dot3(dd, uj) + dot3(d, duj)
        dc = dot3(dui, uj) + dot3(ui, duj)
        du_e = h_ee * de + h_ea * da + h_eb * db + h_ec * dc
        du_a = h_ea * de + h_aa * da + h_ab * db + h_ac * dc
        du_b = h_eb * de + h_ab * da + h_bb * db + h_bc * dc
        du_c = h_ec * de + h_ac * da + h_bc * db + h_cc * dc
        force = [du_e * d[k] + u_e * dd[k] + du_b * uj[k] + u_b * duj[k] for k in range(3)]
        turn = [du_a * d[k] + u_a * dd[k] + du_c * uj[k] + u_c * duj[k] for k in range(3)]
        return tuple(total + new for total, new in zip(totals, force + turn + [du_a]))

    def visit(step, totals):
        items, _ = group_items(step, item_ref, item_count)
        start = pl.multiple_of(step * (TERMS * GROUP * SUB), SUB)
        terms = [coef_ref[pl.ds(start + k * GROUP * SUB, GROUP * SUB), :] for k in range(TERMS)]
        return apply(items, terms, totals)

    def visit_again(step, totals):
        items, unused = group_items(step, item_ref, item_count)
        return apply(items, geometry(items, unused, own_frame, frame_skew_ref)[0], totals)

    zero = jnp.zeros((GROUP * SUB, member), jnp.float32)
    totals = lax.fori_loop(0, jnp.minimum(steps, held), visit, (zero,) * 7)
    totals = lax.fori_loop(held, steps, visit_again, totals)
    sums = [folded(total) for total in totals]
    u = [own_frame[k : k + 1] for k in range(3, 6)]
    t = [own_moved[k : k + 1] for k in range(3, 6)]
    kept = kept_ref[0:1, :]
    spin = kept_ref[1:2, :]
    force = [-(sums[k] + u[k] * sums[6] + t[k] * kept) for k in range(3)]
    turn = cross3(u, [sums[3 + k] - t[k] * spin for k in range(3)])
    return force + list(cross3(turn, u))


def spread(rows, out_ref):
    member = out_ref.shape[2]
    count = sum(row.shape[0] for row in rows)
    fill = [jnp.zeros((1, member), jnp.float32)] * (SUB - count)
    block = jnp.concatenate(list(rows) + fill, axis=0)
    out_ref[...] = jnp.broadcast_to(block[None], out_ref.shape)


def pack_kernel(config_ref, start_ref, list_ref, frame_ref, moved_ref):
    u = [config_ref[k : k + 1, :] for k in range(3, 6)]
    w = [start_ref[k : k + 1, :] for k in range(3, 6)]
    spread([config_ref[...], list_ref[...]], frame_ref)
    spread([start_ref[0:3, :], *cross3(w, u), dot3(w, u)], moved_ref)


def prepare_kernel(
    rows,
    cols,
    slots,
    period,
    frame_ref,
    entry_ref,
    item_ref,
    count_ref,
    coef_ref,
    kept_ref,
    skew_ref,
    code_ref,
    code_smem,
    sem,
):
    member = frame_ref.shape[2]
    row_id = lax.axis_index("row")
    col_id = lax.axis_index("col")
    own = row_id * cols + col_id
    blocks = member // SUB

    def field(line, at):
        return line if at == 0 else pltpu.roll(line, member - at * slots, 1)

    def encode(line, partner, side):
        offset = (field(line, 2) * 16.0 + field(line, 3) * 4.0 + field(line, 4)) * side + 21.0
        return partner * float(1 << CODE_BITS) + offset

    row_f = row_id.astype(jnp.float32)
    col_f = col_id.astype(jnp.float32)
    for col in range(cols):
        line = frame_ref[row_id * cols + col, LIST_ROW : LIST_ROW + 1, :]
        code = encode(line, field(line, 1) * float(cols) + float(col), 1.0)
        code_ref[col : col + 1, :] = jnp.where(line == col_f, code, -1.0).astype(jnp.int32)
    for row in range(rows):
        line = frame_ref[row * cols + col_id, LIST_ROW : LIST_ROW + 1, :]
        code = encode(line, float(row * cols) + line, -1.0)
        hit = (field(line, 1) == row_f) & (line >= 0.0)
        code_ref[cols + row : cols + row + 1, :] = jnp.where(hit, code, -1.0).astype(jnp.int32)
    copy = pltpu.make_async_copy(code_ref, code_smem, sem)
    copy.start()
    copy.wait()

    entry_ref[0] = own * (1 << CODE_BITS) + 21

    def gather(line, count):
        for slot in range(slots):
            code = code_smem[line, slot]
            entry_ref[count] = code
            count = count + (code >= 0).astype(jnp.int32)
        return count

    entries = lax.fori_loop(0, rows + cols, gather, jnp.int32(1))
    own_frame = frame_ref[own]

    def prepare(entry, count):
        frame = frame_of(entry_ref[entry], period, frame_ref)
        skew_entry(entry, frame, skew_ref)
        bits = near_blocks(own_frame, frame)
        for block in range(blocks):
            item_ref[count] = entry * blocks + block
            count = count + (bits >> block & 1)
        return count

    items = lax.fori_loop(0, entries, prepare, jnp.int32(0))
    for part in range(GROUP):
        item_ref[items + part] = 0
    count_ref[0] = entries
    count_ref[1] = items

    held = coef_ref.shape[0] // (TERMS * GROUP * SUB)
    steps = (items + GROUP - 1) // GROUP

    def derive(step, totals):
        group, unused = group_items(step, item_ref, items)
        terms, sums = geometry(group, unused, own_frame, skew_ref)
        return terms, tuple(total + new for total, new in zip(totals, sums))

    def keep(step, totals):
        terms, totals = derive(step, totals)
        start = pl.multiple_of(step * (TERMS * GROUP * SUB), SUB)
        for k in range(TERMS):
            coef_ref[pl.ds(start + k * GROUP * SUB, GROUP * SUB), :] = terms[k]
        return totals

    zero = jnp.zeros((GROUP * SUB, member), jnp.float32)
    totals = lax.fori_loop(0, jnp.minimum(steps, held), keep, (zero,) * 2)
    totals = lax.fori_loop(held, steps, lambda step, before: derive(step, before)[1], totals)
    kept_ref[...] = jnp.concatenate([folded(total) for total in totals], axis=0)


def first_kernel(
    cols,
    period,
    entry_ref,
    item_ref,
    count_ref,
    coef_ref,
    kept_ref,
    frame_ref,
    moved_ref,
    out_ref,
    skew_ref,
    frame_skew_ref,
):
    own = lax.axis_index("row") * cols + lax.axis_index("col")
    product = tile_product(
        count_ref[0],
        count_ref[1],
        entry_ref,
        item_ref,
        coef_ref,
        kept_ref,
        own,
        frame_ref,
        moved_ref,
        period,
        (skew_ref, frame_skew_ref),
    )
    spread(product, out_ref)


def whole_sum(left_ref, right_ref):
    total = jnp.sum(left_ref[...] * right_ref[...], axis=0)
    return jnp.sum(jnp.sum(total, axis=0, keepdims=True), axis=1, keepdims=True)


def scalar_of(block):
    return jnp.sum(jnp.sum(block, axis=0, keepdims=True), axis=1, keepdims=True)


def second_kernel(
    cols,
    total_entries,
    period,
    entry_ref,
    item_ref,
    count_ref,
    coef_ref,
    kept_ref,
    frame_ref,
    basis_ref,
    image_ref,
    out_ref,
    pair_ref,
    scalar_ref,
    second_ref,
    skew_ref,
    frame_skew_ref,
):
    own = lax.axis_index("row") * cols + lax.axis_index("col")
    member = frame_ref.shape[2]
    norm_sq = whole_sum(basis_ref, basis_ref) / total_entries + norm_eps
    alpha = whole_sum(basis_ref, image_ref) / total_entries / norm_sq
    second_ref[...] = image_ref[...] - alpha * basis_ref[...]
    beta = jnp.sqrt(whole_sum(second_ref, second_ref) / total_entries / norm_sq + norm_eps)
    scale = lax.rsqrt(norm_sq) / beta
    product = tile_product(
        count_ref[0],
        count_ref[1],
        entry_ref,
        item_ref,
        coef_ref,
        kept_ref,
        own,
        frame_ref,
        second_ref,
        period,
        (skew_ref, frame_skew_ref),
    )
    fill = [jnp.zeros((1, member), jnp.float32)] * (SUB - len(product))
    image = jnp.concatenate(product + fill, axis=0) * scale - (beta * lax.rsqrt(norm_sq)) * basis_ref[own]
    second = second_ref[own] * scale
    inner = scalar_of(second * image)
    weight = scalar_of(second * second)
    local_alpha = jnp.where(weight > 1e-30, inner / jnp.maximum(weight, 1e-30), 0.0)
    rest = image - local_alpha * second
    size = scalar_of(rest * rest)
    slant = scalar_of(second * rest)
    lane = lax.broadcasted_iota(jnp.int32, (1, member), 1)
    line = jnp.zeros((1, member), jnp.float32)
    for at, value in enumerate((inner, weight, local_alpha, size, slant)):
        line = jnp.where(lane == at, value, line)
    out_ref[...] = jnp.broadcast_to(line[None], out_ref.shape)
    pair_ref[0] = second
    pair_ref[1] = image
    scalar_ref[...] = jnp.where(lane == 0, alpha, jnp.where(lane == 1, beta, 0.0))


def last_kernel(total_entries, config_ref, pair_ref, scalar_ref, line_ref, mode_ref, coefficient_ref):
    lines = line_ref[:, 0, :]
    alpha = jnp.sum(lines[:, 0:1], axis=0, keepdims=True) / total_entries
    away = lines[:, 2:3] - alpha
    parts = lines[:, 3:4] + away * (away * lines[:, 1:2] + 2.0 * lines[:, 4:5])
    beta = jnp.sqrt(jnp.sum(parts, axis=0, keepdims=True) / total_entries + norm_eps)
    mine = (pair_ref[1] - alpha * pair_ref[0]) / beta
    u = [config_ref[k : k + 1, :] for k in range(3, 6)]
    turn = cross3(u, [mine[k : k + 1] for k in range(3, 6)])
    along = mine[6:7]
    mode_ref[...] = jnp.concatenate([mine[0:3]] + [turn[k] + along * u[k] for k in range(3)], axis=0)
    lane = lax.broadcasted_iota(jnp.int32, scalar_ref.shape, 1)
    coefficient_ref[...] = jnp.where(lane == 2, alpha, jnp.where(lane == 3, beta, scalar_ref[...]))


def local(config, start, tile_list, tile_count):
    dof, member = config.shape
    row_devices = lax.axis_size("row")
    col_devices = lax.axis_size("col")
    devices = row_devices * col_devices
    total_entries = float(dof * member * devices)
    period = (5.0, 5.0, 3.5 * (member // 16))
    entries = tile_list[0, 0]
    slots, fields = entries.shape
    longest = (row_devices + col_devices) * slots + 1

    def shaped(*shape):
        return jax.ShapeDtypeStruct(shape, jnp.float32)

    def everywhere(copies):
        return lax.all_to_all(copies, ("row", "col"), 0, 0, tiled=True)

    params = pltpu.CompilerParams(vmem_limit_bytes=VMEM_LIMIT)
    vmem = pl.BlockSpec(memory_space=pltpu.VMEM)
    smem = pl.BlockSpec(memory_space=pltpu.SMEM)

    in_use = jnp.arange(slots, dtype=jnp.int32) < tile_count[0, 0]
    fields_f = jnp.where(in_use[:, None], entries, -9).astype(jnp.float32).T.reshape(1, fields * slots)
    list_row = jnp.pad(fields_f, ((0, 0), (0, member - fields * slots)), constant_values=-9.0)

    frames, basis = pl.pallas_call(
        pack_kernel,
        out_shape=(shaped(devices, SUB, member), shaped(devices, SUB, member)),
        in_specs=[vmem] * 3,
        out_specs=(vmem, vmem),
        compiler_params=params,
    )(config, start, list_row)
    frames = everywhere(frames)
    basis = everywhere(basis)

    skew = pltpu.VMEM((longest * SUB * SUB, member), jnp.float32)
    held_rows = HELD // GROUP * (TERMS * GROUP * SUB)
    codes, items, counts, terms, kept = pl.pallas_call(
        functools.partial(prepare_kernel, row_devices, col_devices, slots, period),
        out_shape=(
            jax.ShapeDtypeStruct((longest + 1,), jnp.int32),
            jax.ShapeDtypeStruct((longest * (member // SUB) + GROUP,), jnp.int32),
            jax.ShapeDtypeStruct((2,), jnp.int32),
            shaped(held_rows, member),
            shaped(2, member),
        ),
        in_specs=[vmem],
        out_specs=(smem, smem, smem, vmem, vmem),
        scratch_shapes=[
            skew,
            pltpu.VMEM((row_devices + col_devices, member), jnp.int32),
            pltpu.SMEM((row_devices + col_devices, member), jnp.int32),
            pltpu.SemaphoreType.DMA,
        ],
        compiler_params=params,
    )(frames)

    image = pl.pallas_call(
        functools.partial(first_kernel, col_devices, period),
        out_shape=shaped(devices, SUB, member),
        in_specs=[smem] * 3 + [vmem] * 4,
        out_specs=vmem,
        scratch_shapes=[skew, skew],
        compiler_params=params,
    )(codes, items, counts, terms, kept, frames, basis)
    image = everywhere(image)

    line, pair, scalars = pl.pallas_call(
        functools.partial(second_kernel, col_devices, total_entries, period),
        out_shape=(shaped(devices, 1, member), shaped(2, SUB, member), shaped(1, member)),
        in_specs=[smem] * 3 + [vmem] * 5,
        out_specs=(vmem, vmem, vmem),
        scratch_shapes=[pltpu.VMEM((devices, SUB, member), jnp.float32), skew, skew],
        compiler_params=params,
    )(codes, items, counts, terms, kept, frames, basis, image)
    line = everywhere(line)

    mode, coefficients = pl.pallas_call(
        functools.partial(last_kernel, total_entries),
        out_shape=(shaped(dof, member), shaped(1, member)),
        in_specs=[vmem] * 4,
        out_specs=(vmem, vmem),
        compiler_params=params,
    )(config, pair, scalars, line)
    return (coefficients[0, :4], mode)


def solution(mesh):
    placed = (
        P(None, ("row", "col")),
        P(None, ("row", "col")),
        P("row", "col", None, None),
        P("row", "col"),
    )
    return jax.shard_map(
        local, mesh=mesh, in_specs=placed, out_specs=(P(), P(None, ("row", "col"))), check_vma=False
    )
```

```python
import functools
import math

import jax
import jax.numpy as jnp
from jax import lax
from jax.experimental import pallas as pl
from jax.experimental.pallas import tpu as pltpu
from jax.sharding import PartitionSpec as P

chi_shape = 0.8
chi_energy = (math.sqrt(5.0) - 1.0) / (math.sqrt(5.0) + 1.0)
well_depth = 0.005
cutoff_sq = 20.25
norm_eps = 1e-06

SUB = 8
LIST_ROW = 14
CODE_BITS = 6
ITEM_BITS = 8
ITEM_MASK = 255
GROUP = 2
TERMS = 20
HELD = 128
VMEM_LIMIT = 32 * 1024 * 1024


def dot3(a, b):
    return a[0] * b[0] + a[1] * b[1] + a[2] * b[2]


def cross3(a, b):
    return (
        a[1] * b[2] - a[2] * b[1],
        a[2] * b[0] - a[0] * b[2],
        a[0] * b[1] - a[1] * b[0],
    )


def bracket(chi, scaled, factor, p, a, b):
    f = factor * (a - scaled * b)
    g = factor * (b - scaled * a)
    y = p * (a * f + b * g)
    cross = factor * scaled
    f_c = chi * (cross * f - factor * g)
    g_c = chi * (cross * g - factor * f)
    return f, g, y, cross, f_c, g_c


def pair_coefficients(d, ui, uj, lift):
    r_sq = dot3(d, d) + lift
    a = dot3(d, ui)
    b = dot3(d, uj)
    c = dot3(ui, uj)
    r_inv = lax.rsqrt(r_sq)
    p = r_inv * r_inv
    p2 = 2.0 * p
    r = r_sq * r_inv
    x = jnp.maximum(1.0 - r_sq * (1.0 / cutoff_sq), 0.0)
    c_shape = chi_shape * c
    c_energy = chi_energy * c
    e1 = lax.rsqrt(1.0 - c_shape * c_shape)
    q = e1 * e1
    q2 = 1.0 / (1.0 - c_energy * c_energy)
    f, g, y, m, f_c, g_c = bracket(chi_shape, c_shape, q, p, a, b)
    f2, g2, y2, m2, f2_c, g2_c = bracket(chi_energy, c_energy, q2, p, a, b)
    sigma = lax.rsqrt(1.0 - chi_shape * y)
    sigma_sq = sigma * sigma
    psi = 1.0 - chi_energy * y2
    s = 1.0 / (r - sigma + 1.0)
    s_sq = s * s
    s6 = s_sq * s_sq * s_sq
    t0 = s6 * (s6 - 1.0)
    t1 = s6 * s * (6.0 - 12.0 * s6)
    t2 = s6 * s_sq * (156.0 * s6 - 42.0)
    ke = (4.0 * well_depth) * e1
    kx = ke * x
    v_ee = kx * (24.0 / cutoff_sq**2)
    kxx = kx * x
    v_e = kxx * (-6.0 / cutoff_sq)
    v = kxx * x
    psi_sq = psi * psi
    psi_sq_t0 = psi_sq * t0
    psi_sq_t1 = psi_sq * t1
    u = v * psi_sq_t0
    slope = v * psi_sq_t1
    slope2 = v * psi_sq * t2
    tau = (-0.5 * chi_shape) * sigma_sq * sigma
    push = (-2.0 * chi_energy) * psi
    v_t1 = v * t1
    d1 = slope * tau
    d2 = push * (v * t0)
    h1 = p2 * d1
    h2 = p2 * d2
    kc = chi_shape * c_shape * q
    fg = chi_shape * f * g
    fg2 = chi_energy * f2 * g2
    u_a = h1 * f + h2 * f2
    u_b = h1 * g + h2 * g2
    u_fg = h1 * fg + h2 * fg2
    u_c = u * kc - u_fg
    v_e_t0 = v_e * psi_sq_t0
    d_e = r_inv * slope + v_e_t0
    u_e = d_e - (h1 * y + h2 * y2)

    p2_sq = p2 * p2
    k11 = p2_sq * (tau * (slope2 * tau + (1.5 * chi_shape) * sigma_sq * slope))
    k12 = p2_sq * (push * v_t1 * tau)
    k22 = p2_sq * ((2.0 * chi_energy * chi_energy) * (v * t0))
    steep = v_e * psi_sq_t1 + slope2 * r_inv
    l1 = p2 * (steep * tau - h1)
    l2 = p2 * (push * (v_e * t0 + v_t1 * r_inv) - h2)
    j1 = (y, f, g, fg)
    j2 = (y2, f2, g2, fg2)
    w1 = [k11 * one + k12 * two for one, two in zip(j1, j2)]
    w2 = [k12 * one + k22 * two for one, two in zip(j1, j2)]

    def quadratic(m_at, n_at):
        return w1[m_at] * j1[n_at] + w2[m_at] * j2[n_at]

    d_ee = v_ee * psi_sq_t0 + r_inv * (2.0 * (v_e * psi_sq_t1)) + p * (slope2 - slope * r_inv)
    h_ee = quadratic(0, 0) - 2.0 * (l1 * y + l2 * y2) + d_ee
    h_ea = l1 * f + l2 * f2 - quadratic(0, 1)
    h_eb = l1 * g + l2 * g2 - quadratic(0, 2)
    h_ec = quadratic(0, 3) - (l1 * fg + l2 * fg2) + kc * u_e
    straight = h1 * q + h2 * q2
    h_aa = quadratic(1, 1) + straight
    h_ab = quadratic(1, 2) - (h1 * m + h2 * m2)
    h_ac = kc * u_a - quadratic(1, 3) + (h1 * f_c + h2 * f2_c)
    h_bb = quadratic(2, 2) + straight
    h_bc = kc * u_b - quadratic(2, 3) + (h1 * g_c + h2 * g2_c)
    bent = (chi_shape * h1) * (f_c * g + f * g_c) + (chi_energy * h2) * (f2_c * g2 + f2 * g2_c)
    twist = kc * kc + (chi_shape * chi_shape) * q * (2.0 * q - 1.0)
    h_cc = quadratic(3, 3) - bent - 2.0 * (kc * u_fg) + u * twist
    gradient = (u_e, u_a, u_b, u_c)
    return gradient, (h_ee, h_ea, h_eb, h_ec, h_aa, h_ab, h_ac, h_bb, h_bc, h_cc), u_a * a + u_c * c


def offsets_of(code, period):
    return [((code >> bits & 3) - 1).astype(jnp.float32) * size for bits, size in zip((4, 2, 0), period)]


def offset_rows(code, period, member):
    row = lax.broadcasted_iota(jnp.int32, (SUB, member), 0)
    shift = offsets_of(code, period)
    third = jnp.where(row == 1, shift[1], shift[2])
    return jnp.where(row < 3, jnp.where(row == 0, shift[0], third), 0.0)


def skew_entry(entry, block, skew_ref):
    for s in range(SUB):
        at = entry * (SUB * SUB) + s
        skew_ref[pl.ds(at, SUB, stride=SUB), :] = pltpu.roll(block, s, 1) if s else block


def frame_of(code, period, all_ref):
    return all_ref[code >> CODE_BITS, SUB : 2 * SUB, :] + offset_rows(code, period, all_ref.shape[2])


def near_blocks(own_frame, partner_frame):
    member = own_frame.shape[1]
    row = lax.broadcasted_iota(jnp.int32, (SUB, member), 0)
    sign = jnp.where(row < 3, 1.0, jnp.where(row < 6, -1.0, 0.0))

    def doubled(block):
        centre = jnp.where(row < 3, block, 0.0)
        return centre + pltpu.roll(centre, 3, 0)

    box = doubled(partner_frame) * sign
    for bit in (1, 2, 4):
        box = jnp.maximum(box, pltpu.roll(box, bit, 1))
    here = doubled(own_frame) * sign
    blocks = member // SUB
    reach = []
    for k in range(blocks):
        gap = jnp.maximum(here - (pltpu.roll(box, k * SUB, 1) if k else box), 0.0)
        reach.append(jnp.sum(gap * gap, axis=0, keepdims=True))
    nearest = jnp.min(jnp.concatenate(reach, axis=0), axis=1, keepdims=True)
    weight = (1 << lax.broadcasted_iota(jnp.int32, (blocks, 1), 0)).astype(jnp.float32)
    return jnp.sum(jnp.where(nearest < cutoff_sq * 1.001, weight, 0.0)).astype(jnp.int32)


def stacked(parts):
    return jnp.concatenate(parts, axis=0)


def wide(block, k):
    return jnp.broadcast_to(block[k : k + 1], (GROUP * SUB, block.shape[1]))


def turned(skew_ref, items, k):
    parts = []
    for item in items:
        start = pl.multiple_of((item >> ITEM_BITS) * (SUB * SUB) + k * SUB, SUB)
        parts.append(pltpu.roll(skew_ref[pl.ds(start, SUB), :], item & ITEM_MASK, 1))
    return stacked(parts)


def folded(total):
    return jnp.sum(total, axis=0, keepdims=True)


def geometry(items, unused, own_wide, skew_ref):
    member = skew_ref.shape[1]
    first_row = (lax.broadcasted_iota(jnp.int32, (SUB, member), 0) == 0).astype(jnp.float32)
    itself = [jnp.where(item == 0, 2.0 * cutoff_sq, 0.0) for item in items]
    lift = stacked([first_row * one + jnp.where(two, 2.0 * cutoff_sq, 0.0) for one, two in zip(itself, unused)])
    d = [turned(skew_ref, items, k) - own_wide[k] for k in range(3)]
    uj = [turned(skew_ref, items, 3 + k) for k in range(3)]
    gradient, hessian, spin = pair_coefficients(d, own_wide[3:], uj, lift)
    return list(gradient) + list(hessian) + d + uj, (gradient[1], spin)


def apply(items, terms, own_wide, moved_wide, skew_ref):
    u_e, u_a, u_b, u_c, h_ee, h_ea, h_eb, h_ec, h_aa, h_ab, h_ac, h_bb, h_bc, h_cc = terms[:14]
    d = terms[14:17]
    uj = terms[17:20]
    ui = own_wide[3:]
    dui = moved_wide[3:]
    dd = [turned(skew_ref, items, k) - moved_wide[k] for k in range(3)]
    duj = [turned(skew_ref, items, 3 + k) for k in range(3)]
    de = dot3(d, dd)
    da = dot3(dd, ui) + dot3(d, dui)
    db = dot3(dd, uj) + dot3(d, duj)
    dc = dot3(dui, uj) + dot3(ui, duj)
    du_e = h_ee * de + h_ea * da + h_eb * db + h_ec * dc
    du_a = h_ea * de + h_aa * da + h_ab * db + h_ac * dc
    du_b = h_eb * de + h_ab * da + h_bb * db + h_bc * dc
    du_c = h_ec * de + h_ac * da + h_bc * db + h_cc * dc
    force = [du_e * d[k] + u_e * dd[k] + du_b * uj[k] + u_b * duj[k] for k in range(3)]
    turn = [du_a * d[k] + u_a * dd[k] + du_c * uj[k] + u_c * duj[k] for k in range(3)]
    return force + turn + [du_a]


def group_items(step, item_ref, item_count):
    at = [step * GROUP + part for part in range(GROUP)]
    return [item_ref[place] for place in at], [place >= item_count for place in at]


def added(totals, news):
    return tuple(
        total + sum(new[part * SUB : (part + 1) * SUB] for part in range(GROUP)) for total, new in zip(totals, news)
    )


def close(sums, kept, spin, own_frame, own_moved):
    u = [own_frame[k : k + 1] for k in range(3, 6)]
    t = [own_moved[k : k + 1] for k in range(3, 6)]
    force = [-(sums[k] + u[k] * sums[6] + t[k] * kept) for k in range(3)]
    turn = cross3(u, [sums[3 + k] - t[k] * spin for k in range(3)])
    return force + list(cross3(turn, u))


def spread(rows, out_ref):
    member = out_ref.shape[2]
    count = sum(row.shape[0] for row in rows)
    fill = [jnp.zeros((1, member), jnp.float32)] * (out_ref.shape[1] - count)
    block = jnp.concatenate(list(rows) + fill, axis=0)
    out_ref[...] = jnp.broadcast_to(block[None], out_ref.shape)


def pack_kernel(config_ref, start_ref, list_ref, out_ref):
    member = out_ref.shape[2]
    u = [config_ref[k : k + 1, :] for k in range(3, 6)]
    w = [start_ref[k : k + 1, :] for k in range(3, 6)]
    zero = jnp.zeros((1, member), jnp.float32)
    spread([start_ref[0:3, :], *cross3(w, u), dot3(w, u), zero, config_ref[...], list_ref[...], zero], out_ref)


def first_kernel(
    rows,
    cols,
    slots,
    period,
    all_ref,
    out_ref,
    entry_ref,
    item_ref,
    count_ref,
    coef_ref,
    kept_ref,
    skew_ref,
    frame_skew_ref,
    code_ref,
    code_smem,
    sem,
):
    member = all_ref.shape[2]
    row_id = lax.axis_index("row")
    col_id = lax.axis_index("col")
    own = row_id * cols + col_id
    blocks = member // SUB

    def field(line, at):
        return line if at == 0 else pltpu.roll(line, member - at * slots, 1)

    def encode(line, partner, side):
        offset = (field(line, 2) * 16.0 + field(line, 3) * 4.0 + field(line, 4)) * side + 21.0
        return partner * float(1 << CODE_BITS) + offset

    row_f = row_id.astype(jnp.float32)
    col_f = col_id.astype(jnp.float32)
    for col in range(cols):
        line = all_ref[row_id * cols + col, LIST_ROW : LIST_ROW + 1, :]
        code = encode(line, field(line, 1) * float(cols) + float(col), 1.0)
        code_ref[col : col + 1, :] = jnp.where(line == col_f, code, -1.0).astype(jnp.int32)
    for row in range(rows):
        line = all_ref[row * cols + col_id, LIST_ROW : LIST_ROW + 1, :]
        code = encode(line, float(row * cols) + line, -1.0)
        hit = (field(line, 1) == row_f) & (line >= 0.0)
        code_ref[cols + row : cols + row + 1, :] = jnp.where(hit, code, -1.0).astype(jnp.int32)
    copy = pltpu.make_async_copy(code_ref, code_smem, sem)
    copy.start()
    copy.wait()

    entry_ref[0] = own * (1 << CODE_BITS) + 21

    def gather(line, count):
        for slot in range(slots):
            code = code_smem[line, slot]
            entry_ref[count] = code
            count = count + (code >= 0).astype(jnp.int32)
        return count

    entries = lax.fori_loop(0, rows + cols, gather, jnp.int32(1))
    own_frame = all_ref[own, SUB : 2 * SUB, :]
    own_moved = all_ref[own, 0:SUB, :]

    def prepare(entry, count):
        code = entry_ref[entry]
        frame = frame_of(code, period, all_ref)
        skew_entry(entry, frame, frame_skew_ref)
        skew_entry(entry, all_ref[code >> CODE_BITS, 0:SUB, :], skew_ref)
        bits = near_blocks(own_frame, frame)
        for block in range(blocks):
            item_ref[count] = (entry << ITEM_BITS) + block * SUB
            count = count + (bits >> block & 1)
        return count

    items = lax.fori_loop(0, entries, prepare, jnp.int32(0))
    for part in range(GROUP):
        item_ref[items + part] = 0
    count_ref[0] = entries
    count_ref[1] = items

    held = coef_ref.shape[0] // (TERMS * GROUP * SUB)
    steps = (items + GROUP - 1) // GROUP
    own_wide = [wide(own_frame, k) for k in range(6)]
    moved_wide = [wide(own_moved, k) for k in range(6)]

    def derive(step, totals):
        group, unused = group_items(step, item_ref, items)
        terms, sums = geometry(group, unused, own_wide, frame_skew_ref)
        return terms, added(totals, apply(group, terms, own_wide, moved_wide, skew_ref) + list(sums))

    def keep(step, totals):
        terms, totals = derive(step, totals)
        start = pl.multiple_of(step * (TERMS * GROUP * SUB), SUB)
        for k in range(TERMS):
            coef_ref[pl.ds(start + k * GROUP * SUB, GROUP * SUB), :] = terms[k]
        return totals

    zero = jnp.zeros((SUB, member), jnp.float32)
    totals = lax.fori_loop(0, jnp.minimum(steps, held), keep, (zero,) * 9)
    totals = lax.fori_loop(held, steps, lambda step, before: derive(step, before)[1], totals)
    sums = [folded(total) for total in totals]
    kept_ref[...] = jnp.concatenate(sums[7:], axis=0)
    spread(close(sums, sums[7], sums[8], own_frame, own_moved), out_ref)


def whole_sum(left_ref, right_ref):
    total = jnp.sum(left_ref[...] * right_ref[...], axis=0)
    return jnp.sum(jnp.sum(total, axis=0, keepdims=True), axis=1, keepdims=True)


def scalar_of(block):
    return jnp.sum(jnp.sum(block, axis=0, keepdims=True), axis=1, keepdims=True)


def second_kernel(
    cols,
    total_entries,
    period,
    entry_ref,
    item_ref,
    count_ref,
    coef_ref,
    kept_ref,
    all_ref,
    image_ref,
    out_ref,
    pair_ref,
    scalar_ref,
    basis_ref,
    second_ref,
    skew_ref,
    frame_skew_ref,
):
    own = lax.axis_index("row") * cols + lax.axis_index("col")
    member = all_ref.shape[2]
    basis_ref[...] = all_ref[:, 0:SUB, :]
    norm_sq = whole_sum(basis_ref, basis_ref) / total_entries + norm_eps
    alpha = whole_sum(basis_ref, image_ref) / total_entries / norm_sq
    second_ref[...] = image_ref[...] - alpha * basis_ref[...]
    beta = jnp.sqrt(whole_sum(second_ref, second_ref) / total_entries / norm_sq + norm_eps)
    scale = lax.rsqrt(norm_sq) / beta

    entries = count_ref[0]
    items = count_ref[1]
    held = coef_ref.shape[0] // (TERMS * GROUP * SUB)
    steps = (items + GROUP - 1) // GROUP

    def prepare(entry, carry):
        skew_entry(entry, second_ref[entry_ref[entry] >> CODE_BITS], skew_ref)
        return carry

    lax.fori_loop(0, entries, prepare, 0)

    def prepare_frame(entry, carry):
        skew_entry(entry, frame_of(entry_ref[entry], period, all_ref), frame_skew_ref)
        return carry

    lax.fori_loop(0, jnp.where(steps > held, entries, 0), prepare_frame, 0)

    own_frame = all_ref[own, SUB : 2 * SUB, :]
    own_moved = second_ref[own]
    own_wide = [wide(own_frame, k) for k in range(6)]
    moved_wide = [wide(own_moved, k) for k in range(6)]

    def visit(step, totals):
        group, _ = group_items(step, item_ref, items)
        start = pl.multiple_of(step * (TERMS * GROUP * SUB), SUB)
        terms = [coef_ref[pl.ds(start + k * GROUP * SUB, GROUP * SUB), :] for k in range(TERMS)]
        return added(totals, apply(group, terms, own_wide, moved_wide, skew_ref))

    def visit_again(step, totals):
        group, unused = group_items(step, item_ref, items)
        terms, _ = geometry(group, unused, own_wide, frame_skew_ref)
        return added(totals, apply(group, terms, own_wide, moved_wide, skew_ref))

    zero = jnp.zeros((SUB, member), jnp.float32)
    totals = lax.fori_loop(0, jnp.minimum(steps, held), visit, (zero,) * 7)
    totals = lax.fori_loop(held, steps, visit_again, totals)
    sums = [folded(total) for total in totals]
    product = close(sums, kept_ref[0:1, :], kept_ref[1:2, :], own_frame, own_moved)
    fill = [jnp.zeros((1, member), jnp.float32)] * (SUB - len(product))
    image = jnp.concatenate(product + fill, axis=0) * scale - (beta * lax.rsqrt(norm_sq)) * basis_ref[own]
    second = second_ref[own] * scale
    inner = scalar_of(second * image)
    weight = scalar_of(second * second)
    local_alpha = jnp.where(weight > 1e-30, inner / jnp.maximum(weight, 1e-30), 0.0)
    rest = image - local_alpha * second
    size = scalar_of(rest * rest)
    slant = scalar_of(second * rest)
    lane = lax.broadcasted_iota(jnp.int32, (1, member), 1)
    line = jnp.zeros((1, member), jnp.float32)
    for at, value in enumerate((inner, weight, local_alpha, size, slant)):
        line = jnp.where(lane == at, value, line)
    out_ref[...] = jnp.broadcast_to(line[None], out_ref.shape)
    pair_ref[0] = second
    pair_ref[1] = image
    scalar_ref[...] = jnp.where(lane == 0, alpha, jnp.where(lane == 1, beta, 0.0))


def last_kernel(total_entries, config_ref, pair_ref, scalar_ref, line_ref, mode_ref, coefficient_ref):
    lines = line_ref[:, 0, :]
    alpha = jnp.sum(lines[:, 0:1], axis=0, keepdims=True) / total_entries
    away = lines[:, 2:3] - alpha
    parts = lines[:, 3:4] + away * (away * lines[:, 1:2] + 2.0 * lines[:, 4:5])
    beta = jnp.sqrt(jnp.sum(parts, axis=0, keepdims=True) / total_entries + norm_eps)
    mine = (pair_ref[1] - alpha * pair_ref[0]) / beta
    u = [config_ref[k : k + 1, :] for k in range(3, 6)]
    turn = cross3(u, [mine[k : k + 1] for k in range(3, 6)])
    along = mine[6:7]
    mode_ref[...] = jnp.concatenate([mine[0:3]] + [turn[k] + along * u[k] for k in range(3)], axis=0)
    lane = lax.broadcasted_iota(jnp.int32, scalar_ref.shape, 1)
    coefficient_ref[...] = jnp.where(lane == 2, alpha, jnp.where(lane == 3, beta, scalar_ref[...]))


def local(config, start, tile_list, tile_count):
    dof, member = config.shape
    row_devices = lax.axis_size("row")
    col_devices = lax.axis_size("col")
    devices = row_devices * col_devices
    total_entries = float(dof * member * devices)
    period = (5.0, 5.0, 3.5 * (member // 16))
    entries = tile_list[0, 0]
    slots, fields = entries.shape
    longest = (row_devices + col_devices) * slots + 1

    def shaped(*shape):
        return jax.ShapeDtypeStruct(shape, jnp.float32)

    def everywhere(copies):
        return lax.all_to_all(copies, ("row", "col"), 0, 0, tiled=True)

    params = pltpu.CompilerParams(vmem_limit_bytes=VMEM_LIMIT)
    vmem = pl.BlockSpec(memory_space=pltpu.VMEM)
    smem = pl.BlockSpec(memory_space=pltpu.SMEM)

    in_use = jnp.arange(slots, dtype=jnp.int32) < tile_count[0, 0]
    fields_f = jnp.where(in_use[:, None], entries, -9).astype(jnp.float32).T.reshape(1, fields * slots)
    list_row = jnp.pad(fields_f, ((0, 0), (0, member - fields * slots)), constant_values=-9.0)

    packed = pl.pallas_call(
        pack_kernel,
        out_shape=shaped(devices, 2 * SUB, member),
        in_specs=[vmem] * 3,
        out_specs=vmem,
        compiler_params=params,
    )(config, start, list_row)
    together = everywhere(packed)

    skew = pltpu.VMEM((longest * SUB * SUB, member), jnp.float32)
    held_rows = HELD // GROUP * (TERMS * GROUP * SUB)
    image, codes, items, counts, terms, kept = pl.pallas_call(
        functools.partial(first_kernel, row_devices, col_devices, slots, period),
        out_shape=(
            shaped(devices, SUB, member),
            jax.ShapeDtypeStruct((longest + 1,), jnp.int32),
            jax.ShapeDtypeStruct((longest * (member // SUB) + GROUP,), jnp.int32),
            jax.ShapeDtypeStruct((2,), jnp.int32),
            shaped(held_rows, member),
            shaped(2, member),
        ),
        in_specs=[vmem],
        out_specs=(vmem, smem, smem, smem, vmem, vmem),
        scratch_shapes=[
            skew,
            skew,
            pltpu.VMEM((row_devices + col_devices, member), jnp.int32),
            pltpu.SMEM((row_devices + col_devices, member), jnp.int32),
            pltpu.SemaphoreType.DMA,
        ],
        compiler_params=params,
    )(together)
    image = everywhere(image)

    line, pair, scalars = pl.pallas_call(
        functools.partial(second_kernel, col_devices, total_entries, period),
        out_shape=(shaped(devices, 1, member), shaped(2, SUB, member), shaped(1, member)),
        in_specs=[smem] * 3 + [vmem] * 4,
        out_specs=(vmem, vmem, vmem),
        scratch_shapes=[
            pltpu.VMEM((devices, SUB, member), jnp.float32),
            pltpu.VMEM((devices, SUB, member), jnp.float32),
            skew,
            skew,
        ],
        compiler_params=params,
    )(codes, items, counts, terms, kept, together, image)
    line = everywhere(line)

    mode, coefficients = pl.pallas_call(
        functools.partial(last_kernel, total_entries),
        out_shape=(shaped(dof, member), shaped(1, member)),
        in_specs=[vmem] * 4,
        out_specs=(vmem, vmem),
        compiler_params=params,
    )(config, pair, scalars, line)
    return (coefficients[0, :4], mode)


def solution(mesh):
    placed = (
        P(None, ("row", "col")),
        P(None, ("row", "col")),
        P("row", "col", None, None),
        P("row", "col"),
    )
    return jax.shard_map(
        local, mesh=mesh, in_specs=placed, out_specs=(P(), P(None, ("row", "col"))), check_vma=False
    )
```

```python
import functools
import math

import jax
import jax.numpy as jnp
from jax import lax
from jax.experimental import pallas as pl
from jax.experimental.pallas import tpu as pltpu
from jax.sharding import PartitionSpec as P

chi_shape = 0.8
chi_energy = (math.sqrt(5.0) - 1.0) / (math.sqrt(5.0) + 1.0)
well_depth = 0.005
cutoff_sq = 20.25
norm_eps = 1e-06

SUB = 8
LIST_ROW = 14
CODE_BITS = 6
ITEM_BITS = 8
ITEM_MASK = 255
LAYER = 16
GROUP = 2
TERMS = 20
HELD = 128
VMEM_LIMIT = 32 * 1024 * 1024


def dot3(a, b):
    return a[0] * b[0] + a[1] * b[1] + a[2] * b[2]


def cross3(a, b):
    return (
        a[1] * b[2] - a[2] * b[1],
        a[2] * b[0] - a[0] * b[2],
        a[0] * b[1] - a[1] * b[0],
    )


def bracket(chi, scaled, factor, p, a, b):
    f = factor * (a - scaled * b)
    g = factor * (b - scaled * a)
    y = p * (a * f + b * g)
    cross = factor * scaled
    f_c = chi * (cross * f - factor * g)
    g_c = chi * (cross * g - factor * f)
    return f, g, y, cross, f_c, g_c


def pair_coefficients(d, ui, uj, lift):
    r_sq = dot3(d, d) + lift
    a = dot3(d, ui)
    b = dot3(d, uj)
    c = dot3(ui, uj)
    r_inv = lax.rsqrt(r_sq)
    p = r_inv * r_inv
    p2 = 2.0 * p
    r = r_sq * r_inv
    x = jnp.maximum(1.0 - r_sq * (1.0 / cutoff_sq), 0.0)
    c_shape = chi_shape * c
    c_energy = chi_energy * c
    e1 = lax.rsqrt(1.0 - c_shape * c_shape)
    q = e1 * e1
    q2 = 1.0 / (1.0 - c_energy * c_energy)
    f, g, y, m, f_c, g_c = bracket(chi_shape, c_shape, q, p, a, b)
    f2, g2, y2, m2, f2_c, g2_c = bracket(chi_energy, c_energy, q2, p, a, b)
    sigma = lax.rsqrt(1.0 - chi_shape * y)
    sigma_sq = sigma * sigma
    psi = 1.0 - chi_energy * y2
    s = 1.0 / (r - sigma + 1.0)
    s_sq = s * s
    s6 = s_sq * s_sq * s_sq
    t0 = s6 * (s6 - 1.0)
    t1 = s6 * s * (6.0 - 12.0 * s6)
    t2 = s6 * s_sq * (156.0 * s6 - 42.0)
    ke = (4.0 * well_depth) * e1
    kx = ke * x
    v_ee = kx * (24.0 / cutoff_sq**2)
    kxx = kx * x
    v_e = kxx * (-6.0 / cutoff_sq)
    v = kxx * x
    psi_sq = psi * psi
    psi_sq_t0 = psi_sq * t0
    psi_sq_t1 = psi_sq * t1
    u = v * psi_sq_t0
    slope = v * psi_sq_t1
    slope2 = v * psi_sq * t2
    tau = (-0.5 * chi_shape) * sigma_sq * sigma
    push = (-2.0 * chi_energy) * psi
    v_t1 = v * t1
    d1 = slope * tau
    d2 = push * (v * t0)
    h1 = p2 * d1
    h2 = p2 * d2
    kc = chi_shape * c_shape * q
    fg = chi_shape * f * g
    fg2 = chi_energy * f2 * g2
    u_a = h1 * f + h2 * f2
    u_b = h1 * g + h2 * g2
    u_fg = h1 * fg + h2 * fg2
    u_c = u * kc - u_fg
    v_e_t0 = v_e * psi_sq_t0
    d_e = r_inv * slope + v_e_t0
    u_e = d_e - (h1 * y + h2 * y2)

    p2_sq = p2 * p2
    k11 = p2_sq * (tau * (slope2 * tau + (1.5 * chi_shape) * sigma_sq * slope))
    k12 = p2_sq * (push * v_t1 * tau)
    k22 = p2_sq * ((2.0 * chi_energy * chi_energy) * (v * t0))
    steep = v_e * psi_sq_t1 + slope2 * r_inv
    l1 = p2 * (steep * tau - h1)
    l2 = p2 * (push * (v_e * t0 + v_t1 * r_inv) - h2)
    j1 = (y, f, g, fg)
    j2 = (y2, f2, g2, fg2)
    w1 = [k11 * one + k12 * two for one, two in zip(j1, j2)]
    w2 = [k12 * one + k22 * two for one, two in zip(j1, j2)]

    def quadratic(m_at, n_at):
        return w1[m_at] * j1[n_at] + w2[m_at] * j2[n_at]

    d_ee = v_ee * psi_sq_t0 + r_inv * (2.0 * (v_e * psi_sq_t1)) + p * (slope2 - slope * r_inv)
    h_ee = quadratic(0, 0) - 2.0 * (l1 * y + l2 * y2) + d_ee
    h_ea = l1 * f + l2 * f2 - quadratic(0, 1)
    h_eb = l1 * g + l2 * g2 - quadratic(0, 2)
    h_ec = quadratic(0, 3) - (l1 * fg + l2 * fg2) + kc * u_e
    straight = h1 * q + h2 * q2
    h_aa = quadratic(1, 1) + straight
    h_ab = quadratic(1, 2) - (h1 * m + h2 * m2)
    h_ac = kc * u_a - quadratic(1, 3) + (h1 * f_c + h2 * f2_c)
    h_bb = quadratic(2, 2) + straight
    h_bc = kc * u_b - quadratic(2, 3) + (h1 * g_c + h2 * g2_c)
    bent = (chi_shape * h1) * (f_c * g + f * g_c) + (chi_energy * h2) * (f2_c * g2 + f2 * g2_c)
    twist = kc * kc + (chi_shape * chi_shape) * q * (2.0 * q - 1.0)
    h_cc = quadratic(3, 3) - bent - 2.0 * (kc * u_fg) + u * twist
    gradient = (u_e, u_a, u_b, u_c)
    return gradient, (h_ee, h_ea, h_eb, h_ec, h_aa, h_ab, h_ac, h_bb, h_bc, h_cc), u_a * a + u_c * c


def offsets_of(code, period):
    return [((code >> bits & 3) - 1).astype(jnp.float32) * size for bits, size in zip((4, 2, 0), period)]


def offset_rows(code, period, member):
    row = lax.broadcasted_iota(jnp.int32, (SUB, member), 0)
    shift = offsets_of(code, period)
    third = jnp.where(row == 1, shift[1], shift[2])
    return jnp.where(row < 3, jnp.where(row == 0, shift[0], third), 0.0)


def frame_of(code, period, all_ref):
    return all_ref[code >> CODE_BITS, SUB : 2 * SUB, :] + offset_rows(code, period, all_ref.shape[2])


def lanes_of(block, member):
    row = lax.broadcasted_iota(jnp.int32, (SUB, member), 0)
    lane = lax.broadcasted_iota(jnp.int32, (SUB, member), 1)
    group = (lane & -LAYER) - (block >> 1) * LAYER
    return (group & (member - 1)) + ((block & 1) * SUB + row)


def picked(block, lanes):
    return jnp.take_along_axis(block, lanes, axis=1, mode="promise_in_bounds")


def near_blocks(own_frame, partner_frame, box_lanes_ref):
    member = own_frame.shape[1]
    row = lax.broadcasted_iota(jnp.int32, (SUB, member), 0)
    sign = jnp.where(row < 3, 1.0, jnp.where(row < 6, -1.0, 0.0))

    def doubled(block):
        centre = jnp.where(row < 3, block, 0.0)
        return centre + pltpu.roll(centre, 3, 0)

    box = doubled(partner_frame) * sign
    for bit in (1, 2, 4):
        box = jnp.maximum(box, pltpu.roll(box, member - bit, 1))
    here = doubled(own_frame) * sign
    blocks = member // SUB
    reach = []
    for k in range(blocks):
        gap = jnp.maximum(here - picked(box, box_lanes_ref[k * SUB : (k + 1) * SUB, :]), 0.0)
        reach.append(jnp.sum(gap * gap, axis=0, keepdims=True))
    nearest = jnp.min(jnp.concatenate(reach, axis=0), axis=1, keepdims=True)
    weight = (1 << lax.broadcasted_iota(jnp.int32, (blocks, 1), 0)).astype(jnp.float32)
    return jnp.sum(jnp.where(nearest < cutoff_sq * 1.001, weight, 0.0)).astype(jnp.int32)


def stacked(parts):
    return jnp.concatenate(parts, axis=0)


def wide(block, k):
    return jnp.broadcast_to(block[k : k + 1], (GROUP * SUB, block.shape[1]))


def partner_rows(tiles_ref, items, lanes, first):
    member = tiles_ref.shape[2]
    rows = []
    for k in range(6):
        parts = []
        for item, lane in zip(items, lanes):
            row = tiles_ref[item >> (ITEM_BITS + CODE_BITS), first + k : first + k + 1, :]
            parts.append(picked(jnp.broadcast_to(row, (SUB, member)), lane))
        rows.append(stacked(parts))
    return rows


def folded(total):
    return jnp.sum(total, axis=0, keepdims=True)


def geometry(items, unused, lanes, own_code, own_wide, period, all_ref):
    member = all_ref.shape[2]
    lane = lax.broadcasted_iota(jnp.int32, (SUB, member), 1)
    lift = []
    shifts = []
    for item, idle, other in zip(items, unused, lanes):
        code = item >> ITEM_BITS
        itself = jnp.where(other == lane, jnp.where(code == own_code, 2.0 * cutoff_sq, 0.0), 0.0)
        lift.append(itself + jnp.where(idle, 2.0 * cutoff_sq, 0.0))
        shifts.append(offsets_of(code, period))
    rows = partner_rows(all_ref, items, lanes, SUB)
    shift = [stacked([jnp.full((SUB, member), one[k]) for one in shifts]) for k in range(3)]
    d = [rows[k] + shift[k] - own_wide[k] for k in range(3)]
    uj = rows[3:]
    gradient, hessian, spin = pair_coefficients(d, own_wide[3:], uj, stacked(lift))
    return list(gradient) + list(hessian) + d + uj, (gradient[1], spin)


def apply(moved_rows, terms, own_wide, moved_wide):
    u_e, u_a, u_b, u_c, h_ee, h_ea, h_eb, h_ec, h_aa, h_ab, h_ac, h_bb, h_bc, h_cc = terms[:14]
    d = terms[14:17]
    uj = terms[17:20]
    ui = own_wide[3:]
    dui = moved_wide[3:]
    dd = [moved_rows[k] - moved_wide[k] for k in range(3)]
    duj = moved_rows[3:]
    de = dot3(d, dd)
    da = dot3(dd, ui) + dot3(d, dui)
    db = dot3(dd, uj) + dot3(d, duj)
    dc = dot3(dui, uj) + dot3(ui, duj)
    du_e = h_ee * de + h_ea * da + h_eb * db + h_ec * dc
    du_a = h_ea * de + h_aa * da + h_ab * db + h_ac * dc
    du_b = h_eb * de + h_ab * da + h_bb * db + h_bc * dc
    du_c = h_ec * de + h_ac * da + h_bc * db + h_cc * dc
    force = [du_e * d[k] + u_e * dd[k] + du_b * uj[k] + u_b * duj[k] for k in range(3)]
    turn = [du_a * d[k] + u_a * dd[k] + du_c * uj[k] + u_c * duj[k] for k in range(3)]
    return force + turn + [du_a]


def group_items(step, item_ref, item_count):
    at = [step * GROUP + part for part in range(GROUP)]
    return [item_ref[place] for place in at], [place >= item_count for place in at]


def added(totals, news):
    return tuple(
        total + sum(new[part * SUB : (part + 1) * SUB] for part in range(GROUP)) for total, new in zip(totals, news)
    )


def close(sums, kept, spin, own_frame, own_moved):
    u = [own_frame[k : k + 1] for k in range(3, 6)]
    t = [own_moved[k : k + 1] for k in range(3, 6)]
    force = [-(sums[k] + u[k] * sums[6] + t[k] * kept) for k in range(3)]
    turn = cross3(u, [sums[3 + k] - t[k] * spin for k in range(3)])
    return force + list(cross3(turn, u))


def spread(rows, out_ref):
    member = out_ref.shape[2]
    count = sum(row.shape[0] for row in rows)
    fill = [jnp.zeros((1, member), jnp.float32)] * (out_ref.shape[1] - count)
    block = jnp.concatenate(list(rows) + fill, axis=0)
    out_ref[...] = jnp.broadcast_to(block[None], out_ref.shape)


def pack_kernel(config_ref, start_ref, list_ref, out_ref):
    member = out_ref.shape[2]
    u = [config_ref[k : k + 1, :] for k in range(3, 6)]
    w = [start_ref[k : k + 1, :] for k in range(3, 6)]
    zero = jnp.zeros((1, member), jnp.float32)
    spread([start_ref[0:3, :], *cross3(w, u), dot3(w, u), zero, config_ref[...], list_ref[...], zero], out_ref)


def first_kernel(
    rows,
    cols,
    slots,
    period,
    all_ref,
    out_ref,
    item_ref,
    count_ref,
    coef_ref,
    kept_ref,
    entry_ref,
    box_lanes_ref,
    code_ref,
    code_smem,
    sem,
):
    member = all_ref.shape[2]
    row_id = lax.axis_index("row")
    col_id = lax.axis_index("col")
    own = row_id * cols + col_id
    blocks = member // SUB

    def field(line, at):
        return line if at == 0 else pltpu.roll(line, member - at * slots, 1)

    def encode(line, partner, side):
        offset = (field(line, 2) * 16.0 + field(line, 3) * 4.0 + field(line, 4)) * side + 21.0
        return partner * float(1 << CODE_BITS) + offset

    row_f = row_id.astype(jnp.float32)
    col_f = col_id.astype(jnp.float32)
    for col in range(cols):
        line = all_ref[row_id * cols + col, LIST_ROW : LIST_ROW + 1, :]
        code = encode(line, field(line, 1) * float(cols) + float(col), 1.0)
        code_ref[col : col + 1, :] = jnp.where(line == col_f, code, -1.0).astype(jnp.int32)
    for row in range(rows):
        line = all_ref[row * cols + col_id, LIST_ROW : LIST_ROW + 1, :]
        code = encode(line, float(row * cols) + line, -1.0)
        hit = (field(line, 1) == row_f) & (line >= 0.0)
        code_ref[cols + row : cols + row + 1, :] = jnp.where(hit, code, -1.0).astype(jnp.int32)
    copy = pltpu.make_async_copy(code_ref, code_smem, sem)
    copy.start()
    for block in range(blocks):
        box_lanes_ref[block * SUB : (block + 1) * SUB, :] = lanes_of(block, member) & -SUB
    copy.wait()

    own_code = own * (1 << CODE_BITS) + 21
    entry_ref[0] = own_code

    def gather(line, count):
        for slot in range(slots):
            code = code_smem[line, slot]
            entry_ref[count] = code
            count = count + (code >= 0).astype(jnp.int32)
        return count

    entries = lax.fori_loop(0, rows + cols, gather, jnp.int32(1))
    own_frame = all_ref[own, SUB : 2 * SUB, :]
    own_moved = all_ref[own, 0:SUB, :]

    def prepare(entry, count):
        code = entry_ref[entry]
        frame = frame_of(code, period, all_ref)
        bits = near_blocks(own_frame, frame, box_lanes_ref)
        for block in range(blocks):
            item_ref[count] = (code << ITEM_BITS) + block
            count = count + (bits >> block & 1)
        return count

    items = lax.fori_loop(0, entries, prepare, jnp.int32(0))
    for part in range(GROUP):
        item_ref[items + part] = own_code << ITEM_BITS
    count_ref[0] = items

    held = coef_ref.shape[0] // (TERMS * GROUP * SUB)
    steps = (items + GROUP - 1) // GROUP
    own_wide = [wide(own_frame, k) for k in range(6)]
    moved_wide = [wide(own_moved, k) for k in range(6)]

    def derive(step, totals):
        group, unused = group_items(step, item_ref, items)
        lanes = [lanes_of(item & ITEM_MASK, member) for item in group]
        terms, sums = geometry(group, unused, lanes, own_code, own_wide, period, all_ref)
        moved_rows = partner_rows(all_ref, group, lanes, 0)
        return terms, added(totals, apply(moved_rows, terms, own_wide, moved_wide) + list(sums))

    def keep(step, totals):
        terms, totals = derive(step, totals)
        start = pl.multiple_of(step * (TERMS * GROUP * SUB), SUB)
        for k in range(TERMS):
            coef_ref[pl.ds(start + k * GROUP * SUB, GROUP * SUB), :] = terms[k]
        return totals

    zero = jnp.zeros((SUB, member), jnp.float32)
    totals = lax.fori_loop(0, jnp.minimum(steps, held), keep, (zero,) * 9)
    totals = lax.fori_loop(held, steps, lambda step, before: derive(step, before)[1], totals)
    sums = [folded(total) for total in totals]
    kept_ref[...] = jnp.concatenate(sums[7:], axis=0)
    spread(close(sums, sums[7], sums[8], own_frame, own_moved), out_ref)


def whole_sum(left_ref, right_ref):
    total = jnp.sum(left_ref[...] * right_ref[...], axis=0)
    return jnp.sum(jnp.sum(total, axis=0, keepdims=True), axis=1, keepdims=True)


def scalar_of(block):
    return jnp.sum(jnp.sum(block, axis=0, keepdims=True), axis=1, keepdims=True)


def second_kernel(
    cols,
    total_entries,
    period,
    item_ref,
    count_ref,
    coef_ref,
    kept_ref,
    all_ref,
    image_ref,
    out_ref,
    pair_ref,
    scalar_ref,
    basis_ref,
    second_ref,
):
    own = lax.axis_index("row") * cols + lax.axis_index("col")
    member = all_ref.shape[2]
    basis_ref[...] = all_ref[:, 0:SUB, :]
    norm_sq = whole_sum(basis_ref, basis_ref) / total_entries + norm_eps
    alpha = whole_sum(basis_ref, image_ref) / total_entries / norm_sq
    second_ref[...] = image_ref[...] - alpha * basis_ref[...]
    beta = jnp.sqrt(whole_sum(second_ref, second_ref) / total_entries / norm_sq + norm_eps)
    scale = lax.rsqrt(norm_sq) / beta

    own_code = own * (1 << CODE_BITS) + 21
    items = count_ref[0]
    held = coef_ref.shape[0] // (TERMS * GROUP * SUB)
    steps = (items + GROUP - 1) // GROUP
    own_frame = all_ref[own, SUB : 2 * SUB, :]
    own_moved = second_ref[own]
    own_wide = [wide(own_frame, k) for k in range(6)]
    moved_wide = [wide(own_moved, k) for k in range(6)]

    def visit(step, totals):
        group, _ = group_items(step, item_ref, items)
        lanes = [lanes_of(item & ITEM_MASK, member) for item in group]
        start = pl.multiple_of(step * (TERMS * GROUP * SUB), SUB)
        terms = [coef_ref[pl.ds(start + k * GROUP * SUB, GROUP * SUB), :] for k in range(TERMS)]
        return added(totals, apply(partner_rows(second_ref, group, lanes, 0), terms, own_wide, moved_wide))

    def visit_again(step, totals):
        group, unused = group_items(step, item_ref, items)
        lanes = [lanes_of(item & ITEM_MASK, member) for item in group]
        terms, _ = geometry(group, unused, lanes, own_code, own_wide, period, all_ref)
        return added(totals, apply(partner_rows(second_ref, group, lanes, 0), terms, own_wide, moved_wide))

    zero = jnp.zeros((SUB, member), jnp.float32)
    totals = lax.fori_loop(0, jnp.minimum(steps, held), visit, (zero,) * 7)
    totals = lax.fori_loop(held, steps, visit_again, totals)
    sums = [folded(total) for total in totals]
    product = close(sums, kept_ref[0:1, :], kept_ref[1:2, :], own_frame, own_moved)
    fill = [jnp.zeros((1, member), jnp.float32)] * (SUB - len(product))
    image = jnp.concatenate(product + fill, axis=0) * scale - (beta * lax.rsqrt(norm_sq)) * basis_ref[own]
    second = second_ref[own] * scale
    inner = scalar_of(second * image)
    weight = scalar_of(second * second)
    local_alpha = jnp.where(weight > 1e-30, inner / jnp.maximum(weight, 1e-30), 0.0)
    rest = image - local_alpha * second
    size = scalar_of(rest * rest)
    slant = scalar_of(second * rest)
    lane = lax.broadcasted_iota(jnp.int32, (1, member), 1)
    line = jnp.zeros((1, member), jnp.float32)
    for at, value in enumerate((inner, weight, local_alpha, size, slant)):
        line = jnp.where(lane == at, value, line)
    out_ref[...] = jnp.broadcast_to(line[None], out_ref.shape)
    pair_ref[0] = second
    pair_ref[1] = image
    scalar_ref[...] = jnp.where(lane == 0, alpha, jnp.where(lane == 1, beta, 0.0))


def last_kernel(total_entries, config_ref, pair_ref, scalar_ref, line_ref, mode_ref, coefficient_ref):
    lines = line_ref[:, 0, :]
    alpha = jnp.sum(lines[:, 0:1], axis=0, keepdims=True) / total_entries
    away = lines[:, 2:3] - alpha
    parts = lines[:, 3:4] + away * (away * lines[:, 1:2] + 2.0 * lines[:, 4:5])
    beta = jnp.sqrt(jnp.sum(parts, axis=0, keepdims=True) / total_entries + norm_eps)
    mine = (pair_ref[1] - alpha * pair_ref[0]) / beta
    u = [config_ref[k : k + 1, :] for k in range(3, 6)]
    turn = cross3(u, [mine[k : k + 1] for k in range(3, 6)])
    along = mine[6:7]
    mode_ref[...] = jnp.concatenate([mine[0:3]] + [turn[k] + along * u[k] for k in range(3)], axis=0)
    lane = lax.broadcasted_iota(jnp.int32, scalar_ref.shape, 1)
    coefficient_ref[...] = jnp.where(lane == 2, alpha, jnp.where(lane == 3, beta, scalar_ref[...]))


def local(config, start, tile_list, tile_count):
    dof, member = config.shape
    row_devices = lax.axis_size("row")
    col_devices = lax.axis_size("col")
    devices = row_devices * col_devices
    total_entries = float(dof * member * devices)
    period = (5.0, 5.0, 3.5 * (member // 16))
    entries = tile_list[0, 0]
    slots, fields = entries.shape
    longest = (row_devices + col_devices) * slots + 1

    def shaped(*shape):
        return jax.ShapeDtypeStruct(shape, jnp.float32)

    def everywhere(copies):
        return lax.all_to_all(copies, ("row", "col"), 0, 0, tiled=True)

    params = pltpu.CompilerParams(vmem_limit_bytes=VMEM_LIMIT)
    vmem = pl.BlockSpec(memory_space=pltpu.VMEM)
    smem = pl.BlockSpec(memory_space=pltpu.SMEM)

    in_use = jnp.arange(slots, dtype=jnp.int32) < tile_count[0, 0]
    fields_f = jnp.where(in_use[:, None], entries, -9).astype(jnp.float32).T.reshape(1, fields * slots)
    list_row = jnp.pad(fields_f, ((0, 0), (0, member - fields * slots)), constant_values=-9.0)

    packed = pl.pallas_call(
        pack_kernel,
        out_shape=shaped(devices, 2 * SUB, member),
        in_specs=[vmem] * 3,
        out_specs=vmem,
        compiler_params=params,
    )(config, start, list_row)
    together = everywhere(packed)

    held_rows = HELD // GROUP * (TERMS * GROUP * SUB)
    image, items, counts, terms, kept = pl.pallas_call(
        functools.partial(first_kernel, row_devices, col_devices, slots, period),
        out_shape=(
            shaped(devices, SUB, member),
            jax.ShapeDtypeStruct((longest * (member // SUB) + GROUP,), jnp.int32),
            jax.ShapeDtypeStruct((1,), jnp.int32),
            shaped(held_rows, member),
            shaped(2, member),
        ),
        in_specs=[vmem],
        out_specs=(vmem, smem, smem, vmem, vmem),
        scratch_shapes=[
            pltpu.SMEM((longest + 1,), jnp.int32),
            pltpu.VMEM((member, member), jnp.int32),
            pltpu.VMEM((row_devices + col_devices, member), jnp.int32),
            pltpu.SMEM((row_devices + col_devices, member), jnp.int32),
            pltpu.SemaphoreType.DMA,
        ],
        compiler_params=params,
    )(together)
    image = everywhere(image)

    line, pair, scalars = pl.pallas_call(
        functools.partial(second_kernel, col_devices, total_entries, period),
        out_shape=(shaped(devices, 1, member), shaped(2, SUB, member), shaped(1, member)),
        in_specs=[smem] * 2 + [vmem] * 4,
        out_specs=(vmem, vmem, vmem),
        scratch_shapes=[
            pltpu.VMEM((devices, SUB, member), jnp.float32),
            pltpu.VMEM((devices, SUB, member), jnp.float32),
        ],
        compiler_params=params,
    )(items, counts, terms, kept, together, image)
    line = everywhere(line)

    mode, coefficients = pl.pallas_call(
        functools.partial(last_kernel, total_entries),
        out_shape=(shaped(dof, member), shaped(1, member)),
        in_specs=[vmem] * 4,
        out_specs=(vmem, vmem),
        compiler_params=params,
    )(config, pair, scalars, line)
    return (coefficients[0, :4], mode)


def solution(mesh):
    placed = (
        P(None, ("row", "col")),
        P(None, ("row", "col")),
        P("row", "col", None, None),
        P("row", "col"),
    )
    return jax.shard_map(
        local, mesh=mesh, in_specs=placed, out_specs=(P(), P(None, ("row", "col"))), check_vma=False
    )
```

```python
import functools
import math

import jax
import jax.numpy as jnp
from jax import lax
from jax.experimental import pallas as pl
from jax.experimental.pallas import tpu as pltpu
from jax.sharding import PartitionSpec as P

chi_shape = 0.8
chi_energy = (math.sqrt(5.0) - 1.0) / (math.sqrt(5.0) + 1.0)
well_depth = 0.005
cutoff_sq = 20.25
norm_eps = 1e-06

SUB = 8
LIST_ROW = 14
CODE_BITS = 6
ITEM_BITS = 8
ITEM_MASK = 255
LAYER = 16
TESTS = 4
GROUP = 2
TERMS = 20
HELD = 128
VMEM_LIMIT = 32 * 1024 * 1024
PACK_LIMIT = 60 * 1024 * 1024


def dot3(a, b):
    return a[0] * b[0] + a[1] * b[1] + a[2] * b[2]


def cross3(a, b):
    return (
        a[1] * b[2] - a[2] * b[1],
        a[2] * b[0] - a[0] * b[2],
        a[0] * b[1] - a[1] * b[0],
    )


def bracket(chi, scaled, factor, p, a, b):
    f = factor * (a - scaled * b)
    g = factor * (b - scaled * a)
    y = p * (a * f + b * g)
    cross = factor * scaled
    f_c = chi * (cross * f - factor * g)
    g_c = chi * (cross * g - factor * f)
    return f, g, y, cross, f_c, g_c


def pair_coefficients(d, ui, uj, lift):
    r_sq = dot3(d, d) + lift
    a = dot3(d, ui)
    b = dot3(d, uj)
    c = dot3(ui, uj)
    r_inv = lax.rsqrt(r_sq)
    p = r_inv * r_inv
    p2 = 2.0 * p
    r = r_sq * r_inv
    x = jnp.maximum(1.0 - r_sq * (1.0 / cutoff_sq), 0.0)
    c_shape = chi_shape * c
    c_energy = chi_energy * c
    e1 = lax.rsqrt(1.0 - c_shape * c_shape)
    q = e1 * e1
    q2 = 1.0 / (1.0 - c_energy * c_energy)
    f, g, y, m, f_c, g_c = bracket(chi_shape, c_shape, q, p, a, b)
    f2, g2, y2, m2, f2_c, g2_c = bracket(chi_energy, c_energy, q2, p, a, b)
    sigma = lax.rsqrt(1.0 - chi_shape * y)
    sigma_sq = sigma * sigma
    psi = 1.0 - chi_energy * y2
    s = 1.0 / (r - sigma + 1.0)
    s_sq = s * s
    s6 = s_sq * s_sq * s_sq
    t0 = s6 * (s6 - 1.0)
    t1 = s6 * s * (6.0 - 12.0 * s6)
    t2 = s6 * s_sq * (156.0 * s6 - 42.0)
    ke = (4.0 * well_depth) * e1
    kx = ke * x
    v_ee = kx * (24.0 / cutoff_sq**2)
    kxx = kx * x
    v_e = kxx * (-6.0 / cutoff_sq)
    v = kxx * x
    psi_sq = psi * psi
    psi_sq_t0 = psi_sq * t0
    psi_sq_t1 = psi_sq * t1
    u = v * psi_sq_t0
    slope = v * psi_sq_t1
    slope2 = v * psi_sq * t2
    tau = (-0.5 * chi_shape) * sigma_sq * sigma
    push = (-2.0 * chi_energy) * psi
    v_t1 = v * t1
    d1 = slope * tau
    d2 = push * (v * t0)
    h1 = p2 * d1
    h2 = p2 * d2
    kc = chi_shape * c_shape * q
    fg = chi_shape * f * g
    fg2 = chi_energy * f2 * g2
    u_a = h1 * f + h2 * f2
    u_b = h1 * g + h2 * g2
    u_fg = h1 * fg + h2 * fg2
    u_c = u * kc - u_fg
    v_e_t0 = v_e * psi_sq_t0
    d_e = r_inv * slope + v_e_t0
    u_e = d_e - (h1 * y + h2 * y2)

    p2_sq = p2 * p2
    k11 = p2_sq * (tau * (slope2 * tau + (1.5 * chi_shape) * sigma_sq * slope))
    k12 = p2_sq * (push * v_t1 * tau)
    k22 = p2_sq * ((2.0 * chi_energy * chi_energy) * (v * t0))
    steep = v_e * psi_sq_t1 + slope2 * r_inv
    l1 = p2 * (steep * tau - h1)
    l2 = p2 * (push * (v_e * t0 + v_t1 * r_inv) - h2)
    j1 = (y, f, g, fg)
    j2 = (y2, f2, g2, fg2)
    w1 = [k11 * one + k12 * two for one, two in zip(j1, j2)]
    w2 = [k12 * one + k22 * two for one, two in zip(j1, j2)]

    def quadratic(m_at, n_at):
        return w1[m_at] * j1[n_at] + w2[m_at] * j2[n_at]

    d_ee = v_ee * psi_sq_t0 + r_inv * (2.0 * (v_e * psi_sq_t1)) + p * (slope2 - slope * r_inv)
    h_ee = quadratic(0, 0) - 2.0 * (l1 * y + l2 * y2) + d_ee
    h_ea = l1 * f + l2 * f2 - quadratic(0, 1)
    h_eb = l1 * g + l2 * g2 - quadratic(0, 2)
    h_ec = quadratic(0, 3) - (l1 * fg + l2 * fg2) + kc * u_e
    straight = h1 * q + h2 * q2
    h_aa = quadratic(1, 1) + straight
    h_ab = quadratic(1, 2) - (h1 * m + h2 * m2)
    h_ac = kc * u_a - quadratic(1, 3) + (h1 * f_c + h2 * f2_c)
    h_bb = quadratic(2, 2) + straight
    h_bc = kc * u_b - quadratic(2, 3) + (h1 * g_c + h2 * g2_c)
    bent = (chi_shape * h1) * (f_c * g + f * g_c) + (chi_energy * h2) * (f2_c * g2 + f2 * g2_c)
    twist = kc * kc + (chi_shape * chi_shape) * q * (2.0 * q - 1.0)
    h_cc = quadratic(3, 3) - bent - 2.0 * (kc * u_fg) + u * twist
    gradient = (u_e, u_a, u_b, u_c)
    return gradient, (h_ee, h_ea, h_eb, h_ec, h_aa, h_ab, h_ac, h_bb, h_bc, h_cc), u_a * a + u_c * c


def offsets_of(code, period):
    return [((code >> bits & 3) - 1).astype(jnp.float32) * size for bits, size in zip((4, 2, 0), period)]


def offset_rows(code, period, member):
    row = lax.broadcasted_iota(jnp.int32, (SUB, member), 0)
    shift = offsets_of(code, period)
    third = jnp.where(row == 1, shift[1], shift[2])
    return jnp.where(row < 3, jnp.where(row == 0, shift[0], third), 0.0)


def frame_of(code, period, all_ref):
    return all_ref[code >> CODE_BITS, SUB : 2 * SUB, :] + offset_rows(code, period, all_ref.shape[2])


def lanes_of(block, member):
    row = lax.broadcasted_iota(jnp.int32, (SUB, member), 0)
    lane = lax.broadcasted_iota(jnp.int32, (SUB, member), 1)
    group = (lane & -LAYER) - (block >> 1) * LAYER
    return (group & (member - 1)) + ((block & 1) * SUB + row)


def picked(block, lanes):
    return jnp.take_along_axis(block, lanes, axis=1, mode="promise_in_bounds")


def box_lanes(member):
    block = lax.broadcasted_iota(jnp.int32, (member // SUB, member), 0)
    lane = lax.broadcasted_iota(jnp.int32, (member // SUB, member), 1)
    return (((lane & -LAYER) - (block >> 1) * LAYER) & (member - 1)) + (block & 1) * SUB


def near_blocks(own_centre, partner_frame, lanes):
    blocks, member = lanes.shape
    row = lax.broadcasted_iota(jnp.int32, (SUB, member), 0)
    centre = jnp.where(row < 3, partner_frame, 0.0)
    box = centre - pltpu.roll(centre, 3, 0)
    for bit in (1, 2, 4):
        box = jnp.maximum(box, pltpu.roll(box, member - bit, 1))

    def seen(k):
        line = jnp.broadcast_to(box[k : k + 1], (SUB, member))
        return stacked([picked(line, lanes[at : at + SUB]) for at in range(0, blocks, SUB)])

    reach = 0.0
    for k in range(3):
        above = own_centre[k] - seen(k)
        below = -own_centre[k] - seen(3 + k)
        gap = jnp.maximum(jnp.maximum(above, below), 0.0)
        reach = reach + gap * gap
    nearest = jnp.min(reach, axis=1, keepdims=True)
    weight = (1 << lax.broadcasted_iota(jnp.int32, (blocks, 1), 0)).astype(jnp.float32)
    return jnp.sum(jnp.where(nearest < cutoff_sq * 1.001, weight, 0.0)).astype(jnp.int32)


def stacked(parts):
    return jnp.concatenate(parts, axis=0)


def wide(block, k):
    return jnp.broadcast_to(block[k : k + 1], (GROUP * SUB, block.shape[1]))


def partner_rows(tiles_ref, items, lanes, first):
    member = tiles_ref.shape[2]
    rows = []
    for k in range(6):
        parts = []
        for item, lane in zip(items, lanes):
            row = tiles_ref[item >> (ITEM_BITS + CODE_BITS), first + k : first + k + 1, :]
            parts.append(picked(jnp.broadcast_to(row, (SUB, member)), lane))
        rows.append(stacked(parts))
    return rows


def folded(total):
    return jnp.sum(total, axis=0, keepdims=True)


def geometry(items, unused, lanes, own_code, own_wide, period, all_ref):
    member = all_ref.shape[2]
    lane = lax.broadcasted_iota(jnp.int32, (SUB, member), 1)
    lift = []
    shifts = []
    for item, idle, other in zip(items, unused, lanes):
        code = item >> ITEM_BITS
        itself = jnp.where(other == lane, jnp.where(code == own_code, 2.0 * cutoff_sq, 0.0), 0.0)
        lift.append(itself + jnp.where(idle, 2.0 * cutoff_sq, 0.0))
        shifts.append(offsets_of(code, period))
    rows = partner_rows(all_ref, items, lanes, SUB)
    shift = [stacked([jnp.full((SUB, member), one[k]) for one in shifts]) for k in range(3)]
    d = [rows[k] + shift[k] - own_wide[k] for k in range(3)]
    uj = rows[3:]
    gradient, hessian, spin = pair_coefficients(d, own_wide[3:], uj, stacked(lift))
    return list(gradient) + list(hessian) + d + uj, (gradient[1], spin)


def apply(moved_rows, terms, own_wide, moved_wide):
    u_e, u_a, u_b, u_c, h_ee, h_ea, h_eb, h_ec, h_aa, h_ab, h_ac, h_bb, h_bc, h_cc = terms[:14]
    d = terms[14:17]
    uj = terms[17:20]
    ui = own_wide[3:]
    dui = moved_wide[3:]
    dd = [moved_rows[k] - moved_wide[k] for k in range(3)]
    duj = moved_rows[3:]
    de = dot3(d, dd)
    da = dot3(dd, ui) + dot3(d, dui)
    db = dot3(dd, uj) + dot3(d, duj)
    dc = dot3(dui, uj) + dot3(ui, duj)
    du_e = h_ee * de + h_ea * da + h_eb * db + h_ec * dc
    du_a = h_ea * de + h_aa * da + h_ab * db + h_ac * dc
    du_b = h_eb * de + h_ab * da + h_bb * db + h_bc * dc
    du_c = h_ec * de + h_ac * da + h_bc * db + h_cc * dc
    force = [du_e * d[k] + u_e * dd[k] + du_b * uj[k] + u_b * duj[k] for k in range(3)]
    turn = [du_a * d[k] + u_a * dd[k] + du_c * uj[k] + u_c * duj[k] for k in range(3)]
    return force + turn + [du_a]


def group_items(step, item_ref, item_count):
    at = [step * GROUP + part for part in range(GROUP)]
    return [item_ref[place] for place in at], [place >= item_count for place in at]


def added(totals, news):
    return tuple(
        total + sum(new[part * SUB : (part + 1) * SUB] for part in range(GROUP)) for total, new in zip(totals, news)
    )


def close(sums, kept, spin, own_frame, own_moved):
    u = [own_frame[k : k + 1] for k in range(3, 6)]
    t = [own_moved[k : k + 1] for k in range(3, 6)]
    force = [-(sums[k] + u[k] * sums[6] + t[k] * kept) for k in range(3)]
    turn = cross3(u, [sums[3 + k] - t[k] * spin for k in range(3)])
    return force + list(cross3(turn, u))


def spread(rows, out_ref):
    member = out_ref.shape[2]
    count = sum(row.shape[0] for row in rows)
    fill = [jnp.zeros((1, member), jnp.float32)] * (out_ref.shape[1] - count)
    block = jnp.concatenate(list(rows) + fill, axis=0)
    out_ref[...] = jnp.broadcast_to(block[None], out_ref.shape)


def pack_kernel(*refs):
    sources, out_ref, targets, sems = refs[:4], refs[4], refs[5:9], refs[9]
    config_ref, start_ref, list_ref, count_ref = targets
    member = out_ref.shape[2]
    copies = [
        pltpu.make_async_copy(source, target, sems.at[at]) for at, (source, target) in enumerate(zip(sources, targets))
    ]
    for copy in copies:
        copy.start()
    copies[2].wait()
    copies[3].wait()
    lane = lax.broadcasted_iota(jnp.int32, (1, member), 1)
    fields, slots = list_ref.shape[1], list_ref.shape[3]
    line = jnp.full((1, member), -9, jnp.int32)
    for field in range(fields):
        for slot in range(slots):
            line = jnp.where(lane == field * slots + slot, list_ref[0, field, 0, slot], line)
    line = jnp.where((lane >= count_ref[0, 0]) & (lane < slots), -9, line).astype(jnp.float32)
    copies[0].wait()
    copies[1].wait()
    u = [config_ref[k : k + 1, :] for k in range(3, 6)]
    w = [start_ref[k : k + 1, :] for k in range(3, 6)]
    zero = jnp.zeros((1, member), jnp.float32)
    spread([start_ref[0:3, :], *cross3(w, u), dot3(w, u), zero, config_ref[...], line, zero], out_ref)


def first_kernel(
    rows,
    cols,
    slots,
    period,
    all_ref,
    out_ref,
    item_ref,
    count_ref,
    coef_ref,
    kept_ref,
    entry_ref,
    code_ref,
    code_smem,
    sem,
):
    member = all_ref.shape[2]
    row_id = lax.axis_index("row")
    col_id = lax.axis_index("col")
    own = row_id * cols + col_id
    blocks = member // SUB

    def field(line, at):
        return line if at == 0 else pltpu.roll(line, member - at * slots, 1)

    row_f = row_id.astype(jnp.float32)
    col_f = col_id.astype(jnp.float32)
    lines = [all_ref[row_id * cols + col, LIST_ROW : LIST_ROW + 1, :] for col in range(cols)]
    lines += [all_ref[row * cols + col_id, LIST_ROW : LIST_ROW + 1, :] for row in range(rows)]
    line = jnp.concatenate(lines, axis=0)
    at = lax.broadcasted_iota(jnp.int32, line.shape, 0).astype(jnp.float32)
    near = at < float(cols)
    other = field(line, 1)
    offset = field(line, 2) * 16.0 + field(line, 3) * 4.0 + field(line, 4)
    partner = jnp.where(near, other * float(cols) + at, (at - float(cols)) * float(cols) + line)
    code = partner * float(1 << CODE_BITS) + (jnp.where(near, offset, -offset) + 21.0)
    hit = jnp.where(near, line - col_f, jnp.where(line >= 0.0, other - row_f, 1.0)) == 0.0
    code_ref[...] = jnp.where(hit, code, -1.0).astype(jnp.int32)
    copy = pltpu.make_async_copy(code_ref, code_smem, sem)
    copy.start()
    own_code = own * (1 << CODE_BITS) + 21
    own_frame = all_ref[own, SUB : 2 * SUB, :]
    own_moved = all_ref[own, 0:SUB, :]
    lanes = box_lanes(member)
    own_centre = [jnp.broadcast_to(own_frame[k : k + 1], lanes.shape) for k in range(3)]

    def append(code, bits, count):
        for block in range(blocks):
            item_ref[count] = (code << ITEM_BITS) + block
            count = count + (bits >> block & 1)
        return count

    items = append(own_code, near_blocks(own_centre, own_frame, lanes), jnp.int32(0))
    copy.wait()

    def gather(line, count):
        for slot in range(slots):
            code = code_smem[line, slot]
            entry_ref[count] = code
            count = count + (code >= 0).astype(jnp.int32)
        return count

    entries = lax.fori_loop(0, rows + cols, gather, jnp.int32(0))
    for part in range(TESTS):
        entry_ref[entries + part] = own_code

    def prepare(step, count):
        codes = [entry_ref[step * TESTS + part] for part in range(TESTS)]
        bits = [near_blocks(own_centre, frame_of(code, period, all_ref), lanes) for code in codes]
        for part in range(TESTS):
            count = append(codes[part], jnp.where(step * TESTS + part < entries, bits[part], 0), count)
        return count

    items = lax.fori_loop(0, (entries + TESTS - 1) // TESTS, prepare, items)
    for part in range(GROUP):
        item_ref[items + part] = own_code << ITEM_BITS
    count_ref[0] = items

    held = coef_ref.shape[0] // (TERMS * GROUP * SUB)
    steps = (items + GROUP - 1) // GROUP
    own_wide = [wide(own_frame, k) for k in range(6)]
    moved_wide = [wide(own_moved, k) for k in range(6)]

    def derive(step, totals):
        group, unused = group_items(step, item_ref, items)
        lanes = [lanes_of(item & ITEM_MASK, member) for item in group]
        terms, sums = geometry(group, unused, lanes, own_code, own_wide, period, all_ref)
        moved_rows = partner_rows(all_ref, group, lanes, 0)
        return terms, added(totals, apply(moved_rows, terms, own_wide, moved_wide) + list(sums))

    def keep(step, totals):
        terms, totals = derive(step, totals)
        start = pl.multiple_of(step * (TERMS * GROUP * SUB), SUB)
        for k in range(TERMS):
            coef_ref[pl.ds(start + k * GROUP * SUB, GROUP * SUB), :] = terms[k]
        return totals

    zero = jnp.zeros((SUB, member), jnp.float32)
    totals = lax.fori_loop(0, jnp.minimum(steps, held), keep, (zero,) * 9)
    totals = lax.fori_loop(held, steps, lambda step, before: derive(step, before)[1], totals)
    sums = [folded(total) for total in totals]
    kept_ref[...] = jnp.concatenate(sums[7:], axis=0)
    spread(close(sums, sums[7], sums[8], own_frame, own_moved), out_ref)


def scalar_of(block):
    return jnp.sum(jnp.sum(block, axis=0, keepdims=True), axis=1, keepdims=True)


def second_kernel(
    cols,
    total_entries,
    period,
    item_ref,
    count_ref,
    coef_ref,
    kept_ref,
    all_ref,
    image_ref,
    out_ref,
    pair_ref,
    scalar_ref,
    second_ref,
):
    own = lax.axis_index("row") * cols + lax.axis_index("col")
    member = all_ref.shape[2]
    basis = all_ref[:, 0:SUB, :]
    portion = 1.0 / total_entries
    norm_sq = scalar_of(jnp.sum(basis * basis, axis=0)) * portion + norm_eps
    norm_inv = lax.rsqrt(norm_sq)
    alpha = scalar_of(jnp.sum(basis * image_ref[...], axis=0)) * portion / norm_sq
    second = image_ref[...] - alpha * basis
    second_ref[...] = second
    beta_sq = scalar_of(jnp.sum(second * second, axis=0)) * portion / norm_sq + norm_eps
    beta = jnp.sqrt(beta_sq)
    scale = norm_inv * lax.rsqrt(beta_sq)

    own_code = own * (1 << CODE_BITS) + 21
    items = count_ref[0]
    held = coef_ref.shape[0] // (TERMS * GROUP * SUB)
    steps = (items + GROUP - 1) // GROUP
    own_frame = all_ref[own, SUB : 2 * SUB, :]
    own_moved = second_ref[own]
    own_wide = [wide(own_frame, k) for k in range(6)]
    moved_wide = [wide(own_moved, k) for k in range(6)]

    def visit(step, totals):
        group, _ = group_items(step, item_ref, items)
        lanes = [lanes_of(item & ITEM_MASK, member) for item in group]
        start = pl.multiple_of(step * (TERMS * GROUP * SUB), SUB)
        terms = [coef_ref[pl.ds(start + k * GROUP * SUB, GROUP * SUB), :] for k in range(TERMS)]
        return added(totals, apply(partner_rows(second_ref, group, lanes, 0), terms, own_wide, moved_wide))

    def visit_again(step, totals):
        group, unused = group_items(step, item_ref, items)
        lanes = [lanes_of(item & ITEM_MASK, member) for item in group]
        terms, _ = geometry(group, unused, lanes, own_code, own_wide, period, all_ref)
        return added(totals, apply(partner_rows(second_ref, group, lanes, 0), terms, own_wide, moved_wide))

    zero = jnp.zeros((SUB, member), jnp.float32)
    totals = lax.fori_loop(0, jnp.minimum(steps, held), visit, (zero,) * 7)
    totals = lax.fori_loop(held, steps, visit_again, totals)
    sums = [folded(total) for total in totals]
    product = close(sums, kept_ref[0:1, :], kept_ref[1:2, :], own_frame, own_moved)
    fill = [jnp.zeros((1, member), jnp.float32)] * (SUB - len(product))
    image = jnp.concatenate(product + fill, axis=0) * scale - (beta * norm_inv) * all_ref[own, 0:SUB, :]
    second = second_ref[own] * scale
    inner = scalar_of(second * image)
    weight = scalar_of(second * second)
    local_alpha = jnp.where(weight > 1e-30, inner / jnp.maximum(weight, 1e-30), 0.0)
    rest = image - local_alpha * second
    size = scalar_of(rest * rest)
    slant = scalar_of(second * rest)
    lane = lax.broadcasted_iota(jnp.int32, (1, member), 1)
    line = jnp.zeros((1, member), jnp.float32)
    for at, value in enumerate((inner, weight, local_alpha, size, slant)):
        line = jnp.where(lane == at, value, line)
    out_ref[...] = jnp.broadcast_to(line[None], out_ref.shape)
    pair_ref[0] = second
    pair_ref[1] = image
    scalar_ref[...] = jnp.where(lane == 0, alpha, jnp.where(lane == 1, beta, 0.0))


def last_kernel(total_entries, config_ref, pair_ref, scalar_ref, line_ref, mode_ref, coefficient_ref):
    lines = line_ref[:, 0, :]
    alpha = jnp.sum(lines[:, 0:1], axis=0, keepdims=True) / total_entries
    away = lines[:, 2:3] - alpha
    parts = lines[:, 3:4] + away * (away * lines[:, 1:2] + 2.0 * lines[:, 4:5])
    beta = jnp.sqrt(jnp.sum(parts, axis=0, keepdims=True) / total_entries + norm_eps)
    mine = (pair_ref[1] - alpha * pair_ref[0]) / beta
    u = [config_ref[k : k + 1, :] for k in range(3, 6)]
    turn = cross3(u, [mine[k : k + 1] for k in range(3, 6)])
    along = mine[6:7]
    mode_ref[...] = jnp.concatenate([mine[0:3]] + [turn[k] + along * u[k] for k in range(3)], axis=0)
    for at, value in enumerate((scalar_ref[0:1, 0:1], scalar_ref[0:1, 1:2], alpha, beta)):
        coefficient_ref[at] = jnp.sum(value)


def local(config, start, tile_list, tile_count):
    dof, member = config.shape
    row_devices = lax.axis_size("row")
    col_devices = lax.axis_size("col")
    devices = row_devices * col_devices
    total_entries = float(dof * member * devices)
    period = (5.0, 5.0, 3.5 * (member // 16))
    slots = tile_list.shape[2]
    longest = (row_devices + col_devices) * slots + 1

    def shaped(*shape):
        return jax.ShapeDtypeStruct(shape, jnp.float32)

    def everywhere(copies):
        return lax.all_to_all(copies, ("row", "col"), 0, 0, tiled=True)

    params = pltpu.CompilerParams(vmem_limit_bytes=VMEM_LIMIT)
    vmem = pl.BlockSpec(memory_space=pltpu.VMEM)
    smem = pl.BlockSpec(memory_space=pltpu.SMEM)

    outside = pl.BlockSpec(memory_space=pl.ANY)
    packed = pl.pallas_call(
        pack_kernel,
        out_shape=shaped(devices, 2 * SUB, member),
        in_specs=[outside] * 4,
        out_specs=vmem,
        scratch_shapes=[
            pltpu.VMEM((dof, member), jnp.float32),
            pltpu.VMEM((dof, member), jnp.float32),
            pltpu.SMEM((1, tile_list.shape[3], 1, slots), jnp.int32),
            pltpu.SMEM((1, 1), jnp.int32),
            pltpu.SemaphoreType.DMA((4,)),
        ],
        compiler_params=pltpu.CompilerParams(vmem_limit_bytes=PACK_LIMIT),
    )(config, start, jnp.transpose(tile_list, (0, 3, 1, 2)), tile_count)
    together = everywhere(packed)

    held_rows = HELD // GROUP * (TERMS * GROUP * SUB)
    image, items, counts, terms, kept = pl.pallas_call(
        functools.partial(first_kernel, row_devices, col_devices, slots, period),
        out_shape=(
            shaped(devices, SUB, member),
            jax.ShapeDtypeStruct((longest * (member // SUB) + GROUP,), jnp.int32),
            jax.ShapeDtypeStruct((1,), jnp.int32),
            shaped(held_rows, member),
            shaped(2, member),
        ),
        in_specs=[vmem],
        out_specs=(vmem, smem, smem, vmem, vmem),
        scratch_shapes=[
            pltpu.SMEM((longest + TESTS,), jnp.int32),
            pltpu.VMEM((row_devices + col_devices, member), jnp.int32),
            pltpu.SMEM((row_devices + col_devices, member), jnp.int32),
            pltpu.SemaphoreType.DMA,
        ],
        compiler_params=params,
    )(together)
    image = everywhere(image)

    line, pair, scalars = pl.pallas_call(
        functools.partial(second_kernel, col_devices, total_entries, period),
        out_shape=(shaped(devices, 1, member), shaped(2, SUB, member), shaped(1, member)),
        in_specs=[smem] * 2 + [vmem] * 4,
        out_specs=(vmem, vmem, vmem),
        scratch_shapes=[
            pltpu.VMEM((devices, SUB, member), jnp.float32),
        ],
        compiler_params=params,
    )(items, counts, terms, kept, together, image)
    line = everywhere(line)

    mode, coefficients = pl.pallas_call(
        functools.partial(last_kernel, total_entries),
        out_shape=(shaped(dof, member), shaped(4)),
        in_specs=[vmem] * 4,
        out_specs=(vmem, smem),
        compiler_params=params,
    )(config, pair, scalars, line)
    return (coefficients, mode)


def solution(mesh):
    placed = (
        P(None, ("row", "col")),
        P(None, ("row", "col")),
        P("row", "col", None, None),
        P("row", "col"),
    )
    return jax.shard_map(
        local, mesh=mesh, in_specs=placed, out_specs=(P(), P(None, ("row", "col"))), check_vma=False
    )
```

```python
import functools
import math

import jax
import jax.numpy as jnp
from jax import lax
from jax.experimental import pallas as pl
from jax.experimental.pallas import tpu as pltpu
from jax.sharding import PartitionSpec as P

chi_shape = 0.8
chi_energy = (math.sqrt(5.0) - 1.0) / (math.sqrt(5.0) + 1.0)
well_depth = 0.005
cutoff_sq = 20.25
norm_eps = 1e-06

SUB = 8
LIST_ROW = 14
CODE_BITS = 6
ITEM_BITS = 8
ITEM_MASK = 255
LAYER = 16
TESTS = 4
GROUP = 4
TERMS = 20
HELD = 128
VMEM_LIMIT = 32 * 1024 * 1024
PACK_LIMIT = 60 * 1024 * 1024


def dot3(a, b):
    return a[0] * b[0] + a[1] * b[1] + a[2] * b[2]


def cross3(a, b):
    return (
        a[1] * b[2] - a[2] * b[1],
        a[2] * b[0] - a[0] * b[2],
        a[0] * b[1] - a[1] * b[0],
    )


def bracket(chi, scaled, factor, p, a, b):
    f = factor * (a - scaled * b)
    g = factor * (b - scaled * a)
    y = p * (a * f + b * g)
    cross = factor * scaled
    f_c = chi * (cross * f - factor * g)
    g_c = chi * (cross * g - factor * f)
    return f, g, y, cross, f_c, g_c


def pair_coefficients(d, ui, uj, lift):
    r_sq = dot3(d, d) + lift
    a = dot3(d, ui)
    b = dot3(d, uj)
    c = dot3(ui, uj)
    r_inv = lax.rsqrt(r_sq)
    p = r_inv * r_inv
    p2 = 2.0 * p
    r = r_sq * r_inv
    x = jnp.maximum(1.0 - r_sq * (1.0 / cutoff_sq), 0.0)
    c_shape = chi_shape * c
    c_energy = chi_energy * c
    e1 = lax.rsqrt(1.0 - c_shape * c_shape)
    q = e1 * e1
    q2 = 1.0 / (1.0 - c_energy * c_energy)
    f, g, y, m, f_c, g_c = bracket(chi_shape, c_shape, q, p, a, b)
    f2, g2, y2, m2, f2_c, g2_c = bracket(chi_energy, c_energy, q2, p, a, b)
    sigma = lax.rsqrt(1.0 - chi_shape * y)
    sigma_sq = sigma * sigma
    psi = 1.0 - chi_energy * y2
    s = 1.0 / (r - sigma + 1.0)
    s_sq = s * s
    s6 = s_sq * s_sq * s_sq
    t0 = s6 * (s6 - 1.0)
    t1 = s6 * s * (6.0 - 12.0 * s6)
    t2 = s6 * s_sq * (156.0 * s6 - 42.0)
    ke = (4.0 * well_depth) * e1
    kx = ke * x
    v_ee = kx * (24.0 / cutoff_sq**2)
    kxx = kx * x
    v_e = kxx * (-6.0 / cutoff_sq)
    v = kxx * x
    psi_sq = psi * psi
    psi_sq_t0 = psi_sq * t0
    psi_sq_t1 = psi_sq * t1
    u = v * psi_sq_t0
    slope = v * psi_sq_t1
    slope2 = v * psi_sq * t2
    tau = (-0.5 * chi_shape) * sigma_sq * sigma
    push = (-2.0 * chi_energy) * psi
    v_t1 = v * t1
    d1 = slope * tau
    d2 = push * (v * t0)
    h1 = p2 * d1
    h2 = p2 * d2
    kc = chi_shape * c_shape * q
    fg = chi_shape * f * g
    fg2 = chi_energy * f2 * g2
    u_a = h1 * f + h2 * f2
    u_b = h1 * g + h2 * g2
    u_fg = h1 * fg + h2 * fg2
    u_c = u * kc - u_fg
    v_e_t0 = v_e * psi_sq_t0
    d_e = r_inv * slope + v_e_t0
    u_e = d_e - (h1 * y + h2 * y2)

    p2_sq = p2 * p2
    k11 = p2_sq * (tau * (slope2 * tau + (1.5 * chi_shape) * sigma_sq * slope))
    k12 = p2_sq * (push * v_t1 * tau)
    k22 = p2_sq * ((2.0 * chi_energy * chi_energy) * (v * t0))
    steep = v_e * psi_sq_t1 + slope2 * r_inv
    l1 = p2 * (steep * tau - h1)
    l2 = p2 * (push * (v_e * t0 + v_t1 * r_inv) - h2)
    j1 = (y, f, g, fg)
    j2 = (y2, f2, g2, fg2)
    w1 = [k11 * one + k12 * two for one, two in zip(j1, j2)]
    w2 = [k12 * one + k22 * two for one, two in zip(j1, j2)]

    def quadratic(m_at, n_at):
        return w1[m_at] * j1[n_at] + w2[m_at] * j2[n_at]

    d_ee = v_ee * psi_sq_t0 + r_inv * (2.0 * (v_e * psi_sq_t1)) + p * (slope2 - slope * r_inv)
    h_ee = quadratic(0, 0) - 2.0 * (l1 * y + l2 * y2) + d_ee
    h_ea = l1 * f + l2 * f2 - quadratic(0, 1)
    h_eb = l1 * g + l2 * g2 - quadratic(0, 2)
    h_ec = quadratic(0, 3) - (l1 * fg + l2 * fg2) + kc * u_e
    straight = h1 * q + h2 * q2
    h_aa = quadratic(1, 1) + straight
    h_ab = quadratic(1, 2) - (h1 * m + h2 * m2)
    h_ac = kc * u_a - quadratic(1, 3) + (h1 * f_c + h2 * f2_c)
    h_bb = quadratic(2, 2) + straight
    h_bc = kc * u_b - quadratic(2, 3) + (h1 * g_c + h2 * g2_c)
    bent = (chi_shape * h1) * (f_c * g + f * g_c) + (chi_energy * h2) * (f2_c * g2 + f2 * g2_c)
    twist = kc * kc + (chi_shape * chi_shape) * q * (2.0 * q - 1.0)
    h_cc = quadratic(3, 3) - bent - 2.0 * (kc * u_fg) + u * twist
    gradient = (u_e, u_a, u_b, u_c)
    return gradient, (h_ee, h_ea, h_eb, h_ec, h_aa, h_ab, h_ac, h_bb, h_bc, h_cc), u_a * a + u_c * c


def offsets_of(code, period):
    return [((code >> bits & 3) - 1).astype(jnp.float32) * size for bits, size in zip((4, 2, 0), period)]


def offset_rows(code, period, member):
    row = lax.broadcasted_iota(jnp.int32, (SUB, member), 0)
    shift = offsets_of(code, period)
    third = jnp.where(row == 1, shift[1], shift[2])
    return jnp.where(row < 3, jnp.where(row == 0, shift[0], third), 0.0)


def frame_of(code, period, all_ref):
    return all_ref[code >> CODE_BITS, SUB : 2 * SUB, :] + offset_rows(code, period, all_ref.shape[2])


def lanes_of(block, member):
    row = lax.broadcasted_iota(jnp.int32, (SUB, member), 0)
    lane = lax.broadcasted_iota(jnp.int32, (SUB, member), 1)
    group = (lane & -LAYER) - (block >> 1) * LAYER
    return (group & (member - 1)) + ((block & 1) * SUB + row)


def picked(block, lanes):
    return jnp.take_along_axis(block, lanes, axis=1, mode="promise_in_bounds")


def box_lanes(member):
    block = lax.broadcasted_iota(jnp.int32, (member // SUB, member), 0)
    lane = lax.broadcasted_iota(jnp.int32, (member // SUB, member), 1)
    return (((lane & -LAYER) - (block >> 1) * LAYER) & (member - 1)) + (block & 1) * SUB


def near_blocks(own_centre, partner_frame, lanes):
    blocks, member = lanes.shape
    row = lax.broadcasted_iota(jnp.int32, (SUB, member), 0)
    centre = jnp.where(row < 3, partner_frame, 0.0)
    box = centre - pltpu.roll(centre, 3, 0)
    for bit in (1, 2, 4):
        box = jnp.maximum(box, pltpu.roll(box, member - bit, 1))

    def seen(k):
        line = jnp.broadcast_to(box[k : k + 1], (SUB, member))
        return stacked([picked(line, lanes[at : at + SUB]) for at in range(0, blocks, SUB)])

    reach = 0.0
    for k in range(3):
        above = own_centre[k] - seen(k)
        below = -own_centre[k] - seen(3 + k)
        gap = jnp.maximum(jnp.maximum(above, below), 0.0)
        reach = reach + gap * gap
    nearest = jnp.min(reach, axis=1, keepdims=True)
    weight = (1 << lax.broadcasted_iota(jnp.int32, (blocks, 1), 0)).astype(jnp.float32)
    return jnp.sum(jnp.where(nearest < cutoff_sq * 1.001, weight, 0.0)).astype(jnp.int32)


def stacked(parts):
    return jnp.concatenate(parts, axis=0)


def wide(block, k):
    return jnp.broadcast_to(block[k : k + 1], (GROUP * SUB, block.shape[1]))


def partner_rows(tiles_ref, items, lanes, first):
    member = tiles_ref.shape[2]
    rows = []
    for k in range(6):
        parts = []
        for item, lane in zip(items, lanes):
            row = tiles_ref[item >> (ITEM_BITS + CODE_BITS), first + k : first + k + 1, :]
            parts.append(picked(jnp.broadcast_to(row, (SUB, member)), lane))
        rows.append(stacked(parts))
    return rows


def folded(total):
    return jnp.sum(total, axis=0, keepdims=True)


def geometry(items, unused, lanes, own_code, own_wide, period, all_ref):
    member = all_ref.shape[2]
    lane = lax.broadcasted_iota(jnp.int32, (SUB, member), 1)
    lift = []
    shifts = []
    for item, idle, other in zip(items, unused, lanes):
        code = item >> ITEM_BITS
        itself = jnp.where(other == lane, jnp.where(code == own_code, 2.0 * cutoff_sq, 0.0), 0.0)
        lift.append(itself + jnp.where(idle, 2.0 * cutoff_sq, 0.0))
        shifts.append(offsets_of(code, period))
    rows = partner_rows(all_ref, items, lanes, SUB)
    shift = [stacked([jnp.full((SUB, member), one[k]) for one in shifts]) for k in range(3)]
    d = [rows[k] + shift[k] - own_wide[k] for k in range(3)]
    uj = rows[3:]
    gradient, hessian, spin = pair_coefficients(d, own_wide[3:], uj, stacked(lift))
    return list(gradient) + list(hessian) + d + uj, (gradient[1], spin)


def apply(moved_rows, terms, own_wide, moved_wide):
    u_e, u_a, u_b, u_c, h_ee, h_ea, h_eb, h_ec, h_aa, h_ab, h_ac, h_bb, h_bc, h_cc = terms[:14]
    d = terms[14:17]
    uj = terms[17:20]
    ui = own_wide[3:]
    dui = moved_wide[3:]
    dd = [moved_rows[k] - moved_wide[k] for k in range(3)]
    duj = moved_rows[3:]
    de = dot3(d, dd)
    da = dot3(dd, ui) + dot3(d, dui)
    db = dot3(dd, uj) + dot3(d, duj)
    dc = dot3(dui, uj) + dot3(ui, duj)
    du_e = h_ee * de + h_ea * da + h_eb * db + h_ec * dc
    du_a = h_ea * de + h_aa * da + h_ab * db + h_ac * dc
    du_b = h_eb * de + h_ab * da + h_bb * db + h_bc * dc
    du_c = h_ec * de + h_ac * da + h_bc * db + h_cc * dc
    force = [du_e * d[k] + u_e * dd[k] + du_b * uj[k] + u_b * duj[k] for k in range(3)]
    turn = [du_a * d[k] + u_a * dd[k] + du_c * uj[k] + u_c * duj[k] for k in range(3)]
    return force + turn + [du_a]


def group_items(step, item_ref, item_count):
    at = [step * GROUP + part for part in range(GROUP)]
    return [item_ref[place] for place in at], [place >= item_count for place in at]


def added(totals, news):
    return tuple(
        total + sum(new[part * SUB : (part + 1) * SUB] for part in range(GROUP)) for total, new in zip(totals, news)
    )


def close(sums, kept, spin, own_frame, own_moved):
    u = [own_frame[k : k + 1] for k in range(3, 6)]
    t = [own_moved[k : k + 1] for k in range(3, 6)]
    force = [-(sums[k] + u[k] * sums[6] + t[k] * kept) for k in range(3)]
    turn = cross3(u, [sums[3 + k] - t[k] * spin for k in range(3)])
    return force + list(cross3(turn, u))


def spread(rows, out_ref):
    member = out_ref.shape[2]
    count = sum(row.shape[0] for row in rows)
    fill = [jnp.zeros((1, member), jnp.float32)] * (out_ref.shape[1] - count)
    block = jnp.concatenate(list(rows) + fill, axis=0)
    out_ref[...] = jnp.broadcast_to(block[None], out_ref.shape)


def pack_kernel(*refs):
    sources, out_ref, targets, sems = refs[:4], refs[4], refs[5:9], refs[9]
    config_ref, start_ref, list_ref, count_ref = targets
    member = out_ref.shape[2]
    copies = [
        pltpu.make_async_copy(source, target, sems.at[at]) for at, (source, target) in enumerate(zip(sources, targets))
    ]
    for copy in copies:
        copy.start()
    copies[2].wait()
    copies[3].wait()
    lane = lax.broadcasted_iota(jnp.int32, (1, member), 1)
    fields, slots = list_ref.shape[1], list_ref.shape[3]
    line = jnp.full((1, member), -9, jnp.int32)
    for field in range(fields):
        for slot in range(slots):
            line = jnp.where(lane == field * slots + slot, list_ref[0, field, 0, slot], line)
    line = jnp.where((lane >= count_ref[0, 0]) & (lane < slots), -9, line).astype(jnp.float32)
    copies[0].wait()
    copies[1].wait()
    u = [config_ref[k : k + 1, :] for k in range(3, 6)]
    w = [start_ref[k : k + 1, :] for k in range(3, 6)]
    zero = jnp.zeros((1, member), jnp.float32)
    spread([start_ref[0:3, :], *cross3(w, u), dot3(w, u), zero, config_ref[...], line, zero], out_ref)


def first_kernel(
    rows,
    cols,
    slots,
    period,
    all_ref,
    out_ref,
    item_ref,
    count_ref,
    coef_ref,
    kept_ref,
    entry_ref,
    code_ref,
    code_smem,
    sem,
):
    member = all_ref.shape[2]
    row_id = lax.axis_index("row")
    col_id = lax.axis_index("col")
    own = row_id * cols + col_id
    blocks = member // SUB

    def field(line, at):
        return line if at == 0 else pltpu.roll(line, member - at * slots, 1)

    row_f = row_id.astype(jnp.float32)
    col_f = col_id.astype(jnp.float32)
    lines = [all_ref[row_id * cols + col, LIST_ROW : LIST_ROW + 1, :] for col in range(cols)]
    lines += [all_ref[row * cols + col_id, LIST_ROW : LIST_ROW + 1, :] for row in range(rows)]
    line = jnp.concatenate(lines, axis=0)
    at = lax.broadcasted_iota(jnp.int32, line.shape, 0).astype(jnp.float32)
    near = at < float(cols)
    other = field(line, 1)
    offset = field(line, 2) * 16.0 + field(line, 3) * 4.0 + field(line, 4)
    partner = jnp.where(near, other * float(cols) + at, (at - float(cols)) * float(cols) + line)
    code = partner * float(1 << CODE_BITS) + (jnp.where(near, offset, -offset) + 21.0)
    hit = jnp.where(near, line - col_f, jnp.where(line >= 0.0, other - row_f, 1.0)) == 0.0
    code_ref[...] = jnp.where(hit, code, -1.0).astype(jnp.int32)
    copy = pltpu.make_async_copy(code_ref, code_smem, sem)
    copy.start()
    own_code = own * (1 << CODE_BITS) + 21
    own_frame = all_ref[own, SUB : 2 * SUB, :]
    own_moved = all_ref[own, 0:SUB, :]
    lanes = box_lanes(member)
    own_centre = [jnp.broadcast_to(own_frame[k : k + 1], lanes.shape) for k in range(3)]

    def append(code, bits, count):
        for block in range(blocks):
            item_ref[count] = (code << ITEM_BITS) + block
            count = count + (bits >> block & 1)
        return count

    items = append(own_code, near_blocks(own_centre, own_frame, lanes), jnp.int32(0))
    copy.wait()

    def gather(line, count):
        for slot in range(slots):
            code = code_smem[line, slot]
            entry_ref[count] = code
            count = count + (code >= 0).astype(jnp.int32)
        return count

    entries = lax.fori_loop(0, rows + cols, gather, jnp.int32(0))
    for part in range(TESTS):
        entry_ref[entries + part] = own_code

    def prepare(step, count):
        codes = [entry_ref[step * TESTS + part] for part in range(TESTS)]
        bits = [near_blocks(own_centre, frame_of(code, period, all_ref), lanes) for code in codes]
        for part in range(TESTS):
            count = append(codes[part], jnp.where(step * TESTS + part < entries, bits[part], 0), count)
        return count

    items = lax.fori_loop(0, (entries + TESTS - 1) // TESTS, prepare, items)
    for part in range(GROUP):
        item_ref[items + part] = own_code << ITEM_BITS
    count_ref[0] = items

    held = coef_ref.shape[0] // (TERMS * GROUP * SUB)
    steps = (items + GROUP - 1) // GROUP
    own_wide = [wide(own_frame, k) for k in range(6)]
    moved_wide = [wide(own_moved, k) for k in range(6)]

    def derive(step, totals):
        group, unused = group_items(step, item_ref, items)
        lanes = [lanes_of(item & ITEM_MASK, member) for item in group]
        terms, sums = geometry(group, unused, lanes, own_code, own_wide, period, all_ref)
        moved_rows = partner_rows(all_ref, group, lanes, 0)
        return terms, added(totals, apply(moved_rows, terms, own_wide, moved_wide) + list(sums))

    def keep(step, totals):
        terms, totals = derive(step, totals)
        start = pl.multiple_of(step * (TERMS * GROUP * SUB), SUB)
        for k in range(TERMS):
            coef_ref[pl.ds(start + k * GROUP * SUB, GROUP * SUB), :] = terms[k]
        return totals

    zero = jnp.zeros((SUB, member), jnp.float32)
    totals = lax.fori_loop(0, jnp.minimum(steps, held), keep, (zero,) * 9)
    totals = lax.fori_loop(held, steps, lambda step, before: derive(step, before)[1], totals)
    sums = [folded(total) for total in totals]
    kept_ref[...] = jnp.concatenate(sums[7:], axis=0)
    spread(close(sums, sums[7], sums[8], own_frame, own_moved), out_ref)


def scalar_of(block):
    return jnp.sum(jnp.sum(block, axis=0, keepdims=True), axis=1, keepdims=True)


def second_kernel(
    cols,
    total_entries,
    period,
    item_ref,
    count_ref,
    coef_ref,
    kept_ref,
    all_ref,
    image_ref,
    out_ref,
    pair_ref,
    scalar_ref,
    second_ref,
):
    own = lax.axis_index("row") * cols + lax.axis_index("col")
    member = all_ref.shape[2]
    basis = all_ref[:, 0:SUB, :]
    portion = 1.0 / total_entries
    norm_sq = scalar_of(jnp.sum(basis * basis, axis=0)) * portion + norm_eps
    norm_inv = lax.rsqrt(norm_sq)
    alpha = scalar_of(jnp.sum(basis * image_ref[...], axis=0)) * portion / norm_sq
    second = image_ref[...] - alpha * basis
    second_ref[...] = second
    beta_sq = scalar_of(jnp.sum(second * second, axis=0)) * portion / norm_sq + norm_eps
    beta = jnp.sqrt(beta_sq)
    scale = norm_inv * lax.rsqrt(beta_sq)

    own_code = own * (1 << CODE_BITS) + 21
    items = count_ref[0]
    held = coef_ref.shape[0] // (TERMS * GROUP * SUB)
    steps = (items + GROUP - 1) // GROUP
    own_frame = all_ref[own, SUB : 2 * SUB, :]
    own_moved = second_ref[own]
    own_wide = [wide(own_frame, k) for k in range(6)]
    moved_wide = [wide(own_moved, k) for k in range(6)]

    def visit(step, totals):
        group, _ = group_items(step, item_ref, items)
        lanes = [lanes_of(item & ITEM_MASK, member) for item in group]
        start = pl.multiple_of(step * (TERMS * GROUP * SUB), SUB)
        terms = [coef_ref[pl.ds(start + k * GROUP * SUB, GROUP * SUB), :] for k in range(TERMS)]
        return added(totals, apply(partner_rows(second_ref, group, lanes, 0), terms, own_wide, moved_wide))

    def visit_again(step, totals):
        group, unused = group_items(step, item_ref, items)
        lanes = [lanes_of(item & ITEM_MASK, member) for item in group]
        terms, _ = geometry(group, unused, lanes, own_code, own_wide, period, all_ref)
        return added(totals, apply(partner_rows(second_ref, group, lanes, 0), terms, own_wide, moved_wide))

    zero = jnp.zeros((SUB, member), jnp.float32)
    totals = lax.fori_loop(0, jnp.minimum(steps, held), visit, (zero,) * 7)
    totals = lax.fori_loop(held, steps, visit_again, totals)
    sums = [folded(total) for total in totals]
    product = close(sums, kept_ref[0:1, :], kept_ref[1:2, :], own_frame, own_moved)
    fill = [jnp.zeros((1, member), jnp.float32)] * (SUB - len(product))
    image = jnp.concatenate(product + fill, axis=0) * scale - (beta * norm_inv) * all_ref[own, 0:SUB, :]
    second = second_ref[own] * scale
    inner = scalar_of(second * image)
    weight = scalar_of(second * second)
    local_alpha = jnp.where(weight > 1e-30, inner / jnp.maximum(weight, 1e-30), 0.0)
    rest = image - local_alpha * second
    size = scalar_of(rest * rest)
    slant = scalar_of(second * rest)
    lane = lax.broadcasted_iota(jnp.int32, (1, member), 1)
    line = jnp.zeros((1, member), jnp.float32)
    for at, value in enumerate((inner, weight, local_alpha, size, slant)):
        line = jnp.where(lane == at, value, line)
    out_ref[...] = jnp.broadcast_to(line[None], out_ref.shape)
    pair_ref[0] = second
    pair_ref[1] = image
    scalar_ref[...] = jnp.where(lane == 0, alpha, jnp.where(lane == 1, beta, 0.0))


def last_kernel(total_entries, config_ref, pair_ref, scalar_ref, line_ref, mode_ref, coefficient_ref):
    lines = line_ref[:, 0, :]
    alpha = jnp.sum(lines[:, 0:1], axis=0, keepdims=True) / total_entries
    away = lines[:, 2:3] - alpha
    parts = lines[:, 3:4] + away * (away * lines[:, 1:2] + 2.0 * lines[:, 4:5])
    beta = jnp.sqrt(jnp.sum(parts, axis=0, keepdims=True) / total_entries + norm_eps)
    mine = (pair_ref[1] - alpha * pair_ref[0]) / beta
    u = [config_ref[k : k + 1, :] for k in range(3, 6)]
    turn = cross3(u, [mine[k : k + 1] for k in range(3, 6)])
    along = mine[6:7]
    mode_ref[...] = jnp.concatenate([mine[0:3]] + [turn[k] + along * u[k] for k in range(3)], axis=0)
    for at, value in enumerate((scalar_ref[0:1, 0:1], scalar_ref[0:1, 1:2], alpha, beta)):
        coefficient_ref[at] = jnp.sum(value)


def local(config, start, tile_list, tile_count):
    dof, member = config.shape
    row_devices = lax.axis_size("row")
    col_devices = lax.axis_size("col")
    devices = row_devices * col_devices
    total_entries = float(dof * member * devices)
    period = (5.0, 5.0, 3.5 * (member // 16))
    slots = tile_list.shape[2]
    longest = (row_devices + col_devices) * slots + 1

    def shaped(*shape):
        return jax.ShapeDtypeStruct(shape, jnp.float32)

    def everywhere(copies):
        return lax.all_to_all(copies, ("row", "col"), 0, 0, tiled=True)

    params = pltpu.CompilerParams(vmem_limit_bytes=VMEM_LIMIT)
    vmem = pl.BlockSpec(memory_space=pltpu.VMEM)
    smem = pl.BlockSpec(memory_space=pltpu.SMEM)

    outside = pl.BlockSpec(memory_space=pl.ANY)
    packed = pl.pallas_call(
        pack_kernel,
        out_shape=shaped(devices, 2 * SUB, member),
        in_specs=[outside] * 4,
        out_specs=vmem,
        scratch_shapes=[
            pltpu.VMEM((dof, member), jnp.float32),
            pltpu.VMEM((dof, member), jnp.float32),
            pltpu.SMEM((1, tile_list.shape[3], 1, slots), jnp.int32),
            pltpu.SMEM((1, 1), jnp.int32),
            pltpu.SemaphoreType.DMA((4,)),
        ],
        compiler_params=pltpu.CompilerParams(vmem_limit_bytes=PACK_LIMIT),
    )(config, start, jnp.transpose(tile_list, (0, 3, 1, 2)), tile_count)
    together = everywhere(packed)

    held_rows = HELD // GROUP * (TERMS * GROUP * SUB)
    image, items, counts, terms, kept = pl.pallas_call(
        functools.partial(first_kernel, row_devices, col_devices, slots, period),
        out_shape=(
            shaped(devices, SUB, member),
            jax.ShapeDtypeStruct((longest * (member // SUB) + GROUP,), jnp.int32),
            jax.ShapeDtypeStruct((1,), jnp.int32),
            shaped(held_rows, member),
            shaped(2, member),
        ),
        in_specs=[vmem],
        out_specs=(vmem, smem, smem, vmem, vmem),
        scratch_shapes=[
            pltpu.SMEM((longest + TESTS,), jnp.int32),
            pltpu.VMEM((row_devices + col_devices, member), jnp.int32),
            pltpu.SMEM((row_devices + col_devices, member), jnp.int32),
            pltpu.SemaphoreType.DMA,
        ],
        compiler_params=params,
    )(together)
    image = everywhere(image)

    line, pair, scalars = pl.pallas_call(
        functools.partial(second_kernel, col_devices, total_entries, period),
        out_shape=(shaped(devices, 1, member), shaped(2, SUB, member), shaped(1, member)),
        in_specs=[smem] * 2 + [vmem] * 4,
        out_specs=(vmem, vmem, vmem),
        scratch_shapes=[
            pltpu.VMEM((devices, SUB, member), jnp.float32),
        ],
        compiler_params=params,
    )(items, counts, terms, kept, together, image)
    line = everywhere(line)

    mode, coefficients = pl.pallas_call(
        functools.partial(last_kernel, total_entries),
        out_shape=(shaped(dof, member), shaped(4)),
        in_specs=[vmem] * 4,
        out_specs=(vmem, smem),
        compiler_params=params,
    )(config, pair, scalars, line)
    return (coefficients, mode)


def solution(mesh):
    placed = (
        P(None, ("row", "col")),
        P(None, ("row", "col")),
        P("row", "col", None, None),
        P("row", "col"),
    )
    return jax.shard_map(
        local, mesh=mesh, in_specs=placed, out_specs=(P(), P(None, ("row", "col"))), check_vma=False
    )
```

```python
import functools
import math

import jax
import jax.numpy as jnp
from jax import lax
from jax.experimental import pallas as pl
from jax.experimental.pallas import tpu as pltpu
from jax.sharding import PartitionSpec as P

chi_shape = 0.8
chi_energy = (math.sqrt(5.0) - 1.0) / (math.sqrt(5.0) + 1.0)
well_depth = 0.005
cutoff_sq = 20.25
norm_eps = 1e-06

SUB = 8
CENTRE = 6
LIST_ROW = 12
CODE_BITS = 6
ITEM_BITS = 8
ITEM_MASK = 255
LAYER = 16
TESTS = 4
GROUP = 4
TERMS = 20
HELD = 128
VMEM_LIMIT = 32 * 1024 * 1024
PACK_LIMIT = 60 * 1024 * 1024


def dot3(a, b):
    return a[0] * b[0] + a[1] * b[1] + a[2] * b[2]


def cross3(a, b):
    return (
        a[1] * b[2] - a[2] * b[1],
        a[2] * b[0] - a[0] * b[2],
        a[0] * b[1] - a[1] * b[0],
    )


def bracket(chi, scaled, factor, p, a, b):
    f = factor * (a - scaled * b)
    g = factor * (b - scaled * a)
    y = p * (a * f + b * g)
    cross = factor * scaled
    f_c = chi * (cross * f - factor * g)
    g_c = chi * (cross * g - factor * f)
    return f, g, y, cross, f_c, g_c


def pair_coefficients(d, ui, uj, lift):
    r_sq = dot3(d, d) + lift
    a = dot3(d, ui)
    b = dot3(d, uj)
    c = dot3(ui, uj)
    r_inv = lax.rsqrt(r_sq)
    p = r_inv * r_inv
    p2 = 2.0 * p
    r = r_sq * r_inv
    x = jnp.maximum(1.0 - r_sq * (1.0 / cutoff_sq), 0.0)
    c_shape = chi_shape * c
    c_energy = chi_energy * c
    e1 = lax.rsqrt(1.0 - c_shape * c_shape)
    q = e1 * e1
    q2 = 1.0 / (1.0 - c_energy * c_energy)
    f, g, y, m, f_c, g_c = bracket(chi_shape, c_shape, q, p, a, b)
    f2, g2, y2, m2, f2_c, g2_c = bracket(chi_energy, c_energy, q2, p, a, b)
    sigma = lax.rsqrt(1.0 - chi_shape * y)
    sigma_sq = sigma * sigma
    psi = 1.0 - chi_energy * y2
    s = 1.0 / (r - sigma + 1.0)
    s_sq = s * s
    s6 = s_sq * s_sq * s_sq
    t0 = s6 * (s6 - 1.0)
    t1 = s6 * s * (6.0 - 12.0 * s6)
    t2 = s6 * s_sq * (156.0 * s6 - 42.0)
    ke = (4.0 * well_depth) * e1
    kx = ke * x
    v_ee = kx * (24.0 / cutoff_sq**2)
    kxx = kx * x
    v_e = kxx * (-6.0 / cutoff_sq)
    v = kxx * x
    psi_sq = psi * psi
    psi_sq_t0 = psi_sq * t0
    psi_sq_t1 = psi_sq * t1
    u = v * psi_sq_t0
    slope = v * psi_sq_t1
    slope2 = v * psi_sq * t2
    tau = (-0.5 * chi_shape) * sigma_sq * sigma
    push = (-2.0 * chi_energy) * psi
    v_t1 = v * t1
    d1 = slope * tau
    d2 = push * (v * t0)
    h1 = p2 * d1
    h2 = p2 * d2
    kc = chi_shape * c_shape * q
    fg = chi_shape * f * g
    fg2 = chi_energy * f2 * g2
    u_a = h1 * f + h2 * f2
    u_b = h1 * g + h2 * g2
    u_fg = h1 * fg + h2 * fg2
    u_c = u * kc - u_fg
    v_e_t0 = v_e * psi_sq_t0
    d_e = r_inv * slope + v_e_t0
    u_e = d_e - (h1 * y + h2 * y2)

    p2_sq = p2 * p2
    k11 = p2_sq * (tau * (slope2 * tau + (1.5 * chi_shape) * sigma_sq * slope))
    k12 = p2_sq * (push * v_t1 * tau)
    k22 = p2_sq * ((2.0 * chi_energy * chi_energy) * (v * t0))
    steep = v_e * psi_sq_t1 + slope2 * r_inv
    l1 = p2 * (steep * tau - h1)
    l2 = p2 * (push * (v_e * t0 + v_t1 * r_inv) - h2)
    j1 = (y, f, g, fg)
    j2 = (y2, f2, g2, fg2)
    w1 = [k11 * one + k12 * two for one, two in zip(j1, j2)]
    w2 = [k12 * one + k22 * two for one, two in zip(j1, j2)]

    def quadratic(m_at, n_at):
        return w1[m_at] * j1[n_at] + w2[m_at] * j2[n_at]

    d_ee = v_ee * psi_sq_t0 + r_inv * (2.0 * (v_e * psi_sq_t1)) + p * (slope2 - slope * r_inv)
    h_ee = quadratic(0, 0) - 2.0 * (l1 * y + l2 * y2) + d_ee
    h_ea = l1 * f + l2 * f2 - quadratic(0, 1)
    h_eb = l1 * g + l2 * g2 - quadratic(0, 2)
    h_ec = quadratic(0, 3) - (l1 * fg + l2 * fg2) + kc * u_e
    straight = h1 * q + h2 * q2
    h_aa = quadratic(1, 1) + straight
    h_ab = quadratic(1, 2) - (h1 * m + h2 * m2)
    h_ac = kc * u_a - quadratic(1, 3) + (h1 * f_c + h2 * f2_c)
    h_bb = quadratic(2, 2) + straight
    h_bc = kc * u_b - quadratic(2, 3) + (h1 * g_c + h2 * g2_c)
    bent = (chi_shape * h1) * (f_c * g + f * g_c) + (chi_energy * h2) * (f2_c * g2 + f2 * g2_c)
    twist = kc * kc + (chi_shape * chi_shape) * q * (2.0 * q - 1.0)
    h_cc = quadratic(3, 3) - bent - 2.0 * (kc * u_fg) + u * twist
    gradient = (u_e, u_a, u_b, u_c)
    return gradient, (h_ee, h_ea, h_eb, h_ec, h_aa, h_ab, h_ac, h_bb, h_bc, h_cc), u_a * a + u_c * c


def offsets_of(code, period):
    return [((code >> bits & 3) - 1).astype(jnp.float32) * size for bits, size in zip((4, 2, 0), period)]


def row_of(tiles_ref, tile, k, member):
    return tiles_ref[tile, :, k * member : (k + 1) * member]


def centre_of(code, period, all_ref, member):
    shift = offsets_of(code, period)
    return [row_of(all_ref, code >> CODE_BITS, CENTRE + k, member) + shift[k] for k in range(3)]


def lanes_of(block, member):
    row = lax.broadcasted_iota(jnp.int32, (SUB, member), 0)
    lane = lax.broadcasted_iota(jnp.int32, (SUB, member), 1)
    group = (lane & -LAYER) - (block >> 1) * LAYER
    return (group & (member - 1)) + ((block & 1) * SUB + row)


def picked(block, lanes):
    return jnp.take_along_axis(block, lanes, axis=1, mode="promise_in_bounds")


def box_lanes(member):
    block = lax.broadcasted_iota(jnp.int32, (member // SUB, member), 0)
    lane = lax.broadcasted_iota(jnp.int32, (member // SUB, member), 1)
    return (((lane & -LAYER) - (block >> 1) * LAYER) & (member - 1)) + (block & 1) * SUB


def near_blocks(own_centre, partner, lanes):
    blocks, member = lanes.shape
    zero = jnp.zeros((1, member), jnp.float32)
    box = stacked(partner + [-line for line in partner] + [zero, zero])
    for bit in (1, 2, 4):
        box = jnp.maximum(box, pltpu.roll(box, member - bit, 1))

    def seen(k):
        line = jnp.broadcast_to(box[k : k + 1], (SUB, member))
        return stacked([picked(line, lanes[at : at + SUB]) for at in range(0, blocks, SUB)])

    reach = 0.0
    for k in range(3):
        above = own_centre[k] - seen(k)
        below = -own_centre[k] - seen(3 + k)
        gap = jnp.maximum(jnp.maximum(above, below), 0.0)
        reach = reach + gap * gap
    nearest = jnp.min(reach, axis=1, keepdims=True)
    weight = (1 << lax.broadcasted_iota(jnp.int32, (blocks, 1), 0)).astype(jnp.float32)
    return jnp.sum(jnp.where(nearest < cutoff_sq * 1.001, weight, 0.0)).astype(jnp.int32)


def stacked(parts):
    return jnp.concatenate(parts, axis=0)


def wide(row):
    return jnp.broadcast_to(row, (GROUP * SUB, row.shape[1]))


def partner_rows(row_at, items, lanes):
    rows = []
    for k in range(6):
        parts = []
        for item, lane in zip(items, lanes):
            row = row_at(item >> (ITEM_BITS + CODE_BITS), k)
            parts.append(picked(jnp.broadcast_to(row, lane.shape), lane))
        rows.append(stacked(parts))
    return rows


def folded(total):
    return jnp.sum(total, axis=0, keepdims=True)


def geometry(items, unused, lanes, own_code, own_wide, period, all_ref):
    member = lanes[0].shape[1]
    lane = lax.broadcasted_iota(jnp.int32, (SUB, member), 1)
    lift = []
    shifts = []
    for item, idle, other in zip(items, unused, lanes):
        code = item >> ITEM_BITS
        itself = jnp.where(other == lane, jnp.where(code == own_code, 2.0 * cutoff_sq, 0.0), 0.0)
        lift.append(itself + jnp.where(idle, 2.0 * cutoff_sq, 0.0))
        shifts.append(offsets_of(code, period))
    rows = partner_rows(lambda tile, k: row_of(all_ref, tile, CENTRE + k, member), items, lanes)
    shift = [stacked([jnp.full((SUB, member), one[k]) for one in shifts]) for k in range(3)]
    d = [rows[k] + shift[k] - own_wide[k] for k in range(3)]
    uj = rows[3:]
    gradient, hessian, spin = pair_coefficients(d, own_wide[3:], uj, stacked(lift))
    return list(gradient) + list(hessian) + d + uj, (gradient[1], spin)


def apply(moved_rows, terms, own_wide, moved_wide):
    u_e, u_a, u_b, u_c, h_ee, h_ea, h_eb, h_ec, h_aa, h_ab, h_ac, h_bb, h_bc, h_cc = terms[:14]
    d = terms[14:17]
    uj = terms[17:20]
    ui = own_wide[3:]
    dui = moved_wide[3:]
    dd = [moved_rows[k] - moved_wide[k] for k in range(3)]
    duj = cross3(moved_rows[3:], uj)
    de = dot3(d, dd)
    da = dot3(dd, ui) + dot3(d, dui)
    db = dot3(dd, uj) + dot3(d, duj)
    dc = dot3(dui, uj) + dot3(ui, duj)
    du_e = h_ee * de + h_ea * da + h_eb * db + h_ec * dc
    du_a = h_ea * de + h_aa * da + h_ab * db + h_ac * dc
    du_b = h_eb * de + h_ab * da + h_bb * db + h_bc * dc
    du_c = h_ec * de + h_ac * da + h_bc * db + h_cc * dc
    force = [du_e * d[k] + u_e * dd[k] + du_b * uj[k] + u_b * duj[k] for k in range(3)]
    turn = [du_a * d[k] + u_a * dd[k] + du_c * uj[k] + u_c * duj[k] for k in range(3)]
    return force + turn + [du_a]


def group_items(step, item_ref, item_count):
    at = [step * GROUP + part for part in range(GROUP)]
    return [item_ref[1 + place] for place in at], [place >= item_count for place in at]


def added(totals, news):
    return tuple(
        total + sum(new[part * SUB : (part + 1) * SUB] for part in range(GROUP)) for total, new in zip(totals, news)
    )


def close(sums, kept, spin, u, t):
    force = [-(sums[k] + u[k] * sums[6] + t[k] * kept) for k in range(3)]
    return force + list(cross3(u, [sums[3 + k] - t[k] * spin for k in range(3)]))


def spread(rows, out_ref):
    member = rows[0].shape[1]
    for k, row in enumerate(rows):
        out_ref[:, :, k * member : (k + 1) * member] = jnp.broadcast_to(row[None], (out_ref.shape[0], 1, member))


def pack_kernel(*refs):
    sources, out_ref, targets, sems = refs[:4], refs[4], refs[5:9], refs[9]
    config_ref, start_ref, list_ref, count_ref = targets
    copies = [
        pltpu.make_async_copy(source, target, sems.at[at]) for at, (source, target) in enumerate(zip(sources, targets))
    ]
    for copy in copies:
        copy.start()
    copies[2].wait()
    copies[3].wait()
    member = config_ref.shape[1]
    lane = lax.broadcasted_iota(jnp.int32, (1, member), 1)
    fields, slots = list_ref.shape[1], list_ref.shape[3]
    line = jnp.full((1, member), -9, jnp.int32)
    for field in range(fields):
        for slot in range(slots):
            line = jnp.where(lane == field * slots + slot, list_ref[0, field, 0, slot], line)
    line = jnp.where((lane >= count_ref[0, 0]) & (lane < slots), -9, line).astype(jnp.float32)
    copies[0].wait()
    copies[1].wait()
    rows = [ref[k : k + 1, :] for ref in (start_ref, config_ref) for k in range(6)]
    spread(rows + [line], out_ref)


def first_kernel(
    rows,
    cols,
    slots,
    period,
    all_ref,
    out_ref,
    item_ref,
    coef_ref,
    kept_ref,
    entry_ref,
    code_ref,
    code_smem,
    sem,
):
    member = kept_ref.shape[1]
    row_id = lax.axis_index("row")
    col_id = lax.axis_index("col")
    own = row_id * cols + col_id
    blocks = member // SUB

    def field(line, at):
        return line if at == 0 else pltpu.roll(line, member - at * slots, 1)

    row_f = row_id.astype(jnp.float32)
    col_f = col_id.astype(jnp.float32)
    lines = [row_of(all_ref, row_id * cols + col, LIST_ROW, member) for col in range(cols)]
    lines += [row_of(all_ref, row * cols + col_id, LIST_ROW, member) for row in range(rows)]
    line = jnp.concatenate(lines, axis=0)
    at = lax.broadcasted_iota(jnp.int32, line.shape, 0).astype(jnp.float32)
    near = at < float(cols)
    other = field(line, 1)
    offset = field(line, 2) * 16.0 + field(line, 3) * 4.0 + field(line, 4)
    partner = jnp.where(near, other * float(cols) + at, (at - float(cols)) * float(cols) + line)
    code = partner * float(1 << CODE_BITS) + (jnp.where(near, offset, -offset) + 21.0)
    hit = jnp.where(near, line - col_f, jnp.where(line >= 0.0, other - row_f, 1.0)) == 0.0
    code_ref[...] = jnp.where(hit, code, -1.0).astype(jnp.int32)
    copy = pltpu.make_async_copy(code_ref, code_smem, sem)
    copy.start()
    own_code = own * (1 << CODE_BITS) + 21
    own_moved = [row_of(all_ref, own, k, member) for k in range(6)]
    own_frame = [row_of(all_ref, own, CENTRE + k, member) for k in range(6)]
    lanes = box_lanes(member)
    own_centre = [jnp.broadcast_to(line, lanes.shape) for line in own_frame[:3]]

    def append(code, bits, count):
        for block in range(blocks):
            item_ref[1 + count] = (code << ITEM_BITS) + block
            count = count + (bits >> block & 1)
        return count

    items = append(own_code, near_blocks(own_centre, own_frame[:3], lanes), jnp.int32(0))
    copy.wait()

    def gather(line, count):
        for slot in range(slots):
            code = code_smem[line, slot]
            entry_ref[count] = code
            count = count + (code >= 0).astype(jnp.int32)
        return count

    entries = lax.fori_loop(0, rows + cols, gather, jnp.int32(0))
    for part in range(TESTS):
        entry_ref[entries + part] = own_code

    def prepare(step, count):
        codes = [entry_ref[step * TESTS + part] for part in range(TESTS)]
        bits = [near_blocks(own_centre, centre_of(code, period, all_ref, member), lanes) for code in codes]
        for part in range(TESTS):
            count = append(codes[part], jnp.where(step * TESTS + part < entries, bits[part], 0), count)
        return count

    items = lax.fori_loop(0, (entries + TESTS - 1) // TESTS, prepare, items)
    for part in range(GROUP):
        item_ref[1 + items + part] = own_code << ITEM_BITS
    item_ref[0] = items

    held = coef_ref.shape[0] // (TERMS * GROUP * SUB)
    steps = (items + GROUP - 1) // GROUP
    u = own_frame[3:]
    t = cross3(own_moved[3:], u)
    own_wide = [wide(line) for line in own_frame]
    moved_wide = [wide(line) for line in [*own_moved[:3], *t]]

    def derive(step, totals):
        group, unused = group_items(step, item_ref, items)
        lanes = [lanes_of(item & ITEM_MASK, member) for item in group]
        terms, sums = geometry(group, unused, lanes, own_code, own_wide, period, all_ref)
        moved_rows = partner_rows(lambda tile, k: row_of(all_ref, tile, k, member), group, lanes)
        return terms, added(totals, apply(moved_rows, terms, own_wide, moved_wide) + list(sums))

    def keep(step, totals):
        terms, totals = derive(step, totals)
        start = pl.multiple_of(step * (TERMS * GROUP * SUB), SUB)
        for k in range(TERMS):
            coef_ref[pl.ds(start + k * GROUP * SUB, GROUP * SUB), :] = terms[k]
        return totals

    zero = jnp.zeros((SUB, member), jnp.float32)
    totals = lax.fori_loop(0, jnp.minimum(steps, held), keep, (zero,) * 9)
    totals = lax.fori_loop(held, steps, lambda step, before: derive(step, before)[1], totals)
    sums = [folded(total) for total in totals]
    kept_ref[...] = jnp.concatenate(sums[7:], axis=0)
    spread(close(sums, sums[7], sums[8], u, t), out_ref)


def scalar_of(block):
    return jnp.sum(jnp.sum(block, axis=0, keepdims=True), axis=1, keepdims=True)


def second_kernel(
    cols,
    total_entries,
    period,
    item_ref,
    coef_ref,
    kept_ref,
    all_ref,
    image_ref,
    out_ref,
    pair_ref,
    scalar_ref,
    second_ref,
):
    own = lax.axis_index("row") * cols + lax.axis_index("col")
    member = kept_ref.shape[1]
    basis = all_ref[:, 0, 0 : 6 * member]
    image = image_ref[:, 0, :]
    portion = 1.0 / total_entries

    def total_of(block):
        return scalar_of(sum(block[:, k * member : (k + 1) * member] for k in range(6)))

    norm_sq = total_of(basis * basis) * portion + norm_eps
    norm_inv = lax.rsqrt(norm_sq)
    alpha = total_of(basis * image) * portion / norm_sq
    second = image - alpha * basis
    second_ref[:, 0, :] = second
    beta_sq = total_of(second * second) * portion / norm_sq + norm_eps
    beta = jnp.sqrt(beta_sq)
    scale = norm_inv * lax.rsqrt(beta_sq)

    own_code = own * (1 << CODE_BITS) + 21
    items = item_ref[0]
    held = coef_ref.shape[0] // (TERMS * GROUP * SUB)
    steps = (items + GROUP - 1) // GROUP

    def moved_row(tile, k):
        return row_of(second_ref, tile, k, member)

    own_moved = [moved_row(own, k) for k in range(6)]
    own_frame = [row_of(all_ref, own, CENTRE + k, member) for k in range(6)]
    u = own_frame[3:]
    t = cross3(own_moved[3:], u)
    own_wide = [wide(line) for line in own_frame]
    moved_wide = [wide(line) for line in [*own_moved[:3], *t]]

    def visit(step, totals):
        group, _ = group_items(step, item_ref, items)
        lanes = [lanes_of(item & ITEM_MASK, member) for item in group]
        start = pl.multiple_of(step * (TERMS * GROUP * SUB), SUB)
        terms = [coef_ref[pl.ds(start + k * GROUP * SUB, GROUP * SUB), :] for k in range(TERMS)]
        return added(totals, apply(partner_rows(moved_row, group, lanes), terms, own_wide, moved_wide))

    def visit_again(step, totals):
        group, unused = group_items(step, item_ref, items)
        lanes = [lanes_of(item & ITEM_MASK, member) for item in group]
        terms, _ = geometry(group, unused, lanes, own_code, own_wide, period, all_ref)
        return added(totals, apply(partner_rows(moved_row, group, lanes), terms, own_wide, moved_wide))

    zero = jnp.zeros((SUB, member), jnp.float32)
    totals = lax.fori_loop(0, jnp.minimum(steps, held), visit, (zero,) * 7)
    totals = lax.fori_loop(held, steps, visit_again, totals)
    sums = [folded(total) for total in totals]
    product = close(sums, kept_ref[0:1, :], kept_ref[1:2, :], u, t)
    fill = [jnp.zeros((1, member), jnp.float32)] * (SUB - len(product))
    first = stacked([row_of(all_ref, own, k, member) for k in range(6)] + fill)
    image = stacked(product + fill) * scale - (beta * norm_inv) * first
    second = stacked(own_moved + fill) * scale
    inner = scalar_of(second * image)
    weight = scalar_of(second * second)
    local_alpha = jnp.where(weight > 1e-30, inner / jnp.maximum(weight, 1e-30), 0.0)
    rest = image - local_alpha * second
    size = scalar_of(rest * rest)
    slant = scalar_of(second * rest)
    lane = lax.broadcasted_iota(jnp.int32, (1, member), 1)
    line = jnp.zeros((1, member), jnp.float32)
    for at, value in enumerate((inner, weight, local_alpha, size, slant)):
        line = jnp.where(lane == at, value, line)
    out_ref[...] = jnp.broadcast_to(line[None], out_ref.shape)
    pair_ref[0] = second
    pair_ref[1] = image
    scalar_ref[...] = jnp.where(lane == 0, alpha, jnp.where(lane == 1, beta, 0.0))


def last_kernel(total_entries, pair_ref, scalar_ref, line_ref, mode_ref, coefficient_ref):
    lines = line_ref[:, 0, :]
    alpha = jnp.sum(lines[:, 0:1], axis=0, keepdims=True) / total_entries
    away = lines[:, 2:3] - alpha
    parts = lines[:, 3:4] + away * (away * lines[:, 1:2] + 2.0 * lines[:, 4:5])
    beta = jnp.sqrt(jnp.sum(parts, axis=0, keepdims=True) / total_entries + norm_eps)
    mode = (pair_ref[1] - alpha * pair_ref[0]) / beta
    mode_ref[...] = mode[: mode_ref.shape[0]]
    for at, value in enumerate((scalar_ref[0:1, 0:1], scalar_ref[0:1, 1:2], alpha, beta)):
        coefficient_ref[at] = jnp.sum(value)


def local(config, start, tile_list, tile_count):
    dof, member = config.shape
    row_devices = lax.axis_size("row")
    col_devices = lax.axis_size("col")
    devices = row_devices * col_devices
    total_entries = float(dof * member * devices)
    period = (5.0, 5.0, 3.5 * (member // 16))
    slots = tile_list.shape[2]
    longest = (row_devices + col_devices) * slots + 1

    def shaped(*shape):
        return jax.ShapeDtypeStruct(shape, jnp.float32)

    def everywhere(copies):
        return lax.all_to_all(copies, ("row", "col"), 0, 0, tiled=True)

    params = pltpu.CompilerParams(vmem_limit_bytes=VMEM_LIMIT)
    vmem = pl.BlockSpec(memory_space=pltpu.VMEM)
    smem = pl.BlockSpec(memory_space=pltpu.SMEM)

    outside = pl.BlockSpec(memory_space=pl.ANY)
    packed = pl.pallas_call(
        pack_kernel,
        out_shape=shaped(devices, 1, (LIST_ROW + 1) * member),
        in_specs=[outside] * 4,
        out_specs=vmem,
        scratch_shapes=[
            pltpu.VMEM((dof, member), jnp.float32),
            pltpu.VMEM((dof, member), jnp.float32),
            pltpu.SMEM((1, tile_list.shape[3], 1, slots), jnp.int32),
            pltpu.SMEM((1, 1), jnp.int32),
            pltpu.SemaphoreType.DMA((4,)),
        ],
        compiler_params=pltpu.CompilerParams(vmem_limit_bytes=PACK_LIMIT),
    )(config, start, jnp.transpose(tile_list, (0, 3, 1, 2)), tile_count)
    together = everywhere(packed)

    held_rows = HELD // GROUP * (TERMS * GROUP * SUB)
    image, items, terms, kept = pl.pallas_call(
        functools.partial(first_kernel, row_devices, col_devices, slots, period),
        out_shape=(
            shaped(devices, 1, dof * member),
            jax.ShapeDtypeStruct((1 + longest * (member // SUB) + GROUP,), jnp.int32),
            shaped(held_rows, member),
            shaped(2, member),
        ),
        in_specs=[vmem],
        out_specs=(vmem, smem, vmem, vmem),
        scratch_shapes=[
            pltpu.SMEM((longest + TESTS,), jnp.int32),
            pltpu.VMEM((row_devices + col_devices, member), jnp.int32),
            pltpu.SMEM((row_devices + col_devices, member), jnp.int32),
            pltpu.SemaphoreType.DMA,
        ],
        compiler_params=params,
    )(together)
    image = everywhere(image)

    line, pair, scalars = pl.pallas_call(
        functools.partial(second_kernel, col_devices, total_entries, period),
        out_shape=(shaped(devices, 1, member), shaped(2, SUB, member), shaped(1, member)),
        in_specs=[smem] + [vmem] * 4,
        out_specs=(vmem, vmem, vmem),
        scratch_shapes=[
            pltpu.VMEM((devices, 1, dof * member), jnp.float32),
        ],
        compiler_params=params,
    )(items, terms, kept, together, image)
    line = everywhere(line)

    mode, coefficients = pl.pallas_call(
        functools.partial(last_kernel, total_entries),
        out_shape=(shaped(dof, member), shaped(4)),
        in_specs=[vmem] * 3,
        out_specs=(vmem, smem),
        compiler_params=params,
    )(pair, scalars, line)
    return (coefficients, mode)


def solution(mesh):
    placed = (
        P(None, ("row", "col")),
        P(None, ("row", "col")),
        P("row", "col", None, None),
        P("row", "col"),
    )
    return jax.shard_map(
        local, mesh=mesh, in_specs=placed, out_specs=(P(), P(None, ("row", "col"))), check_vma=False
    )
```

```python
import functools
import math

import jax
import jax.numpy as jnp
from jax import lax
from jax.experimental import pallas as pl
from jax.experimental.pallas import tpu as pltpu
from jax.sharding import PartitionSpec as P

chi_shape = 0.8
chi_energy = (math.sqrt(5.0) - 1.0) / (math.sqrt(5.0) + 1.0)
well_depth = 0.005
cutoff_sq = 20.25
norm_eps = 1e-06

SUB = 8
CENTRE = 6
LIST_ROW = 12
CODE_BITS = 6
ITEM_BITS = 8
ITEM_MASK = 255
LAYER = 16
TESTS = 5
ITEMS = 2
GROUP = 4
TERMS = 20
HELD = 64
VMEM_LIMIT = 32 * 1024 * 1024
PACK_LIMIT = 60 * 1024 * 1024


def dot3(a, b):
    return a[0] * b[0] + a[1] * b[1] + a[2] * b[2]


def cross3(a, b):
    return (
        a[1] * b[2] - a[2] * b[1],
        a[2] * b[0] - a[0] * b[2],
        a[0] * b[1] - a[1] * b[0],
    )


def inverse(value):
    guess = pl.reciprocal(value, approx=True)
    return guess * (2.0 - value * guess)


def bracket(chi, scaled, factor, p, a, b):
    f = factor * (a - scaled * b)
    g = factor * (b - scaled * a)
    y = p * (a * f + b * g)
    cross = factor * scaled
    f_c = chi * (cross * f - factor * g)
    g_c = chi * (cross * g - factor * f)
    return f, g, y, cross, f_c, g_c


def pair_coefficients(d, ui, uj, lift):
    r_sq = dot3(d, d) + lift
    a = dot3(d, ui)
    b = dot3(d, uj)
    c = dot3(ui, uj)
    r_inv = lax.rsqrt(r_sq)
    p = r_inv * r_inv
    p2 = 2.0 * p
    r = r_sq * r_inv
    x = jnp.maximum(1.0 - r_sq * (1.0 / cutoff_sq), 0.0)
    c_shape = chi_shape * c
    c_energy = chi_energy * c
    e1 = lax.rsqrt(1.0 - c_shape * c_shape)
    q = e1 * e1
    q2 = inverse(1.0 - c_energy * c_energy)
    f, g, y, m, f_c, g_c = bracket(chi_shape, c_shape, q, p, a, b)
    f2, g2, y2, m2, f2_c, g2_c = bracket(chi_energy, c_energy, q2, p, a, b)
    sigma = lax.rsqrt(1.0 - chi_shape * y)
    sigma_sq = sigma * sigma
    psi = 1.0 - chi_energy * y2
    s = inverse(r - sigma + 1.0)
    s_sq = s * s
    s6 = s_sq * s_sq * s_sq
    t0 = s6 * (s6 - 1.0)
    t1 = s6 * s * (6.0 - 12.0 * s6)
    t2 = s6 * s_sq * (156.0 * s6 - 42.0)
    ke = (4.0 * well_depth) * e1
    kx = ke * x
    v_ee = kx * (24.0 / cutoff_sq**2)
    kxx = kx * x
    v_e = kxx * (-6.0 / cutoff_sq)
    v = kxx * x
    psi_sq = psi * psi
    psi_sq_t0 = psi_sq * t0
    psi_sq_t1 = psi_sq * t1
    u = v * psi_sq_t0
    slope = v * psi_sq_t1
    slope2 = v * psi_sq * t2
    tau = (-0.5 * chi_shape) * sigma_sq * sigma
    push = (-2.0 * chi_energy) * psi
    v_t1 = v * t1
    d1 = slope * tau
    d2 = push * (v * t0)
    h1 = p2 * d1
    h2 = p2 * d2
    kc = chi_shape * c_shape * q
    fg = chi_shape * f * g
    fg2 = chi_energy * f2 * g2
    u_a = h1 * f + h2 * f2
    u_b = h1 * g + h2 * g2
    u_fg = h1 * fg + h2 * fg2
    u_c = u * kc - u_fg
    v_e_t0 = v_e * psi_sq_t0
    d_e = r_inv * slope + v_e_t0
    u_e = d_e - (h1 * y + h2 * y2)

    p2_sq = p2 * p2
    k11 = p2_sq * (tau * (slope2 * tau + (1.5 * chi_shape) * sigma_sq * slope))
    k12 = p2_sq * (push * v_t1 * tau)
    k22 = p2_sq * ((2.0 * chi_energy * chi_energy) * (v * t0))
    steep = v_e * psi_sq_t1 + slope2 * r_inv
    l1 = p2 * (steep * tau - h1)
    l2 = p2 * (push * (v_e * t0 + v_t1 * r_inv) - h2)
    j1 = (y, f, g, fg)
    j2 = (y2, f2, g2, fg2)
    w1 = [k11 * one + k12 * two for one, two in zip(j1, j2)]
    w2 = [k12 * one + k22 * two for one, two in zip(j1, j2)]

    def quadratic(m_at, n_at):
        return w1[m_at] * j1[n_at] + w2[m_at] * j2[n_at]

    d_ee = v_ee * psi_sq_t0 + r_inv * (2.0 * (v_e * psi_sq_t1)) + p * (slope2 - slope * r_inv)
    h_ee = quadratic(0, 0) - 2.0 * (l1 * y + l2 * y2) + d_ee
    h_ea = l1 * f + l2 * f2 - quadratic(0, 1)
    h_eb = l1 * g + l2 * g2 - quadratic(0, 2)
    h_ec = quadratic(0, 3) - (l1 * fg + l2 * fg2) + kc * u_e
    straight = h1 * q + h2 * q2
    h_aa = quadratic(1, 1) + straight
    h_ab = quadratic(1, 2) - (h1 * m + h2 * m2)
    h_ac = kc * u_a - quadratic(1, 3) + (h1 * f_c + h2 * f2_c)
    h_bb = quadratic(2, 2) + straight
    h_bc = kc * u_b - quadratic(2, 3) + (h1 * g_c + h2 * g2_c)
    bent = (chi_shape * h1) * (f_c * g + f * g_c) + (chi_energy * h2) * (f2_c * g2 + f2 * g2_c)
    twist = kc * kc + (chi_shape * chi_shape) * q * (2.0 * q - 1.0)
    h_cc = quadratic(3, 3) - bent - 2.0 * (kc * u_fg) + u * twist
    gradient = (u_e, u_a, u_b, u_c)
    return gradient, (h_ee, h_ea, h_eb, h_ec, h_aa, h_ab, h_ac, h_bb, h_bc, h_cc), u_a * a + u_c * c


def offsets_of(code, period):
    return [((code >> bits & 3) - 1).astype(jnp.float32) * size for bits, size in zip((4, 2, 0), period)]


def row_of(tiles_ref, tile, k, member):
    return tiles_ref[tile, :, k * member : (k + 1) * member]


def centre_of(code, period, all_ref, member):
    shift = offsets_of(code, period)
    return [row_of(all_ref, code >> CODE_BITS, CENTRE + k, member) + shift[k] for k in range(3)]


def lanes_of(block, member):
    row = lax.broadcasted_iota(jnp.int32, (SUB, member), 0)
    lane = lax.broadcasted_iota(jnp.int32, (SUB, member), 1)
    low = (((lane & -LAYER) - block * LAYER) & (member - 1)) + row
    return [low + at for at in range(0, LAYER, SUB)]


def picked(block, lanes):
    return jnp.take_along_axis(block, lanes, axis=1, mode="promise_in_bounds")


def box_lanes(member):
    block = lax.broadcasted_iota(jnp.int32, (member // LAYER, member), 0)
    lane = lax.broadcasted_iota(jnp.int32, (member // LAYER, member), 1)
    return ((lane & -LAYER) - block * LAYER) & (member - 1)


def near_blocks(own_centre, partner, lanes):
    blocks, member = lanes.shape
    zero = jnp.zeros((1, member), jnp.float32)
    box = stacked(partner + [-line for line in partner] + [zero, zero])
    for bit in (1, 2, 4, 8):
        box = jnp.maximum(box, pltpu.roll(box, member - bit, 1))

    def seen(k):
        return picked(jnp.broadcast_to(box[k : k + 1], lanes.shape), lanes)

    reach = 0.0
    for k in range(3):
        above = own_centre[k] - seen(k)
        below = -own_centre[k] - seen(3 + k)
        gap = jnp.maximum(jnp.maximum(above, below), 0.0)
        reach = reach + gap * gap
    nearest = jnp.min(reach, axis=1, keepdims=True)
    weight = (1 << lax.broadcasted_iota(jnp.int32, (blocks, 1), 0)).astype(jnp.float32)
    return jnp.sum(jnp.where(nearest < cutoff_sq * 1.001, weight, 0.0)).astype(jnp.int32)


def stacked(parts):
    return jnp.concatenate(parts, axis=0)


def wide(row):
    return jnp.broadcast_to(row, (GROUP * SUB, row.shape[1]))


def partner_rows(row_at, items, lanes):
    rows = []
    for k in range(6):
        parts = []
        for item, lane in zip(items, lanes):
            row = row_at(item >> (ITEM_BITS + CODE_BITS), k)
            parts += [picked(jnp.broadcast_to(row, half.shape), half) for half in lane]
        rows.append(stacked(parts))
    return rows


def folded(total):
    return jnp.sum(total, axis=0, keepdims=True)


def geometry(items, unused, lanes, own_code, own_wide, period, all_ref):
    member = lanes[0][0].shape[1]
    lane = lax.broadcasted_iota(jnp.int32, (SUB, member), 1)
    lift = []
    shifts = []
    for item, idle, other in zip(items, unused, lanes):
        code = item >> ITEM_BITS
        own_lift = jnp.where(code == own_code, 2.0 * cutoff_sq, 0.0)
        idle_lift = jnp.where(idle, 2.0 * cutoff_sq, 0.0)
        lift += [jnp.where(half == lane, own_lift, 0.0) + idle_lift for half in other]
        shifts.append(offsets_of(code, period))
    rows = partner_rows(lambda tile, k: row_of(all_ref, tile, CENTRE + k, member), items, lanes)
    shift = [stacked([jnp.full((LAYER, member), one[k]) for one in shifts]) for k in range(3)]
    d = [rows[k] + shift[k] - own_wide[k] for k in range(3)]
    uj = rows[3:]
    gradient, hessian, spin = pair_coefficients(d, own_wide[3:], uj, stacked(lift))
    return list(gradient) + list(hessian) + d + uj, (gradient[1], spin)


def apply(moved_rows, terms, own_wide, moved_wide):
    u_e, u_a, u_b, u_c, h_ee, h_ea, h_eb, h_ec, h_aa, h_ab, h_ac, h_bb, h_bc, h_cc = terms[:14]
    d = terms[14:17]
    uj = terms[17:20]
    ui = own_wide[3:]
    dui = moved_wide[3:]
    dd = [moved_rows[k] - moved_wide[k] for k in range(3)]
    duj = cross3(moved_rows[3:], uj)
    de = dot3(d, dd)
    da = dot3(dd, ui) + dot3(d, dui)
    db = dot3(dd, uj) + dot3(d, duj)
    dc = dot3(dui, uj) + dot3(ui, duj)
    du_e = h_ee * de + h_ea * da + h_eb * db + h_ec * dc
    du_a = h_ea * de + h_aa * da + h_ab * db + h_ac * dc
    du_b = h_eb * de + h_ab * da + h_bb * db + h_bc * dc
    du_c = h_ec * de + h_ac * da + h_bc * db + h_cc * dc
    force = [du_e * d[k] + u_e * dd[k] + du_b * uj[k] + u_b * duj[k] for k in range(3)]
    turn = [du_a * d[k] + u_a * dd[k] + du_c * uj[k] + u_c * duj[k] for k in range(3)]
    return force + turn + [du_a]


def group_items(step, item_ref, item_count):
    at = [step * ITEMS + part for part in range(ITEMS)]
    return [item_ref[1 + place] for place in at], [place >= item_count for place in at]


def added(totals, news):
    return tuple(
        total + sum(new[part * SUB : (part + 1) * SUB] for part in range(GROUP)) for total, new in zip(totals, news)
    )


def close(sums, kept, spin, u, t):
    force = [-(sums[k] + u[k] * sums[6] + t[k] * kept) for k in range(3)]
    return force + list(cross3(u, [sums[3 + k] - t[k] * spin for k in range(3)]))


def spread(rows, out_ref):
    member = rows[0].shape[1]
    for k, row in enumerate(rows):
        out_ref[:, :, k * member : (k + 1) * member] = jnp.broadcast_to(row[None], (out_ref.shape[0], 1, member))


def pack_kernel(*refs):
    sources, out_ref, targets, sems = refs[:4], refs[4], refs[5:9], refs[9]
    config_ref, start_ref, list_ref, count_ref = targets
    copies = [
        pltpu.make_async_copy(source, target, sems.at[at]) for at, (source, target) in enumerate(zip(sources, targets))
    ]
    for copy in copies:
        copy.start()
    copies[2].wait()
    copies[3].wait()
    member = config_ref.shape[1]
    lane = lax.broadcasted_iota(jnp.int32, (1, member), 1)
    fields, slots = list_ref.shape[1], list_ref.shape[3]
    line = jnp.full((1, member), -9, jnp.int32)
    for field in range(fields):
        for slot in range(slots):
            line = jnp.where(lane == field * slots + slot, list_ref[0, field, 0, slot], line)
    line = jnp.where((lane >= count_ref[0, 0]) & (lane < slots), -9, line).astype(jnp.float32)
    copies[0].wait()
    copies[1].wait()
    rows = [ref[k : k + 1, :] for ref in (start_ref, config_ref) for k in range(6)]
    spread(rows + [line], out_ref)


def first_kernel(
    rows,
    cols,
    slots,
    period,
    all_ref,
    out_ref,
    item_ref,
    coef_ref,
    kept_ref,
    entry_ref,
    code_ref,
    code_smem,
    sem,
):
    member = kept_ref.shape[1]
    row_id = lax.axis_index("row")
    col_id = lax.axis_index("col")
    own = row_id * cols + col_id
    blocks = member // LAYER

    def field(line, at):
        return line if at == 0 else pltpu.roll(line, member - at * slots, 1)

    row_f = row_id.astype(jnp.float32)
    col_f = col_id.astype(jnp.float32)
    lines = [row_of(all_ref, row_id * cols + col, LIST_ROW, member) for col in range(cols)]
    lines += [row_of(all_ref, row * cols + col_id, LIST_ROW, member) for row in range(rows)]
    line = jnp.concatenate(lines, axis=0)
    at = lax.broadcasted_iota(jnp.int32, line.shape, 0).astype(jnp.float32)
    near = at < float(cols)
    other = field(line, 1)
    offset = field(line, 2) * 16.0 + field(line, 3) * 4.0 + field(line, 4)
    partner = jnp.where(near, other * float(cols) + at, (at - float(cols)) * float(cols) + line)
    code = partner * float(1 << CODE_BITS) + (jnp.where(near, offset, -offset) + 21.0)
    hit = jnp.where(near, line - col_f, jnp.where(line >= 0.0, other - row_f, 1.0)) == 0.0
    code_ref[...] = jnp.where(hit, code, -1.0).astype(jnp.int32)
    copy = pltpu.make_async_copy(code_ref, code_smem, sem)
    copy.start()
    own_code = own * (1 << CODE_BITS) + 21
    own_moved = [row_of(all_ref, own, k, member) for k in range(6)]
    own_frame = [row_of(all_ref, own, CENTRE + k, member) for k in range(6)]
    lanes = box_lanes(member)
    own_centre = [jnp.broadcast_to(line, lanes.shape) for line in own_frame[:3]]

    def append(code, bits, count):
        for block in range(blocks):
            item_ref[1 + count] = (code << ITEM_BITS) + block
            count = count + (bits >> block & 1)
        return count

    items = append(own_code, near_blocks(own_centre, own_frame[:3], lanes), jnp.int32(0))
    copy.wait()

    def gather(line, count):
        for slot in range(slots):
            code = code_smem[line, slot]
            entry_ref[count] = code
            count = count + (code >= 0).astype(jnp.int32)
        return count

    entries = lax.fori_loop(0, rows + cols, gather, jnp.int32(0))
    for part in range(TESTS):
        entry_ref[entries + part] = own_code

    def prepare(step, count):
        codes = [entry_ref[step * TESTS + part] for part in range(TESTS)]
        bits = [near_blocks(own_centre, centre_of(code, period, all_ref, member), lanes) for code in codes]
        for part in range(TESTS):
            count = append(codes[part], jnp.where(step * TESTS + part < entries, bits[part], 0), count)
        return count

    items = lax.fori_loop(0, (entries + TESTS - 1) // TESTS, prepare, items)
    for part in range(ITEMS):
        item_ref[1 + items + part] = own_code << ITEM_BITS
    item_ref[0] = items

    held = coef_ref.shape[0] // (TERMS * GROUP * SUB)
    steps = (items + ITEMS - 1) // ITEMS
    u = own_frame[3:]
    t = cross3(own_moved[3:], u)
    own_wide = [wide(line) for line in own_frame]
    moved_wide = [wide(line) for line in [*own_moved[:3], *t]]

    def derive(step, totals):
        group, unused = group_items(step, item_ref, items)
        lanes = [lanes_of(item & ITEM_MASK, member) for item in group]
        terms, sums = geometry(group, unused, lanes, own_code, own_wide, period, all_ref)
        moved_rows = partner_rows(lambda tile, k: row_of(all_ref, tile, k, member), group, lanes)
        return terms, added(totals, apply(moved_rows, terms, own_wide, moved_wide) + list(sums))

    def keep(step, totals):
        terms, totals = derive(step, totals)
        start = pl.multiple_of(step * (TERMS * GROUP * SUB), SUB)
        for k in range(TERMS):
            coef_ref[pl.ds(start + k * GROUP * SUB, GROUP * SUB), :] = terms[k]
        return totals

    zero = jnp.zeros((SUB, member), jnp.float32)
    totals = lax.fori_loop(0, jnp.minimum(steps, held), keep, (zero,) * 9)
    totals = lax.fori_loop(held, steps, lambda step, before: derive(step, before)[1], totals)
    sums = [folded(total) for total in totals]
    kept_ref[...] = jnp.concatenate(sums[7:], axis=0)
    spread(close(sums, sums[7], sums[8], u, t), out_ref)


def scalar_of(block):
    return jnp.sum(jnp.sum(block, axis=0, keepdims=True), axis=1, keepdims=True)


def second_kernel(
    cols,
    total_entries,
    period,
    item_ref,
    coef_ref,
    kept_ref,
    all_ref,
    image_ref,
    out_ref,
    pair_ref,
    scalar_ref,
    second_ref,
):
    own = lax.axis_index("row") * cols + lax.axis_index("col")
    member = kept_ref.shape[1]
    basis = all_ref[:, 0, 0 : 6 * member]
    image = image_ref[:, 0, :]
    portion = 1.0 / total_entries

    def total_of(block):
        return scalar_of(sum(block[:, k * member : (k + 1) * member] for k in range(6)))

    norm_sq = total_of(basis * basis) * portion + norm_eps
    norm_inv = lax.rsqrt(norm_sq)
    alpha = total_of(basis * image) * portion / norm_sq
    second = image - alpha * basis
    second_ref[:, 0, :] = second
    beta_sq = total_of(second * second) * portion / norm_sq + norm_eps
    beta = jnp.sqrt(beta_sq)
    scale = norm_inv * lax.rsqrt(beta_sq)

    own_code = own * (1 << CODE_BITS) + 21
    items = item_ref[0]
    held = coef_ref.shape[0] // (TERMS * GROUP * SUB)
    steps = (items + ITEMS - 1) // ITEMS

    def moved_row(tile, k):
        return row_of(second_ref, tile, k, member)

    own_moved = [moved_row(own, k) for k in range(6)]
    own_frame = [row_of(all_ref, own, CENTRE + k, member) for k in range(6)]
    u = own_frame[3:]
    t = cross3(own_moved[3:], u)
    own_wide = [wide(line) for line in own_frame]
    moved_wide = [wide(line) for line in [*own_moved[:3], *t]]

    def visit(step, totals):
        group, _ = group_items(step, item_ref, items)
        lanes = [lanes_of(item & ITEM_MASK, member) for item in group]
        start = pl.multiple_of(step * (TERMS * GROUP * SUB), SUB)
        terms = [coef_ref[pl.ds(start + k * GROUP * SUB, GROUP * SUB), :] for k in range(TERMS)]
        return added(totals, apply(partner_rows(moved_row, group, lanes), terms, own_wide, moved_wide))

    def visit_again(step, totals):
        group, unused = group_items(step, item_ref, items)
        lanes = [lanes_of(item & ITEM_MASK, member) for item in group]
        terms, _ = geometry(group, unused, lanes, own_code, own_wide, period, all_ref)
        return added(totals, apply(partner_rows(moved_row, group, lanes), terms, own_wide, moved_wide))

    zero = jnp.zeros((SUB, member), jnp.float32)
    totals = lax.fori_loop(0, jnp.minimum(steps, held), visit, (zero,) * 7)
    totals = lax.fori_loop(held, steps, visit_again, totals)
    sums = [folded(total) for total in totals]
    product = close(sums, kept_ref[0:1, :], kept_ref[1:2, :], u, t)
    fill = [jnp.zeros((1, member), jnp.float32)] * (SUB - len(product))
    first = stacked([row_of(all_ref, own, k, member) for k in range(6)] + fill)
    image = stacked(product + fill) * scale - (beta * norm_inv) * first
    second = stacked(own_moved + fill) * scale
    inner = scalar_of(second * image)
    weight = scalar_of(second * second)
    local_alpha = jnp.where(weight > 1e-30, inner / jnp.maximum(weight, 1e-30), 0.0)
    rest = image - local_alpha * second
    size = scalar_of(rest * rest)
    slant = scalar_of(second * rest)
    lane = lax.broadcasted_iota(jnp.int32, (1, member), 1)
    line = jnp.zeros((1, member), jnp.float32)
    for at, value in enumerate((inner, weight, local_alpha, size, slant)):
        line = jnp.where(lane == at, value, line)
    out_ref[...] = jnp.broadcast_to(line[None], out_ref.shape)
    pair_ref[0] = second
    pair_ref[1] = image
    scalar_ref[...] = jnp.where(lane == 0, alpha, jnp.where(lane == 1, beta, 0.0))


def last_kernel(total_entries, pair_ref, scalar_ref, line_ref, mode_ref, coefficient_ref):
    lines = line_ref[:, 0, :]
    alpha = jnp.sum(lines[:, 0:1], axis=0, keepdims=True) / total_entries
    away = lines[:, 2:3] - alpha
    parts = lines[:, 3:4] + away * (away * lines[:, 1:2] + 2.0 * lines[:, 4:5])
    beta = jnp.sqrt(jnp.sum(parts, axis=0, keepdims=True) / total_entries + norm_eps)
    mode = (pair_ref[1] - alpha * pair_ref[0]) / beta
    mode_ref[...] = mode[: mode_ref.shape[0]]
    for at, value in enumerate((scalar_ref[0:1, 0:1], scalar_ref[0:1, 1:2], alpha, beta)):
        coefficient_ref[at] = jnp.sum(value)


def local(config, start, tile_list, tile_count):
    dof, member = config.shape
    row_devices = lax.axis_size("row")
    col_devices = lax.axis_size("col")
    devices = row_devices * col_devices
    total_entries = float(dof * member * devices)
    period = (5.0, 5.0, 3.5 * (member // 16))
    slots = tile_list.shape[2]
    longest = (row_devices + col_devices) * slots + 1

    def shaped(*shape):
        return jax.ShapeDtypeStruct(shape, jnp.float32)

    def everywhere(copies):
        return lax.all_to_all(copies, ("row", "col"), 0, 0, tiled=True)

    params = pltpu.CompilerParams(vmem_limit_bytes=VMEM_LIMIT)
    vmem = pl.BlockSpec(memory_space=pltpu.VMEM)
    smem = pl.BlockSpec(memory_space=pltpu.SMEM)

    outside = pl.BlockSpec(memory_space=pl.ANY)
    packed = pl.pallas_call(
        pack_kernel,
        out_shape=shaped(devices, 1, (LIST_ROW + 1) * member),
        in_specs=[outside] * 4,
        out_specs=vmem,
        scratch_shapes=[
            pltpu.VMEM((dof, member), jnp.float32),
            pltpu.VMEM((dof, member), jnp.float32),
            pltpu.SMEM((1, tile_list.shape[3], 1, slots), jnp.int32),
            pltpu.SMEM((1, 1), jnp.int32),
            pltpu.SemaphoreType.DMA((4,)),
        ],
        compiler_params=pltpu.CompilerParams(vmem_limit_bytes=PACK_LIMIT),
    )(config, start, jnp.transpose(tile_list, (0, 3, 1, 2)), tile_count)
    together = everywhere(packed)

    held_rows = HELD * (TERMS * LAYER)
    image, items, terms, kept = pl.pallas_call(
        functools.partial(first_kernel, row_devices, col_devices, slots, period),
        out_shape=(
            shaped(devices, 1, dof * member),
            jax.ShapeDtypeStruct((1 + longest * (member // LAYER) + ITEMS,), jnp.int32),
            shaped(held_rows, member),
            shaped(2, member),
        ),
        in_specs=[vmem],
        out_specs=(vmem, smem, vmem, vmem),
        scratch_shapes=[
            pltpu.SMEM((longest + TESTS,), jnp.int32),
            pltpu.VMEM((row_devices + col_devices, member), jnp.int32),
            pltpu.SMEM((row_devices + col_devices, member), jnp.int32),
            pltpu.SemaphoreType.DMA,
        ],
        compiler_params=params,
    )(together)
    image = everywhere(image)

    line, pair, scalars = pl.pallas_call(
        functools.partial(second_kernel, col_devices, total_entries, period),
        out_shape=(shaped(devices, 1, member), shaped(2, SUB, member), shaped(1, member)),
        in_specs=[smem] + [vmem] * 4,
        out_specs=(vmem, vmem, vmem),
        scratch_shapes=[
            pltpu.VMEM((devices, 1, dof * member), jnp.float32),
        ],
        compiler_params=params,
    )(items, terms, kept, together, image)
    line = everywhere(line)

    mode, coefficients = pl.pallas_call(
        functools.partial(last_kernel, total_entries),
        out_shape=(shaped(dof, member), shaped(4)),
        in_specs=[vmem] * 3,
        out_specs=(vmem, smem),
        compiler_params=params,
    )(pair, scalars, line)
    return (coefficients, mode)


def solution(mesh):
    placed = (
        P(None, ("row", "col")),
        P(None, ("row", "col")),
        P("row", "col", None, None),
        P("row", "col"),
    )
    return jax.shard_map(
        local, mesh=mesh, in_specs=placed, out_specs=(P(), P(None, ("row", "col"))), check_vma=False
    )
```

```python
import functools
import math

import jax
import jax.numpy as jnp
from jax import lax
from jax.experimental import pallas as pl
from jax.experimental.pallas import tpu as pltpu
from jax.sharding import PartitionSpec as P

chi_shape = 0.8
chi_energy = (math.sqrt(5.0) - 1.0) / (math.sqrt(5.0) + 1.0)
well_depth = 0.005
cutoff_sq = 20.25
norm_eps = 1e-06

SUB = 8
CENTRE = 6
LIST_ROW = 12
CODE_BITS = 6
ITEM_BITS = 8
ITEM_MASK = 255
LAYER = 16
TESTS = 5
GROUP = 4
TERMS = 20
HELD = 128
VMEM_LIMIT = 32 * 1024 * 1024
PACK_LIMIT = 60 * 1024 * 1024


def dot3(a, b):
    return a[0] * b[0] + a[1] * b[1] + a[2] * b[2]


def cross3(a, b):
    return (
        a[1] * b[2] - a[2] * b[1],
        a[2] * b[0] - a[0] * b[2],
        a[0] * b[1] - a[1] * b[0],
    )


def inverse(value):
    guess = pl.reciprocal(value, approx=True)
    return guess * (2.0 - value * guess)


def bracket(chi, scaled, factor, p, a, b):
    f = factor * (a - scaled * b)
    g = factor * (b - scaled * a)
    y = p * (a * f + b * g)
    cross = factor * scaled
    f_c = chi * (cross * f - factor * g)
    g_c = chi * (cross * g - factor * f)
    return f, g, y, cross, f_c, g_c


def pair_coefficients(d, ui, uj, lift):
    r_sq = dot3(d, d) + lift
    a = dot3(d, ui)
    b = dot3(d, uj)
    c = dot3(ui, uj)
    r_inv = lax.rsqrt(r_sq)
    p = r_inv * r_inv
    p2 = 2.0 * p
    r = r_sq * r_inv
    x = jnp.maximum(1.0 - r_sq * (1.0 / cutoff_sq), 0.0)
    c_shape = chi_shape * c
    c_energy = chi_energy * c
    e1 = lax.rsqrt(1.0 - c_shape * c_shape)
    q = e1 * e1
    q2 = inverse(1.0 - c_energy * c_energy)
    f, g, y, m, f_c, g_c = bracket(chi_shape, c_shape, q, p, a, b)
    f2, g2, y2, m2, f2_c, g2_c = bracket(chi_energy, c_energy, q2, p, a, b)
    sigma = lax.rsqrt(1.0 - chi_shape * y)
    sigma_sq = sigma * sigma
    psi = 1.0 - chi_energy * y2
    s = inverse(r - sigma + 1.0)
    s_sq = s * s
    s6 = s_sq * s_sq * s_sq
    t0 = s6 * (s6 - 1.0)
    t1 = s6 * s * (6.0 - 12.0 * s6)
    t2 = s6 * s_sq * (156.0 * s6 - 42.0)
    ke = (4.0 * well_depth) * e1
    kx = ke * x
    v_ee = kx * (24.0 / cutoff_sq**2)
    kxx = kx * x
    v_e = kxx * (-6.0 / cutoff_sq)
    v = kxx * x
    psi_sq = psi * psi
    psi_sq_t0 = psi_sq * t0
    psi_sq_t1 = psi_sq * t1
    u = v * psi_sq_t0
    slope = v * psi_sq_t1
    slope2 = v * psi_sq * t2
    tau = (-0.5 * chi_shape) * sigma_sq * sigma
    push = (-2.0 * chi_energy) * psi
    v_t1 = v * t1
    d1 = slope * tau
    d2 = push * (v * t0)
    h1 = p2 * d1
    h2 = p2 * d2
    kc = chi_shape * c_shape * q
    fg = chi_shape * f * g
    fg2 = chi_energy * f2 * g2
    u_a = h1 * f + h2 * f2
    u_b = h1 * g + h2 * g2
    u_fg = h1 * fg + h2 * fg2
    u_c = u * kc - u_fg
    v_e_t0 = v_e * psi_sq_t0
    d_e = r_inv * slope + v_e_t0
    u_e = d_e - (h1 * y + h2 * y2)

    p2_sq = p2 * p2
    k11 = p2_sq * (tau * (slope2 * tau + (1.5 * chi_shape) * sigma_sq * slope))
    k12 = p2_sq * (push * v_t1 * tau)
    k22 = p2_sq * ((2.0 * chi_energy * chi_energy) * (v * t0))
    steep = v_e * psi_sq_t1 + slope2 * r_inv
    l1 = p2 * (steep * tau - h1)
    l2 = p2 * (push * (v_e * t0 + v_t1 * r_inv) - h2)
    j1 = (y, f, g, fg)
    j2 = (y2, f2, g2, fg2)
    w1 = [k11 * one + k12 * two for one, two in zip(j1, j2)]
    w2 = [k12 * one + k22 * two for one, two in zip(j1, j2)]

    def quadratic(m_at, n_at):
        return w1[m_at] * j1[n_at] + w2[m_at] * j2[n_at]

    d_ee = v_ee * psi_sq_t0 + r_inv * (2.0 * (v_e * psi_sq_t1)) + p * (slope2 - slope * r_inv)
    h_ee = quadratic(0, 0) - 2.0 * (l1 * y + l2 * y2) + d_ee
    h_ea = l1 * f + l2 * f2 - quadratic(0, 1)
    h_eb = l1 * g + l2 * g2 - quadratic(0, 2)
    h_ec = quadratic(0, 3) - (l1 * fg + l2 * fg2) + kc * u_e
    straight = h1 * q + h2 * q2
    h_aa = quadratic(1, 1) + straight
    h_ab = quadratic(1, 2) - (h1 * m + h2 * m2)
    h_ac = kc * u_a - quadratic(1, 3) + (h1 * f_c + h2 * f2_c)
    h_bb = quadratic(2, 2) + straight
    h_bc = kc * u_b - quadratic(2, 3) + (h1 * g_c + h2 * g2_c)
    bent = (chi_shape * h1) * (f_c * g + f * g_c) + (chi_energy * h2) * (f2_c * g2 + f2 * g2_c)
    twist = kc * kc + (chi_shape * chi_shape) * q * (2.0 * q - 1.0)
    h_cc = quadratic(3, 3) - bent - 2.0 * (kc * u_fg) + u * twist
    gradient = (u_e, u_a, u_b, u_c)
    return gradient, (h_ee, h_ea, h_eb, h_ec, h_aa, h_ab, h_ac, h_bb, h_bc, h_cc), u_a * a + u_c * c


def offsets_of(code, period):
    return [((code >> bits & 3) - 1).astype(jnp.float32) * size for bits, size in zip((4, 2, 0), period)]


def row_of(tiles_ref, tile, k, member):
    return tiles_ref[tile, :, k * member : (k + 1) * member]


def centre_of(code, period, all_ref, member):
    shift = offsets_of(code, period)
    return [row_of(all_ref, code >> CODE_BITS, CENTRE + k, member) + shift[k] for k in range(3)]


def lanes_of(block, member):
    row = lax.broadcasted_iota(jnp.int32, (SUB, member), 0)
    lane = lax.broadcasted_iota(jnp.int32, (SUB, member), 1)
    group = (lane & -LAYER) - (block >> 1) * LAYER
    return (group & (member - 1)) + ((block & 1) * SUB + row)


def picked(block, lanes):
    return jnp.take_along_axis(block, lanes, axis=1, mode="promise_in_bounds")


def box_lanes(member):
    block = lax.broadcasted_iota(jnp.int32, (member // SUB, member), 0)
    lane = lax.broadcasted_iota(jnp.int32, (member // SUB, member), 1)
    return (((lane & -LAYER) - (block >> 1) * LAYER) & (member - 1)) + (block & 1) * SUB


def near_blocks(own_centre, partner, lanes):
    blocks, member = lanes.shape
    zero = jnp.zeros((1, member), jnp.float32)
    box = stacked(partner + [-line for line in partner] + [zero, zero])
    for bit in (1, 2, 4):
        box = jnp.maximum(box, pltpu.roll(box, member - bit, 1))

    def seen(k):
        line = jnp.broadcast_to(box[k : k + 1], (SUB, member))
        return stacked([picked(line, lanes[at : at + SUB]) for at in range(0, blocks, SUB)])

    reach = 0.0
    for k in range(3):
        above = own_centre[k] - seen(k)
        below = -own_centre[k] - seen(3 + k)
        gap = jnp.maximum(jnp.maximum(above, below), 0.0)
        reach = reach + gap * gap
    nearest = jnp.min(reach, axis=1, keepdims=True)
    weight = (1 << lax.broadcasted_iota(jnp.int32, (blocks, 1), 0)).astype(jnp.float32)
    return jnp.sum(jnp.where(nearest < cutoff_sq * 1.001, weight, 0.0)).astype(jnp.int32)


def stacked(parts):
    return jnp.concatenate(parts, axis=0)


def wide(row):
    return jnp.broadcast_to(row, (GROUP * SUB, row.shape[1]))


def partner_rows(row_at, items, lanes):
    rows = []
    for k in range(6):
        parts = []
        for item, lane in zip(items, lanes):
            row = row_at(item >> (ITEM_BITS + CODE_BITS), k)
            parts.append(picked(jnp.broadcast_to(row, lane.shape), lane))
        rows.append(stacked(parts))
    return rows


def folded(total):
    return jnp.sum(total, axis=0, keepdims=True)


def geometry(items, unused, lanes, own_code, own_wide, period, all_ref):
    member = lanes[0].shape[1]
    lane = lax.broadcasted_iota(jnp.int32, (SUB, member), 1)
    lift = []
    shifts = []
    for item, idle, other in zip(items, unused, lanes):
        code = item >> ITEM_BITS
        itself = jnp.where(other == lane, jnp.where(code == own_code, 2.0 * cutoff_sq, 0.0), 0.0)
        lift.append(itself + jnp.where(idle, 2.0 * cutoff_sq, 0.0))
        shifts.append(offsets_of(code, period))
    rows = partner_rows(lambda tile, k: row_of(all_ref, tile, CENTRE + k, member), items, lanes)
    shift = [stacked([jnp.full((SUB, member), one[k]) for one in shifts]) for k in range(3)]
    d = [rows[k] + shift[k] - own_wide[k] for k in range(3)]
    uj = rows[3:]
    gradient, hessian, spin = pair_coefficients(d, own_wide[3:], uj, stacked(lift))
    return list(gradient) + list(hessian) + d + uj, (gradient[1], spin)


def apply(moved_rows, terms, own_wide, moved_wide):
    u_e, u_a, u_b, u_c, h_ee, h_ea, h_eb, h_ec, h_aa, h_ab, h_ac, h_bb, h_bc, h_cc = terms[:14]
    d = terms[14:17]
    uj = terms[17:20]
    ui = own_wide[3:]
    dui = moved_wide[3:]
    dd = [moved_rows[k] - moved_wide[k] for k in range(3)]
    duj = cross3(moved_rows[3:], uj)
    de = dot3(d, dd)
    da = dot3(dd, ui) + dot3(d, dui)
    db = dot3(dd, uj) + dot3(d, duj)
    dc = dot3(dui, uj) + dot3(ui, duj)
    du_e = h_ee * de + h_ea * da + h_eb * db + h_ec * dc
    du_a = h_ea * de + h_aa * da + h_ab * db + h_ac * dc
    du_b = h_eb * de + h_ab * da + h_bb * db + h_bc * dc
    du_c = h_ec * de + h_ac * da + h_bc * db + h_cc * dc
    force = [du_e * d[k] + u_e * dd[k] + du_b * uj[k] + u_b * duj[k] for k in range(3)]
    turn = [du_a * d[k] + u_a * dd[k] + du_c * uj[k] + u_c * duj[k] for k in range(3)]
    return force + turn + [du_a]


def group_items(step, item_ref, item_count):
    at = [step * GROUP + part for part in range(GROUP)]
    return [item_ref[1 + place] for place in at], [place >= item_count for place in at]


def added(totals, news):
    return tuple(
        total + sum(new[part * SUB : (part + 1) * SUB] for part in range(GROUP)) for total, new in zip(totals, news)
    )


def close(sums, kept, spin, u, t):
    force = [-(sums[k] + u[k] * sums[6] + t[k] * kept) for k in range(3)]
    return force + list(cross3(u, [sums[3 + k] - t[k] * spin for k in range(3)]))


def spread(rows, out_ref):
    member = rows[0].shape[1]
    for k, row in enumerate(rows):
        out_ref[:, :, k * member : (k + 1) * member] = jnp.broadcast_to(row[None], (out_ref.shape[0], 1, member))


def pack_kernel(*refs):
    sources, out_ref, targets, sems = refs[:4], refs[4], refs[5:9], refs[9]
    config_ref, start_ref, list_ref, count_ref = targets
    copies = [
        pltpu.make_async_copy(source, target, sems.at[at]) for at, (source, target) in enumerate(zip(sources, targets))
    ]
    for copy in copies:
        copy.start()
    copies[2].wait()
    copies[3].wait()
    member = config_ref.shape[1]
    lane = lax.broadcasted_iota(jnp.int32, (1, member), 1)
    fields, slots = list_ref.shape[1], list_ref.shape[3]
    line = jnp.full((1, member), -9, jnp.int32)
    for field in range(fields):
        for slot in range(slots):
            line = jnp.where(lane == field * slots + slot, list_ref[0, field, 0, slot], line)
    line = jnp.where((lane >= count_ref[0, 0]) & (lane < slots), -9, line).astype(jnp.float32)
    copies[0].wait()
    copies[1].wait()
    rows = [ref[k : k + 1, :] for ref in (start_ref, config_ref) for k in range(6)]
    spread(rows + [line], out_ref)


def first_kernel(
    rows,
    cols,
    slots,
    period,
    all_ref,
    out_ref,
    item_ref,
    coef_ref,
    kept_ref,
    entry_ref,
    code_ref,
    code_smem,
    sem,
):
    member = kept_ref.shape[1]
    row_id = lax.axis_index("row")
    col_id = lax.axis_index("col")
    own = row_id * cols + col_id
    blocks = member // SUB

    def field(line, at):
        return line if at == 0 else pltpu.roll(line, member - at * slots, 1)

    row_f = row_id.astype(jnp.float32)
    col_f = col_id.astype(jnp.float32)
    lines = [row_of(all_ref, row_id * cols + col, LIST_ROW, member) for col in range(cols)]
    lines += [row_of(all_ref, row * cols + col_id, LIST_ROW, member) for row in range(rows)]
    line = jnp.concatenate(lines, axis=0)
    at = lax.broadcasted_iota(jnp.int32, line.shape, 0).astype(jnp.float32)
    near = at < float(cols)
    other = field(line, 1)
    offset = field(line, 2) * 16.0 + field(line, 3) * 4.0 + field(line, 4)
    partner = jnp.where(near, other * float(cols) + at, (at - float(cols)) * float(cols) + line)
    code = partner * float(1 << CODE_BITS) + (jnp.where(near, offset, -offset) + 21.0)
    hit = jnp.where(near, line - col_f, jnp.where(line >= 0.0, other - row_f, 1.0)) == 0.0
    code_ref[...] = jnp.where(hit, code, -1.0).astype(jnp.int32)
    copy = pltpu.make_async_copy(code_ref, code_smem, sem)
    copy.start()
    own_code = own * (1 << CODE_BITS) + 21
    own_moved = [row_of(all_ref, own, k, member) for k in range(6)]
    own_frame = [row_of(all_ref, own, CENTRE + k, member) for k in range(6)]
    lanes = box_lanes(member)
    own_centre = [jnp.broadcast_to(line, lanes.shape) for line in own_frame[:3]]

    def append(code, bits, count):
        for block in range(blocks):
            item_ref[1 + count] = (code << ITEM_BITS) + block
            count = count + (bits >> block & 1)
        return count

    items = append(own_code, near_blocks(own_centre, own_frame[:3], lanes), jnp.int32(0))
    copy.wait()

    def gather(line, count):
        for slot in range(slots):
            code = code_smem[line, slot]
            entry_ref[count] = code
            count = count + (code >= 0).astype(jnp.int32)
        return count

    entries = lax.fori_loop(0, rows + cols, gather, jnp.int32(0))
    for part in range(TESTS):
        entry_ref[entries + part] = own_code

    def prepare(step, count):
        codes = [entry_ref[step * TESTS + part] for part in range(TESTS)]
        bits = [near_blocks(own_centre, centre_of(code, period, all_ref, member), lanes) for code in codes]
        for part in range(TESTS):
            count = append(codes[part], jnp.where(step * TESTS + part < entries, bits[part], 0), count)
        return count

    items = lax.fori_loop(0, (entries + TESTS - 1) // TESTS, prepare, items)
    for part in range(GROUP):
        item_ref[1 + items + part] = own_code << ITEM_BITS
    item_ref[0] = items

    held = coef_ref.shape[0] // (TERMS * GROUP * SUB)
    steps = (items + GROUP - 1) // GROUP
    u = own_frame[3:]
    t = cross3(own_moved[3:], u)
    own_wide = [wide(line) for line in own_frame]
    moved_wide = [wide(line) for line in [*own_moved[:3], *t]]

    def derive(step, totals):
        group, unused = group_items(step, item_ref, items)
        lanes = [lanes_of(item & ITEM_MASK, member) for item in group]
        terms, sums = geometry(group, unused, lanes, own_code, own_wide, period, all_ref)
        moved_rows = partner_rows(lambda tile, k: row_of(all_ref, tile, k, member), group, lanes)
        return terms, added(totals, apply(moved_rows, terms, own_wide, moved_wide) + list(sums))

    def keep(step, totals):
        terms, totals = derive(step, totals)
        start = pl.multiple_of(step * (TERMS * GROUP * SUB), SUB)
        for k in range(TERMS):
            coef_ref[pl.ds(start + k * GROUP * SUB, GROUP * SUB), :] = terms[k]
        return totals

    zero = jnp.zeros((SUB, member), jnp.float32)
    totals = lax.fori_loop(0, jnp.minimum(steps, held), keep, (zero,) * 9)
    totals = lax.fori_loop(held, steps, lambda step, before: derive(step, before)[1], totals)
    sums = [folded(total) for total in totals]
    kept_ref[...] = jnp.concatenate(sums[7:], axis=0)
    spread(close(sums, sums[7], sums[8], u, t), out_ref)


def scalar_of(block):
    return jnp.sum(jnp.sum(block, axis=0, keepdims=True), axis=1, keepdims=True)


def second_kernel(
    cols,
    total_entries,
    period,
    item_ref,
    coef_ref,
    kept_ref,
    all_ref,
    image_ref,
    out_ref,
    pair_ref,
    scalar_ref,
    second_ref,
):
    own = lax.axis_index("row") * cols + lax.axis_index("col")
    member = kept_ref.shape[1]
    basis = all_ref[:, 0, 0 : 6 * member]
    image = image_ref[:, 0, :]
    portion = 1.0 / total_entries

    def total_of(block):
        return scalar_of(sum(block[:, k * member : (k + 1) * member] for k in range(6)))

    norm_sq = total_of(basis * basis) * portion + norm_eps
    norm_inv = lax.rsqrt(norm_sq)
    alpha = total_of(basis * image) * portion / norm_sq
    second = image - alpha * basis
    second_ref[:, 0, :] = second
    beta_sq = total_of(second * second) * portion / norm_sq + norm_eps
    beta = jnp.sqrt(beta_sq)
    scale = norm_inv * lax.rsqrt(beta_sq)

    own_code = own * (1 << CODE_BITS) + 21
    items = item_ref[0]
    held = coef_ref.shape[0] // (TERMS * GROUP * SUB)
    steps = (items + GROUP - 1) // GROUP

    def moved_row(tile, k):
        return row_of(second_ref, tile, k, member)

    own_moved = [moved_row(own, k) for k in range(6)]
    own_frame = [row_of(all_ref, own, CENTRE + k, member) for k in range(6)]
    u = own_frame[3:]
    t = cross3(own_moved[3:], u)
    own_wide = [wide(line) for line in own_frame]
    moved_wide = [wide(line) for line in [*own_moved[:3], *t]]

    def visit(step, totals):
        group, _ = group_items(step, item_ref, items)
        lanes = [lanes_of(item & ITEM_MASK, member) for item in group]
        start = pl.multiple_of(step * (TERMS * GROUP * SUB), SUB)
        terms = [coef_ref[pl.ds(start + k * GROUP * SUB, GROUP * SUB), :] for k in range(TERMS)]
        return added(totals, apply(partner_rows(moved_row, group, lanes), terms, own_wide, moved_wide))

    def visit_again(step, totals):
        group, unused = group_items(step, item_ref, items)
        lanes = [lanes_of(item & ITEM_MASK, member) for item in group]
        terms, _ = geometry(group, unused, lanes, own_code, own_wide, period, all_ref)
        return added(totals, apply(partner_rows(moved_row, group, lanes), terms, own_wide, moved_wide))

    zero = jnp.zeros((SUB, member), jnp.float32)
    totals = lax.fori_loop(0, jnp.minimum(steps, held), visit, (zero,) * 7)
    totals = lax.fori_loop(held, steps, visit_again, totals)
    sums = [folded(total) for total in totals]
    product = close(sums, kept_ref[0:1, :], kept_ref[1:2, :], u, t)
    fill = [jnp.zeros((1, member), jnp.float32)] * (SUB - len(product))
    first = stacked([row_of(all_ref, own, k, member) for k in range(6)] + fill)
    image = stacked(product + fill) * scale - (beta * norm_inv) * first
    second = stacked(own_moved + fill) * scale
    inner = scalar_of(second * image)
    weight = scalar_of(second * second)
    local_alpha = jnp.where(weight > 1e-30, inner / jnp.maximum(weight, 1e-30), 0.0)
    rest = image - local_alpha * second
    size = scalar_of(rest * rest)
    slant = scalar_of(second * rest)
    lane = lax.broadcasted_iota(jnp.int32, (1, member), 1)
    line = jnp.zeros((1, member), jnp.float32)
    for at, value in enumerate((inner, weight, local_alpha, size, slant)):
        line = jnp.where(lane == at, value, line)
    out_ref[...] = jnp.broadcast_to(line[None], out_ref.shape)
    pair_ref[0] = second
    pair_ref[1] = image
    scalar_ref[...] = jnp.where(lane == 0, alpha, jnp.where(lane == 1, beta, 0.0))


def last_kernel(total_entries, pair_ref, scalar_ref, line_ref, mode_ref, coefficient_ref):
    lines = line_ref[:, 0, :]
    alpha = jnp.sum(lines[:, 0:1], axis=0, keepdims=True) / total_entries
    away = lines[:, 2:3] - alpha
    parts = lines[:, 3:4] + away * (away * lines[:, 1:2] + 2.0 * lines[:, 4:5])
    beta = jnp.sqrt(jnp.sum(parts, axis=0, keepdims=True) / total_entries + norm_eps)
    mode = (pair_ref[1] - alpha * pair_ref[0]) / beta
    mode_ref[...] = mode[: mode_ref.shape[0]]
    for at, value in enumerate((scalar_ref[0:1, 0:1], scalar_ref[0:1, 1:2], alpha, beta)):
        coefficient_ref[at] = jnp.sum(value)


def local(config, start, tile_list, tile_count):
    dof, member = config.shape
    row_devices = lax.axis_size("row")
    col_devices = lax.axis_size("col")
    devices = row_devices * col_devices
    total_entries = float(dof * member * devices)
    period = (5.0, 5.0, 3.5 * (member // 16))
    slots = tile_list.shape[2]
    longest = (row_devices + col_devices) * slots + 1

    def shaped(*shape):
        return jax.ShapeDtypeStruct(shape, jnp.float32)

    def everywhere(copies):
        return lax.all_to_all(copies, ("row", "col"), 0, 0, tiled=True)

    params = pltpu.CompilerParams(vmem_limit_bytes=VMEM_LIMIT)
    vmem = pl.BlockSpec(memory_space=pltpu.VMEM)
    smem = pl.BlockSpec(memory_space=pltpu.SMEM)

    outside = pl.BlockSpec(memory_space=pl.ANY)
    packed = pl.pallas_call(
        pack_kernel,
        out_shape=shaped(devices, 1, (LIST_ROW + 1) * member),
        in_specs=[outside] * 4,
        out_specs=vmem,
        scratch_shapes=[
            pltpu.VMEM((dof, member), jnp.float32),
            pltpu.VMEM((dof, member), jnp.float32),
            pltpu.SMEM((1, tile_list.shape[3], 1, slots), jnp.int32),
            pltpu.SMEM((1, 1), jnp.int32),
            pltpu.SemaphoreType.DMA((4,)),
        ],
        compiler_params=pltpu.CompilerParams(vmem_limit_bytes=PACK_LIMIT),
    )(config, start, jnp.transpose(tile_list, (0, 3, 1, 2)), tile_count)
    together = everywhere(packed)

    held_rows = HELD // GROUP * (TERMS * GROUP * SUB)
    image, items, terms, kept = pl.pallas_call(
        functools.partial(first_kernel, row_devices, col_devices, slots, period),
        out_shape=(
            shaped(devices, 1, dof * member),
            jax.ShapeDtypeStruct((1 + longest * (member // SUB) + GROUP,), jnp.int32),
            shaped(held_rows, member),
            shaped(2, member),
        ),
        in_specs=[vmem],
        out_specs=(vmem, smem, vmem, vmem),
        scratch_shapes=[
            pltpu.SMEM((longest + TESTS,), jnp.int32),
            pltpu.VMEM((row_devices + col_devices, member), jnp.int32),
            pltpu.SMEM((row_devices + col_devices, member), jnp.int32),
            pltpu.SemaphoreType.DMA,
        ],
        compiler_params=params,
    )(together)
    image = everywhere(image)

    line, pair, scalars = pl.pallas_call(
        functools.partial(second_kernel, col_devices, total_entries, period),
        out_shape=(shaped(devices, 1, member), shaped(2, SUB, member), shaped(1, member)),
        in_specs=[smem] + [vmem] * 4,
        out_specs=(vmem, vmem, vmem),
        scratch_shapes=[
            pltpu.VMEM((devices, 1, dof * member), jnp.float32),
        ],
        compiler_params=params,
    )(items, terms, kept, together, image)
    line = everywhere(line)

    mode, coefficients = pl.pallas_call(
        functools.partial(last_kernel, total_entries),
        out_shape=(shaped(dof, member), shaped(4)),
        in_specs=[vmem] * 3,
        out_specs=(vmem, smem),
        compiler_params=params,
    )(pair, scalars, line)
    return (coefficients, mode)


def solution(mesh):
    placed = (
        P(None, ("row", "col")),
        P(None, ("row", "col")),
        P("row", "col", None, None),
        P("row", "col"),
    )
    return jax.shard_map(
        local, mesh=mesh, in_specs=placed, out_specs=(P(), P(None, ("row", "col"))), check_vma=False
    )
```

```python
import functools
import math

import jax
import jax.numpy as jnp
from jax import lax
from jax.experimental import pallas as pl
from jax.experimental.pallas import tpu as pltpu
from jax.sharding import PartitionSpec as P

chi_shape = 0.8
chi_energy = (math.sqrt(5.0) - 1.0) / (math.sqrt(5.0) + 1.0)
well_depth = 0.005
cutoff_sq = 20.25
norm_eps = 1e-06

SUB = 8
CENTRE = 6
LIST_ROW = 12
CODE_BITS = 6
ITEM_BITS = 8
BLOCK_BITS = 16
ITEM_MASK = 255
LAYER = 16
TESTS = 5
GROUP = 4
TERMS = 20
HELD = 128
VMEM_LIMIT = 32 * 1024 * 1024
PACK_LIMIT = 60 * 1024 * 1024


def dot3(a, b):
    return a[0] * b[0] + a[1] * b[1] + a[2] * b[2]


def cross3(a, b):
    return (
        a[1] * b[2] - a[2] * b[1],
        a[2] * b[0] - a[0] * b[2],
        a[0] * b[1] - a[1] * b[0],
    )


def inverse(value):
    guess = pl.reciprocal(value, approx=True)
    return guess * (2.0 - value * guess)


def bracket(chi, scaled, factor, p, a, b):
    f = factor * (a - scaled * b)
    g = factor * (b - scaled * a)
    y = p * (a * f + b * g)
    cross = factor * scaled
    f_c = chi * (cross * f - factor * g)
    g_c = chi * (cross * g - factor * f)
    return f, g, y, cross, f_c, g_c


def pair_coefficients(d, ui, uj, lift):
    r_sq = dot3(d, d) + lift
    a = dot3(d, ui)
    b = dot3(d, uj)
    c = dot3(ui, uj)
    r_inv = lax.rsqrt(r_sq)
    p = r_inv * r_inv
    p2 = 2.0 * p
    r = r_sq * r_inv
    x = jnp.maximum(1.0 - r_sq * (1.0 / cutoff_sq), 0.0)
    c_shape = chi_shape * c
    c_energy = chi_energy * c
    e1 = lax.rsqrt(1.0 - c_shape * c_shape)
    q = e1 * e1
    q2 = inverse(1.0 - c_energy * c_energy)
    f, g, y, m, f_c, g_c = bracket(chi_shape, c_shape, q, p, a, b)
    f2, g2, y2, m2, f2_c, g2_c = bracket(chi_energy, c_energy, q2, p, a, b)
    sigma = lax.rsqrt(1.0 - chi_shape * y)
    sigma_sq = sigma * sigma
    psi = 1.0 - chi_energy * y2
    s = inverse(r - sigma + 1.0)
    s_sq = s * s
    s6 = s_sq * s_sq * s_sq
    t0 = s6 * (s6 - 1.0)
    t1 = s6 * s * (6.0 - 12.0 * s6)
    t2 = s6 * s_sq * (156.0 * s6 - 42.0)
    ke = (4.0 * well_depth) * e1
    kx = ke * x
    v_ee = kx * (24.0 / cutoff_sq**2)
    kxx = kx * x
    v_e = kxx * (-6.0 / cutoff_sq)
    v = kxx * x
    psi_sq = psi * psi
    psi_sq_t0 = psi_sq * t0
    psi_sq_t1 = psi_sq * t1
    u = v * psi_sq_t0
    slope = v * psi_sq_t1
    slope2 = v * psi_sq * t2
    tau = (-0.5 * chi_shape) * sigma_sq * sigma
    push = (-2.0 * chi_energy) * psi
    v_t1 = v * t1
    d1 = slope * tau
    d2 = push * (v * t0)
    h1 = p2 * d1
    h2 = p2 * d2
    kc = chi_shape * c_shape * q
    fg = chi_shape * f * g
    fg2 = chi_energy * f2 * g2
    u_a = h1 * f + h2 * f2
    u_b = h1 * g + h2 * g2
    u_fg = h1 * fg + h2 * fg2
    u_c = u * kc - u_fg
    v_e_t0 = v_e * psi_sq_t0
    d_e = r_inv * slope + v_e_t0
    u_e = d_e - (h1 * y + h2 * y2)

    p2_sq = p2 * p2
    k11 = p2_sq * (tau * (slope2 * tau + (1.5 * chi_shape) * sigma_sq * slope))
    k12 = p2_sq * (push * v_t1 * tau)
    k22 = p2_sq * ((2.0 * chi_energy * chi_energy) * (v * t0))
    steep = v_e * psi_sq_t1 + slope2 * r_inv
    l1 = p2 * (steep * tau - h1)
    l2 = p2 * (push * (v_e * t0 + v_t1 * r_inv) - h2)
    j1 = (y, f, g, fg)
    j2 = (y2, f2, g2, fg2)
    w1 = [k11 * one + k12 * two for one, two in zip(j1, j2)]
    w2 = [k12 * one + k22 * two for one, two in zip(j1, j2)]

    def quadratic(m_at, n_at):
        return w1[m_at] * j1[n_at] + w2[m_at] * j2[n_at]

    d_ee = v_ee * psi_sq_t0 + r_inv * (2.0 * (v_e * psi_sq_t1)) + p * (slope2 - slope * r_inv)
    h_ee = quadratic(0, 0) - 2.0 * (l1 * y + l2 * y2) + d_ee
    h_ea = l1 * f + l2 * f2 - quadratic(0, 1)
    h_eb = l1 * g + l2 * g2 - quadratic(0, 2)
    h_ec = quadratic(0, 3) - (l1 * fg + l2 * fg2) + kc * u_e
    straight = h1 * q + h2 * q2
    h_aa = quadratic(1, 1) + straight
    h_ab = quadratic(1, 2) - (h1 * m + h2 * m2)
    h_ac = kc * u_a - quadratic(1, 3) + (h1 * f_c + h2 * f2_c)
    h_bb = quadratic(2, 2) + straight
    h_bc = kc * u_b - quadratic(2, 3) + (h1 * g_c + h2 * g2_c)
    bent = (chi_shape * h1) * (f_c * g + f * g_c) + (chi_energy * h2) * (f2_c * g2 + f2 * g2_c)
    twist = kc * kc + (chi_shape * chi_shape) * q * (2.0 * q - 1.0)
    h_cc = quadratic(3, 3) - bent - 2.0 * (kc * u_fg) + u * twist
    gradient = (u_e, u_a, u_b, u_c)
    return gradient, (h_ee, h_ea, h_eb, h_ec, h_aa, h_ab, h_ac, h_bb, h_bc, h_cc), u_a * a + u_c * c


def offsets_of(code, period):
    return [((code >> bits & 3) - 1).astype(jnp.float32) * size for bits, size in zip((4, 2, 0), period)]


def row_of(tiles_ref, tile, k, member):
    return tiles_ref[tile, :, k * member : (k + 1) * member]


def centre_of(code, period, all_ref, member):
    shift = offsets_of(code, period)
    return [row_of(all_ref, code >> CODE_BITS, CENTRE + k, member) + shift[k] for k in range(3)]


def lanes_of(block, member):
    row = lax.broadcasted_iota(jnp.int32, (SUB, member), 0)
    lane = lax.broadcasted_iota(jnp.int32, (SUB, member), 1)
    group = (lane & -LAYER) - (block >> 1) * LAYER
    return (group & (member - 1)) + ((block & 1) * SUB + row)


def picked(block, lanes):
    return jnp.take_along_axis(block, lanes, axis=1, mode="promise_in_bounds")


def box_lanes(member):
    block = lax.broadcasted_iota(jnp.int32, (member // SUB, member), 0)
    lane = lax.broadcasted_iota(jnp.int32, (member // SUB, member), 1)
    return (((lane & -LAYER) - (block >> 1) * LAYER) & (member - 1)) + (block & 1) * SUB


def near_blocks(own_centre, partner, lanes):
    blocks, member = lanes.shape
    zero = jnp.zeros((1, member), jnp.float32)
    box = stacked(partner + [-line for line in partner] + [zero, zero])
    for bit in (1, 2, 4):
        box = jnp.maximum(box, pltpu.roll(box, member - bit, 1))

    def seen(k):
        line = jnp.broadcast_to(box[k : k + 1], (SUB, member))
        return stacked([picked(line, lanes[at : at + SUB]) for at in range(0, blocks, SUB)])

    reach = 0.0
    for k in range(3):
        above = own_centre[k] - seen(k)
        below = -own_centre[k] - seen(3 + k)
        gap = jnp.maximum(jnp.maximum(above, below), 0.0)
        reach = reach + gap * gap
    nearest = jnp.min(reach, axis=1, keepdims=True)
    weight = (1 << lax.broadcasted_iota(jnp.int32, (blocks, 1), 0)).astype(jnp.float32)
    return jnp.sum(jnp.where(nearest < cutoff_sq * 1.001, weight, 0.0)).astype(jnp.int32)


def stacked(parts):
    return jnp.concatenate(parts, axis=0)


def wide(row):
    return jnp.broadcast_to(row, (GROUP * SUB, row.shape[1]))


def partner_rows(row_at, items, lanes):
    rows = []
    for k in range(6):
        parts = []
        for item, lane in zip(items, lanes):
            row = row_at(item >> (ITEM_BITS + CODE_BITS), k)
            parts.append(picked(jnp.broadcast_to(row, lane.shape), lane))
        rows.append(stacked(parts))
    return rows


def folded(total):
    return jnp.sum(total, axis=0, keepdims=True)


def geometry(items, unused, lanes, own_code, own_wide, period, all_ref):
    member = lanes[0].shape[1]
    lane = lax.broadcasted_iota(jnp.int32, (SUB, member), 1)
    lift = []
    shifts = []
    for item, idle, other in zip(items, unused, lanes):
        code = item >> ITEM_BITS
        itself = jnp.where(other == lane, jnp.where(code == own_code, 2.0 * cutoff_sq, 0.0), 0.0)
        lift.append(itself + jnp.where(idle, 2.0 * cutoff_sq, 0.0))
        shifts.append(offsets_of(code, period))
    rows = partner_rows(lambda tile, k: row_of(all_ref, tile, CENTRE + k, member), items, lanes)
    shift = [stacked([jnp.full((SUB, member), one[k]) for one in shifts]) for k in range(3)]
    d = [rows[k] + shift[k] - own_wide[k] for k in range(3)]
    uj = rows[3:]
    gradient, hessian, spin = pair_coefficients(d, own_wide[3:], uj, stacked(lift))
    return list(gradient) + list(hessian) + d + uj, (gradient[1], spin)


def apply(moved_rows, terms, own_wide, moved_wide):
    u_e, u_a, u_b, u_c, h_ee, h_ea, h_eb, h_ec, h_aa, h_ab, h_ac, h_bb, h_bc, h_cc = terms[:14]
    d = terms[14:17]
    uj = terms[17:20]
    ui = own_wide[3:]
    dui = moved_wide[3:]
    dd = [moved_rows[k] - moved_wide[k] for k in range(3)]
    duj = cross3(moved_rows[3:], uj)
    de = dot3(d, dd)
    da = dot3(dd, ui) + dot3(d, dui)
    db = dot3(dd, uj) + dot3(d, duj)
    dc = dot3(dui, uj) + dot3(ui, duj)
    du_e = h_ee * de + h_ea * da + h_eb * db + h_ec * dc
    du_a = h_ea * de + h_aa * da + h_ab * db + h_ac * dc
    du_b = h_eb * de + h_ab * da + h_bb * db + h_bc * dc
    du_c = h_ec * de + h_ac * da + h_bc * db + h_cc * dc
    force = [du_e * d[k] + u_e * dd[k] + du_b * uj[k] + u_b * duj[k] for k in range(3)]
    turn = [du_a * d[k] + u_a * dd[k] + du_c * uj[k] + u_c * duj[k] for k in range(3)]
    return force + turn + [du_a]


def append(item_ref, code, bits, count, blocks):
    for block in range(blocks):
        item_ref[count] = (code << ITEM_BITS) + block
        count = count + (bits >> block & 1)
    return count


def group_items(step, item_ref, item_count):
    at = [step * GROUP + part for part in range(GROUP)]
    return [item_ref[place] for place in at], [place >= item_count for place in at]


def added(totals, news):
    return tuple(
        total + sum(new[part * SUB : (part + 1) * SUB] for part in range(GROUP)) for total, new in zip(totals, news)
    )


def close(sums, kept, spin, u, t):
    force = [-(sums[k] + u[k] * sums[6] + t[k] * kept) for k in range(3)]
    return force + list(cross3(u, [sums[3 + k] - t[k] * spin for k in range(3)]))


def spread(rows, out_ref):
    member = rows[0].shape[1]
    for k, row in enumerate(rows):
        out_ref[:, :, k * member : (k + 1) * member] = jnp.broadcast_to(row[None], (out_ref.shape[0], 1, member))


def pack_kernel(*refs):
    sources, out_ref, targets, sems = refs[:4], refs[4], refs[5:9], refs[9]
    config_ref, start_ref, list_ref, count_ref = targets
    copies = [
        pltpu.make_async_copy(source, target, sems.at[at]) for at, (source, target) in enumerate(zip(sources, targets))
    ]
    for copy in copies:
        copy.start()
    copies[2].wait()
    copies[3].wait()
    member = config_ref.shape[1]
    lane = lax.broadcasted_iota(jnp.int32, (1, member), 1)
    fields, slots = list_ref.shape[1], list_ref.shape[3]
    line = jnp.full((1, member), -9, jnp.int32)
    for field in range(fields):
        for slot in range(slots):
            line = jnp.where(lane == field * slots + slot, list_ref[0, field, 0, slot], line)
    line = jnp.where((lane >= count_ref[0, 0]) & (lane < slots), -9, line).astype(jnp.float32)
    copies[0].wait()
    copies[1].wait()
    rows = [ref[k : k + 1, :] for ref in (start_ref, config_ref) for k in range(6)]
    spread(rows + [line], out_ref)


def first_kernel(
    rows,
    cols,
    slots,
    period,
    all_ref,
    out_ref,
    entry_ref,
    coef_ref,
    kept_ref,
    item_ref,
    code_ref,
    code_smem,
    sem,
):
    member = kept_ref.shape[1]
    row_id = lax.axis_index("row")
    col_id = lax.axis_index("col")
    own = row_id * cols + col_id
    blocks = member // SUB

    def field(line, at):
        return line if at == 0 else pltpu.roll(line, member - at * slots, 1)

    row_f = row_id.astype(jnp.float32)
    col_f = col_id.astype(jnp.float32)
    lines = [row_of(all_ref, row_id * cols + col, LIST_ROW, member) for col in range(cols)]
    lines += [row_of(all_ref, row * cols + col_id, LIST_ROW, member) for row in range(rows)]
    line = jnp.concatenate(lines, axis=0)
    at = lax.broadcasted_iota(jnp.int32, line.shape, 0).astype(jnp.float32)
    near = at < float(cols)
    other = field(line, 1)
    offset = field(line, 2) * 16.0 + field(line, 3) * 4.0 + field(line, 4)
    partner = jnp.where(near, other * float(cols) + at, (at - float(cols)) * float(cols) + line)
    code = partner * float(1 << CODE_BITS) + (jnp.where(near, offset, -offset) + 21.0)
    hit = jnp.where(near, line - col_f, jnp.where(line >= 0.0, other - row_f, 1.0)) == 0.0
    found = jnp.where(hit, code + 1.0, 0.0)
    found = jnp.where(lax.broadcasted_iota(jnp.int32, found.shape, 1) < slots, found, 0.0)
    held_lines = member // slots
    for group in range(code_ref.shape[0]):
        packed = -1.0
        for at in range(group * held_lines, min((group + 1) * held_lines, rows + cols)):
            part = found[at : at + 1]
            by = (at - group * held_lines) * slots
            packed = packed + (pltpu.roll(part, by, 1) if by else part)
        code_ref[group : group + 1, :] = packed.astype(jnp.int32)
    copy = pltpu.make_async_copy(code_ref, code_smem, sem)
    copy.start()
    own_code = own * (1 << CODE_BITS) + 21
    own_moved = [row_of(all_ref, own, k, member) for k in range(6)]
    own_frame = [row_of(all_ref, own, CENTRE + k, member) for k in range(6)]
    lanes = box_lanes(member)
    own_centre = [jnp.broadcast_to(line, lanes.shape) for line in own_frame[:3]]

    own_bits = near_blocks(own_centre, own_frame[:3], lanes)
    entry_ref[1] = (own_code << BLOCK_BITS) + own_bits
    items = append(item_ref, own_code, own_bits, jnp.int32(0), blocks)
    copy.wait()

    def gather(group, at, count):
        for slot in range(slots):
            code = code_smem[group, at * slots + slot]
            entry_ref[2 + count] = code
            count = count + (code >= 0).astype(jnp.int32)
        return count

    entries = jnp.int32(0)
    for group in range(code_ref.shape[0]):
        some = min(held_lines, rows + cols - group * held_lines)
        entries = lax.fori_loop(0, some, functools.partial(gather, group), entries)
    for part in range(TESTS):
        entry_ref[2 + entries + part] = own_code

    def prepare(step, count):
        codes = [entry_ref[2 + step * TESTS + part] for part in range(TESTS)]
        bits = [near_blocks(own_centre, centre_of(code, period, all_ref, member), lanes) for code in codes]
        for part in range(TESTS):
            some = jnp.where(step * TESTS + part < entries, bits[part], 0)
            entry_ref[2 + step * TESTS + part] = (codes[part] << BLOCK_BITS) + some
            count = append(item_ref, codes[part], some, count, blocks)
        return count

    items = lax.fori_loop(0, (entries + TESTS - 1) // TESTS, prepare, items)
    entry_ref[0] = entries + 1
    for part in range(GROUP):
        item_ref[items + part] = own_code << ITEM_BITS

    held = coef_ref.shape[0] // (TERMS * GROUP * SUB)
    steps = (items + GROUP - 1) // GROUP
    u = own_frame[3:]
    t = cross3(own_moved[3:], u)
    own_wide = [wide(line) for line in own_frame]
    moved_wide = [wide(line) for line in [*own_moved[:3], *t]]

    def derive(step, totals):
        group, unused = group_items(step, item_ref, items)
        lanes = [lanes_of(item & ITEM_MASK, member) for item in group]
        terms, sums = geometry(group, unused, lanes, own_code, own_wide, period, all_ref)
        moved_rows = partner_rows(lambda tile, k: row_of(all_ref, tile, k, member), group, lanes)
        return terms, added(totals, apply(moved_rows, terms, own_wide, moved_wide) + list(sums))

    def keep(step, totals):
        terms, totals = derive(step, totals)
        start = pl.multiple_of(step * (TERMS * GROUP * SUB), SUB)
        for k in range(TERMS):
            coef_ref[pl.ds(start + k * GROUP * SUB, GROUP * SUB), :] = terms[k]
        return totals

    zero = jnp.zeros((SUB, member), jnp.float32)
    totals = lax.fori_loop(0, jnp.minimum(steps, held), keep, (zero,) * 9)
    totals = lax.fori_loop(held, steps, lambda step, before: derive(step, before)[1], totals)
    sums = [folded(total) for total in totals]
    kept_ref[...] = jnp.concatenate(sums[7:], axis=0)
    spread(close(sums, sums[7], sums[8], u, t), out_ref)


def scalar_of(block):
    return jnp.sum(jnp.sum(block, axis=0, keepdims=True), axis=1, keepdims=True)


def second_kernel(
    cols,
    total_entries,
    period,
    entry_ref,
    coef_ref,
    kept_ref,
    all_ref,
    image_ref,
    out_ref,
    pair_ref,
    scalar_ref,
    second_ref,
    item_ref,
):
    own = lax.axis_index("row") * cols + lax.axis_index("col")
    member = kept_ref.shape[1]
    basis = all_ref[:, 0, 0 : 6 * member]
    image = image_ref[:, 0, :]
    portion = 1.0 / total_entries

    def total_of(block):
        return scalar_of(sum(block[:, k * member : (k + 1) * member] for k in range(6)))

    norm_sq = total_of(basis * basis) * portion + norm_eps
    norm_inv = lax.rsqrt(norm_sq)
    alpha = total_of(basis * image) * portion / norm_sq
    second = image - alpha * basis
    second_ref[:, 0, :] = second
    beta_sq = total_of(second * second) * portion / norm_sq + norm_eps
    beta = jnp.sqrt(beta_sq)
    scale = norm_inv * lax.rsqrt(beta_sq)

    own_code = own * (1 << CODE_BITS) + 21
    blocks = member // SUB

    def relist(entry, count):
        word = entry_ref[1 + entry]
        return append(item_ref, word >> BLOCK_BITS, word & ((1 << BLOCK_BITS) - 1), count, blocks)

    items = lax.fori_loop(0, entry_ref[0], relist, jnp.int32(0))
    for part in range(GROUP):
        item_ref[items + part] = own_code << ITEM_BITS
    held = coef_ref.shape[0] // (TERMS * GROUP * SUB)
    steps = (items + GROUP - 1) // GROUP

    def moved_row(tile, k):
        return row_of(second_ref, tile, k, member)

    own_moved = [moved_row(own, k) for k in range(6)]
    own_frame = [row_of(all_ref, own, CENTRE + k, member) for k in range(6)]
    u = own_frame[3:]
    t = cross3(own_moved[3:], u)
    own_wide = [wide(line) for line in own_frame]
    moved_wide = [wide(line) for line in [*own_moved[:3], *t]]

    def visit(step, totals):
        group, _ = group_items(step, item_ref, items)
        lanes = [lanes_of(item & ITEM_MASK, member) for item in group]
        start = pl.multiple_of(step * (TERMS * GROUP * SUB), SUB)
        terms = [coef_ref[pl.ds(start + k * GROUP * SUB, GROUP * SUB), :] for k in range(TERMS)]
        return added(totals, apply(partner_rows(moved_row, group, lanes), terms, own_wide, moved_wide))

    def visit_again(step, totals):
        group, unused = group_items(step, item_ref, items)
        lanes = [lanes_of(item & ITEM_MASK, member) for item in group]
        terms, _ = geometry(group, unused, lanes, own_code, own_wide, period, all_ref)
        return added(totals, apply(partner_rows(moved_row, group, lanes), terms, own_wide, moved_wide))

    zero = jnp.zeros((SUB, member), jnp.float32)
    totals = lax.fori_loop(0, jnp.minimum(steps, held), visit, (zero,) * 7)
    totals = lax.fori_loop(held, steps, visit_again, totals)
    sums = [folded(total) for total in totals]
    product = close(sums, kept_ref[0:1, :], kept_ref[1:2, :], u, t)
    fill = [jnp.zeros((1, member), jnp.float32)] * (SUB - len(product))
    first = stacked([row_of(all_ref, own, k, member) for k in range(6)] + fill)
    image = stacked(product + fill) * scale - (beta * norm_inv) * first
    second = stacked(own_moved + fill) * scale
    inner = scalar_of(second * image)
    weight = scalar_of(second * second)
    local_alpha = jnp.where(weight > 1e-30, inner / jnp.maximum(weight, 1e-30), 0.0)
    rest = image - local_alpha * second
    size = scalar_of(rest * rest)
    slant = scalar_of(second * rest)
    lane = lax.broadcasted_iota(jnp.int32, (1, member), 1)
    line = jnp.zeros((1, member), jnp.float32)
    for at, value in enumerate((inner, weight, local_alpha, size, slant)):
        line = jnp.where(lane == at, value, line)
    out_ref[...] = jnp.broadcast_to(line[None], out_ref.shape)
    pair_ref[0] = second
    pair_ref[1] = image
    scalar_ref[...] = jnp.where(lane == 0, alpha, jnp.where(lane == 1, beta, 0.0))


def last_kernel(total_entries, pair_ref, scalar_ref, line_ref, mode_ref, coefficient_ref):
    lines = line_ref[:, 0, :]
    alpha = jnp.sum(lines[:, 0:1], axis=0, keepdims=True) / total_entries
    away = lines[:, 2:3] - alpha
    parts = lines[:, 3:4] + away * (away * lines[:, 1:2] + 2.0 * lines[:, 4:5])
    beta = jnp.sqrt(jnp.sum(parts, axis=0, keepdims=True) / total_entries + norm_eps)
    mode = (pair_ref[1] - alpha * pair_ref[0]) / beta
    mode_ref[...] = mode[: mode_ref.shape[0]]
    for at, value in enumerate((scalar_ref[0:1, 0:1], scalar_ref[0:1, 1:2], alpha, beta)):
        coefficient_ref[at] = jnp.sum(value)


def local(config, start, tile_list, tile_count):
    dof, member = config.shape
    row_devices = lax.axis_size("row")
    col_devices = lax.axis_size("col")
    devices = row_devices * col_devices
    total_entries = float(dof * member * devices)
    period = (5.0, 5.0, 3.5 * (member // 16))
    slots = tile_list.shape[2]
    longest = (row_devices + col_devices) * slots + 1

    def shaped(*shape):
        return jax.ShapeDtypeStruct(shape, jnp.float32)

    def everywhere(copies):
        return lax.all_to_all(copies, ("row", "col"), 0, 0, tiled=True)

    params = pltpu.CompilerParams(vmem_limit_bytes=VMEM_LIMIT)
    vmem = pl.BlockSpec(memory_space=pltpu.VMEM)
    smem = pl.BlockSpec(memory_space=pltpu.SMEM)

    outside = pl.BlockSpec(memory_space=pl.ANY)
    packed = pl.pallas_call(
        pack_kernel,
        out_shape=shaped(devices, 1, (LIST_ROW + 1) * member),
        in_specs=[outside] * 4,
        out_specs=vmem,
        scratch_shapes=[
            pltpu.VMEM((dof, member), jnp.float32),
            pltpu.VMEM((dof, member), jnp.float32),
            pltpu.SMEM((1, tile_list.shape[3], 1, slots), jnp.int32),
            pltpu.SMEM((1, 1), jnp.int32),
            pltpu.SemaphoreType.DMA((4,)),
        ],
        compiler_params=pltpu.CompilerParams(vmem_limit_bytes=PACK_LIMIT),
    )(config, start, jnp.transpose(tile_list, (0, 3, 1, 2)), tile_count)
    together = everywhere(packed)

    item_list = pltpu.SMEM((longest * (member // SUB) + GROUP,), jnp.int32)
    code_rows = -(-(row_devices + col_devices) * slots // member)
    held_rows = HELD // GROUP * (TERMS * GROUP * SUB)
    image, entries, terms, kept = pl.pallas_call(
        functools.partial(first_kernel, row_devices, col_devices, slots, period),
        out_shape=(
            shaped(devices, 1, dof * member),
            jax.ShapeDtypeStruct((1 + longest + TESTS,), jnp.int32),
            shaped(held_rows, member),
            shaped(2, member),
        ),
        in_specs=[vmem],
        out_specs=(vmem, smem, vmem, vmem),
        scratch_shapes=[
            item_list,
            pltpu.VMEM((code_rows, member), jnp.int32),
            pltpu.SMEM((code_rows, member), jnp.int32),
            pltpu.SemaphoreType.DMA,
        ],
        compiler_params=params,
    )(together)
    image = everywhere(image)

    line, pair, scalars = pl.pallas_call(
        functools.partial(second_kernel, col_devices, total_entries, period),
        out_shape=(shaped(devices, 1, member), shaped(2, SUB, member), shaped(1, member)),
        in_specs=[smem] + [vmem] * 4,
        out_specs=(vmem, vmem, vmem),
        scratch_shapes=[
            pltpu.VMEM((devices, 1, dof * member), jnp.float32),
            item_list,
        ],
        compiler_params=params,
    )(entries, terms, kept, together, image)
    line = everywhere(line)

    mode, coefficients = pl.pallas_call(
        functools.partial(last_kernel, total_entries),
        out_shape=(shaped(dof, member), shaped(4)),
        in_specs=[vmem] * 3,
        out_specs=(vmem, smem),
        compiler_params=params,
    )(pair, scalars, line)
    return (coefficients, mode)


def solution(mesh):
    placed = (
        P(None, ("row", "col")),
        P(None, ("row", "col")),
        P("row", "col", None, None),
        P("row", "col"),
    )
    return jax.shard_map(
        local, mesh=mesh, in_specs=placed, out_specs=(P(), P(None, ("row", "col"))), check_vma=False
    )
```

```python
import functools
import math

import jax
import jax.numpy as jnp
from jax import lax
from jax.experimental import pallas as pl
from jax.experimental.pallas import tpu as pltpu
from jax.sharding import PartitionSpec as P

chi_shape = 0.8
chi_energy = (math.sqrt(5.0) - 1.0) / (math.sqrt(5.0) + 1.0)
well_depth = 0.005
cutoff_sq = 20.25
norm_eps = 1e-06

SUB = 8
CENTRE = 6
LIST_ROW = 12
CODE_BITS = 6
ITEM_BITS = 8
ITEM_MASK = 255
LAYER = 16
TESTS = 5
GROUP = 4
TERMS = 20
HELD = 128
VMEM_LIMIT = 32 * 1024 * 1024
PACK_LIMIT = 60 * 1024 * 1024


def dot3(a, b):
    return a[0] * b[0] + a[1] * b[1] + a[2] * b[2]


def cross3(a, b):
    return (
        a[1] * b[2] - a[2] * b[1],
        a[2] * b[0] - a[0] * b[2],
        a[0] * b[1] - a[1] * b[0],
    )


def inverse(value):
    guess = pl.reciprocal(value, approx=True)
    return guess * (2.0 - value * guess)


def bracket(chi, scaled, factor, p, a, b):
    f = factor * (a - scaled * b)
    g = factor * (b - scaled * a)
    y = p * (a * f + b * g)
    cross = factor * scaled
    f_c = chi * (cross * f - factor * g)
    g_c = chi * (cross * g - factor * f)
    return f, g, y, cross, f_c, g_c


def pair_coefficients(d, ui, uj, lift):
    r_sq = dot3(d, d) + lift
    a = dot3(d, ui)
    b = dot3(d, uj)
    c = dot3(ui, uj)
    r_inv = lax.rsqrt(r_sq)
    p = r_inv * r_inv
    p2 = 2.0 * p
    r = r_sq * r_inv
    x = jnp.maximum(1.0 - r_sq * (1.0 / cutoff_sq), 0.0)
    c_shape = chi_shape * c
    c_energy = chi_energy * c
    e1 = lax.rsqrt(1.0 - c_shape * c_shape)
    q = e1 * e1
    q2 = inverse(1.0 - c_energy * c_energy)
    f, g, y, m, f_c, g_c = bracket(chi_shape, c_shape, q, p, a, b)
    f2, g2, y2, m2, f2_c, g2_c = bracket(chi_energy, c_energy, q2, p, a, b)
    sigma = lax.rsqrt(1.0 - chi_shape * y)
    sigma_sq = sigma * sigma
    psi = 1.0 - chi_energy * y2
    s = inverse(r - sigma + 1.0)
    s_sq = s * s
    s6 = s_sq * s_sq * s_sq
    t0 = s6 * (s6 - 1.0)
    t1 = s6 * s * (6.0 - 12.0 * s6)
    t2 = s6 * s_sq * (156.0 * s6 - 42.0)
    ke = (4.0 * well_depth) * e1
    kx = ke * x
    v_ee = kx * (24.0 / cutoff_sq**2)
    kxx = kx * x
    v_e = kxx * (-6.0 / cutoff_sq)
    v = kxx * x
    psi_sq = psi * psi
    psi_sq_t0 = psi_sq * t0
    psi_sq_t1 = psi_sq * t1
    u = v * psi_sq_t0
    slope = v * psi_sq_t1
    slope2 = v * psi_sq * t2
    tau = (-0.5 * chi_shape) * sigma_sq * sigma
    push = (-2.0 * chi_energy) * psi
    v_t1 = v * t1
    d1 = slope * tau
    d2 = push * (v * t0)
    h1 = p2 * d1
    h2 = p2 * d2
    kc = chi_shape * c_shape * q
    fg = chi_shape * f * g
    fg2 = chi_energy * f2 * g2
    u_a = h1 * f + h2 * f2
    u_b = h1 * g + h2 * g2
    u_fg = h1 * fg + h2 * fg2
    u_c = u * kc - u_fg
    v_e_t0 = v_e * psi_sq_t0
    d_e = r_inv * slope + v_e_t0
    u_e = d_e - (h1 * y + h2 * y2)

    p2_sq = p2 * p2
    k11 = p2_sq * (tau * (slope2 * tau + (1.5 * chi_shape) * sigma_sq * slope))
    k12 = p2_sq * (push * v_t1 * tau)
    k22 = p2_sq * ((2.0 * chi_energy * chi_energy) * (v * t0))
    steep = v_e * psi_sq_t1 + slope2 * r_inv
    l1 = p2 * (steep * tau - h1)
    l2 = p2 * (push * (v_e * t0 + v_t1 * r_inv) - h2)
    j1 = (y, f, g, fg)
    j2 = (y2, f2, g2, fg2)
    w1 = [k11 * one + k12 * two for one, two in zip(j1, j2)]
    w2 = [k12 * one + k22 * two for one, two in zip(j1, j2)]

    def quadratic(m_at, n_at):
        return w1[m_at] * j1[n_at] + w2[m_at] * j2[n_at]

    d_ee = v_ee * psi_sq_t0 + r_inv * (2.0 * (v_e * psi_sq_t1)) + p * (slope2 - slope * r_inv)
    h_ee = quadratic(0, 0) - 2.0 * (l1 * y + l2 * y2) + d_ee
    h_ea = l1 * f + l2 * f2 - quadratic(0, 1)
    h_eb = l1 * g + l2 * g2 - quadratic(0, 2)
    h_ec = quadratic(0, 3) - (l1 * fg + l2 * fg2) + kc * u_e
    straight = h1 * q + h2 * q2
    h_aa = quadratic(1, 1) + straight
    h_ab = quadratic(1, 2) - (h1 * m + h2 * m2)
    h_ac = kc * u_a - quadratic(1, 3) + (h1 * f_c + h2 * f2_c)
    h_bb = quadratic(2, 2) + straight
    h_bc = kc * u_b - quadratic(2, 3) + (h1 * g_c + h2 * g2_c)
    bent = (chi_shape * h1) * (f_c * g + f * g_c) + (chi_energy * h2) * (f2_c * g2 + f2 * g2_c)
    twist = kc * kc + (chi_shape * chi_shape) * q * (2.0 * q - 1.0)
    h_cc = quadratic(3, 3) - bent - 2.0 * (kc * u_fg) + u * twist
    gradient = (u_e, u_a, u_b, u_c)
    return gradient, (h_ee, h_ea, h_eb, h_ec, h_aa, h_ab, h_ac, h_bb, h_bc, h_cc), u_a * a + u_c * c


def offsets_of(code, period):
    return [((code >> bits & 3) - 1).astype(jnp.float32) * size for bits, size in zip((4, 2, 0), period)]


def row_of(tiles_ref, tile, k, member):
    return tiles_ref[tile, :, k * member : (k + 1) * member]


def centre_of(code, period, all_ref, member):
    shift = offsets_of(code, period)
    return [row_of(all_ref, code >> CODE_BITS, CENTRE + k, member) + shift[k] for k in range(3)]


def lanes_of(block, member):
    row = lax.broadcasted_iota(jnp.int32, (SUB, member), 0)
    lane = lax.broadcasted_iota(jnp.int32, (SUB, member), 1)
    group = (lane & -LAYER) - (block >> 1) * LAYER
    return (group & (member - 1)) + ((block & 1) * SUB + row)


def picked(block, lanes):
    return jnp.take_along_axis(block, lanes, axis=1, mode="promise_in_bounds")


def box_lanes(member):
    block = lax.broadcasted_iota(jnp.int32, (member // SUB, member), 0)
    lane = lax.broadcasted_iota(jnp.int32, (member // SUB, member), 1)
    return (((lane & -LAYER) - (block >> 1) * LAYER) & (member - 1)) + (block & 1) * SUB


def near_blocks(own_centre, partner, lanes):
    blocks, member = lanes.shape
    zero = jnp.zeros((1, member), jnp.float32)
    box = stacked(partner + [-line for line in partner] + [zero, zero])
    for bit in (1, 2, 4):
        box = jnp.maximum(box, pltpu.roll(box, member - bit, 1))

    def seen(k):
        line = jnp.broadcast_to(box[k : k + 1], (SUB, member))
        return stacked([picked(line, lanes[at : at + SUB]) for at in range(0, blocks, SUB)])

    reach = 0.0
    for k in range(3):
        above = own_centre[k] - seen(k)
        below = -own_centre[k] - seen(3 + k)
        gap = jnp.maximum(jnp.maximum(above, below), 0.0)
        reach = reach + gap * gap
    nearest = jnp.min(reach, axis=1, keepdims=True)
    weight = (1 << lax.broadcasted_iota(jnp.int32, (blocks, 1), 0)).astype(jnp.float32)
    return jnp.sum(jnp.where(nearest < cutoff_sq * 1.001, weight, 0.0)).astype(jnp.int32)


def stacked(parts):
    return jnp.concatenate(parts, axis=0)


def wide(row, blocks=GROUP):
    return jnp.broadcast_to(row, (blocks * SUB, row.shape[1]))


def partner_rows(row_at, items, lanes):
    rows = []
    for k in range(6):
        parts = []
        for item, lane in zip(items, lanes):
            row = row_at(item >> (ITEM_BITS + CODE_BITS), k)
            parts.append(picked(jnp.broadcast_to(row, lane.shape), lane))
        rows.append(stacked(parts))
    return rows


def folded(total):
    return jnp.sum(total, axis=0, keepdims=True)


def geometry(items, unused, lanes, own_code, own_wide, period, all_ref):
    member = lanes[0].shape[1]
    lane = lax.broadcasted_iota(jnp.int32, (SUB, member), 1)
    lift = []
    shifts = []
    for item, idle, other in zip(items, unused, lanes):
        code = item >> ITEM_BITS
        itself = jnp.where(other == lane, jnp.where(code == own_code, 2.0 * cutoff_sq, 0.0), 0.0)
        lift.append(itself + jnp.where(idle, 2.0 * cutoff_sq, 0.0))
        shifts.append(offsets_of(code, period))
    rows = partner_rows(lambda tile, k: row_of(all_ref, tile, CENTRE + k, member), items, lanes)
    shift = [stacked([jnp.full((SUB, member), one[k]) for one in shifts]) for k in range(3)]
    d = [rows[k] + shift[k] - own_wide[k] for k in range(3)]
    uj = rows[3:]
    gradient, hessian, spin = pair_coefficients(d, own_wide[3:], uj, stacked(lift))
    return list(gradient) + list(hessian) + d + uj, (gradient[1], spin)


def apply(moved_rows, terms, own_wide, moved_wide):
    u_e, u_a, u_b, u_c, h_ee, h_ea, h_eb, h_ec, h_aa, h_ab, h_ac, h_bb, h_bc, h_cc = terms[:14]
    d = terms[14:17]
    uj = terms[17:20]
    ui = own_wide[3:]
    dui = moved_wide[3:]
    dd = [moved_rows[k] - moved_wide[k] for k in range(3)]
    duj = cross3(moved_rows[3:], uj)
    de = dot3(d, dd)
    da = dot3(dd, ui) + dot3(d, dui)
    db = dot3(dd, uj) + dot3(d, duj)
    dc = dot3(dui, uj) + dot3(ui, duj)
    du_e = h_ee * de + h_ea * da + h_eb * db + h_ec * dc
    du_a = h_ea * de + h_aa * da + h_ab * db + h_ac * dc
    du_b = h_eb * de + h_ab * da + h_bb * db + h_bc * dc
    du_c = h_ec * de + h_ac * da + h_bc * db + h_cc * dc
    force = [du_e * d[k] + u_e * dd[k] + du_b * uj[k] + u_b * duj[k] for k in range(3)]
    turn = [du_a * d[k] + u_a * dd[k] + du_c * uj[k] + u_c * duj[k] for k in range(3)]
    return force + turn + [du_a]


def group_items(step, item_ref, item_count):
    at = [step * GROUP + part for part in range(GROUP)]
    return [item_ref[1 + place] for place in at], [place >= item_count for place in at]


def added(totals, news):
    return tuple(
        total + sum(new[at : at + SUB] for at in range(0, new.shape[0], SUB)) for total, new in zip(totals, news)
    )


def close(sums, kept, spin, u, t):
    force = [-(sums[k] + u[k] * sums[6] + t[k] * kept) for k in range(3)]
    return force + list(cross3(u, [sums[3 + k] - t[k] * spin for k in range(3)]))


def spread(rows, out_ref):
    member = rows[0].shape[1]
    for k, row in enumerate(rows):
        out_ref[:, :, k * member : (k + 1) * member] = jnp.broadcast_to(row[None], (out_ref.shape[0], 1, member))


def pack_kernel(*refs):
    sources, out_ref, targets, sems = refs[:4], refs[4], refs[5:9], refs[9]
    config_ref, start_ref, list_ref, count_ref = targets
    copies = [
        pltpu.make_async_copy(source, target, sems.at[at]) for at, (source, target) in enumerate(zip(sources, targets))
    ]
    for copy in copies:
        copy.start()
    copies[2].wait()
    copies[3].wait()
    member = config_ref.shape[1]
    lane = lax.broadcasted_iota(jnp.int32, (1, member), 1)
    fields, slots = list_ref.shape[1], list_ref.shape[3]
    line = jnp.full((1, member), -9, jnp.int32)
    for field in range(fields):
        for slot in range(slots):
            line = jnp.where(lane == field * slots + slot, list_ref[0, field, 0, slot], line)
    line = jnp.where((lane >= count_ref[0, 0]) & (lane < slots), -9, line).astype(jnp.float32)
    copies[0].wait()
    copies[1].wait()
    rows = [ref[k : k + 1, :] for ref in (start_ref, config_ref) for k in range(6)]
    spread(rows + [line], out_ref)


def first_kernel(
    rows,
    cols,
    slots,
    period,
    all_ref,
    out_ref,
    item_ref,
    coef_ref,
    kept_ref,
    entry_ref,
    code_ref,
    code_smem,
    sem,
):
    member = kept_ref.shape[1]
    row_id = lax.axis_index("row")
    col_id = lax.axis_index("col")
    own = row_id * cols + col_id
    blocks = member // SUB

    def field(line, at):
        return line if at == 0 else pltpu.roll(line, member - at * slots, 1)

    row_f = row_id.astype(jnp.float32)
    col_f = col_id.astype(jnp.float32)
    lines = [row_of(all_ref, row_id * cols + col, LIST_ROW, member) for col in range(cols)]
    lines += [row_of(all_ref, row * cols + col_id, LIST_ROW, member) for row in range(rows)]
    line = jnp.concatenate(lines, axis=0)
    at = lax.broadcasted_iota(jnp.int32, line.shape, 0).astype(jnp.float32)
    near = at < float(cols)
    other = field(line, 1)
    offset = field(line, 2) * 16.0 + field(line, 3) * 4.0 + field(line, 4)
    partner = jnp.where(near, other * float(cols) + at, (at - float(cols)) * float(cols) + line)
    code = partner * float(1 << CODE_BITS) + (jnp.where(near, offset, -offset) + 21.0)
    hit = jnp.where(near, line - col_f, jnp.where(line >= 0.0, other - row_f, 1.0)) == 0.0
    code_ref[...] = jnp.where(hit, code, -1.0).astype(jnp.int32)
    copy = pltpu.make_async_copy(code_ref, code_smem, sem)
    copy.start()
    own_code = own * (1 << CODE_BITS) + 21
    own_moved = [row_of(all_ref, own, k, member) for k in range(6)]
    own_frame = [row_of(all_ref, own, CENTRE + k, member) for k in range(6)]
    lanes = box_lanes(member)
    own_centre = [jnp.broadcast_to(line, lanes.shape) for line in own_frame[:3]]

    def append(code, bits, count):
        for block in range(blocks):
            item_ref[1 + count] = (code << ITEM_BITS) + block
            count = count + (bits >> block & 1)
        return count

    items = append(own_code, near_blocks(own_centre, own_frame[:3], lanes), jnp.int32(0))
    copy.wait()

    def gather(line, count):
        for slot in range(slots):
            code = code_smem[line, slot]
            entry_ref[count] = code
            count = count + (code >= 0).astype(jnp.int32)
        return count

    entries = lax.fori_loop(0, rows + cols, gather, jnp.int32(0))
    for part in range(TESTS):
        entry_ref[entries + part] = own_code

    def prepare(step, count):
        codes = [entry_ref[step * TESTS + part] for part in range(TESTS)]
        bits = [near_blocks(own_centre, centre_of(code, period, all_ref, member), lanes) for code in codes]
        for part in range(TESTS):
            count = append(codes[part], jnp.where(step * TESTS + part < entries, bits[part], 0), count)
        return count

    items = lax.fori_loop(0, (entries + TESTS - 1) // TESTS, prepare, items)
    for part in range(GROUP):
        item_ref[1 + items + part] = own_code << ITEM_BITS
    item_ref[0] = items

    spare = coef_ref.shape[0] // (TERMS * GROUP * SUB) - 1
    steps = (items + GROUP - 1) // GROUP
    u = own_frame[3:]
    t = cross3(own_moved[3:], u)
    own_wide = [wide(line) for line in own_frame]
    moved_wide = [wide(line) for line in [*own_moved[:3], *t]]

    def keep(step, totals):
        group, unused = group_items(step, item_ref, items)
        lanes = [lanes_of(item & ITEM_MASK, member) for item in group]
        terms, sums = geometry(group, unused, lanes, own_code, own_wide, period, all_ref)
        moved_rows = partner_rows(lambda tile, k: row_of(all_ref, tile, k, member), group, lanes)
        start = pl.multiple_of(jnp.minimum(step, spare) * (TERMS * GROUP * SUB), SUB)
        for k in range(TERMS):
            coef_ref[pl.ds(start + k * GROUP * SUB, GROUP * SUB), :] = terms[k]
        return added(totals, apply(moved_rows, terms, own_wide, moved_wide) + list(sums))

    zero = jnp.zeros((SUB, member), jnp.float32)
    totals = lax.fori_loop(0, steps, keep, (zero,) * 9)
    sums = [folded(total) for total in totals]
    kept_ref[...] = jnp.concatenate(sums[7:], axis=0)
    spread(close(sums, sums[7], sums[8], u, t), out_ref)


def scalar_of(block):
    return jnp.sum(jnp.sum(block, axis=0, keepdims=True), axis=1, keepdims=True)


def second_kernel(
    cols,
    total_entries,
    period,
    item_ref,
    coef_ref,
    kept_ref,
    all_ref,
    image_ref,
    out_ref,
    pair_ref,
    scalar_ref,
    second_ref,
):
    own = lax.axis_index("row") * cols + lax.axis_index("col")
    member = kept_ref.shape[1]
    basis = all_ref[:, 0, 0 : 6 * member]
    image = image_ref[:, 0, :]
    portion = 1.0 / total_entries

    def total_of(block):
        return scalar_of(sum(block[:, k * member : (k + 1) * member] for k in range(6)))

    norm_sq = total_of(basis * basis) * portion + norm_eps
    norm_inv = lax.rsqrt(norm_sq)
    alpha = total_of(basis * image) * portion / norm_sq
    second = image - alpha * basis
    second_ref[:, 0, :] = second
    beta_sq = total_of(second * second) * portion / norm_sq + norm_eps
    beta = jnp.sqrt(beta_sq)
    scale = norm_inv * lax.rsqrt(beta_sq)

    own_code = own * (1 << CODE_BITS) + 21
    items = item_ref[0]
    held = coef_ref.shape[0] // (TERMS * GROUP * SUB) - 1
    steps = (items + GROUP - 1) // GROUP

    def moved_row(tile, k):
        return row_of(second_ref, tile, k, member)

    own_moved = [moved_row(own, k) for k in range(6)]
    own_frame = [row_of(all_ref, own, CENTRE + k, member) for k in range(6)]
    u = own_frame[3:]
    t = cross3(own_moved[3:], u)
    own_wide = [wide(line) for line in own_frame]
    moved_wide = [wide(line) for line in [*own_moved[:3], *t]]

    def visit(step, totals):
        group, _ = group_items(step, item_ref, items)
        lanes = [lanes_of(item & ITEM_MASK, member) for item in group]
        start = pl.multiple_of(step * (TERMS * GROUP * SUB), SUB)
        terms = [coef_ref[pl.ds(start + k * GROUP * SUB, GROUP * SUB), :] for k in range(TERMS)]
        return added(totals, apply(partner_rows(moved_row, group, lanes), terms, own_wide, moved_wide))

    own_once = [wide(line, 1) for line in own_frame]
    moved_once = [wide(line, 1) for line in [*own_moved[:3], *t]]

    def visit_again(place, totals):
        item = item_ref[1 + place]
        lanes = lanes_of(item & ITEM_MASK, member)
        terms, _ = geometry([item], [False], [lanes], own_code, own_once, period, all_ref)
        return added(totals, apply(partner_rows(moved_row, [item], [lanes]), terms, own_once, moved_once))

    zero = jnp.zeros((SUB, member), jnp.float32)
    totals = lax.fori_loop(0, jnp.minimum(steps, held), visit, (zero,) * 7)
    totals = lax.fori_loop(held * GROUP, items, visit_again, totals)
    sums = [folded(total) for total in totals]
    product = close(sums, kept_ref[0:1, :], kept_ref[1:2, :], u, t)
    fill = [jnp.zeros((1, member), jnp.float32)] * (SUB - len(product))
    first = stacked([row_of(all_ref, own, k, member) for k in range(6)] + fill)
    image = stacked(product + fill) * scale - (beta * norm_inv) * first
    second = stacked(own_moved + fill) * scale
    inner = scalar_of(second * image)
    weight = scalar_of(second * second)
    local_alpha = jnp.where(weight > 1e-30, inner / jnp.maximum(weight, 1e-30), 0.0)
    rest = image - local_alpha * second
    size = scalar_of(rest * rest)
    slant = scalar_of(second * rest)
    lane = lax.broadcasted_iota(jnp.int32, (1, member), 1)
    line = jnp.zeros((1, member), jnp.float32)
    for at, value in enumerate((inner, weight, local_alpha, size, slant)):
        line = jnp.where(lane == at, value, line)
    out_ref[...] = jnp.broadcast_to(line[None], out_ref.shape)
    pair_ref[0] = second
    pair_ref[1] = image
    scalar_ref[...] = jnp.where(lane == 0, alpha, jnp.where(lane == 1, beta, 0.0))


def last_kernel(total_entries, pair_ref, scalar_ref, line_ref, mode_ref, coefficient_ref):
    lines = line_ref[:, 0, :]
    alpha = jnp.sum(lines[:, 0:1], axis=0, keepdims=True) / total_entries
    away = lines[:, 2:3] - alpha
    parts = lines[:, 3:4] + away * (away * lines[:, 1:2] + 2.0 * lines[:, 4:5])
    beta = jnp.sqrt(jnp.sum(parts, axis=0, keepdims=True) / total_entries + norm_eps)
    mode = (pair_ref[1] - alpha * pair_ref[0]) / beta
    mode_ref[...] = mode[: mode_ref.shape[0]]
    for at, value in enumerate((scalar_ref[0:1, 0:1], scalar_ref[0:1, 1:2], alpha, beta)):
        coefficient_ref[at] = jnp.sum(value)


def local(config, start, tile_list, tile_count):
    dof, member = config.shape
    row_devices = lax.axis_size("row")
    col_devices = lax.axis_size("col")
    devices = row_devices * col_devices
    total_entries = float(dof * member * devices)
    period = (5.0, 5.0, 3.5 * (member // 16))
    slots = tile_list.shape[2]
    longest = (row_devices + col_devices) * slots + 1

    def shaped(*shape):
        return jax.ShapeDtypeStruct(shape, jnp.float32)

    def everywhere(copies):
        return lax.all_to_all(copies, ("row", "col"), 0, 0, tiled=True)

    params = pltpu.CompilerParams(vmem_limit_bytes=VMEM_LIMIT)
    vmem = pl.BlockSpec(memory_space=pltpu.VMEM)
    smem = pl.BlockSpec(memory_space=pltpu.SMEM)

    outside = pl.BlockSpec(memory_space=pl.ANY)
    packed = pl.pallas_call(
        pack_kernel,
        out_shape=shaped(devices, 1, (LIST_ROW + 1) * member),
        in_specs=[outside] * 4,
        out_specs=vmem,
        scratch_shapes=[
            pltpu.VMEM((dof, member), jnp.float32),
            pltpu.VMEM((dof, member), jnp.float32),
            pltpu.SMEM((1, tile_list.shape[3], 1, slots), jnp.int32),
            pltpu.SMEM((1, 1), jnp.int32),
            pltpu.SemaphoreType.DMA((4,)),
        ],
        compiler_params=pltpu.CompilerParams(vmem_limit_bytes=PACK_LIMIT),
    )(config, start, jnp.transpose(tile_list, (0, 3, 1, 2)), tile_count)
    together = everywhere(packed)

    held_rows = (HELD // GROUP + 1) * (TERMS * GROUP * SUB)
    image, items, terms, kept = pl.pallas_call(
        functools.partial(first_kernel, row_devices, col_devices, slots, period),
        out_shape=(
            shaped(devices, 1, dof * member),
            jax.ShapeDtypeStruct((1 + longest * (member // SUB) + GROUP,), jnp.int32),
            shaped(held_rows, member),
            shaped(2, member),
        ),
        in_specs=[vmem],
        out_specs=(vmem, smem, vmem, vmem),
        scratch_shapes=[
            pltpu.SMEM((longest + TESTS,), jnp.int32),
            pltpu.VMEM((row_devices + col_devices, member), jnp.int32),
            pltpu.SMEM((row_devices + col_devices, member), jnp.int32),
            pltpu.SemaphoreType.DMA,
        ],
        compiler_params=params,
    )(together)
    image = everywhere(image)

    line, pair, scalars = pl.pallas_call(
        functools.partial(second_kernel, col_devices, total_entries, period),
        out_shape=(shaped(devices, 1, member), shaped(2, SUB, member), shaped(1, member)),
        in_specs=[smem] + [vmem] * 4,
        out_specs=(vmem, vmem, vmem),
        scratch_shapes=[
            pltpu.VMEM((devices, 1, dof * member), jnp.float32),
        ],
        compiler_params=params,
    )(items, terms, kept, together, image)
    line = everywhere(line)

    mode, coefficients = pl.pallas_call(
        functools.partial(last_kernel, total_entries),
        out_shape=(shaped(dof, member), shaped(4)),
        in_specs=[vmem] * 3,
        out_specs=(vmem, smem),
        compiler_params=params,
    )(pair, scalars, line)
    return (coefficients, mode)


def solution(mesh):
    placed = (
        P(None, ("row", "col")),
        P(None, ("row", "col")),
        P("row", "col", None, None),
        P("row", "col"),
    )
    return jax.shard_map(
        local, mesh=mesh, in_specs=placed, out_specs=(P(), P(None, ("row", "col"))), check_vma=False
    )
```

```python
import functools
import math

import jax
import jax.numpy as jnp
from jax import lax
from jax.experimental import pallas as pl
from jax.experimental.pallas import tpu as pltpu
from jax.sharding import PartitionSpec as P

chi_shape = 0.8
chi_energy = (math.sqrt(5.0) - 1.0) / (math.sqrt(5.0) + 1.0)
well_depth = 0.005
cutoff_sq = 20.25
norm_eps = 1e-06

SUB = 8
CENTRE = 6
LIST_ROW = 12
CODE_BITS = 6
ITEM_BITS = 8
ITEM_MASK = 255
LAYER = 16
TESTS = 5
GROUP = 2
UNROLL = 2
TERMS = 20
HELD = 128
VMEM_LIMIT = 32 * 1024 * 1024
PACK_LIMIT = 60 * 1024 * 1024


def dot3(a, b):
    return a[0] * b[0] + a[1] * b[1] + a[2] * b[2]


def cross3(a, b):
    return (
        a[1] * b[2] - a[2] * b[1],
        a[2] * b[0] - a[0] * b[2],
        a[0] * b[1] - a[1] * b[0],
    )


def inverse(value):
    guess = pl.reciprocal(value, approx=True)
    return guess * (2.0 - value * guess)


def bracket(chi, scaled, factor, p, a, b):
    f = factor * (a - scaled * b)
    g = factor * (b - scaled * a)
    y = p * (a * f + b * g)
    cross = factor * scaled
    f_c = chi * (cross * f - factor * g)
    g_c = chi * (cross * g - factor * f)
    return f, g, y, cross, f_c, g_c


def pair_coefficients(d, ui, uj, lift):
    r_sq = dot3(d, d) + lift
    a = dot3(d, ui)
    b = dot3(d, uj)
    c = dot3(ui, uj)
    r_inv = lax.rsqrt(r_sq)
    p = r_inv * r_inv
    p2 = 2.0 * p
    r = r_sq * r_inv
    x = jnp.maximum(1.0 - r_sq * (1.0 / cutoff_sq), 0.0)
    c_shape = chi_shape * c
    c_energy = chi_energy * c
    e1 = lax.rsqrt(1.0 - c_shape * c_shape)
    q = e1 * e1
    q2 = inverse(1.0 - c_energy * c_energy)
    f, g, y, m, f_c, g_c = bracket(chi_shape, c_shape, q, p, a, b)
    f2, g2, y2, m2, f2_c, g2_c = bracket(chi_energy, c_energy, q2, p, a, b)
    sigma = lax.rsqrt(1.0 - chi_shape * y)
    sigma_sq = sigma * sigma
    psi = 1.0 - chi_energy * y2
    s = inverse(r - sigma + 1.0)
    s_sq = s * s
    s6 = s_sq * s_sq * s_sq
    t0 = s6 * (s6 - 1.0)
    t1 = s6 * s * (6.0 - 12.0 * s6)
    t2 = s6 * s_sq * (156.0 * s6 - 42.0)
    ke = (4.0 * well_depth) * e1
    kx = ke * x
    v_ee = kx * (24.0 / cutoff_sq**2)
    kxx = kx * x
    v_e = kxx * (-6.0 / cutoff_sq)
    v = kxx * x
    psi_sq = psi * psi
    psi_sq_t0 = psi_sq * t0
    psi_sq_t1 = psi_sq * t1
    u = v * psi_sq_t0
    slope = v * psi_sq_t1
    slope2 = v * psi_sq * t2
    tau = (-0.5 * chi_shape) * sigma_sq * sigma
    push = (-2.0 * chi_energy) * psi
    v_t1 = v * t1
    d1 = slope * tau
    d2 = push * (v * t0)
    h1 = p2 * d1
    h2 = p2 * d2
    kc = chi_shape * c_shape * q
    fg = chi_shape * f * g
    fg2 = chi_energy * f2 * g2
    u_a = h1 * f + h2 * f2
    u_b = h1 * g + h2 * g2
    u_fg = h1 * fg + h2 * fg2
    u_c = u * kc - u_fg
    v_e_t0 = v_e * psi_sq_t0
    d_e = r_inv * slope + v_e_t0
    u_e = d_e - (h1 * y + h2 * y2)

    p2_sq = p2 * p2
    k11 = p2_sq * (tau * (slope2 * tau + (1.5 * chi_shape) * sigma_sq * slope))
    k12 = p2_sq * (push * v_t1 * tau)
    k22 = p2_sq * ((2.0 * chi_energy * chi_energy) * (v * t0))
    steep = v_e * psi_sq_t1 + slope2 * r_inv
    l1 = p2 * (steep * tau - h1)
    l2 = p2 * (push * (v_e * t0 + v_t1 * r_inv) - h2)
    j1 = (y, f, g, fg)
    j2 = (y2, f2, g2, fg2)
    w1 = [k11 * one + k12 * two for one, two in zip(j1, j2)]
    w2 = [k12 * one + k22 * two for one, two in zip(j1, j2)]

    def quadratic(m_at, n_at):
        return w1[m_at] * j1[n_at] + w2[m_at] * j2[n_at]

    d_ee = v_ee * psi_sq_t0 + r_inv * (2.0 * (v_e * psi_sq_t1)) + p * (slope2 - slope * r_inv)
    h_ee = quadratic(0, 0) - 2.0 * (l1 * y + l2 * y2) + d_ee
    h_ea = l1 * f + l2 * f2 - quadratic(0, 1)
    h_eb = l1 * g + l2 * g2 - quadratic(0, 2)
    h_ec = quadratic(0, 3) - (l1 * fg + l2 * fg2) + kc * u_e
    straight = h1 * q + h2 * q2
    h_aa = quadratic(1, 1) + straight
    h_ab = quadratic(1, 2) - (h1 * m + h2 * m2)
    h_ac = kc * u_a - quadratic(1, 3) + (h1 * f_c + h2 * f2_c)
    h_bb = quadratic(2, 2) + straight
    h_bc = kc * u_b - quadratic(2, 3) + (h1 * g_c + h2 * g2_c)
    bent = (chi_shape * h1) * (f_c * g + f * g_c) + (chi_energy * h2) * (f2_c * g2 + f2 * g2_c)
    twist = kc * kc + (chi_shape * chi_shape) * q * (2.0 * q - 1.0)
    h_cc = quadratic(3, 3) - bent - 2.0 * (kc * u_fg) + u * twist
    gradient = (u_e, u_a, u_b, u_c)
    return gradient, (h_ee, h_ea, h_eb, h_ec, h_aa, h_ab, h_ac, h_bb, h_bc, h_cc), u_a * a + u_c * c


def offsets_of(code, period):
    return [((code >> bits & 3) - 1).astype(jnp.float32) * size for bits, size in zip((4, 2, 0), period)]


def row_of(tiles_ref, tile, k, member):
    return tiles_ref[tile, :, k * member : (k + 1) * member]


def centre_of(code, period, all_ref, member):
    shift = offsets_of(code, period)
    return [row_of(all_ref, code >> CODE_BITS, CENTRE + k, member) + shift[k] for k in range(3)]


def lanes_of(block, member):
    row = lax.broadcasted_iota(jnp.int32, (SUB, member), 0)
    lane = lax.broadcasted_iota(jnp.int32, (SUB, member), 1)
    group = (lane & -LAYER) - (block >> 1) * LAYER
    return (group & (member - 1)) + ((block & 1) * SUB + row)


def picked(block, lanes):
    return jnp.take_along_axis(block, lanes, axis=1, mode="promise_in_bounds")


def box_lanes(member):
    block = lax.broadcasted_iota(jnp.int32, (member // SUB, member), 0)
    lane = lax.broadcasted_iota(jnp.int32, (member // SUB, member), 1)
    return (((lane & -LAYER) - (block >> 1) * LAYER) & (member - 1)) + (block & 1) * SUB


def near_blocks(own_centre, partner, lanes):
    blocks, member = lanes.shape
    zero = jnp.zeros((1, member), jnp.float32)
    box = stacked(partner + [-line for line in partner] + [zero, zero])
    for bit in (1, 2, 4):
        box = jnp.maximum(box, pltpu.roll(box, member - bit, 1))

    def seen(k):
        line = jnp.broadcast_to(box[k : k + 1], (SUB, member))
        return stacked([picked(line, lanes[at : at + SUB]) for at in range(0, blocks, SUB)])

    reach = 0.0
    for k in range(3):
        above = own_centre[k] - seen(k)
        below = -own_centre[k] - seen(3 + k)
        gap = jnp.maximum(jnp.maximum(above, below), 0.0)
        reach = reach + gap * gap
    nearest = jnp.min(reach, axis=1, keepdims=True)
    weight = (1 << lax.broadcasted_iota(jnp.int32, (blocks, 1), 0)).astype(jnp.float32)
    return jnp.sum(jnp.where(nearest < cutoff_sq * 1.001, weight, 0.0)).astype(jnp.int32)


def stacked(parts):
    return jnp.concatenate(parts, axis=0)


def wide(row):
    return jnp.broadcast_to(row, (GROUP * SUB, row.shape[1]))


def partner_rows(row_at, items, lanes):
    rows = []
    for k in range(6):
        parts = []
        for item, lane in zip(items, lanes):
            row = row_at(item >> (ITEM_BITS + CODE_BITS), k)
            parts.append(picked(jnp.broadcast_to(row, lane.shape), lane))
        rows.append(stacked(parts))
    return rows


def folded(total):
    return jnp.sum(total, axis=0, keepdims=True)


def geometry(items, unused, lanes, own_code, own_wide, period, all_ref):
    member = lanes[0].shape[1]
    lane = lax.broadcasted_iota(jnp.int32, (SUB, member), 1)
    lift = []
    shifts = []
    for item, idle, other in zip(items, unused, lanes):
        code = item >> ITEM_BITS
        itself = jnp.where(other == lane, jnp.where(code == own_code, 2.0 * cutoff_sq, 0.0), 0.0)
        lift.append(itself + jnp.where(idle, 2.0 * cutoff_sq, 0.0))
        shifts.append(offsets_of(code, period))
    rows = partner_rows(lambda tile, k: row_of(all_ref, tile, CENTRE + k, member), items, lanes)
    shift = [stacked([jnp.full((SUB, member), one[k]) for one in shifts]) for k in range(3)]
    d = [rows[k] + shift[k] - own_wide[k] for k in range(3)]
    uj = rows[3:]
    gradient, hessian, spin = pair_coefficients(d, own_wide[3:], uj, stacked(lift))
    return list(gradient) + list(hessian) + d + uj, (gradient[1], spin)


def apply(moved_rows, terms, own_wide, moved_wide):
    u_e, u_a, u_b, u_c, h_ee, h_ea, h_eb, h_ec, h_aa, h_ab, h_ac, h_bb, h_bc, h_cc = terms[:14]
    d = terms[14:17]
    uj = terms[17:20]
    ui = own_wide[3:]
    dui = moved_wide[3:]
    dd = [moved_rows[k] - moved_wide[k] for k in range(3)]
    duj = cross3(moved_rows[3:], uj)
    de = dot3(d, dd)
    da = dot3(dd, ui) + dot3(d, dui)
    db = dot3(dd, uj) + dot3(d, duj)
    dc = dot3(dui, uj) + dot3(ui, duj)
    du_e = h_ee * de + h_ea * da + h_eb * db + h_ec * dc
    du_a = h_ea * de + h_aa * da + h_ab * db + h_ac * dc
    du_b = h_eb * de + h_ab * da + h_bb * db + h_bc * dc
    du_c = h_ec * de + h_ac * da + h_bc * db + h_cc * dc
    force = [du_e * d[k] + u_e * dd[k] + du_b * uj[k] + u_b * duj[k] for k in range(3)]
    turn = [du_a * d[k] + u_a * dd[k] + du_c * uj[k] + u_c * duj[k] for k in range(3)]
    return force + turn + [du_a]


def several(body):
    def step_of(step, totals):
        for part in range(UNROLL):
            totals = body(step * UNROLL + part, totals)
        return totals

    return step_of


def group_items(step, item_ref, item_count):
    at = [step * GROUP + part for part in range(GROUP)]
    return [item_ref[1 + place] for place in at], [place >= item_count for place in at]


def added(totals, news):
    return tuple(
        total + sum(new[part * SUB : (part + 1) * SUB] for part in range(GROUP)) for total, new in zip(totals, news)
    )


def close(sums, kept, spin, u, t):
    force = [-(sums[k] + u[k] * sums[6] + t[k] * kept) for k in range(3)]
    return force + list(cross3(u, [sums[3 + k] - t[k] * spin for k in range(3)]))


def spread(rows, out_ref):
    member = rows[0].shape[1]
    for k, row in enumerate(rows):
        out_ref[:, :, k * member : (k + 1) * member] = jnp.broadcast_to(row[None], (out_ref.shape[0], 1, member))


def pack_kernel(*refs):
    sources, out_ref, targets, sems = refs[:4], refs[4], refs[5:9], refs[9]
    config_ref, start_ref, list_ref, count_ref = targets
    copies = [
        pltpu.make_async_copy(source, target, sems.at[at]) for at, (source, target) in enumerate(zip(sources, targets))
    ]
    for copy in copies:
        copy.start()
    copies[2].wait()
    copies[3].wait()
    member = config_ref.shape[1]
    lane = lax.broadcasted_iota(jnp.int32, (1, member), 1)
    fields, slots = list_ref.shape[1], list_ref.shape[3]
    line = jnp.full((1, member), -9, jnp.int32)
    for field in range(fields):
        for slot in range(slots):
            line = jnp.where(lane == field * slots + slot, list_ref[0, field, 0, slot], line)
    line = jnp.where((lane >= count_ref[0, 0]) & (lane < slots), -9, line).astype(jnp.float32)
    copies[0].wait()
    copies[1].wait()
    rows = [ref[k : k + 1, :] for ref in (start_ref, config_ref) for k in range(6)]
    spread(rows + [line], out_ref)


def first_kernel(
    rows,
    cols,
    slots,
    period,
    all_ref,
    out_ref,
    item_ref,
    coef_ref,
    kept_ref,
    entry_ref,
    code_ref,
    code_smem,
    sem,
):
    member = kept_ref.shape[1]
    row_id = lax.axis_index("row")
    col_id = lax.axis_index("col")
    own = row_id * cols + col_id
    blocks = member // SUB

    def field(line, at):
        return line if at == 0 else pltpu.roll(line, member - at * slots, 1)

    row_f = row_id.astype(jnp.float32)
    col_f = col_id.astype(jnp.float32)
    lines = [row_of(all_ref, row_id * cols + col, LIST_ROW, member) for col in range(cols)]
    lines += [row_of(all_ref, row * cols + col_id, LIST_ROW, member) for row in range(rows)]
    line = jnp.concatenate(lines, axis=0)
    at = lax.broadcasted_iota(jnp.int32, line.shape, 0).astype(jnp.float32)
    near = at < float(cols)
    other = field(line, 1)
    offset = field(line, 2) * 16.0 + field(line, 3) * 4.0 + field(line, 4)
    partner = jnp.where(near, other * float(cols) + at, (at - float(cols)) * float(cols) + line)
    code = partner * float(1 << CODE_BITS) + (jnp.where(near, offset, -offset) + 21.0)
    hit = jnp.where(near, line - col_f, jnp.where(line >= 0.0, other - row_f, 1.0)) == 0.0
    code_ref[...] = jnp.where(hit, code, -1.0).astype(jnp.int32)
    copy = pltpu.make_async_copy(code_ref, code_smem, sem)
    copy.start()
    own_code = own * (1 << CODE_BITS) + 21
    own_moved = [row_of(all_ref, own, k, member) for k in range(6)]
    own_frame = [row_of(all_ref, own, CENTRE + k, member) for k in range(6)]
    lanes = box_lanes(member)
    own_centre = [jnp.broadcast_to(line, lanes.shape) for line in own_frame[:3]]

    def append(code, bits, count):
        for block in range(blocks):
            item_ref[1 + count] = (code << ITEM_BITS) + block
            count = count + (bits >> block & 1)
        return count

    items = append(own_code, near_blocks(own_centre, own_frame[:3], lanes), jnp.int32(0))
    copy.wait()

    def gather(line, count):
        for slot in range(slots):
            code = code_smem[line, slot]
            entry_ref[count] = code
            count = count + (code >= 0).astype(jnp.int32)
        return count

    entries = lax.fori_loop(0, rows + cols, gather, jnp.int32(0))
    for part in range(TESTS):
        entry_ref[entries + part] = own_code

    def prepare(step, count):
        codes = [entry_ref[step * TESTS + part] for part in range(TESTS)]
        bits = [near_blocks(own_centre, centre_of(code, period, all_ref, member), lanes) for code in codes]
        for part in range(TESTS):
            count = append(codes[part], jnp.where(step * TESTS + part < entries, bits[part], 0), count)
        return count

    items = lax.fori_loop(0, (entries + TESTS - 1) // TESTS, prepare, items)
    for part in range(GROUP * UNROLL):
        item_ref[1 + items + part] = own_code << ITEM_BITS
    item_ref[0] = items

    held = coef_ref.shape[0] // (TERMS * GROUP * UNROLL * SUB)
    steps = (items + GROUP * UNROLL - 1) // (GROUP * UNROLL)
    u = own_frame[3:]
    t = cross3(own_moved[3:], u)
    own_wide = [wide(line) for line in own_frame]
    moved_wide = [wide(line) for line in [*own_moved[:3], *t]]

    def derive(step, totals):
        group, unused = group_items(step, item_ref, items)
        lanes = [lanes_of(item & ITEM_MASK, member) for item in group]
        terms, sums = geometry(group, unused, lanes, own_code, own_wide, period, all_ref)
        moved_rows = partner_rows(lambda tile, k: row_of(all_ref, tile, k, member), group, lanes)
        return terms, added(totals, apply(moved_rows, terms, own_wide, moved_wide) + list(sums))

    def keep(step, totals):
        terms, totals = derive(step, totals)
        start = pl.multiple_of(step * (TERMS * GROUP * SUB), SUB)
        for k in range(TERMS):
            coef_ref[pl.ds(start + k * GROUP * SUB, GROUP * SUB), :] = terms[k]
        return totals

    zero = jnp.zeros((SUB, member), jnp.float32)
    totals = lax.fori_loop(0, jnp.minimum(steps, held), several(keep), (zero,) * 9)
    totals = lax.fori_loop(held, steps, several(lambda step, before: derive(step, before)[1]), totals)
    sums = [folded(total) for total in totals]
    kept_ref[...] = jnp.concatenate(sums[7:], axis=0)
    spread(close(sums, sums[7], sums[8], u, t), out_ref)


def scalar_of(block):
    return jnp.sum(jnp.sum(block, axis=0, keepdims=True), axis=1, keepdims=True)


def second_kernel(
    cols,
    total_entries,
    period,
    item_ref,
    coef_ref,
    kept_ref,
    all_ref,
    image_ref,
    out_ref,
    pair_ref,
    scalar_ref,
    second_ref,
):
    own = lax.axis_index("row") * cols + lax.axis_index("col")
    member = kept_ref.shape[1]
    basis = all_ref[:, 0, 0 : 6 * member]
    image = image_ref[:, 0, :]
    portion = 1.0 / total_entries

    def total_of(block):
        return scalar_of(sum(block[:, k * member : (k + 1) * member] for k in range(6)))

    norm_sq = total_of(basis * basis) * portion + norm_eps
    norm_inv = lax.rsqrt(norm_sq)
    alpha = total_of(basis * image) * portion / norm_sq
    second = image - alpha * basis
    second_ref[:, 0, :] = second
    beta_sq = total_of(second * second) * portion / norm_sq + norm_eps
    beta = jnp.sqrt(beta_sq)
    scale = norm_inv * lax.rsqrt(beta_sq)

    own_code = own * (1 << CODE_BITS) + 21
    items = item_ref[0]
    held = coef_ref.shape[0] // (TERMS * GROUP * UNROLL * SUB)
    steps = (items + GROUP * UNROLL - 1) // (GROUP * UNROLL)

    def moved_row(tile, k):
        return row_of(second_ref, tile, k, member)

    own_moved = [moved_row(own, k) for k in range(6)]
    own_frame = [row_of(all_ref, own, CENTRE + k, member) for k in range(6)]
    u = own_frame[3:]
    t = cross3(own_moved[3:], u)
    own_wide = [wide(line) for line in own_frame]
    moved_wide = [wide(line) for line in [*own_moved[:3], *t]]

    def visit(step, totals):
        group, _ = group_items(step, item_ref, items)
        lanes = [lanes_of(item & ITEM_MASK, member) for item in group]
        start = pl.multiple_of(step * (TERMS * GROUP * SUB), SUB)
        terms = [coef_ref[pl.ds(start + k * GROUP * SUB, GROUP * SUB), :] for k in range(TERMS)]
        return added(totals, apply(partner_rows(moved_row, group, lanes), terms, own_wide, moved_wide))

    def visit_again(step, totals):
        group, unused = group_items(step, item_ref, items)
        lanes = [lanes_of(item & ITEM_MASK, member) for item in group]
        terms, _ = geometry(group, unused, lanes, own_code, own_wide, period, all_ref)
        return added(totals, apply(partner_rows(moved_row, group, lanes), terms, own_wide, moved_wide))

    zero = jnp.zeros((SUB, member), jnp.float32)
    totals = lax.fori_loop(0, jnp.minimum(steps, held), several(visit), (zero,) * 7)
    totals = lax.fori_loop(held, steps, several(visit_again), totals)
    sums = [folded(total) for total in totals]
    product = close(sums, kept_ref[0:1, :], kept_ref[1:2, :], u, t)
    fill = [jnp.zeros((1, member), jnp.float32)] * (SUB - len(product))
    first = stacked([row_of(all_ref, own, k, member) for k in range(6)] + fill)
    image = stacked(product + fill) * scale - (beta * norm_inv) * first
    second = stacked(own_moved + fill) * scale
    inner = scalar_of(second * image)
    weight = scalar_of(second * second)
    local_alpha = jnp.where(weight > 1e-30, inner / jnp.maximum(weight, 1e-30), 0.0)
    rest = image - local_alpha * second
    size = scalar_of(rest * rest)
    slant = scalar_of(second * rest)
    lane = lax.broadcasted_iota(jnp.int32, (1, member), 1)
    line = jnp.zeros((1, member), jnp.float32)
    for at, value in enumerate((inner, weight, local_alpha, size, slant)):
        line = jnp.where(lane == at, value, line)
    out_ref[...] = jnp.broadcast_to(line[None], out_ref.shape)
    pair_ref[0] = second
    pair_ref[1] = image
    scalar_ref[...] = jnp.where(lane == 0, alpha, jnp.where(lane == 1, beta, 0.0))


def last_kernel(total_entries, pair_ref, scalar_ref, line_ref, mode_ref, coefficient_ref):
    lines = line_ref[:, 0, :]
    alpha = jnp.sum(lines[:, 0:1], axis=0, keepdims=True) / total_entries
    away = lines[:, 2:3] - alpha
    parts = lines[:, 3:4] + away * (away * lines[:, 1:2] + 2.0 * lines[:, 4:5])
    beta = jnp.sqrt(jnp.sum(parts, axis=0, keepdims=True) / total_entries + norm_eps)
    mode = (pair_ref[1] - alpha * pair_ref[0]) / beta
    mode_ref[...] = mode[: mode_ref.shape[0]]
    for at, value in enumerate((scalar_ref[0:1, 0:1], scalar_ref[0:1, 1:2], alpha, beta)):
        coefficient_ref[at] = jnp.sum(value)


def local(config, start, tile_list, tile_count):
    dof, member = config.shape
    row_devices = lax.axis_size("row")
    col_devices = lax.axis_size("col")
    devices = row_devices * col_devices
    total_entries = float(dof * member * devices)
    period = (5.0, 5.0, 3.5 * (member // 16))
    slots = tile_list.shape[2]
    longest = (row_devices + col_devices) * slots + 1

    def shaped(*shape):
        return jax.ShapeDtypeStruct(shape, jnp.float32)

    def everywhere(copies):
        return lax.all_to_all(copies, ("row", "col"), 0, 0, tiled=True)

    params = pltpu.CompilerParams(vmem_limit_bytes=VMEM_LIMIT)
    vmem = pl.BlockSpec(memory_space=pltpu.VMEM)
    smem = pl.BlockSpec(memory_space=pltpu.SMEM)

    outside = pl.BlockSpec(memory_space=pl.ANY)
    packed = pl.pallas_call(
        pack_kernel,
        out_shape=shaped(devices, 1, (LIST_ROW + 1) * member),
        in_specs=[outside] * 4,
        out_specs=vmem,
        scratch_shapes=[
            pltpu.VMEM((dof, member), jnp.float32),
            pltpu.VMEM((dof, member), jnp.float32),
            pltpu.SMEM((1, tile_list.shape[3], 1, slots), jnp.int32),
            pltpu.SMEM((1, 1), jnp.int32),
            pltpu.SemaphoreType.DMA((4,)),
        ],
        compiler_params=pltpu.CompilerParams(vmem_limit_bytes=PACK_LIMIT),
    )(config, start, jnp.transpose(tile_list, (0, 3, 1, 2)), tile_count)
    together = everywhere(packed)

    held_rows = HELD // GROUP * (TERMS * GROUP * SUB)
    image, items, terms, kept = pl.pallas_call(
        functools.partial(first_kernel, row_devices, col_devices, slots, period),
        out_shape=(
            shaped(devices, 1, dof * member),
            jax.ShapeDtypeStruct((1 + longest * (member // SUB) + GROUP * UNROLL,), jnp.int32),
            shaped(held_rows, member),
            shaped(2, member),
        ),
        in_specs=[vmem],
        out_specs=(vmem, smem, vmem, vmem),
        scratch_shapes=[
            pltpu.SMEM((longest + TESTS,), jnp.int32),
            pltpu.VMEM((row_devices + col_devices, member), jnp.int32),
            pltpu.SMEM((row_devices + col_devices, member), jnp.int32),
            pltpu.SemaphoreType.DMA,
        ],
        compiler_params=params,
    )(together)
    image = everywhere(image)

    line, pair, scalars = pl.pallas_call(
        functools.partial(second_kernel, col_devices, total_entries, period),
        out_shape=(shaped(devices, 1, member), shaped(2, SUB, member), shaped(1, member)),
        in_specs=[smem] + [vmem] * 4,
        out_specs=(vmem, vmem, vmem),
        scratch_shapes=[
            pltpu.VMEM((devices, 1, dof * member), jnp.float32),
        ],
        compiler_params=params,
    )(items, terms, kept, together, image)
    line = everywhere(line)

    mode, coefficients = pl.pallas_call(
        functools.partial(last_kernel, total_entries),
        out_shape=(shaped(dof, member), shaped(4)),
        in_specs=[vmem] * 3,
        out_specs=(vmem, smem),
        compiler_params=params,
    )(pair, scalars, line)
    return (coefficients, mode)


def solution(mesh):
    placed = (
        P(None, ("row", "col")),
        P(None, ("row", "col")),
        P("row", "col", None, None),
        P("row", "col"),
    )
    return jax.shard_map(
        local, mesh=mesh, in_specs=placed, out_specs=(P(), P(None, ("row", "col"))), check_vma=False
    )
```

```python
import functools
import math

import jax
import jax.numpy as jnp
from jax import lax
from jax.experimental import pallas as pl
from jax.experimental.pallas import tpu as pltpu
from jax.sharding import PartitionSpec as P

chi_shape = 0.8
chi_energy = (math.sqrt(5.0) - 1.0) / (math.sqrt(5.0) + 1.0)
well_depth = 0.005
cutoff_sq = 20.25
norm_eps = 1e-06

SUB = 8
CENTRE = 6
LIST_ROW = 12
CODE_BITS = 6
ITEM_BITS = 8
ITEM_MASK = 255
LAYER = 16
TESTS = 5
GROUP = 1
UNROLL = 4
TERMS = 20
HELD = 128
VMEM_LIMIT = 32 * 1024 * 1024
PACK_LIMIT = 60 * 1024 * 1024


def dot3(a, b):
    return a[0] * b[0] + a[1] * b[1] + a[2] * b[2]


def cross3(a, b):
    return (
        a[1] * b[2] - a[2] * b[1],
        a[2] * b[0] - a[0] * b[2],
        a[0] * b[1] - a[1] * b[0],
    )


def inverse(value):
    guess = pl.reciprocal(value, approx=True)
    return guess * (2.0 - value * guess)


def bracket(chi, scaled, factor, p, a, b):
    f = factor * (a - scaled * b)
    g = factor * (b - scaled * a)
    y = p * (a * f + b * g)
    cross = factor * scaled
    f_c = chi * (cross * f - factor * g)
    g_c = chi * (cross * g - factor * f)
    return f, g, y, cross, f_c, g_c


def pair_coefficients(d, ui, uj, lift):
    r_sq = dot3(d, d) + lift
    a = dot3(d, ui)
    b = dot3(d, uj)
    c = dot3(ui, uj)
    r_inv = lax.rsqrt(r_sq)
    p = r_inv * r_inv
    p2 = 2.0 * p
    r = r_sq * r_inv
    x = jnp.maximum(1.0 - r_sq * (1.0 / cutoff_sq), 0.0)
    c_shape = chi_shape * c
    c_energy = chi_energy * c
    e1 = lax.rsqrt(1.0 - c_shape * c_shape)
    q = e1 * e1
    q2 = inverse(1.0 - c_energy * c_energy)
    f, g, y, m, f_c, g_c = bracket(chi_shape, c_shape, q, p, a, b)
    f2, g2, y2, m2, f2_c, g2_c = bracket(chi_energy, c_energy, q2, p, a, b)
    sigma = lax.rsqrt(1.0 - chi_shape * y)
    sigma_sq = sigma * sigma
    psi = 1.0 - chi_energy * y2
    s = inverse(r - sigma + 1.0)
    s_sq = s * s
    s6 = s_sq * s_sq * s_sq
    t0 = s6 * (s6 - 1.0)
    t1 = s6 * s * (6.0 - 12.0 * s6)
    t2 = s6 * s_sq * (156.0 * s6 - 42.0)
    ke = (4.0 * well_depth) * e1
    kx = ke * x
    v_ee = kx * (24.0 / cutoff_sq**2)
    kxx = kx * x
    v_e = kxx * (-6.0 / cutoff_sq)
    v = kxx * x
    psi_sq = psi * psi
    psi_sq_t0 = psi_sq * t0
    psi_sq_t1 = psi_sq * t1
    u = v * psi_sq_t0
    slope = v * psi_sq_t1
    slope2 = v * psi_sq * t2
    tau = (-0.5 * chi_shape) * sigma_sq * sigma
    push = (-2.0 * chi_energy) * psi
    v_t1 = v * t1
    d1 = slope * tau
    d2 = push * (v * t0)
    h1 = p2 * d1
    h2 = p2 * d2
    kc = chi_shape * c_shape * q
    fg = chi_shape * f * g
    fg2 = chi_energy * f2 * g2
    u_a = h1 * f + h2 * f2
    u_b = h1 * g + h2 * g2
    u_fg = h1 * fg + h2 * fg2
    u_c = u * kc - u_fg
    v_e_t0 = v_e * psi_sq_t0
    d_e = r_inv * slope + v_e_t0
    u_e = d_e - (h1 * y + h2 * y2)

    p2_sq = p2 * p2
    k11 = p2_sq * (tau * (slope2 * tau + (1.5 * chi_shape) * sigma_sq * slope))
    k12 = p2_sq * (push * v_t1 * tau)
    k22 = p2_sq * ((2.0 * chi_energy * chi_energy) * (v * t0))
    steep = v_e * psi_sq_t1 + slope2 * r_inv
    l1 = p2 * (steep * tau - h1)
    l2 = p2 * (push * (v_e * t0 + v_t1 * r_inv) - h2)
    j1 = (y, f, g, fg)
    j2 = (y2, f2, g2, fg2)
    w1 = [k11 * one + k12 * two for one, two in zip(j1, j2)]
    w2 = [k12 * one + k22 * two for one, two in zip(j1, j2)]

    def quadratic(m_at, n_at):
        return w1[m_at] * j1[n_at] + w2[m_at] * j2[n_at]

    d_ee = v_ee * psi_sq_t0 + r_inv * (2.0 * (v_e * psi_sq_t1)) + p * (slope2 - slope * r_inv)
    h_ee = quadratic(0, 0) - 2.0 * (l1 * y + l2 * y2) + d_ee
    h_ea = l1 * f + l2 * f2 - quadratic(0, 1)
    h_eb = l1 * g + l2 * g2 - quadratic(0, 2)
    h_ec = quadratic(0, 3) - (l1 * fg + l2 * fg2) + kc * u_e
    straight = h1 * q + h2 * q2
    h_aa = quadratic(1, 1) + straight
    h_ab = quadratic(1, 2) - (h1 * m + h2 * m2)
    h_ac = kc * u_a - quadratic(1, 3) + (h1 * f_c + h2 * f2_c)
    h_bb = quadratic(2, 2) + straight
    h_bc = kc * u_b - quadratic(2, 3) + (h1 * g_c + h2 * g2_c)
    bent = (chi_shape * h1) * (f_c * g + f * g_c) + (chi_energy * h2) * (f2_c * g2 + f2 * g2_c)
    twist = kc * kc + (chi_shape * chi_shape) * q * (2.0 * q - 1.0)
    h_cc = quadratic(3, 3) - bent - 2.0 * (kc * u_fg) + u * twist
    gradient = (u_e, u_a, u_b, u_c)
    return gradient, (h_ee, h_ea, h_eb, h_ec, h_aa, h_ab, h_ac, h_bb, h_bc, h_cc), u_a * a + u_c * c


def offsets_of(code, period):
    return [((code >> bits & 3) - 1).astype(jnp.float32) * size for bits, size in zip((4, 2, 0), period)]


def row_of(tiles_ref, tile, k, member):
    return tiles_ref[tile, :, k * member : (k + 1) * member]


def centre_of(code, period, all_ref, member):
    shift = offsets_of(code, period)
    return [row_of(all_ref, code >> CODE_BITS, CENTRE + k, member) + shift[k] for k in range(3)]


def lanes_of(block, member):
    row = lax.broadcasted_iota(jnp.int32, (SUB, member), 0)
    lane = lax.broadcasted_iota(jnp.int32, (SUB, member), 1)
    group = (lane & -LAYER) - (block >> 1) * LAYER
    return (group & (member - 1)) + ((block & 1) * SUB + row)


def picked(block, lanes):
    return jnp.take_along_axis(block, lanes, axis=1, mode="promise_in_bounds")


def box_lanes(member):
    block = lax.broadcasted_iota(jnp.int32, (member // SUB, member), 0)
    lane = lax.broadcasted_iota(jnp.int32, (member // SUB, member), 1)
    return (((lane & -LAYER) - (block >> 1) * LAYER) & (member - 1)) + (block & 1) * SUB


def near_blocks(own_centre, partner, lanes):
    blocks, member = lanes.shape
    zero = jnp.zeros((1, member), jnp.float32)
    box = stacked(partner + [-line for line in partner] + [zero, zero])
    for bit in (1, 2, 4):
        box = jnp.maximum(box, pltpu.roll(box, member - bit, 1))

    def seen(k):
        line = jnp.broadcast_to(box[k : k + 1], (SUB, member))
        return stacked([picked(line, lanes[at : at + SUB]) for at in range(0, blocks, SUB)])

    reach = 0.0
    for k in range(3):
        above = own_centre[k] - seen(k)
        below = -own_centre[k] - seen(3 + k)
        gap = jnp.maximum(jnp.maximum(above, below), 0.0)
        reach = reach + gap * gap
    nearest = jnp.min(reach, axis=1, keepdims=True)
    weight = (1 << lax.broadcasted_iota(jnp.int32, (blocks, 1), 0)).astype(jnp.float32)
    return jnp.sum(jnp.where(nearest < cutoff_sq * 1.001, weight, 0.0)).astype(jnp.int32)


def stacked(parts):
    return jnp.concatenate(parts, axis=0)


def wide(row):
    return jnp.broadcast_to(row, (GROUP * SUB, row.shape[1]))


def partner_rows(row_at, items, lanes):
    rows = []
    for k in range(6):
        parts = []
        for item, lane in zip(items, lanes):
            row = row_at(item >> (ITEM_BITS + CODE_BITS), k)
            parts.append(picked(jnp.broadcast_to(row, lane.shape), lane))
        rows.append(stacked(parts))
    return rows


def folded(total):
    return jnp.sum(total, axis=0, keepdims=True)


def geometry(items, unused, lanes, own_code, own_wide, period, all_ref):
    member = lanes[0].shape[1]
    lane = lax.broadcasted_iota(jnp.int32, (SUB, member), 1)
    lift = []
    shifts = []
    for item, idle, other in zip(items, unused, lanes):
        code = item >> ITEM_BITS
        itself = jnp.where(other == lane, jnp.where(code == own_code, 2.0 * cutoff_sq, 0.0), 0.0)
        lift.append(itself + jnp.where(idle, 2.0 * cutoff_sq, 0.0))
        shifts.append(offsets_of(code, period))
    rows = partner_rows(lambda tile, k: row_of(all_ref, tile, CENTRE + k, member), items, lanes)
    shift = [stacked([jnp.full((SUB, member), one[k]) for one in shifts]) for k in range(3)]
    d = [rows[k] + shift[k] - own_wide[k] for k in range(3)]
    uj = rows[3:]
    gradient, hessian, spin = pair_coefficients(d, own_wide[3:], uj, stacked(lift))
    return list(gradient) + list(hessian) + d + uj, (gradient[1], spin)


def apply(moved_rows, terms, own_wide, moved_wide):
    u_e, u_a, u_b, u_c, h_ee, h_ea, h_eb, h_ec, h_aa, h_ab, h_ac, h_bb, h_bc, h_cc = terms[:14]
    d = terms[14:17]
    uj = terms[17:20]
    ui = own_wide[3:]
    dui = moved_wide[3:]
    dd = [moved_rows[k] - moved_wide[k] for k in range(3)]
    duj = cross3(moved_rows[3:], uj)
    de = dot3(d, dd)
    da = dot3(dd, ui) + dot3(d, dui)
    db = dot3(dd, uj) + dot3(d, duj)
    dc = dot3(dui, uj) + dot3(ui, duj)
    du_e = h_ee * de + h_ea * da + h_eb * db + h_ec * dc
    du_a = h_ea * de + h_aa * da + h_ab * db + h_ac * dc
    du_b = h_eb * de + h_ab * da + h_bb * db + h_bc * dc
    du_c = h_ec * de + h_ac * da + h_bc * db + h_cc * dc
    force = [du_e * d[k] + u_e * dd[k] + du_b * uj[k] + u_b * duj[k] for k in range(3)]
    turn = [du_a * d[k] + u_a * dd[k] + du_c * uj[k] + u_c * duj[k] for k in range(3)]
    return force + turn + [du_a]


def several(body):
    def step_of(step, totals):
        for part in range(UNROLL):
            totals = body(step * UNROLL + part, totals)
        return totals

    return step_of


def group_items(step, item_ref, item_count):
    at = [step * GROUP + part for part in range(GROUP)]
    return [item_ref[1 + place] for place in at], [place >= item_count for place in at]


def added(totals, news):
    return tuple(
        total + sum(new[part * SUB : (part + 1) * SUB] for part in range(GROUP)) for total, new in zip(totals, news)
    )


def close(sums, kept, spin, u, t):
    force = [-(sums[k] + u[k] * sums[6] + t[k] * kept) for k in range(3)]
    return force + list(cross3(u, [sums[3 + k] - t[k] * spin for k in range(3)]))


def spread(rows, out_ref):
    member = rows[0].shape[1]
    for k, row in enumerate(rows):
        out_ref[:, :, k * member : (k + 1) * member] = jnp.broadcast_to(row[None], (out_ref.shape[0], 1, member))


def pack_kernel(*refs):
    sources, out_ref, targets, sems = refs[:4], refs[4], refs[5:9], refs[9]
    config_ref, start_ref, list_ref, count_ref = targets
    copies = [
        pltpu.make_async_copy(source, target, sems.at[at]) for at, (source, target) in enumerate(zip(sources, targets))
    ]
    for copy in copies:
        copy.start()
    copies[2].wait()
    copies[3].wait()
    member = config_ref.shape[1]
    lane = lax.broadcasted_iota(jnp.int32, (1, member), 1)
    fields, slots = list_ref.shape[1], list_ref.shape[3]
    line = jnp.full((1, member), -9, jnp.int32)
    for field in range(fields):
        for slot in range(slots):
            line = jnp.where(lane == field * slots + slot, list_ref[0, field, 0, slot], line)
    line = jnp.where((lane >= count_ref[0, 0]) & (lane < slots), -9, line).astype(jnp.float32)
    copies[0].wait()
    copies[1].wait()
    rows = [ref[k : k + 1, :] for ref in (start_ref, config_ref) for k in range(6)]
    spread(rows + [line], out_ref)


def first_kernel(
    rows,
    cols,
    slots,
    period,
    all_ref,
    out_ref,
    item_ref,
    coef_ref,
    kept_ref,
    entry_ref,
    code_ref,
    code_smem,
    sem,
):
    member = kept_ref.shape[1]
    row_id = lax.axis_index("row")
    col_id = lax.axis_index("col")
    own = row_id * cols + col_id
    blocks = member // SUB

    def field(line, at):
        return line if at == 0 else pltpu.roll(line, member - at * slots, 1)

    row_f = row_id.astype(jnp.float32)
    col_f = col_id.astype(jnp.float32)
    lines = [row_of(all_ref, row_id * cols + col, LIST_ROW, member) for col in range(cols)]
    lines += [row_of(all_ref, row * cols + col_id, LIST_ROW, member) for row in range(rows)]
    line = jnp.concatenate(lines, axis=0)
    at = lax.broadcasted_iota(jnp.int32, line.shape, 0).astype(jnp.float32)
    near = at < float(cols)
    other = field(line, 1)
    offset = field(line, 2) * 16.0 + field(line, 3) * 4.0 + field(line, 4)
    partner = jnp.where(near, other * float(cols) + at, (at - float(cols)) * float(cols) + line)
    code = partner * float(1 << CODE_BITS) + (jnp.where(near, offset, -offset) + 21.0)
    hit = jnp.where(near, line - col_f, jnp.where(line >= 0.0, other - row_f, 1.0)) == 0.0
    code_ref[...] = jnp.where(hit, code, -1.0).astype(jnp.int32)
    copy = pltpu.make_async_copy(code_ref, code_smem, sem)
    copy.start()
    own_code = own * (1 << CODE_BITS) + 21
    own_moved = [row_of(all_ref, own, k, member) for k in range(6)]
    own_frame = [row_of(all_ref, own, CENTRE + k, member) for k in range(6)]
    lanes = box_lanes(member)
    own_centre = [jnp.broadcast_to(line, lanes.shape) for line in own_frame[:3]]

    def append(code, bits, count):
        for block in range(blocks):
            item_ref[1 + count] = (code << ITEM_BITS) + block
            count = count + (bits >> block & 1)
        return count

    items = append(own_code, near_blocks(own_centre, own_frame[:3], lanes), jnp.int32(0))
    copy.wait()

    def gather(line, count):
        for slot in range(slots):
            code = code_smem[line, slot]
            entry_ref[count] = code
            count = count + (code >= 0).astype(jnp.int32)
        return count

    entries = lax.fori_loop(0, rows + cols, gather, jnp.int32(0))
    for part in range(TESTS):
        entry_ref[entries + part] = own_code

    def prepare(step, count):
        codes = [entry_ref[step * TESTS + part] for part in range(TESTS)]
        bits = [near_blocks(own_centre, centre_of(code, period, all_ref, member), lanes) for code in codes]
        for part in range(TESTS):
            count = append(codes[part], jnp.where(step * TESTS + part < entries, bits[part], 0), count)
        return count

    items = lax.fori_loop(0, (entries + TESTS - 1) // TESTS, prepare, items)
    for part in range(GROUP * UNROLL):
        item_ref[1 + items + part] = own_code << ITEM_BITS
    item_ref[0] = items

    held = coef_ref.shape[0] // (TERMS * GROUP * UNROLL * SUB)
    steps = (items + GROUP * UNROLL - 1) // (GROUP * UNROLL)
    u = own_frame[3:]
    t = cross3(own_moved[3:], u)
    own_wide = [wide(line) for line in own_frame]
    moved_wide = [wide(line) for line in [*own_moved[:3], *t]]

    def derive(step, totals):
        group, unused = group_items(step, item_ref, items)
        lanes = [lanes_of(item & ITEM_MASK, member) for item in group]
        terms, sums = geometry(group, unused, lanes, own_code, own_wide, period, all_ref)
        moved_rows = partner_rows(lambda tile, k: row_of(all_ref, tile, k, member), group, lanes)
        return terms, added(totals, apply(moved_rows, terms, own_wide, moved_wide) + list(sums))

    def keep(step, totals):
        terms, totals = derive(step, totals)
        start = pl.multiple_of(step * (TERMS * GROUP * SUB), SUB)
        for k in range(TERMS):
            coef_ref[pl.ds(start + k * GROUP * SUB, GROUP * SUB), :] = terms[k]
        return totals

    zero = jnp.zeros((SUB, member), jnp.float32)
    totals = lax.fori_loop(0, jnp.minimum(steps, held), several(keep), (zero,) * 9)
    totals = lax.fori_loop(held, steps, several(lambda step, before: derive(step, before)[1]), totals)
    sums = [folded(total) for total in totals]
    kept_ref[...] = jnp.concatenate(sums[7:], axis=0)
    spread(close(sums, sums[7], sums[8], u, t), out_ref)


def scalar_of(block):
    return jnp.sum(jnp.sum(block, axis=0, keepdims=True), axis=1, keepdims=True)


def second_kernel(
    cols,
    total_entries,
    period,
    item_ref,
    coef_ref,
    kept_ref,
    all_ref,
    image_ref,
    out_ref,
    pair_ref,
    scalar_ref,
    second_ref,
):
    own = lax.axis_index("row") * cols + lax.axis_index("col")
    member = kept_ref.shape[1]
    basis = all_ref[:, 0, 0 : 6 * member]
    image = image_ref[:, 0, :]
    portion = 1.0 / total_entries

    def total_of(block):
        return scalar_of(sum(block[:, k * member : (k + 1) * member] for k in range(6)))

    norm_sq = total_of(basis * basis) * portion + norm_eps
    norm_inv = lax.rsqrt(norm_sq)
    alpha = total_of(basis * image) * portion / norm_sq
    second = image - alpha * basis
    second_ref[:, 0, :] = second
    beta_sq = total_of(second * second) * portion / norm_sq + norm_eps
    beta = jnp.sqrt(beta_sq)
    scale = norm_inv * lax.rsqrt(beta_sq)

    own_code = own * (1 << CODE_BITS) + 21
    items = item_ref[0]
    held = coef_ref.shape[0] // (TERMS * GROUP * UNROLL * SUB)
    steps = (items + GROUP * UNROLL - 1) // (GROUP * UNROLL)

    def moved_row(tile, k):
        return row_of(second_ref, tile, k, member)

    own_moved = [moved_row(own, k) for k in range(6)]
    own_frame = [row_of(all_ref, own, CENTRE + k, member) for k in range(6)]
    u = own_frame[3:]
    t = cross3(own_moved[3:], u)
    own_wide = [wide(line) for line in own_frame]
    moved_wide = [wide(line) for line in [*own_moved[:3], *t]]

    def visit(step, totals):
        group, _ = group_items(step, item_ref, items)
        lanes = [lanes_of(item & ITEM_MASK, member) for item in group]
        start = pl.multiple_of(step * (TERMS * GROUP * SUB), SUB)
        terms = [coef_ref[pl.ds(start + k * GROUP * SUB, GROUP * SUB), :] for k in range(TERMS)]
        return added(totals, apply(partner_rows(moved_row, group, lanes), terms, own_wide, moved_wide))

    def visit_again(step, totals):
        group, unused = group_items(step, item_ref, items)
        lanes = [lanes_of(item & ITEM_MASK, member) for item in group]
        terms, _ = geometry(group, unused, lanes, own_code, own_wide, period, all_ref)
        return added(totals, apply(partner_rows(moved_row, group, lanes), terms, own_wide, moved_wide))

    zero = jnp.zeros((SUB, member), jnp.float32)
    totals = lax.fori_loop(0, jnp.minimum(steps, held), several(visit), (zero,) * 7)
    totals = lax.fori_loop(held, steps, several(visit_again), totals)
    sums = [folded(total) for total in totals]
    product = close(sums, kept_ref[0:1, :], kept_ref[1:2, :], u, t)
    fill = [jnp.zeros((1, member), jnp.float32)] * (SUB - len(product))
    first = stacked([row_of(all_ref, own, k, member) for k in range(6)] + fill)
    image = stacked(product + fill) * scale - (beta * norm_inv) * first
    second = stacked(own_moved + fill) * scale
    inner = scalar_of(second * image)
    weight = scalar_of(second * second)
    local_alpha = jnp.where(weight > 1e-30, inner / jnp.maximum(weight, 1e-30), 0.0)
    rest = image - local_alpha * second
    size = scalar_of(rest * rest)
    slant = scalar_of(second * rest)
    lane = lax.broadcasted_iota(jnp.int32, (1, member), 1)
    line = jnp.zeros((1, member), jnp.float32)
    for at, value in enumerate((inner, weight, local_alpha, size, slant)):
        line = jnp.where(lane == at, value, line)
    out_ref[...] = jnp.broadcast_to(line[None], out_ref.shape)
    pair_ref[0] = second
    pair_ref[1] = image
    scalar_ref[...] = jnp.where(lane == 0, alpha, jnp.where(lane == 1, beta, 0.0))


def last_kernel(total_entries, pair_ref, scalar_ref, line_ref, mode_ref, coefficient_ref):
    lines = line_ref[:, 0, :]
    alpha = jnp.sum(lines[:, 0:1], axis=0, keepdims=True) / total_entries
    away = lines[:, 2:3] - alpha
    parts = lines[:, 3:4] + away * (away * lines[:, 1:2] + 2.0 * lines[:, 4:5])
    beta = jnp.sqrt(jnp.sum(parts, axis=0, keepdims=True) / total_entries + norm_eps)
    mode = (pair_ref[1] - alpha * pair_ref[0]) / beta
    mode_ref[...] = mode[: mode_ref.shape[0]]
    for at, value in enumerate((scalar_ref[0:1, 0:1], scalar_ref[0:1, 1:2], alpha, beta)):
        coefficient_ref[at] = jnp.sum(value)


def local(config, start, tile_list, tile_count):
    dof, member = config.shape
    row_devices = lax.axis_size("row")
    col_devices = lax.axis_size("col")
    devices = row_devices * col_devices
    total_entries = float(dof * member * devices)
    period = (5.0, 5.0, 3.5 * (member // 16))
    slots = tile_list.shape[2]
    longest = (row_devices + col_devices) * slots + 1

    def shaped(*shape):
        return jax.ShapeDtypeStruct(shape, jnp.float32)

    def everywhere(copies):
        return lax.all_to_all(copies, ("row", "col"), 0, 0, tiled=True)

    params = pltpu.CompilerParams(vmem_limit_bytes=VMEM_LIMIT)
    vmem = pl.BlockSpec(memory_space=pltpu.VMEM)
    smem = pl.BlockSpec(memory_space=pltpu.SMEM)

    outside = pl.BlockSpec(memory_space=pl.ANY)
    packed = pl.pallas_call(
        pack_kernel,
        out_shape=shaped(devices, 1, (LIST_ROW + 1) * member),
        in_specs=[outside] * 4,
        out_specs=vmem,
        scratch_shapes=[
            pltpu.VMEM((dof, member), jnp.float32),
            pltpu.VMEM((dof, member), jnp.float32),
            pltpu.SMEM((1, tile_list.shape[3], 1, slots), jnp.int32),
            pltpu.SMEM((1, 1), jnp.int32),
            pltpu.SemaphoreType.DMA((4,)),
        ],
        compiler_params=pltpu.CompilerParams(vmem_limit_bytes=PACK_LIMIT),
    )(config, start, jnp.transpose(tile_list, (0, 3, 1, 2)), tile_count)
    together = everywhere(packed)

    held_rows = HELD // GROUP * (TERMS * GROUP * SUB)
    image, items, terms, kept = pl.pallas_call(
        functools.partial(first_kernel, row_devices, col_devices, slots, period),
        out_shape=(
            shaped(devices, 1, dof * member),
            jax.ShapeDtypeStruct((1 + longest * (member // SUB) + GROUP * UNROLL,), jnp.int32),
            shaped(held_rows, member),
            shaped(2, member),
        ),
        in_specs=[vmem],
        out_specs=(vmem, smem, vmem, vmem),
        scratch_shapes=[
            pltpu.SMEM((longest + TESTS,), jnp.int32),
            pltpu.VMEM((row_devices + col_devices, member), jnp.int32),
            pltpu.SMEM((row_devices + col_devices, member), jnp.int32),
            pltpu.SemaphoreType.DMA,
        ],
        compiler_params=params,
    )(together)
    image = everywhere(image)

    line, pair, scalars = pl.pallas_call(
        functools.partial(second_kernel, col_devices, total_entries, period),
        out_shape=(shaped(devices, 1, member), shaped(2, SUB, member), shaped(1, member)),
        in_specs=[smem] + [vmem] * 4,
        out_specs=(vmem, vmem, vmem),
        scratch_shapes=[
            pltpu.VMEM((devices, 1, dof * member), jnp.float32),
        ],
        compiler_params=params,
    )(items, terms, kept, together, image)
    line = everywhere(line)

    mode, coefficients = pl.pallas_call(
        functools.partial(last_kernel, total_entries),
        out_shape=(shaped(dof, member), shaped(4)),
        in_specs=[vmem] * 3,
        out_specs=(vmem, smem),
        compiler_params=params,
    )(pair, scalars, line)
    return (coefficients, mode)


def solution(mesh):
    placed = (
        P(None, ("row", "col")),
        P(None, ("row", "col")),
        P("row", "col", None, None),
        P("row", "col"),
    )
    return jax.shard_map(
        local, mesh=mesh, in_specs=placed, out_specs=(P(), P(None, ("row", "col"))), check_vma=False
    )
```

```python
import functools
import math

import jax
import jax.numpy as jnp
from jax import lax
from jax.experimental import pallas as pl
from jax.experimental.pallas import tpu as pltpu
from jax.sharding import PartitionSpec as P

chi_shape = 0.8
chi_energy = (math.sqrt(5.0) - 1.0) / (math.sqrt(5.0) + 1.0)
well_depth = 0.005
cutoff_sq = 20.25
norm_eps = 1e-06

SUB = 8
CENTRE = 6
LIST_ROW = 12
CODE_BITS = 6
ITEM_BITS = 8
ITEM_MASK = 255
LAYER = 16
TESTS = 5
GROUP = 2
UNROLL = 3
TERMS = 20
HELD = 128
VMEM_LIMIT = 32 * 1024 * 1024
PACK_LIMIT = 60 * 1024 * 1024


def dot3(a, b):
    return a[0] * b[0] + a[1] * b[1] + a[2] * b[2]


def cross3(a, b):
    return (
        a[1] * b[2] - a[2] * b[1],
        a[2] * b[0] - a[0] * b[2],
        a[0] * b[1] - a[1] * b[0],
    )


def inverse(value):
    guess = pl.reciprocal(value, approx=True)
    return guess * (2.0 - value * guess)


def bracket(chi, scaled, factor, p, a, b):
    f = factor * (a - scaled * b)
    g = factor * (b - scaled * a)
    y = p * (a * f + b * g)
    cross = factor * scaled
    f_c = chi * (cross * f - factor * g)
    g_c = chi * (cross * g - factor * f)
    return f, g, y, cross, f_c, g_c


def pair_coefficients(d, ui, uj, lift):
    r_sq = dot3(d, d) + lift
    a = dot3(d, ui)
    b = dot3(d, uj)
    c = dot3(ui, uj)
    r_inv = lax.rsqrt(r_sq)
    p = r_inv * r_inv
    p2 = 2.0 * p
    r = r_sq * r_inv
    x = jnp.maximum(1.0 - r_sq * (1.0 / cutoff_sq), 0.0)
    c_shape = chi_shape * c
    c_energy = chi_energy * c
    e1 = lax.rsqrt(1.0 - c_shape * c_shape)
    q = e1 * e1
    q2 = inverse(1.0 - c_energy * c_energy)
    f, g, y, m, f_c, g_c = bracket(chi_shape, c_shape, q, p, a, b)
    f2, g2, y2, m2, f2_c, g2_c = bracket(chi_energy, c_energy, q2, p, a, b)
    sigma = lax.rsqrt(1.0 - chi_shape * y)
    sigma_sq = sigma * sigma
    psi = 1.0 - chi_energy * y2
    s = inverse(r - sigma + 1.0)
    s_sq = s * s
    s6 = s_sq * s_sq * s_sq
    t0 = s6 * (s6 - 1.0)
    t1 = s6 * s * (6.0 - 12.0 * s6)
    t2 = s6 * s_sq * (156.0 * s6 - 42.0)
    ke = (4.0 * well_depth) * e1
    kx = ke * x
    v_ee = kx * (24.0 / cutoff_sq**2)
    kxx = kx * x
    v_e = kxx * (-6.0 / cutoff_sq)
    v = kxx * x
    psi_sq = psi * psi
    psi_sq_t0 = psi_sq * t0
    psi_sq_t1 = psi_sq * t1
    u = v * psi_sq_t0
    slope = v * psi_sq_t1
    slope2 = v * psi_sq * t2
    tau = (-0.5 * chi_shape) * sigma_sq * sigma
    push = (-2.0 * chi_energy) * psi
    v_t1 = v * t1
    d1 = slope * tau
    d2 = push * (v * t0)
    h1 = p2 * d1
    h2 = p2 * d2
    kc = chi_shape * c_shape * q
    fg = chi_shape * f * g
    fg2 = chi_energy * f2 * g2
    u_a = h1 * f + h2 * f2
    u_b = h1 * g + h2 * g2
    u_fg = h1 * fg + h2 * fg2
    u_c = u * kc - u_fg
    v_e_t0 = v_e * psi_sq_t0
    d_e = r_inv * slope + v_e_t0
    u_e = d_e - (h1 * y + h2 * y2)

    p2_sq = p2 * p2
    k11 = p2_sq * (tau * (slope2 * tau + (1.5 * chi_shape) * sigma_sq * slope))
    k12 = p2_sq * (push * v_t1 * tau)
    k22 = p2_sq * ((2.0 * chi_energy * chi_energy) * (v * t0))
    steep = v_e * psi_sq_t1 + slope2 * r_inv
    l1 = p2 * (steep * tau - h1)
    l2 = p2 * (push * (v_e * t0 + v_t1 * r_inv) - h2)
    j1 = (y, f, g, fg)
    j2 = (y2, f2, g2, fg2)
    w1 = [k11 * one + k12 * two for one, two in zip(j1, j2)]
    w2 = [k12 * one + k22 * two for one, two in zip(j1, j2)]

    def quadratic(m_at, n_at):
        return w1[m_at] * j1[n_at] + w2[m_at] * j2[n_at]

    d_ee = v_ee * psi_sq_t0 + r_inv * (2.0 * (v_e * psi_sq_t1)) + p * (slope2 - slope * r_inv)
    h_ee = quadratic(0, 0) - 2.0 * (l1 * y + l2 * y2) + d_ee
    h_ea = l1 * f + l2 * f2 - quadratic(0, 1)
    h_eb = l1 * g + l2 * g2 - quadratic(0, 2)
    h_ec = quadratic(0, 3) - (l1 * fg + l2 * fg2) + kc * u_e
    straight = h1 * q + h2 * q2
    h_aa = quadratic(1, 1) + straight
    h_ab = quadratic(1, 2) - (h1 * m + h2 * m2)
    h_ac = kc * u_a - quadratic(1, 3) + (h1 * f_c + h2 * f2_c)
    h_bb = quadratic(2, 2) + straight
    h_bc = kc * u_b - quadratic(2, 3) + (h1 * g_c + h2 * g2_c)
    bent = (chi_shape * h1) * (f_c * g + f * g_c) + (chi_energy * h2) * (f2_c * g2 + f2 * g2_c)
    twist = kc * kc + (chi_shape * chi_shape) * q * (2.0 * q - 1.0)
    h_cc = quadratic(3, 3) - bent - 2.0 * (kc * u_fg) + u * twist
    gradient = (u_e, u_a, u_b, u_c)
    return gradient, (h_ee, h_ea, h_eb, h_ec, h_aa, h_ab, h_ac, h_bb, h_bc, h_cc), u_a * a + u_c * c


def offsets_of(code, period):
    return [((code >> bits & 3) - 1).astype(jnp.float32) * size for bits, size in zip((4, 2, 0), period)]


def row_of(tiles_ref, tile, k, member):
    return tiles_ref[tile, :, k * member : (k + 1) * member]


def centre_of(code, period, all_ref, member):
    shift = offsets_of(code, period)
    return [row_of(all_ref, code >> CODE_BITS, CENTRE + k, member) + shift[k] for k in range(3)]


def lanes_of(block, member):
    row = lax.broadcasted_iota(jnp.int32, (SUB, member), 0)
    lane = lax.broadcasted_iota(jnp.int32, (SUB, member), 1)
    group = (lane & -LAYER) - (block >> 1) * LAYER
    return (group & (member - 1)) + ((block & 1) * SUB + row)


def picked(block, lanes):
    return jnp.take_along_axis(block, lanes, axis=1, mode="promise_in_bounds")


def box_lanes(member):
    block = lax.broadcasted_iota(jnp.int32, (member // SUB, member), 0)
    lane = lax.broadcasted_iota(jnp.int32, (member // SUB, member), 1)
    return (((lane & -LAYER) - (block >> 1) * LAYER) & (member - 1)) + (block & 1) * SUB


def near_blocks(own_centre, partner, lanes):
    blocks, member = lanes.shape
    zero = jnp.zeros((1, member), jnp.float32)
    box = stacked(partner + [-line for line in partner] + [zero, zero])
    for bit in (1, 2, 4):
        box = jnp.maximum(box, pltpu.roll(box, member - bit, 1))

    def seen(k):
        line = jnp.broadcast_to(box[k : k + 1], (SUB, member))
        return stacked([picked(line, lanes[at : at + SUB]) for at in range(0, blocks, SUB)])

    reach = 0.0
    for k in range(3):
        above = own_centre[k] - seen(k)
        below = -own_centre[k] - seen(3 + k)
        gap = jnp.maximum(jnp.maximum(above, below), 0.0)
        reach = reach + gap * gap
    nearest = jnp.min(reach, axis=1, keepdims=True)
    weight = (1 << lax.broadcasted_iota(jnp.int32, (blocks, 1), 0)).astype(jnp.float32)
    return jnp.sum(jnp.where(nearest < cutoff_sq * 1.001, weight, 0.0)).astype(jnp.int32)


def stacked(parts):
    return jnp.concatenate(parts, axis=0)


def wide(row):
    return jnp.broadcast_to(row, (GROUP * SUB, row.shape[1]))


def partner_rows(row_at, items, lanes):
    rows = []
    for k in range(6):
        parts = []
        for item, lane in zip(items, lanes):
            row = row_at(item >> (ITEM_BITS + CODE_BITS), k)
            parts.append(picked(jnp.broadcast_to(row, lane.shape), lane))
        rows.append(stacked(parts))
    return rows


def folded(total):
    return jnp.sum(total, axis=0, keepdims=True)


def geometry(items, unused, lanes, own_code, own_wide, period, all_ref):
    member = lanes[0].shape[1]
    lane = lax.broadcasted_iota(jnp.int32, (SUB, member), 1)
    lift = []
    shifts = []
    for item, idle, other in zip(items, unused, lanes):
        code = item >> ITEM_BITS
        itself = jnp.where(other == lane, jnp.where(code == own_code, 2.0 * cutoff_sq, 0.0), 0.0)
        lift.append(itself + jnp.where(idle, 2.0 * cutoff_sq, 0.0))
        shifts.append(offsets_of(code, period))
    rows = partner_rows(lambda tile, k: row_of(all_ref, tile, CENTRE + k, member), items, lanes)
    shift = [stacked([jnp.full((SUB, member), one[k]) for one in shifts]) for k in range(3)]
    d = [rows[k] + shift[k] - own_wide[k] for k in range(3)]
    uj = rows[3:]
    gradient, hessian, spin = pair_coefficients(d, own_wide[3:], uj, stacked(lift))
    return list(gradient) + list(hessian) + d + uj, (gradient[1], spin)


def apply(moved_rows, terms, own_wide, moved_wide):
    u_e, u_a, u_b, u_c, h_ee, h_ea, h_eb, h_ec, h_aa, h_ab, h_ac, h_bb, h_bc, h_cc = terms[:14]
    d = terms[14:17]
    uj = terms[17:20]
    ui = own_wide[3:]
    dui = moved_wide[3:]
    dd = [moved_rows[k] - moved_wide[k] for k in range(3)]
    duj = cross3(moved_rows[3:], uj)
    de = dot3(d, dd)
    da = dot3(dd, ui) + dot3(d, dui)
    db = dot3(dd, uj) + dot3(d, duj)
    dc = dot3(dui, uj) + dot3(ui, duj)
    du_e = h_ee * de + h_ea * da + h_eb * db + h_ec * dc
    du_a = h_ea * de + h_aa * da + h_ab * db + h_ac * dc
    du_b = h_eb * de + h_ab * da + h_bb * db + h_bc * dc
    du_c = h_ec * de + h_ac * da + h_bc * db + h_cc * dc
    force = [du_e * d[k] + u_e * dd[k] + du_b * uj[k] + u_b * duj[k] for k in range(3)]
    turn = [du_a * d[k] + u_a * dd[k] + du_c * uj[k] + u_c * duj[k] for k in range(3)]
    return force + turn + [du_a]


def several(body):
    def step_of(step, totals):
        for part in range(UNROLL):
            totals = body(step * UNROLL + part, totals)
        return totals

    return step_of


def group_items(step, item_ref, item_count):
    at = [step * GROUP + part for part in range(GROUP)]
    return [item_ref[1 + place] for place in at], [place >= item_count for place in at]


def added(totals, news):
    return tuple(
        total + sum(new[part * SUB : (part + 1) * SUB] for part in range(GROUP)) for total, new in zip(totals, news)
    )


def close(sums, kept, spin, u, t):
    force = [-(sums[k] + u[k] * sums[6] + t[k] * kept) for k in range(3)]
    return force + list(cross3(u, [sums[3 + k] - t[k] * spin for k in range(3)]))


def spread(rows, out_ref):
    member = rows[0].shape[1]
    for k, row in enumerate(rows):
        out_ref[:, :, k * member : (k + 1) * member] = jnp.broadcast_to(row[None], (out_ref.shape[0], 1, member))


def pack_kernel(*refs):
    sources, out_ref, targets, sems = refs[:4], refs[4], refs[5:9], refs[9]
    config_ref, start_ref, list_ref, count_ref = targets
    copies = [
        pltpu.make_async_copy(source, target, sems.at[at]) for at, (source, target) in enumerate(zip(sources, targets))
    ]
    for copy in copies:
        copy.start()
    copies[2].wait()
    copies[3].wait()
    member = config_ref.shape[1]
    lane = lax.broadcasted_iota(jnp.int32, (1, member), 1)
    fields, slots = list_ref.shape[1], list_ref.shape[3]
    line = jnp.full((1, member), -9, jnp.int32)
    for field in range(fields):
        for slot in range(slots):
            line = jnp.where(lane == field * slots + slot, list_ref[0, field, 0, slot], line)
    line = jnp.where((lane >= count_ref[0, 0]) & (lane < slots), -9, line).astype(jnp.float32)
    copies[0].wait()
    copies[1].wait()
    rows = [ref[k : k + 1, :] for ref in (start_ref, config_ref) for k in range(6)]
    spread(rows + [line], out_ref)


def first_kernel(
    rows,
    cols,
    slots,
    period,
    all_ref,
    out_ref,
    item_ref,
    coef_ref,
    kept_ref,
    entry_ref,
    code_ref,
    code_smem,
    sem,
):
    member = kept_ref.shape[1]
    row_id = lax.axis_index("row")
    col_id = lax.axis_index("col")
    own = row_id * cols + col_id
    blocks = member // SUB

    def field(line, at):
        return line if at == 0 else pltpu.roll(line, member - at * slots, 1)

    row_f = row_id.astype(jnp.float32)
    col_f = col_id.astype(jnp.float32)
    lines = [row_of(all_ref, row_id * cols + col, LIST_ROW, member) for col in range(cols)]
    lines += [row_of(all_ref, row * cols + col_id, LIST_ROW, member) for row in range(rows)]
    line = jnp.concatenate(lines, axis=0)
    at = lax.broadcasted_iota(jnp.int32, line.shape, 0).astype(jnp.float32)
    near = at < float(cols)
    other = field(line, 1)
    offset = field(line, 2) * 16.0 + field(line, 3) * 4.0 + field(line, 4)
    partner = jnp.where(near, other * float(cols) + at, (at - float(cols)) * float(cols) + line)
    code = partner * float(1 << CODE_BITS) + (jnp.where(near, offset, -offset) + 21.0)
    hit = jnp.where(near, line - col_f, jnp.where(line >= 0.0, other - row_f, 1.0)) == 0.0
    code_ref[...] = jnp.where(hit, code, -1.0).astype(jnp.int32)
    copy = pltpu.make_async_copy(code_ref, code_smem, sem)
    copy.start()
    own_code = own * (1 << CODE_BITS) + 21
    own_moved = [row_of(all_ref, own, k, member) for k in range(6)]
    own_frame = [row_of(all_ref, own, CENTRE + k, member) for k in range(6)]
    lanes = box_lanes(member)
    own_centre = [jnp.broadcast_to(line, lanes.shape) for line in own_frame[:3]]

    def append(code, bits, count):
        for block in range(blocks):
            item_ref[1 + count] = (code << ITEM_BITS) + block
            count = count + (bits >> block & 1)
        return count

    items = append(own_code, near_blocks(own_centre, own_frame[:3], lanes), jnp.int32(0))
    copy.wait()

    def gather(line, count):
        for slot in range(slots):
            code = code_smem[line, slot]
            entry_ref[count] = code
            count = count + (code >= 0).astype(jnp.int32)
        return count

    entries = lax.fori_loop(0, rows + cols, gather, jnp.int32(0))
    for part in range(TESTS):
        entry_ref[entries + part] = own_code

    def prepare(step, count):
        codes = [entry_ref[step * TESTS + part] for part in range(TESTS)]
        bits = [near_blocks(own_centre, centre_of(code, period, all_ref, member), lanes) for code in codes]
        for part in range(TESTS):
            count = append(codes[part], jnp.where(step * TESTS + part < entries, bits[part], 0), count)
        return count

    items = lax.fori_loop(0, (entries + TESTS - 1) // TESTS, prepare, items)
    for part in range(GROUP * UNROLL):
        item_ref[1 + items + part] = own_code << ITEM_BITS
    item_ref[0] = items

    held = coef_ref.shape[0] // (TERMS * GROUP * UNROLL * SUB)
    steps = (items + GROUP * UNROLL - 1) // (GROUP * UNROLL)
    u = own_frame[3:]
    t = cross3(own_moved[3:], u)
    own_wide = [wide(line) for line in own_frame]
    moved_wide = [wide(line) for line in [*own_moved[:3], *t]]

    def derive(step, totals):
        group, unused = group_items(step, item_ref, items)
        lanes = [lanes_of(item & ITEM_MASK, member) for item in group]
        terms, sums = geometry(group, unused, lanes, own_code, own_wide, period, all_ref)
        moved_rows = partner_rows(lambda tile, k: row_of(all_ref, tile, k, member), group, lanes)
        return terms, added(totals, apply(moved_rows, terms, own_wide, moved_wide) + list(sums))

    def keep(step, totals):
        terms, totals = derive(step, totals)
        start = pl.multiple_of(step * (TERMS * GROUP * SUB), SUB)
        for k in range(TERMS):
            coef_ref[pl.ds(start + k * GROUP * SUB, GROUP * SUB), :] = terms[k]
        return totals

    zero = jnp.zeros((SUB, member), jnp.float32)
    totals = lax.fori_loop(0, jnp.minimum(steps, held), several(keep), (zero,) * 9)
    totals = lax.fori_loop(held, steps, several(lambda step, before: derive(step, before)[1]), totals)
    sums = [folded(total) for total in totals]
    kept_ref[...] = jnp.concatenate(sums[7:], axis=0)
    spread(close(sums, sums[7], sums[8], u, t), out_ref)


def scalar_of(block):
    return jnp.sum(jnp.sum(block, axis=0, keepdims=True), axis=1, keepdims=True)


def second_kernel(
    cols,
    total_entries,
    period,
    item_ref,
    coef_ref,
    kept_ref,
    all_ref,
    image_ref,
    out_ref,
    pair_ref,
    scalar_ref,
    second_ref,
):
    own = lax.axis_index("row") * cols + lax.axis_index("col")
    member = kept_ref.shape[1]
    basis = all_ref[:, 0, 0 : 6 * member]
    image = image_ref[:, 0, :]
    portion = 1.0 / total_entries

    def total_of(block):
        return scalar_of(sum(block[:, k * member : (k + 1) * member] for k in range(6)))

    norm_sq = total_of(basis * basis) * portion + norm_eps
    norm_inv = lax.rsqrt(norm_sq)
    alpha = total_of(basis * image) * portion / norm_sq
    second = image - alpha * basis
    second_ref[:, 0, :] = second
    beta_sq = total_of(second * second) * portion / norm_sq + norm_eps
    beta = jnp.sqrt(beta_sq)
    scale = norm_inv * lax.rsqrt(beta_sq)

    own_code = own * (1 << CODE_BITS) + 21
    items = item_ref[0]
    held = coef_ref.shape[0] // (TERMS * GROUP * UNROLL * SUB)
    steps = (items + GROUP * UNROLL - 1) // (GROUP * UNROLL)

    def moved_row(tile, k):
        return row_of(second_ref, tile, k, member)

    own_moved = [moved_row(own, k) for k in range(6)]
    own_frame = [row_of(all_ref, own, CENTRE + k, member) for k in range(6)]
    u = own_frame[3:]
    t = cross3(own_moved[3:], u)
    own_wide = [wide(line) for line in own_frame]
    moved_wide = [wide(line) for line in [*own_moved[:3], *t]]

    def visit(step, totals):
        group, _ = group_items(step, item_ref, items)
        lanes = [lanes_of(item & ITEM_MASK, member) for item in group]
        start = pl.multiple_of(step * (TERMS * GROUP * SUB), SUB)
        terms = [coef_ref[pl.ds(start + k * GROUP * SUB, GROUP * SUB), :] for k in range(TERMS)]
        return added(totals, apply(partner_rows(moved_row, group, lanes), terms, own_wide, moved_wide))

    def visit_again(step, totals):
        group, unused = group_items(step, item_ref, items)
        lanes = [lanes_of(item & ITEM_MASK, member) for item in group]
        terms, _ = geometry(group, unused, lanes, own_code, own_wide, period, all_ref)
        return added(totals, apply(partner_rows(moved_row, group, lanes), terms, own_wide, moved_wide))

    zero = jnp.zeros((SUB, member), jnp.float32)
    totals = lax.fori_loop(0, jnp.minimum(steps, held), several(visit), (zero,) * 7)
    totals = lax.fori_loop(held, steps, several(visit_again), totals)
    sums = [folded(total) for total in totals]
    product = close(sums, kept_ref[0:1, :], kept_ref[1:2, :], u, t)
    fill = [jnp.zeros((1, member), jnp.float32)] * (SUB - len(product))
    first = stacked([row_of(all_ref, own, k, member) for k in range(6)] + fill)
    image = stacked(product + fill) * scale - (beta * norm_inv) * first
    second = stacked(own_moved + fill) * scale
    inner = scalar_of(second * image)
    weight = scalar_of(second * second)
    local_alpha = jnp.where(weight > 1e-30, inner / jnp.maximum(weight, 1e-30), 0.0)
    rest = image - local_alpha * second
    size = scalar_of(rest * rest)
    slant = scalar_of(second * rest)
    lane = lax.broadcasted_iota(jnp.int32, (1, member), 1)
    line = jnp.zeros((1, member), jnp.float32)
    for at, value in enumerate((inner, weight, local_alpha, size, slant)):
        line = jnp.where(lane == at, value, line)
    out_ref[...] = jnp.broadcast_to(line[None], out_ref.shape)
    pair_ref[0] = second
    pair_ref[1] = image
    scalar_ref[...] = jnp.where(lane == 0, alpha, jnp.where(lane == 1, beta, 0.0))


def last_kernel(total_entries, pair_ref, scalar_ref, line_ref, mode_ref, coefficient_ref):
    lines = line_ref[:, 0, :]
    alpha = jnp.sum(lines[:, 0:1], axis=0, keepdims=True) / total_entries
    away = lines[:, 2:3] - alpha
    parts = lines[:, 3:4] + away * (away * lines[:, 1:2] + 2.0 * lines[:, 4:5])
    beta = jnp.sqrt(jnp.sum(parts, axis=0, keepdims=True) / total_entries + norm_eps)
    mode = (pair_ref[1] - alpha * pair_ref[0]) / beta
    mode_ref[...] = mode[: mode_ref.shape[0]]
    for at, value in enumerate((scalar_ref[0:1, 0:1], scalar_ref[0:1, 1:2], alpha, beta)):
        coefficient_ref[at] = jnp.sum(value)


def local(config, start, tile_list, tile_count):
    dof, member = config.shape
    row_devices = lax.axis_size("row")
    col_devices = lax.axis_size("col")
    devices = row_devices * col_devices
    total_entries = float(dof * member * devices)
    period = (5.0, 5.0, 3.5 * (member // 16))
    slots = tile_list.shape[2]
    longest = (row_devices + col_devices) * slots + 1

    def shaped(*shape):
        return jax.ShapeDtypeStruct(shape, jnp.float32)

    def everywhere(copies):
        return lax.all_to_all(copies, ("row", "col"), 0, 0, tiled=True)

    params = pltpu.CompilerParams(vmem_limit_bytes=VMEM_LIMIT)
    vmem = pl.BlockSpec(memory_space=pltpu.VMEM)
    smem = pl.BlockSpec(memory_space=pltpu.SMEM)

    outside = pl.BlockSpec(memory_space=pl.ANY)
    packed = pl.pallas_call(
        pack_kernel,
        out_shape=shaped(devices, 1, (LIST_ROW + 1) * member),
        in_specs=[outside] * 4,
        out_specs=vmem,
        scratch_shapes=[
            pltpu.VMEM((dof, member), jnp.float32),
            pltpu.VMEM((dof, member), jnp.float32),
            pltpu.SMEM((1, tile_list.shape[3], 1, slots), jnp.int32),
            pltpu.SMEM((1, 1), jnp.int32),
            pltpu.SemaphoreType.DMA((4,)),
        ],
        compiler_params=pltpu.CompilerParams(vmem_limit_bytes=PACK_LIMIT),
    )(config, start, jnp.transpose(tile_list, (0, 3, 1, 2)), tile_count)
    together = everywhere(packed)

    held_rows = HELD // GROUP * (TERMS * GROUP * SUB)
    image, items, terms, kept = pl.pallas_call(
        functools.partial(first_kernel, row_devices, col_devices, slots, period),
        out_shape=(
            shaped(devices, 1, dof * member),
            jax.ShapeDtypeStruct((1 + longest * (member // SUB) + GROUP * UNROLL,), jnp.int32),
            shaped(held_rows, member),
            shaped(2, member),
        ),
        in_specs=[vmem],
        out_specs=(vmem, smem, vmem, vmem),
        scratch_shapes=[
            pltpu.SMEM((longest + TESTS,), jnp.int32),
            pltpu.VMEM((row_devices + col_devices, member), jnp.int32),
            pltpu.SMEM((row_devices + col_devices, member), jnp.int32),
            pltpu.SemaphoreType.DMA,
        ],
        compiler_params=params,
    )(together)
    image = everywhere(image)

    line, pair, scalars = pl.pallas_call(
        functools.partial(second_kernel, col_devices, total_entries, period),
        out_shape=(shaped(devices, 1, member), shaped(2, SUB, member), shaped(1, member)),
        in_specs=[smem] + [vmem] * 4,
        out_specs=(vmem, vmem, vmem),
        scratch_shapes=[
            pltpu.VMEM((devices, 1, dof * member), jnp.float32),
        ],
        compiler_params=params,
    )(items, terms, kept, together, image)
    line = everywhere(line)

    mode, coefficients = pl.pallas_call(
        functools.partial(last_kernel, total_entries),
        out_shape=(shaped(dof, member), shaped(4)),
        in_specs=[vmem] * 3,
        out_specs=(vmem, smem),
        compiler_params=params,
    )(pair, scalars, line)
    return (coefficients, mode)


def solution(mesh):
    placed = (
        P(None, ("row", "col")),
        P(None, ("row", "col")),
        P("row", "col", None, None),
        P("row", "col"),
    )
    return jax.shard_map(
        local, mesh=mesh, in_specs=placed, out_specs=(P(), P(None, ("row", "col"))), check_vma=False
    )
```

```python
import functools
import math

import jax
import jax.numpy as jnp
from jax import lax
from jax.experimental import pallas as pl
from jax.experimental.pallas import tpu as pltpu
from jax.sharding import PartitionSpec as P

chi_shape = 0.8
chi_energy = (math.sqrt(5.0) - 1.0) / (math.sqrt(5.0) + 1.0)
well_depth = 0.005
cutoff_sq = 20.25
norm_eps = 1e-06

SUB = 8
CENTRE = 6
LIST_ROW = 12
CODE_BITS = 6
ITEM_BITS = 8
ITEM_MASK = 255
LAYER = 16
TESTS = 10
GROUP = 2
UNROLL = 2
TERMS = 20
HELD = 128
VMEM_LIMIT = 32 * 1024 * 1024
PACK_LIMIT = 60 * 1024 * 1024


def dot3(a, b):
    return a[0] * b[0] + a[1] * b[1] + a[2] * b[2]


def cross3(a, b):
    return (
        a[1] * b[2] - a[2] * b[1],
        a[2] * b[0] - a[0] * b[2],
        a[0] * b[1] - a[1] * b[0],
    )


def inverse(value):
    guess = pl.reciprocal(value, approx=True)
    return guess * (2.0 - value * guess)


def bracket(chi, scaled, factor, p, a, b):
    f = factor * (a - scaled * b)
    g = factor * (b - scaled * a)
    y = p * (a * f + b * g)
    cross = factor * scaled
    f_c = chi * (cross * f - factor * g)
    g_c = chi * (cross * g - factor * f)
    return f, g, y, cross, f_c, g_c


def pair_coefficients(d, ui, uj, lift):
    r_sq = dot3(d, d) + lift
    a = dot3(d, ui)
    b = dot3(d, uj)
    c = dot3(ui, uj)
    r_inv = lax.rsqrt(r_sq)
    p = r_inv * r_inv
    p2 = 2.0 * p
    r = r_sq * r_inv
    x = jnp.maximum(1.0 - r_sq * (1.0 / cutoff_sq), 0.0)
    c_shape = chi_shape * c
    c_energy = chi_energy * c
    e1 = lax.rsqrt(1.0 - c_shape * c_shape)
    q = e1 * e1
    q2 = inverse(1.0 - c_energy * c_energy)
    f, g, y, m, f_c, g_c = bracket(chi_shape, c_shape, q, p, a, b)
    f2, g2, y2, m2, f2_c, g2_c = bracket(chi_energy, c_energy, q2, p, a, b)
    sigma = lax.rsqrt(1.0 - chi_shape * y)
    sigma_sq = sigma * sigma
    psi = 1.0 - chi_energy * y2
    s = inverse(r - sigma + 1.0)
    s_sq = s * s
    s6 = s_sq * s_sq * s_sq
    t0 = s6 * (s6 - 1.0)
    t1 = s6 * s * (6.0 - 12.0 * s6)
    t2 = s6 * s_sq * (156.0 * s6 - 42.0)
    ke = (4.0 * well_depth) * e1
    kx = ke * x
    v_ee = kx * (24.0 / cutoff_sq**2)
    kxx = kx * x
    v_e = kxx * (-6.0 / cutoff_sq)
    v = kxx * x
    psi_sq = psi * psi
    psi_sq_t0 = psi_sq * t0
    psi_sq_t1 = psi_sq * t1
    u = v * psi_sq_t0
    slope = v * psi_sq_t1
    slope2 = v * psi_sq * t2
    tau = (-0.5 * chi_shape) * sigma_sq * sigma
    push = (-2.0 * chi_energy) * psi
    v_t1 = v * t1
    d1 = slope * tau
    d2 = push * (v * t0)
    h1 = p2 * d1
    h2 = p2 * d2
    kc = chi_shape * c_shape * q
    fg = chi_shape * f * g
    fg2 = chi_energy * f2 * g2
    u_a = h1 * f + h2 * f2
    u_b = h1 * g + h2 * g2
    u_fg = h1 * fg + h2 * fg2
    u_c = u * kc - u_fg
    v_e_t0 = v_e * psi_sq_t0
    d_e = r_inv * slope + v_e_t0
    u_e = d_e - (h1 * y + h2 * y2)

    p2_sq = p2 * p2
    k11 = p2_sq * (tau * (slope2 * tau + (1.5 * chi_shape) * sigma_sq * slope))
    k12 = p2_sq * (push * v_t1 * tau)
    k22 = p2_sq * ((2.0 * chi_energy * chi_energy) * (v * t0))
    steep = v_e * psi_sq_t1 + slope2 * r_inv
    l1 = p2 * (steep * tau - h1)
    l2 = p2 * (push * (v_e * t0 + v_t1 * r_inv) - h2)
    j1 = (y, f, g, fg)
    j2 = (y2, f2, g2, fg2)
    w1 = [k11 * one + k12 * two for one, two in zip(j1, j2)]
    w2 = [k12 * one + k22 * two for one, two in zip(j1, j2)]

    def quadratic(m_at, n_at):
        return w1[m_at] * j1[n_at] + w2[m_at] * j2[n_at]

    d_ee = v_ee * psi_sq_t0 + r_inv * (2.0 * (v_e * psi_sq_t1)) + p * (slope2 - slope * r_inv)
    h_ee = quadratic(0, 0) - 2.0 * (l1 * y + l2 * y2) + d_ee
    h_ea = l1 * f + l2 * f2 - quadratic(0, 1)
    h_eb = l1 * g + l2 * g2 - quadratic(0, 2)
    h_ec = quadratic(0, 3) - (l1 * fg + l2 * fg2) + kc * u_e
    straight = h1 * q + h2 * q2
    h_aa = quadratic(1, 1) + straight
    h_ab = quadratic(1, 2) - (h1 * m + h2 * m2)
    h_ac = kc * u_a - quadratic(1, 3) + (h1 * f_c + h2 * f2_c)
    h_bb = quadratic(2, 2) + straight
    h_bc = kc * u_b - quadratic(2, 3) + (h1 * g_c + h2 * g2_c)
    bent = (chi_shape * h1) * (f_c * g + f * g_c) + (chi_energy * h2) * (f2_c * g2 + f2 * g2_c)
    twist = kc * kc + (chi_shape * chi_shape) * q * (2.0 * q - 1.0)
    h_cc = quadratic(3, 3) - bent - 2.0 * (kc * u_fg) + u * twist
    gradient = (u_e, u_a, u_b, u_c)
    return gradient, (h_ee, h_ea, h_eb, h_ec, h_aa, h_ab, h_ac, h_bb, h_bc, h_cc), u_a * a + u_c * c


def offsets_of(code, period):
    return [((code >> bits & 3) - 1).astype(jnp.float32) * size for bits, size in zip((4, 2, 0), period)]


def row_of(tiles_ref, tile, k, member):
    return tiles_ref[tile, :, k * member : (k + 1) * member]


def centre_of(code, period, all_ref, member):
    shift = offsets_of(code, period)
    return [row_of(all_ref, code >> CODE_BITS, CENTRE + k, member) + shift[k] for k in range(3)]


def lanes_of(block, member):
    row = lax.broadcasted_iota(jnp.int32, (SUB, member), 0)
    lane = lax.broadcasted_iota(jnp.int32, (SUB, member), 1)
    group = (lane & -LAYER) - (block >> 1) * LAYER
    return (group & (member - 1)) + ((block & 1) * SUB + row)


def picked(block, lanes):
    return jnp.take_along_axis(block, lanes, axis=1, mode="promise_in_bounds")


def box_lanes(member):
    block = lax.broadcasted_iota(jnp.int32, (member // SUB, member), 0)
    lane = lax.broadcasted_iota(jnp.int32, (member // SUB, member), 1)
    return (((lane & -LAYER) - (block >> 1) * LAYER) & (member - 1)) + (block & 1) * SUB


def near_blocks(own_centre, partner, lanes):
    blocks, member = lanes.shape
    zero = jnp.zeros((1, member), jnp.float32)
    box = stacked(partner + [-line for line in partner] + [zero, zero])
    for bit in (1, 2, 4):
        box = jnp.maximum(box, pltpu.roll(box, member - bit, 1))

    def seen(k):
        line = jnp.broadcast_to(box[k : k + 1], (SUB, member))
        return stacked([picked(line, lanes[at : at + SUB]) for at in range(0, blocks, SUB)])

    reach = 0.0
    for k in range(3):
        above = own_centre[k] - seen(k)
        below = -own_centre[k] - seen(3 + k)
        gap = jnp.maximum(jnp.maximum(above, below), 0.0)
        reach = reach + gap * gap
    nearest = jnp.min(reach, axis=1, keepdims=True)
    weight = (1 << lax.broadcasted_iota(jnp.int32, (blocks, 1), 0)).astype(jnp.float32)
    return jnp.sum(jnp.where(nearest < cutoff_sq * 1.001, weight, 0.0)).astype(jnp.int32)


def stacked(parts):
    return jnp.concatenate(parts, axis=0)


def wide(row):
    return jnp.broadcast_to(row, (GROUP * SUB, row.shape[1]))


def partner_rows(row_at, items, lanes):
    rows = []
    for k in range(6):
        parts = []
        for item, lane in zip(items, lanes):
            row = row_at(item >> (ITEM_BITS + CODE_BITS), k)
            parts.append(picked(jnp.broadcast_to(row, lane.shape), lane))
        rows.append(stacked(parts))
    return rows


def folded(total):
    return jnp.sum(total, axis=0, keepdims=True)


def geometry(items, unused, lanes, own_code, own_wide, period, all_ref):
    member = lanes[0].shape[1]
    lane = lax.broadcasted_iota(jnp.int32, (SUB, member), 1)
    lift = []
    shifts = []
    for item, idle, other in zip(items, unused, lanes):
        code = item >> ITEM_BITS
        itself = jnp.where(other == lane, jnp.where(code == own_code, 2.0 * cutoff_sq, 0.0), 0.0)
        lift.append(itself + jnp.where(idle, 2.0 * cutoff_sq, 0.0))
        shifts.append(offsets_of(code, period))
    rows = partner_rows(lambda tile, k: row_of(all_ref, tile, CENTRE + k, member), items, lanes)
    shift = [stacked([jnp.full((SUB, member), one[k]) for one in shifts]) for k in range(3)]
    d = [rows[k] + shift[k] - own_wide[k] for k in range(3)]
    uj = rows[3:]
    gradient, hessian, spin = pair_coefficients(d, own_wide[3:], uj, stacked(lift))
    return list(gradient) + list(hessian) + d + uj, (gradient[1], spin)


def apply(moved_rows, terms, own_wide, moved_wide):
    u_e, u_a, u_b, u_c, h_ee, h_ea, h_eb, h_ec, h_aa, h_ab, h_ac, h_bb, h_bc, h_cc = terms[:14]
    d = terms[14:17]
    uj = terms[17:20]
    ui = own_wide[3:]
    dui = moved_wide[3:]
    dd = [moved_rows[k] - moved_wide[k] for k in range(3)]
    duj = cross3(moved_rows[3:], uj)
    de = dot3(d, dd)
    da = dot3(dd, ui) + dot3(d, dui)
    db = dot3(dd, uj) + dot3(d, duj)
    dc = dot3(dui, uj) + dot3(ui, duj)
    du_e = h_ee * de + h_ea * da + h_eb * db + h_ec * dc
    du_a = h_ea * de + h_aa * da + h_ab * db + h_ac * dc
    du_b = h_eb * de + h_ab * da + h_bb * db + h_bc * dc
    du_c = h_ec * de + h_ac * da + h_bc * db + h_cc * dc
    force = [du_e * d[k] + u_e * dd[k] + du_b * uj[k] + u_b * duj[k] for k in range(3)]
    turn = [du_a * d[k] + u_a * dd[k] + du_c * uj[k] + u_c * duj[k] for k in range(3)]
    return force + turn + [du_a]


def several(body):
    def step_of(step, totals):
        for part in range(UNROLL):
            totals = body(step * UNROLL + part, totals)
        return totals

    return step_of


def group_items(step, item_ref, item_count):
    at = [step * GROUP + part for part in range(GROUP)]
    return [item_ref[1 + place] for place in at], [place >= item_count for place in at]


def added(totals, news):
    return tuple(
        total + sum(new[part * SUB : (part + 1) * SUB] for part in range(GROUP)) for total, new in zip(totals, news)
    )


def close(sums, kept, spin, u, t):
    force = [-(sums[k] + u[k] * sums[6] + t[k] * kept) for k in range(3)]
    return force + list(cross3(u, [sums[3 + k] - t[k] * spin for k in range(3)]))


def spread(rows, out_ref):
    member = rows[0].shape[1]
    for k, row in enumerate(rows):
        out_ref[:, :, k * member : (k + 1) * member] = jnp.broadcast_to(row[None], (out_ref.shape[0], 1, member))


def pack_kernel(*refs):
    sources, out_ref, targets, sems = refs[:4], refs[4], refs[5:9], refs[9]
    config_ref, start_ref, list_ref, count_ref = targets
    copies = [
        pltpu.make_async_copy(source, target, sems.at[at]) for at, (source, target) in enumerate(zip(sources, targets))
    ]
    for copy in copies:
        copy.start()
    copies[2].wait()
    copies[3].wait()
    member = config_ref.shape[1]
    lane = lax.broadcasted_iota(jnp.int32, (1, member), 1)
    fields, slots = list_ref.shape[1], list_ref.shape[3]
    line = jnp.full((1, member), -9, jnp.int32)
    for field in range(fields):
        for slot in range(slots):
            line = jnp.where(lane == field * slots + slot, list_ref[0, field, 0, slot], line)
    line = jnp.where((lane >= count_ref[0, 0]) & (lane < slots), -9, line).astype(jnp.float32)
    copies[0].wait()
    copies[1].wait()
    rows = [ref[k : k + 1, :] for ref in (start_ref, config_ref) for k in range(6)]
    spread(rows + [line], out_ref)


def first_kernel(
    rows,
    cols,
    slots,
    period,
    all_ref,
    out_ref,
    item_ref,
    coef_ref,
    kept_ref,
    entry_ref,
    code_ref,
    code_smem,
    sem,
):
    member = kept_ref.shape[1]
    row_id = lax.axis_index("row")
    col_id = lax.axis_index("col")
    own = row_id * cols + col_id
    blocks = member // SUB

    def field(line, at):
        return line if at == 0 else pltpu.roll(line, member - at * slots, 1)

    row_f = row_id.astype(jnp.float32)
    col_f = col_id.astype(jnp.float32)
    lines = [row_of(all_ref, row_id * cols + col, LIST_ROW, member) for col in range(cols)]
    lines += [row_of(all_ref, row * cols + col_id, LIST_ROW, member) for row in range(rows)]
    line = jnp.concatenate(lines, axis=0)
    at = lax.broadcasted_iota(jnp.int32, line.shape, 0).astype(jnp.float32)
    near = at < float(cols)
    other = field(line, 1)
    offset = field(line, 2) * 16.0 + field(line, 3) * 4.0 + field(line, 4)
    partner = jnp.where(near, other * float(cols) + at, (at - float(cols)) * float(cols) + line)
    code = partner * float(1 << CODE_BITS) + (jnp.where(near, offset, -offset) + 21.0)
    hit = jnp.where(near, line - col_f, jnp.where(line >= 0.0, other - row_f, 1.0)) == 0.0
    code_ref[...] = jnp.where(hit, code, -1.0).astype(jnp.int32)
    copy = pltpu.make_async_copy(code_ref, code_smem, sem)
    copy.start()
    own_code = own * (1 << CODE_BITS) + 21
    own_moved = [row_of(all_ref, own, k, member) for k in range(6)]
    own_frame = [row_of(all_ref, own, CENTRE + k, member) for k in range(6)]
    lanes = box_lanes(member)
    own_centre = [jnp.broadcast_to(line, lanes.shape) for line in own_frame[:3]]

    def append(code, bits, count):
        for block in range(blocks):
            item_ref[1 + count] = (code << ITEM_BITS) + block
            count = count + (bits >> block & 1)
        return count

    items = append(own_code, near_blocks(own_centre, own_frame[:3], lanes), jnp.int32(0))
    copy.wait()

    def gather(line, count):
        for slot in range(slots):
            code = code_smem[line, slot]
            entry_ref[count] = code
            count = count + (code >= 0).astype(jnp.int32)
        return count

    entries = lax.fori_loop(0, rows + cols, gather, jnp.int32(0))
    for part in range(TESTS):
        entry_ref[entries + part] = own_code

    def prepare(step, count):
        codes = [entry_ref[step * TESTS + part] for part in range(TESTS)]
        bits = [near_blocks(own_centre, centre_of(code, period, all_ref, member), lanes) for code in codes]
        for part in range(TESTS):
            count = append(codes[part], jnp.where(step * TESTS + part < entries, bits[part], 0), count)
        return count

    items = lax.fori_loop(0, (entries + TESTS - 1) // TESTS, prepare, items)
    for part in range(GROUP * UNROLL):
        item_ref[1 + items + part] = own_code << ITEM_BITS
    item_ref[0] = items

    held = coef_ref.shape[0] // (TERMS * GROUP * UNROLL * SUB)
    steps = (items + GROUP * UNROLL - 1) // (GROUP * UNROLL)
    u = own_frame[3:]
    t = cross3(own_moved[3:], u)
    own_wide = [wide(line) for line in own_frame]
    moved_wide = [wide(line) for line in [*own_moved[:3], *t]]

    def derive(step, totals):
        group, unused = group_items(step, item_ref, items)
        lanes = [lanes_of(item & ITEM_MASK, member) for item in group]
        terms, sums = geometry(group, unused, lanes, own_code, own_wide, period, all_ref)
        moved_rows = partner_rows(lambda tile, k: row_of(all_ref, tile, k, member), group, lanes)
        return terms, added(totals, apply(moved_rows, terms, own_wide, moved_wide) + list(sums))

    def keep(step, totals):
        terms, totals = derive(step, totals)
        start = pl.multiple_of(step * (TERMS * GROUP * SUB), SUB)
        for k in range(TERMS):
            coef_ref[pl.ds(start + k * GROUP * SUB, GROUP * SUB), :] = terms[k]
        return totals

    zero = jnp.zeros((SUB, member), jnp.float32)
    totals = lax.fori_loop(0, jnp.minimum(steps, held), several(keep), (zero,) * 9)
    totals = lax.fori_loop(held, steps, several(lambda step, before: derive(step, before)[1]), totals)
    sums = [folded(total) for total in totals]
    kept_ref[...] = jnp.concatenate(sums[7:], axis=0)
    spread(close(sums, sums[7], sums[8], u, t), out_ref)


def scalar_of(block):
    return jnp.sum(jnp.sum(block, axis=0, keepdims=True), axis=1, keepdims=True)


def second_kernel(
    cols,
    total_entries,
    period,
    item_ref,
    coef_ref,
    kept_ref,
    all_ref,
    image_ref,
    out_ref,
    pair_ref,
    scalar_ref,
    second_ref,
):
    own = lax.axis_index("row") * cols + lax.axis_index("col")
    member = kept_ref.shape[1]
    basis = all_ref[:, 0, 0 : 6 * member]
    image = image_ref[:, 0, :]
    portion = 1.0 / total_entries

    def total_of(block):
        return scalar_of(sum(block[:, k * member : (k + 1) * member] for k in range(6)))

    norm_sq = total_of(basis * basis) * portion + norm_eps
    norm_inv = lax.rsqrt(norm_sq)
    alpha = total_of(basis * image) * portion / norm_sq
    second = image - alpha * basis
    second_ref[:, 0, :] = second
    beta_sq = total_of(second * second) * portion / norm_sq + norm_eps
    beta = jnp.sqrt(beta_sq)
    scale = norm_inv * lax.rsqrt(beta_sq)

    own_code = own * (1 << CODE_BITS) + 21
    items = item_ref[0]
    held = coef_ref.shape[0] // (TERMS * GROUP * UNROLL * SUB)
    steps = (items + GROUP * UNROLL - 1) // (GROUP * UNROLL)

    def moved_row(tile, k):
        return row_of(second_ref, tile, k, member)

    own_moved = [moved_row(own, k) for k in range(6)]
    own_frame = [row_of(all_ref, own, CENTRE + k, member) for k in range(6)]
    u = own_frame[3:]
    t = cross3(own_moved[3:], u)
    own_wide = [wide(line) for line in own_frame]
    moved_wide = [wide(line) for line in [*own_moved[:3], *t]]

    def visit(step, totals):
        group, _ = group_items(step, item_ref, items)
        lanes = [lanes_of(item & ITEM_MASK, member) for item in group]
        start = pl.multiple_of(step * (TERMS * GROUP * SUB), SUB)
        terms = [coef_ref[pl.ds(start + k * GROUP * SUB, GROUP * SUB), :] for k in range(TERMS)]
        return added(totals, apply(partner_rows(moved_row, group, lanes), terms, own_wide, moved_wide))

    def visit_again(step, totals):
        group, unused = group_items(step, item_ref, items)
        lanes = [lanes_of(item & ITEM_MASK, member) for item in group]
        terms, _ = geometry(group, unused, lanes, own_code, own_wide, period, all_ref)
        return added(totals, apply(partner_rows(moved_row, group, lanes), terms, own_wide, moved_wide))

    zero = jnp.zeros((SUB, member), jnp.float32)
    totals = lax.fori_loop(0, jnp.minimum(steps, held), several(visit), (zero,) * 7)
    totals = lax.fori_loop(held, steps, several(visit_again), totals)
    sums = [folded(total) for total in totals]
    product = close(sums, kept_ref[0:1, :], kept_ref[1:2, :], u, t)
    fill = [jnp.zeros((1, member), jnp.float32)] * (SUB - len(product))
    first = stacked([row_of(all_ref, own, k, member) for k in range(6)] + fill)
    image = stacked(product + fill) * scale - (beta * norm_inv) * first
    second = stacked(own_moved + fill) * scale
    inner = scalar_of(second * image)
    weight = scalar_of(second * second)
    local_alpha = jnp.where(weight > 1e-30, inner / jnp.maximum(weight, 1e-30), 0.0)
    rest = image - local_alpha * second
    size = scalar_of(rest * rest)
    slant = scalar_of(second * rest)
    lane = lax.broadcasted_iota(jnp.int32, (1, member), 1)
    line = jnp.zeros((1, member), jnp.float32)
    for at, value in enumerate((inner, weight, local_alpha, size, slant)):
        line = jnp.where(lane == at, value, line)
    out_ref[...] = jnp.broadcast_to(line[None], out_ref.shape)
    pair_ref[0] = second
    pair_ref[1] = image
    scalar_ref[...] = jnp.where(lane == 0, alpha, jnp.where(lane == 1, beta, 0.0))


def last_kernel(total_entries, pair_ref, scalar_ref, line_ref, mode_ref, coefficient_ref):
    lines = line_ref[:, 0, :]
    alpha = jnp.sum(lines[:, 0:1], axis=0, keepdims=True) / total_entries
    away = lines[:, 2:3] - alpha
    parts = lines[:, 3:4] + away * (away * lines[:, 1:2] + 2.0 * lines[:, 4:5])
    beta = jnp.sqrt(jnp.sum(parts, axis=0, keepdims=True) / total_entries + norm_eps)
    mode = (pair_ref[1] - alpha * pair_ref[0]) / beta
    mode_ref[...] = mode[: mode_ref.shape[0]]
    for at, value in enumerate((scalar_ref[0:1, 0:1], scalar_ref[0:1, 1:2], alpha, beta)):
        coefficient_ref[at] = jnp.sum(value)


def local(config, start, tile_list, tile_count):
    dof, member = config.shape
    row_devices = lax.axis_size("row")
    col_devices = lax.axis_size("col")
    devices = row_devices * col_devices
    total_entries = float(dof * member * devices)
    period = (5.0, 5.0, 3.5 * (member // 16))
    slots = tile_list.shape[2]
    longest = (row_devices + col_devices) * slots + 1

    def shaped(*shape):
        return jax.ShapeDtypeStruct(shape, jnp.float32)

    def everywhere(copies):
        return lax.all_to_all(copies, ("row", "col"), 0, 0, tiled=True)

    params = pltpu.CompilerParams(vmem_limit_bytes=VMEM_LIMIT)
    vmem = pl.BlockSpec(memory_space=pltpu.VMEM)
    smem = pl.BlockSpec(memory_space=pltpu.SMEM)

    outside = pl.BlockSpec(memory_space=pl.ANY)
    packed = pl.pallas_call(
        pack_kernel,
        out_shape=shaped(devices, 1, (LIST_ROW + 1) * member),
        in_specs=[outside] * 4,
        out_specs=vmem,
        scratch_shapes=[
            pltpu.VMEM((dof, member), jnp.float32),
            pltpu.VMEM((dof, member), jnp.float32),
            pltpu.SMEM((1, tile_list.shape[3], 1, slots), jnp.int32),
            pltpu.SMEM((1, 1), jnp.int32),
            pltpu.SemaphoreType.DMA((4,)),
        ],
        compiler_params=pltpu.CompilerParams(vmem_limit_bytes=PACK_LIMIT),
    )(config, start, jnp.transpose(tile_list, (0, 3, 1, 2)), tile_count)
    together = everywhere(packed)

    held_rows = HELD // GROUP * (TERMS * GROUP * SUB)
    image, items, terms, kept = pl.pallas_call(
        functools.partial(first_kernel, row_devices, col_devices, slots, period),
        out_shape=(
            shaped(devices, 1, dof * member),
            jax.ShapeDtypeStruct((1 + longest * (member // SUB) + GROUP * UNROLL,), jnp.int32),
            shaped(held_rows, member),
            shaped(2, member),
        ),
        in_specs=[vmem],
        out_specs=(vmem, smem, vmem, vmem),
        scratch_shapes=[
            pltpu.SMEM((longest + TESTS,), jnp.int32),
            pltpu.VMEM((row_devices + col_devices, member), jnp.int32),
            pltpu.SMEM((row_devices + col_devices, member), jnp.int32),
            pltpu.SemaphoreType.DMA,
        ],
        compiler_params=params,
    )(together)
    image = everywhere(image)

    line, pair, scalars = pl.pallas_call(
        functools.partial(second_kernel, col_devices, total_entries, period),
        out_shape=(shaped(devices, 1, member), shaped(2, SUB, member), shaped(1, member)),
        in_specs=[smem] + [vmem] * 4,
        out_specs=(vmem, vmem, vmem),
        scratch_shapes=[
            pltpu.VMEM((devices, 1, dof * member), jnp.float32),
        ],
        compiler_params=params,
    )(items, terms, kept, together, image)
    line = everywhere(line)

    mode, coefficients = pl.pallas_call(
        functools.partial(last_kernel, total_entries),
        out_shape=(shaped(dof, member), shaped(4)),
        in_specs=[vmem] * 3,
        out_specs=(vmem, smem),
        compiler_params=params,
    )(pair, scalars, line)
    return (coefficients, mode)


def solution(mesh):
    placed = (
        P(None, ("row", "col")),
        P(None, ("row", "col")),
        P("row", "col", None, None),
        P("row", "col"),
    )
    return jax.shard_map(
        local, mesh=mesh, in_specs=placed, out_specs=(P(), P(None, ("row", "col"))), check_vma=False
    )
```

```python
import functools
import math

import jax
import jax.numpy as jnp
from jax import lax
from jax.experimental import pallas as pl
from jax.experimental.pallas import tpu as pltpu
from jax.sharding import PartitionSpec as P

chi_shape = 0.8
chi_energy = (math.sqrt(5.0) - 1.0) / (math.sqrt(5.0) + 1.0)
well_depth = 0.005
cutoff_sq = 20.25
norm_eps = 1e-06

SUB = 8
CENTRE = 6
LIST_ROW = 12
CODE_BITS = 6
ITEM_BITS = 8
ITEM_MASK = 255
LAYER = 16
TESTS = 10
GROUP = 2
UNROLL = 3
TERMS = 20
HELD = 128
VMEM_LIMIT = 32 * 1024 * 1024
PACK_LIMIT = 60 * 1024 * 1024


def dot3(a, b):
    return a[0] * b[0] + a[1] * b[1] + a[2] * b[2]


def cross3(a, b):
    return (
        a[1] * b[2] - a[2] * b[1],
        a[2] * b[0] - a[0] * b[2],
        a[0] * b[1] - a[1] * b[0],
    )


def inverse(value):
    guess = pl.reciprocal(value, approx=True)
    return guess * (2.0 - value * guess)


def bracket(chi, scaled, factor, p, a, b):
    f = factor * (a - scaled * b)
    g = factor * (b - scaled * a)
    y = p * (a * f + b * g)
    cross = factor * scaled
    f_c = chi * (cross * f - factor * g)
    g_c = chi * (cross * g - factor * f)
    return f, g, y, cross, f_c, g_c


def pair_coefficients(d, ui, uj, lift):
    r_sq = dot3(d, d) + lift
    a = dot3(d, ui)
    b = dot3(d, uj)
    c = dot3(ui, uj)
    r_inv = lax.rsqrt(r_sq)
    p = r_inv * r_inv
    p2 = 2.0 * p
    r = r_sq * r_inv
    x = jnp.maximum(1.0 - r_sq * (1.0 / cutoff_sq), 0.0)
    c_shape = chi_shape * c
    c_energy = chi_energy * c
    e1 = lax.rsqrt(1.0 - c_shape * c_shape)
    q = e1 * e1
    q2 = inverse(1.0 - c_energy * c_energy)
    f, g, y, m, f_c, g_c = bracket(chi_shape, c_shape, q, p, a, b)
    f2, g2, y2, m2, f2_c, g2_c = bracket(chi_energy, c_energy, q2, p, a, b)
    sigma = lax.rsqrt(1.0 - chi_shape * y)
    sigma_sq = sigma * sigma
    psi = 1.0 - chi_energy * y2
    s = inverse(r - sigma + 1.0)
    s_sq = s * s
    s6 = s_sq * s_sq * s_sq
    t0 = s6 * (s6 - 1.0)
    t1 = s6 * s * (6.0 - 12.0 * s6)
    t2 = s6 * s_sq * (156.0 * s6 - 42.0)
    ke = (4.0 * well_depth) * e1
    kx = ke * x
    v_ee = kx * (24.0 / cutoff_sq**2)
    kxx = kx * x
    v_e = kxx * (-6.0 / cutoff_sq)
    v = kxx * x
    psi_sq = psi * psi
    psi_sq_t0 = psi_sq * t0
    psi_sq_t1 = psi_sq * t1
    u = v * psi_sq_t0
    slope = v * psi_sq_t1
    slope2 = v * psi_sq * t2
    tau = (-0.5 * chi_shape) * sigma_sq * sigma
    push = (-2.0 * chi_energy) * psi
    v_t1 = v * t1
    d1 = slope * tau
    d2 = push * (v * t0)
    h1 = p2 * d1
    h2 = p2 * d2
    kc = chi_shape * c_shape * q
    fg = chi_shape * f * g
    fg2 = chi_energy * f2 * g2
    u_a = h1 * f + h2 * f2
    u_b = h1 * g + h2 * g2
    u_fg = h1 * fg + h2 * fg2
    u_c = u * kc - u_fg
    v_e_t0 = v_e * psi_sq_t0
    d_e = r_inv * slope + v_e_t0
    u_e = d_e - (h1 * y + h2 * y2)

    p2_sq = p2 * p2
    k11 = p2_sq * (tau * (slope2 * tau + (1.5 * chi_shape) * sigma_sq * slope))
    k12 = p2_sq * (push * v_t1 * tau)
    k22 = p2_sq * ((2.0 * chi_energy * chi_energy) * (v * t0))
    steep = v_e * psi_sq_t1 + slope2 * r_inv
    l1 = p2 * (steep * tau - h1)
    l2 = p2 * (push * (v_e * t0 + v_t1 * r_inv) - h2)
    j1 = (y, f, g, fg)
    j2 = (y2, f2, g2, fg2)
    w1 = [k11 * one + k12 * two for one, two in zip(j1, j2)]
    w2 = [k12 * one + k22 * two for one, two in zip(j1, j2)]

    def quadratic(m_at, n_at):
        return w1[m_at] * j1[n_at] + w2[m_at] * j2[n_at]

    d_ee = v_ee * psi_sq_t0 + r_inv * (2.0 * (v_e * psi_sq_t1)) + p * (slope2 - slope * r_inv)
    h_ee = quadratic(0, 0) - 2.0 * (l1 * y + l2 * y2) + d_ee
    h_ea = l1 * f + l2 * f2 - quadratic(0, 1)
    h_eb = l1 * g + l2 * g2 - quadratic(0, 2)
    h_ec = quadratic(0, 3) - (l1 * fg + l2 * fg2) + kc * u_e
    straight = h1 * q + h2 * q2
    h_aa = quadratic(1, 1) + straight
    h_ab = quadratic(1, 2) - (h1 * m + h2 * m2)
    h_ac = kc * u_a - quadratic(1, 3) + (h1 * f_c + h2 * f2_c)
    h_bb = quadratic(2, 2) + straight
    h_bc = kc * u_b - quadratic(2, 3) + (h1 * g_c + h2 * g2_c)
    bent = (chi_shape * h1) * (f_c * g + f * g_c) + (chi_energy * h2) * (f2_c * g2 + f2 * g2_c)
    twist = kc * kc + (chi_shape * chi_shape) * q * (2.0 * q - 1.0)
    h_cc = quadratic(3, 3) - bent - 2.0 * (kc * u_fg) + u * twist
    gradient = (u_e, u_a, u_b, u_c)
    return gradient, (h_ee, h_ea, h_eb, h_ec, h_aa, h_ab, h_ac, h_bb, h_bc, h_cc), u_a * a + u_c * c


def offsets_of(code, period):
    return [((code >> bits & 3) - 1).astype(jnp.float32) * size for bits, size in zip((4, 2, 0), period)]


def row_of(tiles_ref, tile, k, member):
    return tiles_ref[tile, :, k * member : (k + 1) * member]


def centre_of(code, period, all_ref, member):
    shift = offsets_of(code, period)
    return [row_of(all_ref, code >> CODE_BITS, CENTRE + k, member) + shift[k] for k in range(3)]


def lanes_of(block, member):
    row = lax.broadcasted_iota(jnp.int32, (SUB, member), 0)
    lane = lax.broadcasted_iota(jnp.int32, (SUB, member), 1)
    group = (lane & -LAYER) - (block >> 1) * LAYER
    return (group & (member - 1)) + ((block & 1) * SUB + row)


def picked(block, lanes):
    return jnp.take_along_axis(block, lanes, axis=1, mode="promise_in_bounds")


def box_lanes(member):
    block = lax.broadcasted_iota(jnp.int32, (member // SUB, member), 0)
    lane = lax.broadcasted_iota(jnp.int32, (member // SUB, member), 1)
    return (((lane & -LAYER) - (block >> 1) * LAYER) & (member - 1)) + (block & 1) * SUB


def near_blocks(own_centre, partner, lanes):
    blocks, member = lanes.shape
    zero = jnp.zeros((1, member), jnp.float32)
    box = stacked(partner + [-line for line in partner] + [zero, zero])
    for bit in (1, 2, 4):
        box = jnp.maximum(box, pltpu.roll(box, member - bit, 1))

    def seen(k):
        line = jnp.broadcast_to(box[k : k + 1], (SUB, member))
        return stacked([picked(line, lanes[at : at + SUB]) for at in range(0, blocks, SUB)])

    reach = 0.0
    for k in range(3):
        above = own_centre[k] - seen(k)
        below = -own_centre[k] - seen(3 + k)
        gap = jnp.maximum(jnp.maximum(above, below), 0.0)
        reach = reach + gap * gap
    nearest = jnp.min(reach, axis=1, keepdims=True)
    weight = (1 << lax.broadcasted_iota(jnp.int32, (blocks, 1), 0)).astype(jnp.float32)
    return jnp.sum(jnp.where(nearest < cutoff_sq * 1.001, weight, 0.0)).astype(jnp.int32)


def stacked(parts):
    return jnp.concatenate(parts, axis=0)


def wide(row):
    return jnp.broadcast_to(row, (GROUP * SUB, row.shape[1]))


def partner_rows(row_at, items, lanes):
    rows = []
    for k in range(6):
        parts = []
        for item, lane in zip(items, lanes):
            row = row_at(item >> (ITEM_BITS + CODE_BITS), k)
            parts.append(picked(jnp.broadcast_to(row, lane.shape), lane))
        rows.append(stacked(parts))
    return rows


def folded(total):
    return jnp.sum(total, axis=0, keepdims=True)


def geometry(items, unused, lanes, own_code, own_wide, period, all_ref):
    member = lanes[0].shape[1]
    lane = lax.broadcasted_iota(jnp.int32, (SUB, member), 1)
    lift = []
    shifts = []
    for item, idle, other in zip(items, unused, lanes):
        code = item >> ITEM_BITS
        itself = jnp.where(other == lane, jnp.where(code == own_code, 2.0 * cutoff_sq, 0.0), 0.0)
        lift.append(itself + jnp.where(idle, 2.0 * cutoff_sq, 0.0))
        shifts.append(offsets_of(code, period))
    rows = partner_rows(lambda tile, k: row_of(all_ref, tile, CENTRE + k, member), items, lanes)
    shift = [stacked([jnp.full((SUB, member), one[k]) for one in shifts]) for k in range(3)]
    d = [rows[k] + shift[k] - own_wide[k] for k in range(3)]
    uj = rows[3:]
    gradient, hessian, spin = pair_coefficients(d, own_wide[3:], uj, stacked(lift))
    return list(gradient) + list(hessian) + d + uj, (gradient[1], spin)


def apply(moved_rows, terms, own_wide, moved_wide):
    u_e, u_a, u_b, u_c, h_ee, h_ea, h_eb, h_ec, h_aa, h_ab, h_ac, h_bb, h_bc, h_cc = terms[:14]
    d = terms[14:17]
    uj = terms[17:20]
    ui = own_wide[3:]
    dui = moved_wide[3:]
    dd = [moved_rows[k] - moved_wide[k] for k in range(3)]
    duj = cross3(moved_rows[3:], uj)
    de = dot3(d, dd)
    da = dot3(dd, ui) + dot3(d, dui)
    db = dot3(dd, uj) + dot3(d, duj)
    dc = dot3(dui, uj) + dot3(ui, duj)
    du_e = h_ee * de + h_ea * da + h_eb * db + h_ec * dc
    du_a = h_ea * de + h_aa * da + h_ab * db + h_ac * dc
    du_b = h_eb * de + h_ab * da + h_bb * db + h_bc * dc
    du_c = h_ec * de + h_ac * da + h_bc * db + h_cc * dc
    force = [du_e * d[k] + u_e * dd[k] + du_b * uj[k] + u_b * duj[k] for k in range(3)]
    turn = [du_a * d[k] + u_a * dd[k] + du_c * uj[k] + u_c * duj[k] for k in range(3)]
    return force + turn + [du_a]


def several(body):
    def step_of(step, totals):
        for part in range(UNROLL):
            totals = body(step * UNROLL + part, totals)
        return totals

    return step_of


def group_items(step, item_ref, item_count):
    at = [step * GROUP + part for part in range(GROUP)]
    return [item_ref[1 + place] for place in at], [place >= item_count for place in at]


def added(totals, news):
    return tuple(
        total + sum(new[part * SUB : (part + 1) * SUB] for part in range(GROUP)) for total, new in zip(totals, news)
    )


def close(sums, kept, spin, u, t):
    force = [-(sums[k] + u[k] * sums[6] + t[k] * kept) for k in range(3)]
    return force + list(cross3(u, [sums[3 + k] - t[k] * spin for k in range(3)]))


def spread(rows, out_ref):
    member = rows[0].shape[1]
    for k, row in enumerate(rows):
        out_ref[:, :, k * member : (k + 1) * member] = jnp.broadcast_to(row[None], (out_ref.shape[0], 1, member))


def pack_kernel(*refs):
    sources, out_ref, targets, sems = refs[:4], refs[4], refs[5:9], refs[9]
    config_ref, start_ref, list_ref, count_ref = targets
    copies = [
        pltpu.make_async_copy(source, target, sems.at[at]) for at, (source, target) in enumerate(zip(sources, targets))
    ]
    for copy in copies:
        copy.start()
    copies[2].wait()
    copies[3].wait()
    member = config_ref.shape[1]
    lane = lax.broadcasted_iota(jnp.int32, (1, member), 1)
    fields, slots = list_ref.shape[1], list_ref.shape[3]
    line = jnp.full((1, member), -9, jnp.int32)
    for field in range(fields):
        for slot in range(slots):
            line = jnp.where(lane == field * slots + slot, list_ref[0, field, 0, slot], line)
    line = jnp.where((lane >= count_ref[0, 0]) & (lane < slots), -9, line).astype(jnp.float32)
    copies[0].wait()
    copies[1].wait()
    rows = [ref[k : k + 1, :] for ref in (start_ref, config_ref) for k in range(6)]
    spread(rows + [line], out_ref)


def first_kernel(
    rows,
    cols,
    slots,
    period,
    all_ref,
    out_ref,
    item_ref,
    coef_ref,
    kept_ref,
    entry_ref,
    code_ref,
    code_smem,
    sem,
):
    member = kept_ref.shape[1]
    row_id = lax.axis_index("row")
    col_id = lax.axis_index("col")
    own = row_id * cols + col_id
    blocks = member // SUB

    def field(line, at):
        return line if at == 0 else pltpu.roll(line, member - at * slots, 1)

    row_f = row_id.astype(jnp.float32)
    col_f = col_id.astype(jnp.float32)
    lines = [row_of(all_ref, row_id * cols + col, LIST_ROW, member) for col in range(cols)]
    lines += [row_of(all_ref, row * cols + col_id, LIST_ROW, member) for row in range(rows)]
    line = jnp.concatenate(lines, axis=0)
    at = lax.broadcasted_iota(jnp.int32, line.shape, 0).astype(jnp.float32)
    near = at < float(cols)
    other = field(line, 1)
    offset = field(line, 2) * 16.0 + field(line, 3) * 4.0 + field(line, 4)
    partner = jnp.where(near, other * float(cols) + at, (at - float(cols)) * float(cols) + line)
    code = partner * float(1 << CODE_BITS) + (jnp.where(near, offset, -offset) + 21.0)
    hit = jnp.where(near, line - col_f, jnp.where(line >= 0.0, other - row_f, 1.0)) == 0.0
    code_ref[...] = jnp.where(hit, code, -1.0).astype(jnp.int32)
    copy = pltpu.make_async_copy(code_ref, code_smem, sem)
    copy.start()
    own_code = own * (1 << CODE_BITS) + 21
    own_moved = [row_of(all_ref, own, k, member) for k in range(6)]
    own_frame = [row_of(all_ref, own, CENTRE + k, member) for k in range(6)]
    lanes = box_lanes(member)
    own_centre = [jnp.broadcast_to(line, lanes.shape) for line in own_frame[:3]]

    def append(code, bits, count):
        for block in range(blocks):
            item_ref[1 + count] = (code << ITEM_BITS) + block
            count = count + (bits >> block & 1)
        return count

    items = append(own_code, near_blocks(own_centre, own_frame[:3], lanes), jnp.int32(0))
    copy.wait()

    def gather(line, count):
        for slot in range(slots):
            code = code_smem[line, slot]
            entry_ref[count] = code
            count = count + (code >= 0).astype(jnp.int32)
        return count

    entries = lax.fori_loop(0, rows + cols, gather, jnp.int32(0))
    for part in range(TESTS):
        entry_ref[entries + part] = own_code

    def prepare(step, count):
        codes = [entry_ref[step * TESTS + part] for part in range(TESTS)]
        bits = [near_blocks(own_centre, centre_of(code, period, all_ref, member), lanes) for code in codes]
        for part in range(TESTS):
            count = append(codes[part], jnp.where(step * TESTS + part < entries, bits[part], 0), count)
        return count

    items = lax.fori_loop(0, (entries + TESTS - 1) // TESTS, prepare, items)
    for part in range(GROUP * UNROLL):
        item_ref[1 + items + part] = own_code << ITEM_BITS
    item_ref[0] = items

    held = coef_ref.shape[0] // (TERMS * GROUP * UNROLL * SUB)
    steps = (items + GROUP * UNROLL - 1) // (GROUP * UNROLL)
    u = own_frame[3:]
    t = cross3(own_moved[3:], u)
    own_wide = [wide(line) for line in own_frame]
    moved_wide = [wide(line) for line in [*own_moved[:3], *t]]

    def derive(step, totals):
        group, unused = group_items(step, item_ref, items)
        lanes = [lanes_of(item & ITEM_MASK, member) for item in group]
        terms, sums = geometry(group, unused, lanes, own_code, own_wide, period, all_ref)
        moved_rows = partner_rows(lambda tile, k: row_of(all_ref, tile, k, member), group, lanes)
        return terms, added(totals, apply(moved_rows, terms, own_wide, moved_wide) + list(sums))

    def keep(step, totals):
        terms, totals = derive(step, totals)
        start = pl.multiple_of(step * (TERMS * GROUP * SUB), SUB)
        for k in range(TERMS):
            coef_ref[pl.ds(start + k * GROUP * SUB, GROUP * SUB), :] = terms[k]
        return totals

    zero = jnp.zeros((SUB, member), jnp.float32)
    totals = lax.fori_loop(0, jnp.minimum(steps, held), several(keep), (zero,) * 9)
    totals = lax.fori_loop(held, steps, several(lambda step, before: derive(step, before)[1]), totals)
    sums = [folded(total) for total in totals]
    kept_ref[...] = jnp.concatenate(sums[7:], axis=0)
    spread(close(sums, sums[7], sums[8], u, t), out_ref)


def scalar_of(block):
    return jnp.sum(jnp.sum(block, axis=0, keepdims=True), axis=1, keepdims=True)


def second_kernel(
    cols,
    total_entries,
    period,
    item_ref,
    coef_ref,
    kept_ref,
    all_ref,
    image_ref,
    out_ref,
    pair_ref,
    scalar_ref,
    second_ref,
):
    own = lax.axis_index("row") * cols + lax.axis_index("col")
    member = kept_ref.shape[1]
    basis = all_ref[:, 0, 0 : 6 * member]
    image = image_ref[:, 0, :]
    portion = 1.0 / total_entries

    def total_of(block):
        return scalar_of(sum(block[:, k * member : (k + 1) * member] for k in range(6)))

    norm_sq = total_of(basis * basis) * portion + norm_eps
    norm_inv = lax.rsqrt(norm_sq)
    alpha = total_of(basis * image) * portion / norm_sq
    second = image - alpha * basis
    second_ref[:, 0, :] = second
    beta_sq = total_of(second * second) * portion / norm_sq + norm_eps
    beta = jnp.sqrt(beta_sq)
    scale = norm_inv * lax.rsqrt(beta_sq)

    own_code = own * (1 << CODE_BITS) + 21
    items = item_ref[0]
    held = coef_ref.shape[0] // (TERMS * GROUP * UNROLL * SUB)
    steps = (items + GROUP * UNROLL - 1) // (GROUP * UNROLL)

    def moved_row(tile, k):
        return row_of(second_ref, tile, k, member)

    own_moved = [moved_row(own, k) for k in range(6)]
    own_frame = [row_of(all_ref, own, CENTRE + k, member) for k in range(6)]
    u = own_frame[3:]
    t = cross3(own_moved[3:], u)
    own_wide = [wide(line) for line in own_frame]
    moved_wide = [wide(line) for line in [*own_moved[:3], *t]]

    def visit(step, totals):
        group, _ = group_items(step, item_ref, items)
        lanes = [lanes_of(item & ITEM_MASK, member) for item in group]
        start = pl.multiple_of(step * (TERMS * GROUP * SUB), SUB)
        terms = [coef_ref[pl.ds(start + k * GROUP * SUB, GROUP * SUB), :] for k in range(TERMS)]
        return added(totals, apply(partner_rows(moved_row, group, lanes), terms, own_wide, moved_wide))

    def visit_again(step, totals):
        group, unused = group_items(step, item_ref, items)
        lanes = [lanes_of(item & ITEM_MASK, member) for item in group]
        terms, _ = geometry(group, unused, lanes, own_code, own_wide, period, all_ref)
        return added(totals, apply(partner_rows(moved_row, group, lanes), terms, own_wide, moved_wide))

    zero = jnp.zeros((SUB, member), jnp.float32)
    totals = lax.fori_loop(0, jnp.minimum(steps, held), several(visit), (zero,) * 7)
    totals = lax.fori_loop(held, steps, several(visit_again), totals)
    sums = [folded(total) for total in totals]
    product = close(sums, kept_ref[0:1, :], kept_ref[1:2, :], u, t)
    fill = [jnp.zeros((1, member), jnp.float32)] * (SUB - len(product))
    first = stacked([row_of(all_ref, own, k, member) for k in range(6)] + fill)
    image = stacked(product + fill) * scale - (beta * norm_inv) * first
    second = stacked(own_moved + fill) * scale
    inner = scalar_of(second * image)
    weight = scalar_of(second * second)
    local_alpha = jnp.where(weight > 1e-30, inner / jnp.maximum(weight, 1e-30), 0.0)
    rest = image - local_alpha * second
    size = scalar_of(rest * rest)
    slant = scalar_of(second * rest)
    lane = lax.broadcasted_iota(jnp.int32, (1, member), 1)
    line = jnp.zeros((1, member), jnp.float32)
    for at, value in enumerate((inner, weight, local_alpha, size, slant)):
        line = jnp.where(lane == at, value, line)
    out_ref[...] = jnp.broadcast_to(line[None], out_ref.shape)
    pair_ref[0] = second
    pair_ref[1] = image
    scalar_ref[...] = jnp.where(lane == 0, alpha, jnp.where(lane == 1, beta, 0.0))


def last_kernel(total_entries, pair_ref, scalar_ref, line_ref, mode_ref, coefficient_ref):
    lines = line_ref[:, 0, :]
    alpha = jnp.sum(lines[:, 0:1], axis=0, keepdims=True) / total_entries
    away = lines[:, 2:3] - alpha
    parts = lines[:, 3:4] + away * (away * lines[:, 1:2] + 2.0 * lines[:, 4:5])
    beta = jnp.sqrt(jnp.sum(parts, axis=0, keepdims=True) / total_entries + norm_eps)
    mode = (pair_ref[1] - alpha * pair_ref[0]) / beta
    mode_ref[...] = mode[: mode_ref.shape[0]]
    for at, value in enumerate((scalar_ref[0:1, 0:1], scalar_ref[0:1, 1:2], alpha, beta)):
        coefficient_ref[at] = jnp.sum(value)


def local(config, start, tile_list, tile_count):
    dof, member = config.shape
    row_devices = lax.axis_size("row")
    col_devices = lax.axis_size("col")
    devices = row_devices * col_devices
    total_entries = float(dof * member * devices)
    period = (5.0, 5.0, 3.5 * (member // 16))
    slots = tile_list.shape[2]
    longest = (row_devices + col_devices) * slots + 1

    def shaped(*shape):
        return jax.ShapeDtypeStruct(shape, jnp.float32)

    def everywhere(copies):
        return lax.all_to_all(copies, ("row", "col"), 0, 0, tiled=True)

    params = pltpu.CompilerParams(vmem_limit_bytes=VMEM_LIMIT)
    vmem = pl.BlockSpec(memory_space=pltpu.VMEM)
    smem = pl.BlockSpec(memory_space=pltpu.SMEM)

    outside = pl.BlockSpec(memory_space=pl.ANY)
    packed = pl.pallas_call(
        pack_kernel,
        out_shape=shaped(devices, 1, (LIST_ROW + 1) * member),
        in_specs=[outside] * 4,
        out_specs=vmem,
        scratch_shapes=[
            pltpu.VMEM((dof, member), jnp.float32),
            pltpu.VMEM((dof, member), jnp.float32),
            pltpu.SMEM((1, tile_list.shape[3], 1, slots), jnp.int32),
            pltpu.SMEM((1, 1), jnp.int32),
            pltpu.SemaphoreType.DMA((4,)),
        ],
        compiler_params=pltpu.CompilerParams(vmem_limit_bytes=PACK_LIMIT),
    )(config, start, jnp.transpose(tile_list, (0, 3, 1, 2)), tile_count)
    together = everywhere(packed)

    held_rows = HELD // GROUP * (TERMS * GROUP * SUB)
    image, items, terms, kept = pl.pallas_call(
        functools.partial(first_kernel, row_devices, col_devices, slots, period),
        out_shape=(
            shaped(devices, 1, dof * member),
            jax.ShapeDtypeStruct((1 + longest * (member // SUB) + GROUP * UNROLL,), jnp.int32),
            shaped(held_rows, member),
            shaped(2, member),
        ),
        in_specs=[vmem],
        out_specs=(vmem, smem, vmem, vmem),
        scratch_shapes=[
            pltpu.SMEM((longest + TESTS,), jnp.int32),
            pltpu.VMEM((row_devices + col_devices, member), jnp.int32),
            pltpu.SMEM((row_devices + col_devices, member), jnp.int32),
            pltpu.SemaphoreType.DMA,
        ],
        compiler_params=params,
    )(together)
    image = everywhere(image)

    line, pair, scalars = pl.pallas_call(
        functools.partial(second_kernel, col_devices, total_entries, period),
        out_shape=(shaped(devices, 1, member), shaped(2, SUB, member), shaped(1, member)),
        in_specs=[smem] + [vmem] * 4,
        out_specs=(vmem, vmem, vmem),
        scratch_shapes=[
            pltpu.VMEM((devices, 1, dof * member), jnp.float32),
        ],
        compiler_params=params,
    )(items, terms, kept, together, image)
    line = everywhere(line)

    mode, coefficients = pl.pallas_call(
        functools.partial(last_kernel, total_entries),
        out_shape=(shaped(dof, member), shaped(4)),
        in_specs=[vmem] * 3,
        out_specs=(vmem, smem),
        compiler_params=params,
    )(pair, scalars, line)
    return (coefficients, mode)


def solution(mesh):
    placed = (
        P(None, ("row", "col")),
        P(None, ("row", "col")),
        P("row", "col", None, None),
        P("row", "col"),
    )
    return jax.shard_map(
        local, mesh=mesh, in_specs=placed, out_specs=(P(), P(None, ("row", "col"))), check_vma=False
    )
```
